32 devices in a mesh: gx: 4 (over z), gy: 4 (over x, core), ha: 2 (over y).
Axes of the slice: x: 2, y: 2, z: 4, core: 2. Of those that a mesh axis runs over, the one named last changes fastest.
Arguments:
- offsets: float32 [3, 8, 8, 4, 128], P(None, 'gx', 'gy', 'ha'), may hold values from 0 to 1
- forces: float32 [3, 8, 8, 4, 128], P(None, 'gx', 'gy', 'ha'), may hold values from -6 to 6
- counts: int32 [8, 8, 4], P('gx', 'gy', 'ha'), may hold values from 16 to 128, as said below
Outputs:
- velocity: float32 [3, 8, 8, 4, 128], P(None, 'gx', 'gy', 'ha')
The draws below stay inside these ranges and needn't reach their ends.
Inputs may be any that keep to these rules, and one draw needn't show every extreme that they name: `counts`: A bin is heavy when its count exceeds 64. The 16 bins that two devices differing only in their ha index hold together include at most 8 heavy bins; in every draw some such pair holds exactly 8, all on one device; some bin holds exactly 128.
All inputs are finite; a program needn't handle non-finite values.
Results may differ from the reference program's by a relative error of at most 0.0003.
Values sent between devices are 32-bit elements; how exact they have to be, the bound alone decides.
No kernel may reach another device: no remote copies, remote signals or barrier semaphores. Data moves between devices by JAX's collectives and lax.ppermute only.
A program may use at most 64 MiB of HBM per device.

```python
import math
import jax
import jax.numpy as jnp
from jax import lax

CAP = 128
HALF = 64
BXY = 2
BZ = 2
NBX = 8
NBY = 8
NBZ = 4
NB_DEV = 8


def draw_counts(key, part):
    pair_x = NBX // BXY
    pair_y = NBY // BXY
    per_pair = BXY * BXY * NBZ
    key_score = jax.random.fold_in(key, 11)
    key_many = jax.random.fold_in(key, 12)
    key_light = jax.random.fold_in(key, 13)
    key_heavy = jax.random.fold_in(key, 14)
    raw_score = jax.random.randint(key_score, (pair_x, pair_y, BXY, BXY, NBZ), 0, 1 << 20)
    index_a = jnp.arange(BXY, dtype=jnp.int32)[None, None, :, None, None]
    index_b = jnp.arange(BXY, dtype=jnp.int32)[None, None, None, :, None]
    index_z = jnp.arange(NBZ, dtype=jnp.int32)[None, None, None, None, :]
    local_ids = index_a * (BXY * NBZ) + index_b * NBZ + index_z
    first_pair = (jnp.arange(pair_x, dtype=jnp.int32)[:, None] == 0) & (jnp.arange(pair_y, dtype=jnp.int32)[None, :] == 0)
    lift = jnp.where(first_pair[:, :, None, None, None], index_z // BZ * (1 << 28), 0)
    score = raw_score * per_pair + local_ids + lift
    score = score.reshape(pair_x, pair_y, per_pair)
    ranks = jnp.argsort(jnp.argsort(score, axis=2), axis=2).astype(jnp.int32)
    many_heavy = jax.random.randint(key_many, (pair_x, pair_y), 0, NB_DEV + 1)
    many_heavy = jnp.where(first_pair, NB_DEV, many_heavy)
    heavy_flag = ranks < many_heavy[:, :, None]
    light_count = jax.random.randint(key_light, (pair_x, pair_y, per_pair), CAP // 8, HALF + 1)
    heavy_count = jax.random.randint(key_heavy, (pair_x, pair_y, per_pair), HALF + 1, CAP + 1)
    result = jnp.where(heavy_flag, heavy_count, light_count)
    result = jnp.where(first_pair[:, :, None] & (ranks == 0), CAP, result)
    result = result.reshape(pair_x, pair_y, BXY, BXY, NBZ).transpose(0, 2, 1, 3, 4)
    return result.reshape(NBX, NBY, NBZ).astype(jnp.int32)


def steps_of(stream_key, shape, cuts, least, largest):
    gain, own = 1.0, jax.random.fold_in(stream_key, 6)
    for position, shards_of in cuts:
        draws = jnp.exp(jax.random.uniform(jax.random.fold_in(own, position), (shards_of,), jnp.float32, least / len(cuts), largest / len(cuts)))
        gain = gain * jnp.repeat(draws, shape[position] // shards_of).reshape([-1 if axis == position else 1 for axis in range(len(shape))])
    return gain


def centred(own_key, dims, deviation, limit, pieces=(), kind=jnp.bfloat16):
    entries = jax.random.normal(own_key, dims, jnp.float32) * deviation
    if len(pieces) > 0:
        entries = steps_of(own_key, dims, pieces, -0.22, 0.18) * entries
    return jnp.clip(entries, min=-limit, max=limit).astype(kind)


def setup_inputs(seed: int = 0) -> dict:
    splits = jax.random.split(jax.random.key(seed), 4)
    return {
        "offsets": jnp.clip(1.0 * jax.random.uniform(splits[0], (3, NBX, NBY, NBZ, CAP), jnp.float32) ** steps_of(splits[0], (3, NBX, NBY, NBZ, CAP), ((1, 4), (2, 4), (3, 2)), -0.2, 0.2), 0.0, 1.0),
        "forces": centred(splits[1], (3, NBX, NBY, NBZ, CAP), 1.0, 6.0, ((1, 4), (2, 4), (3, 2)), jnp.float32),
        "counts": draw_counts(jax.random.fold_in(splits[3], 71), 0),
    }


SPLIT_XI = 2.0
SOFT_SQ = 0.01
GAUSS_COEF = 2.0 * SPLIT_XI / math.sqrt(math.pi)
STOKES_NORM = 1.0 / (8.0 * math.pi)

def pair_kernel(targets, row_ids, source_data, capacity):
    n_source = source_data.shape[1]
    flat_ids = jnp.arange(n_source, dtype=jnp.int32)
    neighbour = flat_ids // capacity
    step_x = (neighbour // 9 - 1).astype(jnp.float32)
    step_y = (neighbour // 3 % 3 - 1).astype(jnp.float32)
    step_z = (neighbour % 3 - 1).astype(jnp.float32)
    delta_x = targets[0][:, None] - (source_data[0] + step_x)[None, :]
    delta_y = targets[1][:, None] - (source_data[1] + step_y)[None, :]
    delta_z = targets[2][:, None] - (source_data[2] + step_z)[None, :]
    square = delta_x * delta_x + delta_y * delta_y + delta_z * delta_z + SOFT_SQ
    radius = jnp.sqrt(square)
    tail_erfc = jax.scipy.special.erfc(SPLIT_XI * radius)
    gaussian = jnp.exp(-SPLIT_XI * SPLIT_XI * square)
    coef_c = tail_erfc / radius + GAUSS_COEF * (2.0 * SPLIT_XI * SPLIT_XI * square - 3.0) * gaussian
    coef_d = (tail_erfc / radius + GAUSS_COEF * (1.0 - 2.0 * SPLIT_XI * SPLIT_XI * square) * gaussian) / square
    keep_pair = flat_ids[None, :] != 13 * capacity + row_ids[:, None]
    coef_c = jnp.where(keep_pair, coef_c, 0.0)
    coef_d = jnp.where(keep_pair, coef_d, 0.0)
    force_x = source_data[3][None, :]
    force_y = source_data[4][None, :]
    force_z = source_data[5][None, :]
    along_d = coef_d * (delta_x * force_x + delta_y * force_y + delta_z * force_z)
    vel_x = lax.optimization_barrier(jnp.sum(coef_c * force_x + along_d * delta_x, axis=1))
    vel_y = lax.optimization_barrier(jnp.sum(coef_c * force_y + along_d * delta_y, axis=1))
    vel_z = lax.optimization_barrier(jnp.sum(coef_c * force_z + along_d * delta_z, axis=1))
    return STOKES_NORM * jnp.stack([vel_x, vel_y, vel_z])

def reference(offsets, forces, counts):
    slot_ids = jnp.arange(CAP, dtype=jnp.int32)
    live_mask = (slot_ids[None, None, None, :] < counts[..., None]).astype(jnp.float32)
    packed = jnp.concatenate([offsets, forces * live_mask[None]], axis=0)
    wrapped = jnp.pad(packed, ((0, 0), (1, 1), (1, 1), (1, 1), (0, 0)), mode='wrap')
    zero_index = jnp.zeros((), jnp.int32)

    def one_bin(flat_id):
        flat_id = flat_id.astype(jnp.int32)
        bin_x = (flat_id // (NBY * NBZ)).astype(jnp.int32)
        bin_y = (flat_id // NBZ % NBY).astype(jnp.int32)
        bin_z = (flat_id % NBZ).astype(jnp.int32)
        window = lax.dynamic_slice(wrapped, (zero_index, bin_x, bin_y, bin_z, zero_index), (6, 3, 3, 3, CAP))
        source_data = window.reshape(6, 27 * CAP)
        targets = window[0:3, 1, 1, 1, :]
        return pair_kernel(targets, slot_ids, source_data, CAP)
    result = lax.map(one_bin, jnp.arange(NBX * NBY * NBZ, dtype=jnp.int32))
    result = result.reshape(NBX, NBY, NBZ, 3, CAP).transpose(3, 0, 1, 2, 4)
    return result * live_mask[None]
```

```python
import functools
import math

import jax
import jax.numpy as jnp
from jax import lax
from jax.experimental import pallas as pl
from jax.experimental.pallas import tpu as pltpu
from jax.sharding import PartitionSpec as P

SPLIT_XI = 2.0
SOFT_SQ = 0.01
GAUSS_COEF = 2.0 * SPLIT_XI / math.sqrt(math.pi)
STOKES_NORM = 1.0 / (8.0 * math.pi)

SOFT_U = SPLIT_XI * SPLIT_XI * SOFT_SQ
LOG2_E = math.log2(math.e)
LOG2_G = math.log2(GAUSS_COEF)
SELF_C = math.erfc(math.sqrt(SOFT_U)) / math.sqrt(SOFT_SQ) + GAUSS_COEF * (
    2.0 * SOFT_U - 3.0
) * math.exp(-SOFT_U)

LANES = 128
ROWS = 8
CHUNK = 32
BLOCK = 2
COUNT_ROW = 6


def assemble(ext, cells, pieces):
    own, other, x_lo, x_hi, y_lo, y_hi = pieces
    row = lax.broadcasted_iota(jnp.int32, (ROWS, LANES), 0)
    lane = lax.broadcasted_iota(jnp.int32, (ROWS, LANES), 1)
    scale = jnp.where(row < 3, SPLIT_XI, 1.0)
    shift = jnp.where(row < 3, -0.5 * SPLIT_XI, 0.0)
    size_x, size_y, size_z = cells
    held = jnp.zeros((ROWS, LANES), jnp.float32)
    for ix in range(size_x + 2):
        for iy in range(size_y + 2):
            for iz in range(2 * size_z):
                if iy == 0:
                    tile = y_lo[ix, 0, iz]
                elif iy == size_y + 1:
                    tile = y_hi[ix, 0, iz]
                elif ix == 0:
                    tile = x_lo[0, iy - 1, iz]
                elif ix == size_x + 1:
                    tile = x_hi[0, iy - 1, iz]
                elif iz < size_z:
                    tile = own[ix - 1, iy - 1, iz]
                else:
                    tile = other[ix - 1, iy - 1, iz - size_z]
                cell = (ix * (size_y + 2) + iy) * 2 * size_z + iz
                ext[cell] = tile * scale + shift
                held = jnp.where(lane == cell, tile, held)
    return held


def pair_block(target, source):
    delta = [target[i] - source[i : i + 1] for i in range(3)]
    force = [source[3 + i : 4 + i] for i in range(3)]
    u = (delta[0] * delta[0] + SOFT_U) + delta[1] * delta[1] + delta[2] * delta[2]
    inv = lax.rsqrt(u)
    tail = (1.0 - lax.erf(u * inv)) * inv
    gauss = jnp.exp2(LOG2_G - u * LOG2_E)
    rest = gauss * (u - 1.5)
    coef_c = tail + rest
    coef_d = ((tail - rest) - gauss) * (inv * inv)
    along = coef_d * (delta[0] * force[0] + delta[1] * force[1] + delta[2] * force[2])
    return [coef_c * force[i] + along * delta[i] for i in range(3)]


def near_kernel(cells, *refs):
    pieces, (out_ref, ext, step_ref, count_v, count_s, sem, listed, spread, summed) = refs[:6], refs[6:]
    size_x, size_y, size_z = cells
    n_z = 2 * size_z
    row = lax.broadcasted_iota(jnp.int32, (ROWS, LANES), 0)
    lane = lax.broadcasted_iota(jnp.int32, (ROWS, LANES), 1)
    zero_tile = jnp.zeros((ROWS, LANES), jnp.float32)

    held = assemble(ext, cells, pieces)
    count_v[...] = held.astype(jnp.int32)
    copy = pltpu.make_async_copy(count_v, count_s, sem)
    copy.start()
    steps = [(0, 0, 0)] + [
        (a, b, c)
        for a in (-1, 0, 1)
        for b in (-1, 0, 1)
        for c in (-1, 0, 1)
        if (a, b, c) != (0, 0, 0)
    ]
    for n, step in enumerate(steps):
        moved = zero_tile
        for i in range(3):
            moved = jnp.where(row == i, SPLIT_XI * step[i], moved)
        step_ref[n] = moved
    copy.wait()

    def one_bin(flat_id, carry):
        bin_x = flat_id // (size_y * size_z)
        bin_y = flat_id // size_z % size_y
        bin_z = flat_id % size_z

        def cell_of(step):
            at_z = lax.rem(bin_z + step[2] + n_z, n_z)
            return ((bin_x + 1 + step[0]) * (size_y + 2) + (bin_y + 1 + step[1])) * n_z + at_z

        current = zero_tile
        filled = jnp.int32(0)
        for n, step in enumerate(steps):
            cell = cell_of(step)
            count = count_s[COUNT_ROW, cell]
            tile_id = lax.shift_right_logical(filled, 7)
            at = lax.bitwise_and(filled, LANES - 1)
            moved = pltpu.roll(ext[cell] + step_ref[n], at, 1)
            behind = lane >= at
            current = jnp.where(behind, moved, current)
            spill = jnp.where(behind, 0.0, moved)
            listed[tile_id] = current
            listed[tile_id + 1] = spill
            filled = filled + count
            current = jnp.where(at + count >= LANES, spill, current)
        last = lax.shift_right_logical(filled, 7)
        for more in range(1, BLOCK):
            listed[last + more] = zero_tile
        n_blocks = lax.div(filled + BLOCK * LANES - 1, BLOCK * LANES)

        own_cell = cell_of((0, 0, 0))
        own_tile = ext[own_cell]
        own_count = count_s[COUNT_ROW, own_cell]
        columns = jnp.transpose(jnp.concatenate([own_tile] * (LANES // ROWS), axis=0))
        for i in range(3):
            spread[i] = jnp.broadcast_to(columns[:, i : i + 1], (LANES, LANES))

        def one_chunk(chunk, carry):
            first = pl.multiple_of(chunk * CHUNK, CHUNK)
            target = [spread[i, pl.ds(first, CHUNK), :] for i in range(3)]

            def one_block(block, sums):
                sums = list(sums)
                for b in range(BLOCK):
                    terms = pair_block(target, listed[block * BLOCK + b])
                    sums = [s + t for s, t in zip(sums, terms)]
                return tuple(sums)

            zero = jnp.zeros((CHUNK, LANES), jnp.float32)
            sums = lax.fori_loop(0, n_blocks, one_block, (zero, zero, zero))
            wide = lax.broadcasted_iota(jnp.int32, (CHUNK, LANES), 1)
            merged = zero
            for i in range(3):
                merged = jnp.where(wide == i, jnp.sum(sums[i], axis=1, keepdims=True), merged)
            summed[pl.ds(first, CHUNK), :] = merged
            return carry

        lax.fori_loop(0, lax.div(own_count + CHUNK - 1, CHUNK), one_chunk, 0)
        result = jnp.transpose(summed[...])[:ROWS]
        slot = lax.broadcasted_iota(jnp.int32, (1, LANES), 1)
        for i in range(3):
            velocity = (2.0 * STOKES_NORM) * result[i : i + 1] - (STOKES_NORM * SELF_C) * own_tile[
                3 + i : 4 + i
            ]
            velocity = jnp.where(slot < own_count, velocity, 0.0)
            out_ref[i, bin_x, bin_y, pl.ds(bin_z, 1), :] = velocity
        return carry

    lax.fori_loop(0, size_x * size_y * size_z, one_bin, 0)


def shifted(array, axis, dim):
    size, length = lax.axis_size(axis), array.shape[dim]
    up = [(i, (i + 1) % size) for i in range(size)]
    down = [(j, i) for i, j in up]
    before = lax.ppermute(lax.slice_in_dim(array, length - 1, length, axis=dim), axis, up)
    after = lax.ppermute(lax.slice_in_dim(array, 0, 1, axis=dim), axis, down)
    return before, after


def on_device(offsets, forces, counts):
    cells = offsets.shape[1:4]
    slots = offsets.shape[4]
    n_cells = (cells[0] + 2) * (cells[1] + 2) * 2 * cells[2]
    live = lax.broadcasted_iota(jnp.int32, cells + (slots,), 3) < counts[..., None]
    spread = jnp.broadcast_to(counts.astype(jnp.float32)[..., None], cells + (slots,))
    rows = [offsets[i] for i in range(3)] + [jnp.where(live, forces[i], 0.0) for i in range(3)]
    rows = rows + [spread, jnp.zeros_like(spread)]
    own = jnp.stack(rows, axis=3)

    size = lax.axis_size("ha")
    other = lax.ppermute(own, "ha", [(i, (i + 1) % size) for i in range(size)])
    column = jnp.concatenate([own, other], axis=2)
    x_lo, x_hi = shifted(column, "gx", 0)
    wide = jnp.concatenate([x_lo, column, x_hi], axis=0)
    y_lo, y_hi = shifted(wide, "gy", 1)

    whole = pl.BlockSpec(memory_space=pltpu.VMEM)
    return pl.pallas_call(
        functools.partial(near_kernel, cells),
        out_shape=jax.ShapeDtypeStruct((3,) + cells + (slots,), jnp.float32),
        in_specs=[whole] * 6,
        out_specs=whole,
        scratch_shapes=[
            pltpu.VMEM((n_cells, ROWS, LANES), jnp.float32),
            pltpu.VMEM((27, ROWS, LANES), jnp.float32),
            pltpu.VMEM((ROWS, LANES), jnp.int32),
            pltpu.SMEM((ROWS, LANES), jnp.int32),
            pltpu.SemaphoreType.DMA,
            pltpu.VMEM((28 + BLOCK, ROWS, LANES), jnp.float32),
            pltpu.VMEM((3, LANES, LANES), jnp.float32),
            pltpu.VMEM((LANES, LANES), jnp.float32),
        ],
        compiler_params=pltpu.CompilerParams(vmem_limit_bytes=16 << 20),
        name="near_field",
    )(own, other, x_lo, x_hi, y_lo, y_hi)


def solution(mesh):
    in_specs = (
        P(None, "gx", "gy", "ha", None),
        P(None, "gx", "gy", "ha", None),
        P("gx", "gy", "ha"),
    )
    out_specs = P(None, "gx", "gy", "ha", None)
    return jax.shard_map(on_device, mesh=mesh, in_specs=in_specs, out_specs=out_specs, check_vma=False)
```

```python
import functools
import math

import jax
import jax.numpy as jnp
from jax import lax
from jax.experimental import pallas as pl
from jax.experimental.pallas import tpu as pltpu
from jax.sharding import PartitionSpec as P

SPLIT_XI = 2.0
SOFT_SQ = 0.01
GAUSS_COEF = 2.0 * SPLIT_XI / math.sqrt(math.pi)
STOKES_NORM = 1.0 / (8.0 * math.pi)

SOFT_U = SPLIT_XI * SPLIT_XI * SOFT_SQ
LOG2_E = math.log2(math.e)
LOG2_G = math.log2(GAUSS_COEF)
SELF_C = math.erfc(math.sqrt(SOFT_U)) / math.sqrt(SOFT_SQ) + GAUSS_COEF * (
    2.0 * SOFT_U - 3.0
) * math.exp(-SOFT_U)

LANES = 128
ROWS = 8
CHUNK = 32
BLOCK = 2
COUNT_ROW = 6


def pack_kernel(cells, count_ref, offset_ref, force_ref, out_ref):
    slot = lax.broadcasted_iota(jnp.int32, (1, LANES), 1)
    for ix in range(cells[0]):
        for iy in range(cells[1]):
            for iz in range(cells[2]):
                count = count_ref[ix, iy, iz]
                for i in range(3):
                    position = offset_ref[i, ix, iy, iz : iz + 1, :]
                    out_ref[ix, iy, iz, i : i + 1, :] = position * SPLIT_XI - 0.5 * SPLIT_XI
                    force = force_ref[i, ix, iy, iz : iz + 1, :]
                    out_ref[ix, iy, iz, 3 + i : 4 + i, :] = jnp.where(slot < count, force, 0.0)
                out_ref[ix, iy, iz, 6:8, :] = jnp.full((2, LANES), count, jnp.int32).astype(jnp.float32)


def window_kernel(cells, n_y, at_ref, gathered_ref, out_ref):
    size_x, size_y, size_z = cells
    gy, ha = at_ref[0], at_ref[1]
    for iy in range(size_y + 2):
        from_y = lax.rem(gy * size_y + iy - 1 + n_y, n_y)
        for iz in range(2 * size_z):
            from_ha = ha if iz < size_z else 1 - ha
            device = 2 * lax.div(from_y, size_y) + from_ha
            for ix in range(size_x):
                out_ref[ix, iy, iz] = gathered_ref[device, ix, lax.rem(from_y, size_y), iz % size_z]


def assemble(ext, cells, pieces):
    inner, x_lo, x_hi = pieces
    lane = lax.broadcasted_iota(jnp.int32, (ROWS, LANES), 1)
    size_x, size_y, size_z = cells
    held = jnp.zeros((ROWS, LANES), jnp.float32)
    for ix in range(size_x + 2):
        for iy in range(size_y + 2):
            for iz in range(2 * size_z):
                if ix == 0:
                    tile = x_lo[0, iy, iz]
                elif ix == size_x + 1:
                    tile = x_hi[0, iy, iz]
                else:
                    tile = inner[ix - 1, iy, iz]
                cell = (ix * (size_y + 2) + iy) * 2 * size_z + iz
                ext[cell] = tile
                held = jnp.where(lane == cell, tile, held)
    return held


def pair_block(target, source):
    delta = [target[i] - source[i : i + 1] for i in range(3)]
    force = [source[3 + i : 4 + i] for i in range(3)]
    u = (delta[0] * delta[0] + SOFT_U) + delta[1] * delta[1] + delta[2] * delta[2]
    inv = lax.rsqrt(u)
    tail = (1.0 - lax.erf(u * inv)) * inv
    gauss = jnp.exp2(LOG2_G - u * LOG2_E)
    rest = gauss * (u - 1.5)
    coef_c = tail + rest
    coef_d = ((tail - rest) - gauss) * (inv * inv)
    along = coef_d * (delta[0] * force[0] + delta[1] * force[1] + delta[2] * force[2])
    return [coef_c * force[i] + along * delta[i] for i in range(3)]


def near_kernel(cells, *refs):
    pieces, (out_ref, ext, step_ref, count_v, count_s, sem, listed, spread, summed) = refs[:3], refs[3:]
    size_x, size_y, size_z = cells
    n_z = 2 * size_z
    row = lax.broadcasted_iota(jnp.int32, (ROWS, LANES), 0)
    lane = lax.broadcasted_iota(jnp.int32, (ROWS, LANES), 1)
    zero_tile = jnp.zeros((ROWS, LANES), jnp.float32)

    held = assemble(ext, cells, pieces)
    count_v[...] = held.astype(jnp.int32)
    copy = pltpu.make_async_copy(count_v, count_s, sem)
    copy.start()
    steps = [(0, 0, 0)] + [
        (a, b, c)
        for a in (-1, 0, 1)
        for b in (-1, 0, 1)
        for c in (-1, 0, 1)
        if (a, b, c) != (0, 0, 0)
    ]
    for n, step in enumerate(steps):
        moved = zero_tile
        for i in range(3):
            moved = jnp.where(row == i, SPLIT_XI * step[i], moved)
        step_ref[n] = moved
    copy.wait()

    def one_bin(flat_id, carry):
        bin_x = flat_id // (size_y * size_z)
        bin_y = flat_id // size_z % size_y
        bin_z = flat_id % size_z

        def cell_of(step):
            at_z = lax.rem(bin_z + step[2] + n_z, n_z)
            return ((bin_x + 1 + step[0]) * (size_y + 2) + (bin_y + 1 + step[1])) * n_z + at_z

        current = zero_tile
        filled = jnp.int32(0)
        for n, step in enumerate(steps):
            cell = cell_of(step)
            count = count_s[COUNT_ROW, cell]
            tile_id = lax.shift_right_logical(filled, 7)
            at = lax.bitwise_and(filled, LANES - 1)
            moved = pltpu.roll(ext[cell] + step_ref[n], at, 1)
            behind = lane >= at
            current = jnp.where(behind, moved, current)
            spill = jnp.where(behind, 0.0, moved)
            listed[tile_id] = current
            listed[tile_id + 1] = spill
            filled = filled + count
            current = jnp.where(at + count >= LANES, spill, current)
        last = lax.shift_right_logical(filled, 7)
        for more in range(1, BLOCK):
            listed[last + more] = zero_tile
        n_blocks = lax.div(filled + BLOCK * LANES - 1, BLOCK * LANES)

        own_cell = cell_of((0, 0, 0))
        own_tile = ext[own_cell]
        own_count = count_s[COUNT_ROW, own_cell]
        columns = jnp.transpose(jnp.concatenate([own_tile] * (LANES // ROWS), axis=0))
        for i in range(3):
            spread[i] = jnp.broadcast_to(columns[:, i : i + 1], (LANES, LANES))

        def one_chunk(chunk, carry):
            first = pl.multiple_of(chunk * CHUNK, CHUNK)
            target = [spread[i, pl.ds(first, CHUNK), :] for i in range(3)]

            def one_block(block, sums):
                sums = list(sums)
                for b in range(BLOCK):
                    terms = pair_block(target, listed[block * BLOCK + b])
                    sums = [s + t for s, t in zip(sums, terms)]
                return tuple(sums)

            zero = jnp.zeros((CHUNK, LANES), jnp.float32)
            sums = lax.fori_loop(0, n_blocks, one_block, (zero, zero, zero))
            wide = lax.broadcasted_iota(jnp.int32, (CHUNK, LANES), 1)
            merged = zero
            for i in range(3):
                merged = jnp.where(wide == i, jnp.sum(sums[i], axis=1, keepdims=True), merged)
            summed[pl.ds(first, CHUNK), :] = merged
            return carry

        lax.fori_loop(0, lax.div(own_count + CHUNK - 1, CHUNK), one_chunk, 0)
        result = jnp.transpose(summed[...])[:ROWS]
        slot = lax.broadcasted_iota(jnp.int32, (1, LANES), 1)
        for i in range(3):
            velocity = (2.0 * STOKES_NORM) * result[i : i + 1] - (STOKES_NORM * SELF_C) * own_tile[
                3 + i : 4 + i
            ]
            velocity = jnp.where(slot < own_count, velocity, 0.0)
            out_ref[i, bin_x, bin_y, pl.ds(bin_z, 1), :] = velocity
        return carry

    lax.fori_loop(0, size_x * size_y * size_z, one_bin, 0)


def shifted(array, axis, dim):
    size, length = lax.axis_size(axis), array.shape[dim]
    up = [(i, (i + 1) % size) for i in range(size)]
    down = [(j, i) for i, j in up]
    before = lax.ppermute(lax.slice_in_dim(array, length - 1, length, axis=dim), axis, up)
    after = lax.ppermute(lax.slice_in_dim(array, 0, 1, axis=dim), axis, down)
    return before, after


def on_device(offsets, forces, counts):
    cells = offsets.shape[1:4]
    slots = offsets.shape[4]
    n_cells = (cells[0] + 2) * (cells[1] + 2) * 2 * cells[2]
    whole = pl.BlockSpec(memory_space=pltpu.VMEM)
    scalars = pl.BlockSpec(memory_space=pltpu.SMEM)
    own = pl.pallas_call(
        functools.partial(pack_kernel, cells),
        out_shape=jax.ShapeDtypeStruct(cells + (ROWS, slots), jnp.float32),
        in_specs=[scalars, whole, whole],
        out_specs=whole,
        name="pack",
    )(counts, offsets, forces)
    gathered = lax.all_gather(own, ("gy", "ha"))
    at = jnp.stack([lax.axis_index("gy"), lax.axis_index("ha")])
    inner = pl.pallas_call(
        functools.partial(window_kernel, cells, lax.axis_size("gy") * cells[1]),
        out_shape=jax.ShapeDtypeStruct((cells[0], cells[1] + 2, 2 * cells[2], ROWS, slots), jnp.float32),
        in_specs=[scalars, whole],
        out_specs=whole,
        name="window",
    )(at, gathered)
    x_lo, x_hi = shifted(inner, "gx", 0)
    return pl.pallas_call(
        functools.partial(near_kernel, cells),
        out_shape=jax.ShapeDtypeStruct((3,) + cells + (slots,), jnp.float32),
        in_specs=[whole] * 3,
        out_specs=whole,
        scratch_shapes=[
            pltpu.VMEM((n_cells, ROWS, LANES), jnp.float32),
            pltpu.VMEM((27, ROWS, LANES), jnp.float32),
            pltpu.VMEM((ROWS, LANES), jnp.int32),
            pltpu.SMEM((ROWS, LANES), jnp.int32),
            pltpu.SemaphoreType.DMA,
            pltpu.VMEM((28 + BLOCK, ROWS, LANES), jnp.float32),
            pltpu.VMEM((3, LANES, LANES), jnp.float32),
            pltpu.VMEM((LANES, LANES), jnp.float32),
        ],
        compiler_params=pltpu.CompilerParams(vmem_limit_bytes=16 << 20),
        name="near_field",
    )(inner, x_lo, x_hi)


def solution(mesh):
    in_specs = (
        P(None, "gx", "gy", "ha", None),
        P(None, "gx", "gy", "ha", None),
        P("gx", "gy", "ha"),
    )
    out_specs = P(None, "gx", "gy", "ha", None)
    return jax.shard_map(on_device, mesh=mesh, in_specs=in_specs, out_specs=out_specs, check_vma=False)
```

```python
import functools
import math

import jax
import jax.numpy as jnp
from jax import lax
from jax.experimental import pallas as pl
from jax.experimental.pallas import tpu as pltpu
from jax.sharding import PartitionSpec as P

SPLIT_XI = 2.0
SOFT_SQ = 0.01
GAUSS_COEF = 2.0 * SPLIT_XI / math.sqrt(math.pi)
STOKES_NORM = 1.0 / (8.0 * math.pi)

SOFT_U = SPLIT_XI * SPLIT_XI * SOFT_SQ
LOG2_E = math.log2(math.e)
LOG2_G = math.log2(GAUSS_COEF)
SELF_C = math.erfc(math.sqrt(SOFT_U)) / math.sqrt(SOFT_SQ) + GAUSS_COEF * (
    2.0 * SOFT_U - 3.0
) * math.exp(-SOFT_U)

LANES = 128
ROWS = 8
CHUNK = 64
WIDE = 2
BLOCK = WIDE * LANES
DEPTH = 64
COUNT_ROW = 3
FORCE_ROW = 4


def rows_and_lanes(shape=(ROWS, LANES)):
    return lax.broadcasted_iota(jnp.int32, shape, 0), lax.broadcasted_iota(jnp.int32, shape, 1)


def pack_kernel(cells, count_ref, offset_ref, force_ref, out_ref):
    slot = lax.broadcasted_iota(jnp.int32, (1, LANES), 1)
    for ix in range(cells[0]):
        for iy in range(cells[1]):
            for iz in range(cells[2]):
                count = count_ref[ix, iy, iz]
                filled = jnp.full((1, LANES), count, jnp.int32).astype(jnp.float32)
                for i in range(3):
                    position = offset_ref[i, ix, iy, iz : iz + 1, :]
                    out_ref[ix, iy, iz, i : i + 1, :] = position * SPLIT_XI - 0.5 * SPLIT_XI
                    force = force_ref[i, ix, iy, iz : iz + 1, :]
                    at = FORCE_ROW + i
                    out_ref[ix, iy, iz, at : at + 1, :] = jnp.where(slot < count, force, 0.0)
                out_ref[ix, iy, iz, 3:4, :] = filled
                out_ref[ix, iy, iz, 7:8, :] = filled


def compact(listed, base, sources):
    _, lane = rows_and_lanes()
    current = jnp.zeros((ROWS, LANES), jnp.float32)
    filled = jnp.int32(0)
    for tile, count in sources:
        tile_id = base + lax.shift_right_logical(filled, 7)
        at = lax.bitwise_and(filled, LANES - 1)
        moved = pltpu.roll(tile, at, 1)
        behind = lane >= at
        current = jnp.where(behind, moved, current)
        spill = jnp.where(behind, 0.0, moved)
        listed[tile_id] = current
        listed[tile_id + 1] = spill
        filled = filled + count
        current = jnp.where(at + count >= LANES, spill, current)
    last = base + lax.shift_right_logical(filled, 7)
    for more in range(1, WIDE):
        listed[last + more] = jnp.zeros((ROWS, LANES), jnp.float32)
    return filled


def parts_of(value):
    high = value.astype(jnp.bfloat16).astype(jnp.float32)
    rest = value - high
    middle = rest.astype(jnp.bfloat16).astype(jnp.float32)
    return high, middle, rest - middle


def completed(tile):
    row, _ = rows_and_lanes()
    wide = [jnp.broadcast_to(tile[i : i + 1], (ROWS, LANES)) for i in range(7)]
    norm = wide[0] * wide[0] + wide[1] * wide[1] + wide[2] * wide[2]
    work = wide[0] * wide[4] + wide[1] * wide[5] + wide[2] * wide[6]
    return jnp.where(row == 3, norm, jnp.where(row == 7, work, tile)), norm


def source_rows(tile):
    high, middle, low = parts_of(completed(tile)[0])
    one = jnp.ones((ROWS, LANES), jnp.float32)
    stack = [high, high, high, middle, middle, low, one, jnp.zeros_like(one)]
    return jnp.concatenate(stack, axis=0).astype(jnp.bfloat16)


def target_rows(tile):
    row, _ = rows_and_lanes()
    zero = jnp.zeros((ROWS, LANES), jnp.float32)
    full, norm = completed(tile)
    high, middle, low = (jnp.where(row < 3, -2.0 * part, 0.0) for part in parts_of(full))
    first = jnp.where(row == 3, 1.0, high)
    sizes = parts_of(norm + SOFT_U)
    constant = jnp.where(
        row == 0, sizes[0], jnp.where(row == 1, sizes[1], jnp.where(row == 2, sizes[2], 0.0))
    )
    square = [first, middle, low, first, middle, first]
    scale = jnp.where(row == 7, -1.0, -0.5)
    along = [pltpu.roll(part, 4, 0) * scale for part in square]
    return [
        jnp.transpose(jnp.concatenate(stack, axis=0)).astype(jnp.bfloat16)
        for stack in (square + [constant, zero], along + [zero, zero])
    ]


def pair_terms(u, along, tile):
    inv = lax.rsqrt(u)
    tail = (1.0 - lax.erf(u * inv)) * inv
    gauss = jnp.exp2(LOG2_G - u * LOG2_E)
    rest = gauss * (u - 1.5)
    coef_c = tail + rest
    coef_a = ((tail - rest) - gauss) * (inv * inv) * along
    terms = []
    for i in range(3):
        terms.append(coef_c * tile[FORCE_ROW + i : FORCE_ROW + i + 1] - coef_a * tile[i : i + 1])
    return terms + [coef_a]


def all_pairs(n_groups, chunks_of, blocks_of, max_chunks, max_blocks, refs):
    listed, source_f, target_u, target_s, buffers, acc, summed = refs

    def issue(buffer, group, chunk, block):
        at = pl.ds(pl.multiple_of((group * max_chunks + chunk) * CHUNK, CHUNK), CHUNK)
        factors = source_f[group * max_blocks + block]
        buffer[0] = jnp.dot(target_u[at, :], factors, preferred_element_type=jnp.float32)
        buffer[1] = jnp.dot(target_s[at, :], factors, preferred_element_type=jnp.float32)

    def process(buffer, group, block):
        sums = [acc[i] for i in range(4)]
        for b in range(WIDE):
            tile = listed[(group * max_blocks + block) * WIDE + b]
            at = slice(b * LANES, (b + 1) * LANES)
            terms = pair_terms(buffer[0, :, at], buffer[1, :, at], tile)
            sums = [s + t for s, t in zip(sums, terms)]
        for i in range(4):
            acc[i] = sums[i]

    def reduce(group, chunk):
        _, lane = rows_and_lanes((CHUNK, LANES))
        merged = jnp.zeros((CHUNK, LANES), jnp.float32)
        for i in range(4):
            merged = jnp.where(lane == i, jnp.sum(acc[i], axis=1, keepdims=True), merged)
            acc[i] = jnp.zeros((CHUNK, LANES), jnp.float32)
        at = pl.multiple_of((group * max_chunks + chunk) * CHUNK, CHUNK)
        summed[pl.ds(at, CHUNK), :] = merged

    total = jnp.int32(0)
    for group in range(n_groups):
        total = total + chunks_of[group] * blocks_of[group]
    acc[...] = jnp.zeros_like(acc)
    issue(buffers[0], 0, 0, 0)

    def two_items(pair, state):
        group, chunk, block = state
        for half in range(2):
            end_block = block + 1 == blocks_of[group]
            next_block = jnp.where(end_block, 0, block + 1)
            next_chunk = jnp.where(end_block, chunk + 1, chunk)
            end_chunk = next_chunk == chunks_of[group]
            next_chunk = jnp.where(end_chunk, 0, next_chunk)
            next_group = jnp.where(end_chunk, jnp.minimum(group + 1, n_groups - 1), group)
            issue(buffers[1 - half], next_group, next_chunk, next_block)
            process(buffers[half], group, block)

            @pl.when(jnp.logical_and(end_block, 2 * pair + half < total))
            def _():
                reduce(group, chunk)

            group, chunk, block = next_group, next_chunk, next_block
        return group, chunk, block

    zero = jnp.int32(0)
    lax.fori_loop(0, lax.div(total + 1, 2), two_items, (zero, zero, zero))


def inner_kernel(cells, count_ref, own_ref, out_ref, chunks_of, blocks_of, *refs):
    listed, source_f, target_u, target_s, buffer_a, buffer_b, acc, summed, result = refs
    row, lane = rows_and_lanes()
    n_bins = cells[0] * cells[1] * cells[2]
    bins = [(i, j, k) for i in range(cells[0]) for j in range(cells[1]) for k in range(cells[2])]
    sources, counts = [], []
    for at in bins:
        moved = jnp.zeros((ROWS, LANES), jnp.float32)
        for i in range(3):
            moved = jnp.where(row == i, SPLIT_XI * (at[i] - 0.5 * (cells[i] - 1)), moved)
        counts.append(count_ref[at])
        sources.append((own_ref[at] + moved, counts[-1]))
    filled = compact(listed, 0, sources)
    n_tiles = lax.div(filled + LANES - 1, LANES)
    n_blocks = lax.div(filled + BLOCK - 1, BLOCK)
    blocks_of[0] = n_blocks
    chunks_of[0] = lax.div(filled + CHUNK - 1, CHUNK)

    def prepare(block, carry):
        for b in range(WIDE):
            tile = listed[block * WIDE + b]
            source_f[block, :, b * LANES : (b + 1) * LANES] = source_rows(tile)
            at = pl.ds(pl.multiple_of((block * WIDE + b) * LANES, LANES), LANES)
            target_u[at, :], target_s[at, :] = target_rows(tile)
        return carry

    lax.fori_loop(0, n_blocks, prepare, 0)
    refs = (listed, source_f, target_u, target_s, (buffer_a, buffer_b), acc, summed)
    all_pairs(1, chunks_of, blocks_of, n_bins * LANES // CHUNK, n_bins // WIDE, refs)

    def finish(tile_id, carry):
        sums = jnp.transpose(summed[pl.ds(pl.multiple_of(tile_id * LANES, LANES), LANES), :])[:ROWS]
        tile = listed[tile_id]
        total = sums + tile * jnp.broadcast_to(sums[3:4], (ROWS, LANES))
        own = pltpu.roll(tile, ROWS - FORCE_ROW, 0)
        result[tile_id] = (2.0 * STOKES_NORM) * total - (STOKES_NORM * SELF_C) * own
        return carry

    lax.fori_loop(0, n_tiles, finish, 0)
    before = jnp.int32(0)
    for at, count in zip(bins, counts):
        tile_id = lax.shift_right_logical(before, 7)
        back = LANES - lax.bitwise_and(before, LANES - 1)
        turn = lax.bitwise_and(back, LANES - 1)
        part = jnp.where(
            lane < back, pltpu.roll(result[tile_id], turn, 1), pltpu.roll(result[tile_id + 1], turn, 1)
        )
        out_ref[at] = part
        before = before + count


def outer_kernel(cells, *refs):
    pieces, (inner_ref, out_ref), refs = refs[:6], refs[6:8], refs[8:]
    ext, count_v, count_s, sem, chunks_of, blocks_of = refs[:6]
    listed, source_f, target_u, target_s, buffer_a, buffer_b, acc, summed = refs[6:]
    own, other, x_lo, x_hi, y_lo, y_hi = pieces
    size_x, size_y, size_z = cells
    n_z = 2 * size_z
    n_bins = size_x * size_y * size_z
    row, lane = rows_and_lanes()

    held = jnp.zeros((ROWS, LANES), jnp.float32)
    for ix in range(size_x + 2):
        for iy in range(size_y + 2):
            for iz in range(n_z):
                if iy == 0:
                    tile = y_lo[ix, 0, iz]
                elif iy == size_y + 1:
                    tile = y_hi[ix, 0, iz]
                elif ix == 0:
                    tile = x_lo[0, iy - 1, iz]
                elif ix == size_x + 1:
                    tile = x_hi[0, iy - 1, iz]
                elif iz < size_z:
                    tile = own[ix - 1, iy - 1, iz]
                else:
                    tile = other[ix - 1, iy - 1, iz - size_z]
                cell = (ix * (size_y + 2) + iy) * n_z + iz
                ext[cell] = tile
                held = jnp.where(lane == cell, tile, held)
    count_v[...] = held.astype(jnp.int32)
    copy = pltpu.make_async_copy(count_v, count_s, sem)
    copy.start()
    copy.wait()

    max_tiles = listed.shape[0] // n_bins
    steps = [
        (a, b, c) for a in (0, -1, 1) for b in (0, -1, 1) for c in (0, -1, 1) if 1 in (a, b, c)
    ]

    def prepare(flat_id, carry):
        at = (flat_id // (size_y * size_z), flat_id // size_z % size_y, flat_id % size_z)
        out = [2 * i - 1 for i in at]
        moves = [
            jnp.where(row == i, (SPLIT_XI * out[i].astype(jnp.float32)), 0.0) for i in range(3)
        ]
        sources = []
        for step in steps:
            moved = sum(s * m for s, m in zip(step, moves) if s != 0)
            x, y, z = (i + s * o for i, s, o in zip(at, step, out))
            cell = ((x + 1) * (size_y + 2) + y + 1) * n_z + lax.rem(z + n_z, n_z)
            sources.append((ext[cell] + moved, count_s[COUNT_ROW, cell]))
        filled = compact(listed, flat_id * max_tiles, sources)
        n_blocks = lax.div(filled + BLOCK - 1, BLOCK)
        own_cell = ((at[0] + 1) * (size_y + 2) + at[1] + 1) * n_z + at[2]
        blocks_of[flat_id] = n_blocks
        chunks_of[flat_id] = lax.div(count_s[COUNT_ROW, own_cell] + CHUNK - 1, CHUNK)

        def factor(block, carry):
            for b in range(WIDE):
                tile = listed[flat_id * max_tiles + block * WIDE + b]
                source_f[flat_id * (max_tiles // WIDE) + block, :, b * LANES : (b + 1) * LANES] = (
                    source_rows(tile)
                )
            return carry

        lax.fori_loop(0, n_blocks, factor, 0)
        rows = pl.ds(pl.multiple_of(flat_id * LANES, LANES), LANES)
        target_u[rows, :], target_s[rows, :] = target_rows(ext[own_cell])
        return carry

    lax.fori_loop(0, n_bins, prepare, 0)
    refs = (listed, source_f, target_u, target_s, (buffer_a, buffer_b), acc, summed)
    all_pairs(n_bins, chunks_of, blocks_of, LANES // CHUNK, max_tiles // WIDE, refs)

    slot = lax.broadcasted_iota(jnp.int32, (1, LANES), 1)
    for ix in range(size_x):
        for iy in range(size_y):
            for iz in range(size_z):
                flat_id = (ix * size_y + iy) * size_z + iz
                sums = jnp.transpose(summed[flat_id * LANES : (flat_id + 1) * LANES, :])[:ROWS]
                total = sums + own[ix, iy, iz] * jnp.broadcast_to(sums[3:4], (ROWS, LANES))
                total = (2.0 * STOKES_NORM) * total + inner_ref[ix, iy, iz]
                count = count_s[COUNT_ROW, ((ix + 1) * (size_y + 2) + iy + 1) * n_z + iz]
                for i in range(3):
                    out_ref[i, ix, iy, iz : iz + 1, :] = jnp.where(
                        slot < count, total[i : i + 1], 0.0
                    )


def shifted(array, axis, dim):
    size, length = lax.axis_size(axis), array.shape[dim]
    up = [(i, (i + 1) % size) for i in range(size)]
    down = [(j, i) for i, j in up]
    before = lax.ppermute(lax.slice_in_dim(array, length - 1, length, axis=dim), axis, up)
    after = lax.ppermute(lax.slice_in_dim(array, 0, 1, axis=dim), axis, down)
    return before, after


def pair_scratch(n_targets, n_tiles):
    return [
        pltpu.VMEM((n_tiles, ROWS, LANES), jnp.float32),
        pltpu.VMEM((n_tiles // WIDE, DEPTH, BLOCK), jnp.bfloat16),
        pltpu.VMEM((n_targets, DEPTH), jnp.bfloat16),
        pltpu.VMEM((n_targets, DEPTH), jnp.bfloat16),
        pltpu.VMEM((2, CHUNK, BLOCK), jnp.float32),
        pltpu.VMEM((2, CHUNK, BLOCK), jnp.float32),
        pltpu.VMEM((4, CHUNK, LANES), jnp.float32),
        pltpu.VMEM((n_targets, LANES), jnp.float32),
    ]


def on_device(offsets, forces, counts):
    cells = offsets.shape[1:4]
    slots = offsets.shape[4]
    n_bins = cells[0] * cells[1] * cells[2]
    n_cells = (cells[0] + 2) * (cells[1] + 2) * 2 * cells[2]
    whole = pl.BlockSpec(memory_space=pltpu.VMEM)
    scalars = pl.BlockSpec(memory_space=pltpu.SMEM)
    tiles = jax.ShapeDtypeStruct(cells + (ROWS, slots), jnp.float32)
    own = pl.pallas_call(
        functools.partial(pack_kernel, cells),
        out_shape=tiles,
        in_specs=[scalars, whole, whole],
        out_specs=whole,
        name="pack",
    )(counts, offsets, forces)

    size = lax.axis_size("ha")
    other = lax.ppermute(own, "ha", [(i, (i + 1) % size) for i in range(size)])
    column = jnp.concatenate([own, other], axis=2)
    x_lo, x_hi = shifted(column, "gx", 0)
    wide = jnp.concatenate([x_lo, column, x_hi], axis=0)
    y_lo, y_hi = shifted(wide, "gy", 1)

    params = pltpu.CompilerParams(vmem_limit_bytes=24 << 20)
    inner = pl.pallas_call(
        functools.partial(inner_kernel, cells),
        out_shape=tiles,
        in_specs=[scalars, whole],
        out_specs=whole,
        scratch_shapes=[pltpu.SMEM((1,), jnp.int32), pltpu.SMEM((1,), jnp.int32)]
        + pair_scratch(n_bins * LANES, n_bins + WIDE)
        + [pltpu.VMEM((n_bins + 2, ROWS, LANES), jnp.float32)],
        compiler_params=params,
        cost_estimate=pl.CostEstimate(flops=1 << 30, bytes_accessed=1 << 16, transcendentals=1 << 22),
        name="inner",
    )(counts, own)
    max_tiles = 20 + WIDE
    return pl.pallas_call(
        functools.partial(outer_kernel, cells),
        out_shape=jax.ShapeDtypeStruct((3,) + cells + (slots,), jnp.float32),
        in_specs=[whole] * 7,
        out_specs=whole,
        scratch_shapes=[
            pltpu.VMEM((n_cells, ROWS, LANES), jnp.float32),
            pltpu.VMEM((ROWS, LANES), jnp.int32),
            pltpu.SMEM((ROWS, LANES), jnp.int32),
            pltpu.SemaphoreType.DMA,
            pltpu.SMEM((n_bins,), jnp.int32),
            pltpu.SMEM((n_bins,), jnp.int32),
        ]
        + pair_scratch(n_bins * LANES, n_bins * max_tiles),
        compiler_params=params,
        name="outer",
    )(own, other, x_lo, x_hi, y_lo, y_hi, inner)


def solution(mesh):
    in_specs = (
        P(None, "gx", "gy", "ha", None),
        P(None, "gx", "gy", "ha", None),
        P("gx", "gy", "ha"),
    )
    out_specs = P(None, "gx", "gy", "ha", None)
    return jax.shard_map(on_device, mesh=mesh, in_specs=in_specs, out_specs=out_specs, check_vma=False)
```

```python
import functools
import math

import jax
import jax.numpy as jnp
from jax import lax
from jax.experimental import pallas as pl
from jax.experimental.pallas import tpu as pltpu
from jax.sharding import PartitionSpec as P

SPLIT_XI = 2.0
SOFT_SQ = 0.01
GAUSS_COEF = 2.0 * SPLIT_XI / math.sqrt(math.pi)
STOKES_NORM = 1.0 / (8.0 * math.pi)

SOFT_U = SPLIT_XI * SPLIT_XI * SOFT_SQ
LOG2_E = math.log2(math.e)
LOG2_G = math.log2(GAUSS_COEF)
SELF_C = math.erfc(math.sqrt(SOFT_U)) / math.sqrt(SOFT_SQ) + GAUSS_COEF * (
    2.0 * SOFT_U - 3.0
) * math.exp(-SOFT_U)

LANES = 128
ROWS = 8
CHUNK = 64
WIDE = 2
BLOCK = WIDE * LANES
GROUP = 16
COUNT_ROW = 3
FORCE_ROW = 4


def rows_and_lanes(shape=(ROWS, LANES)):
    return lax.broadcasted_iota(jnp.int32, shape, 0), lax.broadcasted_iota(jnp.int32, shape, 1)


def pack_kernel(cells, count_ref, offset_ref, force_ref, out_ref):
    slot = lax.broadcasted_iota(jnp.int32, (1, LANES), 1)
    for ix in range(cells[0]):
        for iy in range(cells[1]):
            for iz in range(cells[2]):
                count = count_ref[ix, iy, iz]
                filled = jnp.full((1, LANES), count, jnp.int32).astype(jnp.float32)
                for i in range(3):
                    position = offset_ref[i, ix, iy, iz : iz + 1, :]
                    out_ref[ix, iy, iz, i : i + 1, :] = position * SPLIT_XI - 0.5 * SPLIT_XI
                    force = force_ref[i, ix, iy, iz : iz + 1, :]
                    at = FORCE_ROW + i
                    out_ref[ix, iy, iz, at : at + 1, :] = jnp.where(slot < count, force, 0.0)
                out_ref[ix, iy, iz, 3:4, :] = filled
                out_ref[ix, iy, iz, 7:8, :] = filled


def compact(listed, base, sources):
    _, lane = rows_and_lanes()
    current = jnp.zeros((ROWS, LANES), jnp.float32)
    filled = jnp.int32(0)
    for tile, count in sources:
        tile_id = base + lax.shift_right_logical(filled, 7)
        at = lax.bitwise_and(filled, LANES - 1)
        moved = pltpu.roll(tile, at, 1)
        behind = lane >= at
        current = jnp.where(behind, moved, current)
        spill = jnp.where(behind, 0.0, moved)
        listed[tile_id] = current
        listed[tile_id + 1] = spill
        filled = filled + count
        current = jnp.where(at + count >= LANES, spill, current)
    last = base + lax.shift_right_logical(filled, 7)
    for more in range(1, WIDE):
        listed[last + more] = jnp.zeros((ROWS, LANES), jnp.float32)
    return filled


def spread_targets(spread, first, tile):
    columns = jnp.transpose(jnp.concatenate([tile] * (LANES // ROWS), axis=0))
    for i in range(3):
        spread[i, pl.ds(first, LANES), :] = jnp.broadcast_to(columns[:, i : i + 1], (LANES, LANES))


def pair_terms(target, source, force):
    delta = [t - s for t, s in zip(target, source)]
    u = (delta[0] * delta[0] + SOFT_U) + delta[1] * delta[1] + delta[2] * delta[2]
    inv = lax.rsqrt(u)
    tail = (1.0 - lax.erf(u * inv)) * inv
    gauss = jnp.exp2(LOG2_G - u * LOG2_E)
    rest = gauss * (u - 1.5)
    coef_c = tail + rest
    coef_d = ((tail - rest) - gauss) * (inv * inv)
    along = coef_d * (delta[0] * force[0] + delta[1] * force[1] + delta[2] * force[2])
    return [coef_c * f + along * d for f, d in zip(force, delta)]


def all_pairs(n_groups, chunks_of, blocks_of, max_chunks, max_blocks, refs):
    listed, spread, acc, summed = refs

    def process(group, chunk, block):
        sources = []
        for b in range(WIDE):
            tile_id = (group * max_blocks + block) * WIDE + b
            rows = [listed[tile_id, i : i + 1, :] for i in (0, 1, 2, 4, 5, 6)]
            sources.append((rows[:3], rows[3:]))
        first = (group * max_chunks + chunk) * CHUNK
        for r in range(0, CHUNK, GROUP):
            at = pl.ds(pl.multiple_of(first + r, GROUP), GROUP)
            target = [spread[i, at, :] for i in range(3)]
            sums = None
            for source, force in sources:
                terms = pair_terms(target, source, force)
                sums = terms if sums is None else [s + t for s, t in zip(sums, terms)]
            for i in range(3):
                acc[i, r : r + GROUP, :] = acc[i, r : r + GROUP, :] + sums[i]

    def reduce(group, chunk):
        _, lane = rows_and_lanes((CHUNK, LANES))
        merged = jnp.zeros((CHUNK, LANES), jnp.float32)
        for i in range(3):
            merged = jnp.where(lane == i, jnp.sum(acc[i], axis=1, keepdims=True), merged)
            acc[i] = jnp.zeros((CHUNK, LANES), jnp.float32)
        at = pl.multiple_of((group * max_chunks + chunk) * CHUNK, CHUNK)
        summed[pl.ds(at, CHUNK), :] = merged

    total = jnp.int32(0)
    for group in range(n_groups):
        total = total + chunks_of[group] * blocks_of[group]
    acc[...] = jnp.zeros_like(acc)

    def one_item(item, state):
        group, chunk, block = state
        end_block = block + 1 == blocks_of[group]
        next_block = jnp.where(end_block, 0, block + 1)
        next_chunk = jnp.where(end_block, chunk + 1, chunk)
        end_chunk = next_chunk == chunks_of[group]
        next_chunk = jnp.where(end_chunk, 0, next_chunk)
        next_group = jnp.where(end_chunk, jnp.minimum(group + 1, n_groups - 1), group)
        process(group, chunk, block)

        @pl.when(end_block)
        def _():
            reduce(group, chunk)

        return next_group, next_chunk, next_block

    zero = jnp.int32(0)
    lax.fori_loop(0, total, one_item, (zero, zero, zero))


def inner_kernel(cells, count_ref, own_ref, out_ref, chunks_of, blocks_of, *refs):
    listed, spread, acc, summed, result = refs
    row, lane = rows_and_lanes()
    n_bins = cells[0] * cells[1] * cells[2]
    bins = [(i, j, k) for i in range(cells[0]) for j in range(cells[1]) for k in range(cells[2])]
    sources, counts = [], []
    for at in bins:
        moved = jnp.zeros((ROWS, LANES), jnp.float32)
        for i in range(3):
            moved = jnp.where(row == i, SPLIT_XI * (at[i] - 0.5 * (cells[i] - 1)), moved)
        counts.append(count_ref[at])
        sources.append((own_ref[at] + moved, counts[-1]))
    filled = compact(listed, 0, sources)
    n_tiles = lax.div(filled + LANES - 1, LANES)
    n_blocks = lax.div(filled + BLOCK - 1, BLOCK)
    blocks_of[0] = n_blocks
    chunks_of[0] = lax.div(filled + CHUNK - 1, CHUNK)

    def prepare(tile_id, carry):
        spread_targets(spread, pl.multiple_of(tile_id * LANES, LANES), listed[tile_id])
        return carry

    lax.fori_loop(0, n_tiles, prepare, 0)
    refs = (listed, spread, acc, summed)
    all_pairs(1, chunks_of, blocks_of, n_bins * LANES // CHUNK, n_bins // WIDE, refs)

    def finish(tile_id, carry):
        sums = jnp.transpose(summed[pl.ds(pl.multiple_of(tile_id * LANES, LANES), LANES), :])[:ROWS]
        tile = listed[tile_id]
        own = pltpu.roll(tile, ROWS - FORCE_ROW, 0)
        result[tile_id] = (2.0 * STOKES_NORM) * sums - (STOKES_NORM * SELF_C) * own
        return carry

    lax.fori_loop(0, n_tiles, finish, 0)
    before = jnp.int32(0)
    for at, count in zip(bins, counts):
        tile_id = lax.shift_right_logical(before, 7)
        back = LANES - lax.bitwise_and(before, LANES - 1)
        turn = lax.bitwise_and(back, LANES - 1)
        part = jnp.where(
            lane < back, pltpu.roll(result[tile_id], turn, 1), pltpu.roll(result[tile_id + 1], turn, 1)
        )
        out_ref[at] = part
        before = before + count


def outer_kernel(cells, *refs):
    pieces, (inner_ref, out_ref), refs = refs[:6], refs[6:8], refs[8:]
    ext, count_v, count_s, sem, chunks_of, blocks_of = refs[:6]
    listed, spread, acc, summed = refs[6:]
    own, other, x_lo, x_hi, y_lo, y_hi = pieces
    size_x, size_y, size_z = cells
    n_z = 2 * size_z
    n_bins = size_x * size_y * size_z
    row, lane = rows_and_lanes()

    held = jnp.zeros((ROWS, LANES), jnp.float32)
    for ix in range(size_x + 2):
        for iy in range(size_y + 2):
            for iz in range(n_z):
                if iy == 0:
                    tile = y_lo[ix, 0, iz]
                elif iy == size_y + 1:
                    tile = y_hi[ix, 0, iz]
                elif ix == 0:
                    tile = x_lo[0, iy - 1, iz]
                elif ix == size_x + 1:
                    tile = x_hi[0, iy - 1, iz]
                elif iz < size_z:
                    tile = own[ix - 1, iy - 1, iz]
                else:
                    tile = other[ix - 1, iy - 1, iz - size_z]
                cell = (ix * (size_y + 2) + iy) * n_z + iz
                ext[cell] = tile
                held = jnp.where(lane == cell, tile, held)
    count_v[...] = held.astype(jnp.int32)
    copy = pltpu.make_async_copy(count_v, count_s, sem)
    copy.start()
    copy.wait()

    max_tiles = listed.shape[0] // n_bins
    steps = [
        (a, b, c) for a in (0, -1, 1) for b in (0, -1, 1) for c in (0, -1, 1) if 1 in (a, b, c)
    ]

    def prepare(flat_id, carry):
        at = (flat_id // (size_y * size_z), flat_id // size_z % size_y, flat_id % size_z)
        out = [2 * i - 1 for i in at]
        moves = [
            jnp.where(row == i, (SPLIT_XI * out[i].astype(jnp.float32)), 0.0) for i in range(3)
        ]
        sources = []
        for step in steps:
            moved = sum(s * m for s, m in zip(step, moves) if s != 0)
            x, y, z = (i + s * o for i, s, o in zip(at, step, out))
            cell = ((x + 1) * (size_y + 2) + y + 1) * n_z + lax.rem(z + n_z, n_z)
            sources.append((ext[cell] + moved, count_s[COUNT_ROW, cell]))
        filled = compact(listed, flat_id * max_tiles, sources)
        n_blocks = lax.div(filled + BLOCK - 1, BLOCK)
        own_cell = ((at[0] + 1) * (size_y + 2) + at[1] + 1) * n_z + at[2]
        blocks_of[flat_id] = n_blocks
        chunks_of[flat_id] = lax.div(count_s[COUNT_ROW, own_cell] + CHUNK - 1, CHUNK)

        spread_targets(spread, pl.multiple_of(flat_id * LANES, LANES), ext[own_cell])
        return carry

    lax.fori_loop(0, n_bins, prepare, 0)
    refs = (listed, spread, acc, summed)
    all_pairs(n_bins, chunks_of, blocks_of, LANES // CHUNK, max_tiles // WIDE, refs)

    slot = lax.broadcasted_iota(jnp.int32, (1, LANES), 1)
    for ix in range(size_x):
        for iy in range(size_y):
            for iz in range(size_z):
                flat_id = (ix * size_y + iy) * size_z + iz
                sums = jnp.transpose(summed[flat_id * LANES : (flat_id + 1) * LANES, :])[:ROWS]
                total = (2.0 * STOKES_NORM) * sums + inner_ref[ix, iy, iz]
                count = count_s[COUNT_ROW, ((ix + 1) * (size_y + 2) + iy + 1) * n_z + iz]
                for i in range(3):
                    out_ref[i, ix, iy, iz : iz + 1, :] = jnp.where(
                        slot < count, total[i : i + 1], 0.0
                    )


def shifted(array, axis, dim):
    size, length = lax.axis_size(axis), array.shape[dim]
    up = [(i, (i + 1) % size) for i in range(size)]
    down = [(j, i) for i, j in up]
    before = lax.ppermute(lax.slice_in_dim(array, length - 1, length, axis=dim), axis, up)
    after = lax.ppermute(lax.slice_in_dim(array, 0, 1, axis=dim), axis, down)
    return before, after


def pair_scratch(n_targets, n_tiles):
    return [
        pltpu.VMEM((n_tiles, ROWS, LANES), jnp.float32),
        pltpu.VMEM((3, n_targets, LANES), jnp.float32),
        pltpu.VMEM((3, CHUNK, LANES), jnp.float32),
        pltpu.VMEM((n_targets, LANES), jnp.float32),
    ]


def on_device(offsets, forces, counts):
    cells = offsets.shape[1:4]
    slots = offsets.shape[4]
    n_bins = cells[0] * cells[1] * cells[2]
    n_cells = (cells[0] + 2) * (cells[1] + 2) * 2 * cells[2]
    whole = pl.BlockSpec(memory_space=pltpu.VMEM)
    scalars = pl.BlockSpec(memory_space=pltpu.SMEM)
    tiles = jax.ShapeDtypeStruct(cells + (ROWS, slots), jnp.float32)
    own = pl.pallas_call(
        functools.partial(pack_kernel, cells),
        out_shape=tiles,
        in_specs=[scalars, whole, whole],
        out_specs=whole,
        name="pack",
    )(counts, offsets, forces)

    size = lax.axis_size("ha")
    other = lax.ppermute(own, "ha", [(i, (i + 1) % size) for i in range(size)])
    params = pltpu.CompilerParams(vmem_limit_bytes=24 << 20)
    inner = pl.pallas_call(
        functools.partial(inner_kernel, cells),
        out_shape=tiles,
        in_specs=[scalars, whole],
        out_specs=whole,
        scratch_shapes=[pltpu.SMEM((1,), jnp.int32), pltpu.SMEM((1,), jnp.int32)]
        + pair_scratch(n_bins * LANES, n_bins + WIDE)
        + [pltpu.VMEM((n_bins + 2, ROWS, LANES), jnp.float32)],
        compiler_params=params,
        cost_estimate=pl.CostEstimate(flops=1 << 30, bytes_accessed=1 << 16, transcendentals=1 << 22),
        name="inner",
    )(counts, own)
    other, inner = lax.optimization_barrier((other, inner))
    column = jnp.concatenate([own, other], axis=2)
    x_lo, x_hi = shifted(column, "gx", 0)
    wide = jnp.concatenate([x_lo, column, x_hi], axis=0)
    y_lo, y_hi = shifted(wide, "gy", 1)

    max_tiles = 20 + WIDE
    return pl.pallas_call(
        functools.partial(outer_kernel, cells),
        out_shape=jax.ShapeDtypeStruct((3,) + cells + (slots,), jnp.float32),
        in_specs=[whole] * 7,
        out_specs=whole,
        scratch_shapes=[
            pltpu.VMEM((n_cells, ROWS, LANES), jnp.float32),
            pltpu.VMEM((ROWS, LANES), jnp.int32),
            pltpu.SMEM((ROWS, LANES), jnp.int32),
            pltpu.SemaphoreType.DMA,
            pltpu.SMEM((n_bins,), jnp.int32),
            pltpu.SMEM((n_bins,), jnp.int32),
        ]
        + pair_scratch(n_bins * LANES, n_bins * max_tiles),
        compiler_params=params,
        name="outer",
    )(own, other, x_lo, x_hi, y_lo, y_hi, inner)


def solution(mesh):
    in_specs = (
        P(None, "gx", "gy", "ha", None),
        P(None, "gx", "gy", "ha", None),
        P("gx", "gy", "ha"),
    )
    out_specs = P(None, "gx", "gy", "ha", None)
    return jax.shard_map(on_device, mesh=mesh, in_specs=in_specs, out_specs=out_specs, check_vma=False)
```

```python
import functools
import math

import jax
import jax.numpy as jnp
from jax import lax
from jax.experimental import pallas as pl
from jax.experimental.pallas import tpu as pltpu
from jax.sharding import PartitionSpec as P

SPLIT_XI = 2.0
SOFT_SQ = 0.01
GAUSS_COEF = 2.0 * SPLIT_XI / math.sqrt(math.pi)
STOKES_NORM = 1.0 / (8.0 * math.pi)

SOFT_U = SPLIT_XI * SPLIT_XI * SOFT_SQ
LOG2_E = math.log2(math.e)
LOG2_G = math.log2(GAUSS_COEF)
SELF_C = math.erfc(math.sqrt(SOFT_U)) / math.sqrt(SOFT_SQ) + GAUSS_COEF * (
    2.0 * SOFT_U - 3.0
) * math.exp(-SOFT_U)

LANES = 128
ROWS = 8
CHUNK = 32
WIDE = 2
BLOCK = WIDE * LANES
COUNT_ROW = 3
FORCE_ROW = 4


def rows_and_lanes(shape=(ROWS, LANES)):
    return lax.broadcasted_iota(jnp.int32, shape, 0), lax.broadcasted_iota(jnp.int32, shape, 1)


def pack_kernel(cells, count_ref, offset_ref, force_ref, out_ref):
    slot = lax.broadcasted_iota(jnp.int32, (1, LANES), 1)
    for ix in range(cells[0]):
        for iy in range(cells[1]):
            for iz in range(cells[2]):
                count = count_ref[ix, iy, iz]
                filled = jnp.full((1, LANES), count, jnp.int32).astype(jnp.float32)
                for i in range(3):
                    position = offset_ref[i, ix, iy, iz : iz + 1, :]
                    out_ref[ix, iy, iz, i : i + 1, :] = position * SPLIT_XI - 0.5 * SPLIT_XI
                    force = force_ref[i, ix, iy, iz : iz + 1, :]
                    at = FORCE_ROW + i
                    out_ref[ix, iy, iz, at : at + 1, :] = jnp.where(slot < count, force, 0.0)
                out_ref[ix, iy, iz, 3:4, :] = filled
                out_ref[ix, iy, iz, 7:8, :] = filled


def compact(listed, base, sources):
    _, lane = rows_and_lanes()
    current = jnp.zeros((ROWS, LANES), jnp.float32)
    filled = jnp.int32(0)
    for tile, count in sources:
        tile_id = base + lax.shift_right_logical(filled, 7)
        at = lax.bitwise_and(filled, LANES - 1)
        moved = pltpu.roll(tile, at, 1)
        behind = lane >= at
        current = jnp.where(behind, moved, current)
        spill = jnp.where(behind, 0.0, moved)
        listed[tile_id] = current
        listed[tile_id + 1] = spill
        filled = filled + count
        current = jnp.where(at + count >= LANES, spill, current)
    last = base + lax.shift_right_logical(filled, 7)
    for more in range(1, WIDE):
        listed[last + more] = jnp.zeros((ROWS, LANES), jnp.float32)
    return filled


def spread_targets(spread, first, tile):
    columns = jnp.transpose(jnp.concatenate([tile] * (LANES // ROWS), axis=0))
    for i in range(3):
        spread[i, pl.ds(first, LANES), :] = jnp.broadcast_to(columns[:, i : i + 1], (LANES, LANES))


def coefficients(target, source):
    delta = [t - s for t, s in zip(target, source)]
    u = (delta[0] * delta[0] + SOFT_U) + delta[1] * delta[1] + delta[2] * delta[2]
    inv = lax.rsqrt(u)
    tail = (1.0 - lax.erf(u * inv)) * inv
    gauss = jnp.exp2(LOG2_G - u * LOG2_E)
    rest = gauss * (u - 1.5)
    return tail + rest, ((tail - rest) - gauss) * (inv * inv)


def velocity_terms(target, source, force, coef_c, coef_d):
    delta = [t - s for t, s in zip(target, source)]
    along = coef_d * (delta[0] * force[0] + delta[1] * force[1] + delta[2] * force[2])
    return [coef_c * f + along * d for f, d in zip(force, delta)]


def all_pairs(n_groups, chunks_of, blocks_of, max_chunks, max_blocks, refs):
    listed, spread, coefs, acc = refs
    components = range(3)

    def targets(first):
        at = pl.ds(pl.multiple_of(first, CHUNK), CHUNK)
        return [spread[i, at, :] for i in components]

    def rows(tile_id, at):
        return [[listed[tile_id + b, i : i + 1, :] for i in at] for b in range(WIDE)]

    total = jnp.int32(0)
    for group in range(n_groups):
        total = total + chunks_of[group] * blocks_of[group]
    acc[...] = jnp.zeros_like(acc)
    coefs[...] = jnp.zeros_like(coefs)

    def one_item(item, state):
        group, chunk, block, old_first, old_tile = state
        new_first = (group * max_chunks + chunk) * CHUNK
        new_tile = (group * max_blocks + block) * WIDE
        old_at = pl.ds(pl.multiple_of(old_first, CHUNK), CHUNK)
        old_coefs = [(coefs[b, 0], coefs[b, 1]) for b in range(WIDE)]
        sums = [acc[i, old_at, :] for i in components]
        old_target, old_source = targets(old_first), rows(old_tile, (0, 1, 2))
        old_force = rows(old_tile, (4, 5, 6))
        new_target, new_source = targets(new_first), rows(new_tile, (0, 1, 2))

        new_coefs = [coefficients(new_target, source) for source in new_source]
        for pair in zip(old_source, old_force, old_coefs):
            terms = velocity_terms(old_target, pair[0], pair[1], *pair[2])
            sums = [s + t for s, t in zip(sums, terms)]

        for i in components:
            acc[i, old_at, :] = sums[i]
        for b in range(WIDE):
            coefs[b, 0], coefs[b, 1] = new_coefs[b]

        end_block = block + 1 == blocks_of[group]
        next_block = jnp.where(end_block, 0, block + 1)
        next_chunk = jnp.where(end_block, chunk + 1, chunk)
        end_chunk = next_chunk == chunks_of[group]
        next_chunk = jnp.where(end_chunk, 0, next_chunk)
        next_group = jnp.where(end_chunk, jnp.minimum(group + 1, n_groups - 1), group)
        return next_group, next_chunk, next_block, new_first, new_tile

    lax.fori_loop(0, total + 1, one_item, (jnp.int32(0),) * 5)


def lane_sums(acc, first):
    row, _ = rows_and_lanes()
    one = jnp.ones((ROWS, LANES), jnp.float32)
    merged = jnp.zeros((ROWS, LANES), jnp.float32)
    for i in range(3):
        sums = lax.dot_general(
            one,
            acc[i, pl.ds(first, LANES), :],
            (((1,), (1,)), ((), ())),
            precision=lax.Precision.HIGHEST,
            preferred_element_type=jnp.float32,
        )
        merged = jnp.where(row == i, sums, merged)
    return merged


def inner_kernel(cells, count_ref, own_ref, out_ref, chunks_of, blocks_of, *refs):
    listed, spread, coefs, acc, result = refs
    row, lane = rows_and_lanes()
    n_bins = cells[0] * cells[1] * cells[2]
    bins = [(i, j, k) for i in range(cells[0]) for j in range(cells[1]) for k in range(cells[2])]
    sources, counts = [], []
    for at in bins:
        moved = jnp.zeros((ROWS, LANES), jnp.float32)
        for i in range(3):
            moved = jnp.where(row == i, SPLIT_XI * (at[i] - 0.5 * (cells[i] - 1)), moved)
        counts.append(count_ref[at])
        sources.append((own_ref[at] + moved, counts[-1]))
    filled = compact(listed, 0, sources)
    n_tiles = lax.div(filled + LANES - 1, LANES)
    n_blocks = lax.div(filled + BLOCK - 1, BLOCK)
    blocks_of[0] = n_blocks
    chunks_of[0] = lax.div(filled + CHUNK - 1, CHUNK)

    def prepare(tile_id, carry):
        spread_targets(spread, pl.multiple_of(tile_id * LANES, LANES), listed[tile_id])
        return carry

    lax.fori_loop(0, n_tiles, prepare, 0)
    refs = (listed, spread, coefs, acc)
    all_pairs(1, chunks_of, blocks_of, n_bins * LANES // CHUNK, n_bins // WIDE, refs)

    def finish(tile_id, carry):
        sums = lane_sums(acc, pl.multiple_of(tile_id * LANES, LANES))
        tile = listed[tile_id]
        own = pltpu.roll(tile, ROWS - FORCE_ROW, 0)
        result[tile_id] = (2.0 * STOKES_NORM) * sums - (STOKES_NORM * SELF_C) * own
        return carry

    lax.fori_loop(0, n_tiles, finish, 0)
    before = jnp.int32(0)
    for at, count in zip(bins, counts):
        tile_id = lax.shift_right_logical(before, 7)
        back = LANES - lax.bitwise_and(before, LANES - 1)
        turn = lax.bitwise_and(back, LANES - 1)
        part = jnp.where(
            lane < back, pltpu.roll(result[tile_id], turn, 1), pltpu.roll(result[tile_id + 1], turn, 1)
        )
        out_ref[at] = part
        before = before + count


def outer_kernel(cells, *refs):
    pieces, (inner_ref, out_ref), refs = refs[:6], refs[6:8], refs[8:]
    ext, count_v, count_s, sem, chunks_of, blocks_of = refs[:6]
    listed, spread, coefs, acc = refs[6:]
    own, other, x_lo, x_hi, y_lo, y_hi = pieces
    size_x, size_y, size_z = cells
    n_z = 2 * size_z
    n_bins = size_x * size_y * size_z
    row, lane = rows_and_lanes()

    held = jnp.zeros((ROWS, LANES), jnp.float32)
    for ix in range(size_x + 2):
        for iy in range(size_y + 2):
            for iz in range(n_z):
                if iy == 0:
                    tile = y_lo[ix, 0, iz]
                elif iy == size_y + 1:
                    tile = y_hi[ix, 0, iz]
                elif ix == 0:
                    tile = x_lo[0, iy - 1, iz]
                elif ix == size_x + 1:
                    tile = x_hi[0, iy - 1, iz]
                elif iz < size_z:
                    tile = own[ix - 1, iy - 1, iz]
                else:
                    tile = other[ix - 1, iy - 1, iz - size_z]
                cell = (ix * (size_y + 2) + iy) * n_z + iz
                ext[cell] = tile
                held = jnp.where(lane == cell, tile, held)
    count_v[...] = held.astype(jnp.int32)
    copy = pltpu.make_async_copy(count_v, count_s, sem)
    copy.start()
    copy.wait()

    max_tiles = listed.shape[0] // n_bins
    steps = [
        (a, b, c) for a in (0, -1, 1) for b in (0, -1, 1) for c in (0, -1, 1) if 1 in (a, b, c)
    ]

    def prepare(flat_id, carry):
        at = (flat_id // (size_y * size_z), flat_id // size_z % size_y, flat_id % size_z)
        out = [2 * i - 1 for i in at]
        moves = [
            jnp.where(row == i, (SPLIT_XI * out[i].astype(jnp.float32)), 0.0) for i in range(3)
        ]
        sources = []
        for step in steps:
            moved = sum(s * m for s, m in zip(step, moves) if s != 0)
            x, y, z = (i + s * o for i, s, o in zip(at, step, out))
            cell = ((x + 1) * (size_y + 2) + y + 1) * n_z + lax.rem(z + n_z, n_z)
            sources.append((ext[cell] + moved, count_s[COUNT_ROW, cell]))
        filled = compact(listed, flat_id * max_tiles, sources)
        n_blocks = lax.div(filled + BLOCK - 1, BLOCK)
        own_cell = ((at[0] + 1) * (size_y + 2) + at[1] + 1) * n_z + at[2]
        blocks_of[flat_id] = n_blocks
        chunks_of[flat_id] = lax.div(count_s[COUNT_ROW, own_cell] + CHUNK - 1, CHUNK)

        spread_targets(spread, pl.multiple_of(flat_id * LANES, LANES), ext[own_cell])
        return carry

    lax.fori_loop(0, n_bins, prepare, 0)
    refs = (listed, spread, coefs, acc)
    all_pairs(n_bins, chunks_of, blocks_of, LANES // CHUNK, max_tiles // WIDE, refs)

    slot = lax.broadcasted_iota(jnp.int32, (1, LANES), 1)
    for ix in range(size_x):
        for iy in range(size_y):
            for iz in range(size_z):
                flat_id = (ix * size_y + iy) * size_z + iz
                sums = lane_sums(acc, flat_id * LANES)
                total = (2.0 * STOKES_NORM) * sums + inner_ref[ix, iy, iz]
                count = count_s[COUNT_ROW, ((ix + 1) * (size_y + 2) + iy + 1) * n_z + iz]
                for i in range(3):
                    out_ref[i, ix, iy, iz : iz + 1, :] = jnp.where(
                        slot < count, total[i : i + 1], 0.0
                    )


def shifted(array, axis, dim):
    size, length = lax.axis_size(axis), array.shape[dim]
    up = [(i, (i + 1) % size) for i in range(size)]
    down = [(j, i) for i, j in up]
    before = lax.ppermute(lax.slice_in_dim(array, length - 1, length, axis=dim), axis, up)
    after = lax.ppermute(lax.slice_in_dim(array, 0, 1, axis=dim), axis, down)
    return before, after


def pair_scratch(n_targets, n_tiles):
    return [
        pltpu.VMEM((n_tiles, ROWS, LANES), jnp.float32),
        pltpu.VMEM((3, n_targets, LANES), jnp.float32),
        pltpu.VMEM((WIDE, 2, CHUNK, LANES), jnp.float32),
        pltpu.VMEM((3, n_targets, LANES), jnp.float32),
    ]


def on_device(offsets, forces, counts):
    cells = offsets.shape[1:4]
    slots = offsets.shape[4]
    n_bins = cells[0] * cells[1] * cells[2]
    n_cells = (cells[0] + 2) * (cells[1] + 2) * 2 * cells[2]
    whole = pl.BlockSpec(memory_space=pltpu.VMEM)
    scalars = pl.BlockSpec(memory_space=pltpu.SMEM)
    tiles = jax.ShapeDtypeStruct(cells + (ROWS, slots), jnp.float32)
    own = pl.pallas_call(
        functools.partial(pack_kernel, cells),
        out_shape=tiles,
        in_specs=[scalars, whole, whole],
        out_specs=whole,
        name="pack",
    )(counts, offsets, forces)

    size = lax.axis_size("ha")
    other = lax.ppermute(own, "ha", [(i, (i + 1) % size) for i in range(size)])
    params = pltpu.CompilerParams(vmem_limit_bytes=24 << 20)
    inner = pl.pallas_call(
        functools.partial(inner_kernel, cells),
        out_shape=tiles,
        in_specs=[scalars, whole],
        out_specs=whole,
        scratch_shapes=[pltpu.SMEM((1,), jnp.int32), pltpu.SMEM((1,), jnp.int32)]
        + pair_scratch(n_bins * LANES, n_bins + WIDE)
        + [pltpu.VMEM((n_bins + 2, ROWS, LANES), jnp.float32)],
        compiler_params=params,
        cost_estimate=pl.CostEstimate(flops=1 << 30, bytes_accessed=1 << 16, transcendentals=1 << 22),
        name="inner",
    )(counts, own)
    other, inner = lax.optimization_barrier((other, inner))
    column = jnp.concatenate([own, other], axis=2)
    x_lo, x_hi = shifted(column, "gx", 0)
    wide = jnp.concatenate([x_lo, column, x_hi], axis=0)
    y_lo, y_hi = shifted(wide, "gy", 1)

    max_tiles = 20 + WIDE
    return pl.pallas_call(
        functools.partial(outer_kernel, cells),
        out_shape=jax.ShapeDtypeStruct((3,) + cells + (slots,), jnp.float32),
        in_specs=[whole] * 7,
        out_specs=whole,
        scratch_shapes=[
            pltpu.VMEM((n_cells, ROWS, LANES), jnp.float32),
            pltpu.VMEM((ROWS, LANES), jnp.int32),
            pltpu.SMEM((ROWS, LANES), jnp.int32),
            pltpu.SemaphoreType.DMA,
            pltpu.SMEM((n_bins,), jnp.int32),
            pltpu.SMEM((n_bins,), jnp.int32),
        ]
        + pair_scratch(n_bins * LANES, n_bins * max_tiles),
        compiler_params=params,
        name="outer",
    )(own, other, x_lo, x_hi, y_lo, y_hi, inner)


def solution(mesh):
    in_specs = (
        P(None, "gx", "gy", "ha", None),
        P(None, "gx", "gy", "ha", None),
        P("gx", "gy", "ha"),
    )
    out_specs = P(None, "gx", "gy", "ha", None)
    return jax.shard_map(on_device, mesh=mesh, in_specs=in_specs, out_specs=out_specs, check_vma=False)
```

```python
import functools
import math

import jax
import jax.numpy as jnp
from jax import lax
from jax.experimental import pallas as pl
from jax.experimental.pallas import tpu as pltpu
from jax.sharding import PartitionSpec as P

SPLIT_XI = 2.0
SOFT_SQ = 0.01
GAUSS_COEF = 2.0 * SPLIT_XI / math.sqrt(math.pi)
STOKES_NORM = 1.0 / (8.0 * math.pi)

SOFT_U = SPLIT_XI * SPLIT_XI * SOFT_SQ
ROOT_OF_GAUSS = (
    1.0127987371125773,
    -0.01582481499430155,
    0.0001235945382420463,
    -6.40653408887884e-07,
    2.3853643253743967e-09,
    -5.370953877973602e-12,
)
SELF_C = math.erfc(math.sqrt(SOFT_U)) / math.sqrt(SOFT_SQ) + GAUSS_COEF * (
    2.0 * SOFT_U - 3.0
) * math.exp(-SOFT_U)

LANES = 128
ROWS = 8
CHUNK = 32
WIDE = 2
BLOCK = WIDE * LANES
COUNT_ROW = 3
FORCE_ROW = 4


def rows_and_lanes(shape=(ROWS, LANES)):
    return lax.broadcasted_iota(jnp.int32, shape, 0), lax.broadcasted_iota(jnp.int32, shape, 1)


def pack_kernel(cells, count_ref, offset_ref, force_ref, out_ref, sent_ref):
    slot = lax.broadcasted_iota(jnp.int32, (1, LANES), 1)
    for ix in range(cells[0]):
        for iy in range(cells[1]):
            for iz in range(cells[2]):
                count = count_ref[ix, iy, iz]
                filled = jnp.full((1, LANES), count, jnp.int32).astype(jnp.float32)
                for i in range(3):
                    position = offset_ref[i, ix, iy, iz : iz + 1, :]
                    out_ref[ix, iy, iz, i : i + 1, :] = position * SPLIT_XI - 0.5 * SPLIT_XI
                    force = force_ref[i, ix, iy, iz : iz + 1, :]
                    at = FORCE_ROW + i
                    out_ref[ix, iy, iz, at : at + 1, :] = jnp.where(slot < count, force, 0.0)
                out_ref[ix, iy, iz, 3:4, :] = filled
                out_ref[ix, iy, iz, 7:8, :] = filled
                sent_ref[ix, iy, iz] = out_ref[ix, iy, iz]


def compact(listed, base, sources):
    _, lane = rows_and_lanes()
    current = jnp.zeros((ROWS, LANES), jnp.float32)
    filled = jnp.int32(0)
    for tile, count in sources:
        tile_id = base + lax.shift_right_logical(filled, 7)
        at = lax.bitwise_and(filled, LANES - 1)
        moved = pltpu.roll(tile, at, 1)
        behind = lane >= at
        current = jnp.where(behind, moved, current)
        spill = jnp.where(behind, 0.0, moved)
        listed[tile_id] = current
        listed[tile_id + 1] = spill
        filled = filled + count
        current = jnp.where(at + count >= LANES, spill, current)
    last = base + lax.shift_right_logical(filled, 7)
    for more in range(1, WIDE):
        listed[last + more] = jnp.zeros((ROWS, LANES), jnp.float32)
    return filled


def parts_of(value):
    high = value.astype(jnp.bfloat16)
    rest = value - high.astype(jnp.float32)
    middle = rest.astype(jnp.bfloat16)
    low = rest - middle.astype(jnp.float32)
    return high, middle, low.astype(jnp.bfloat16)


def spread_targets(spread, first, tile):
    parts = jnp.concatenate([p.astype(jnp.float32) for p in parts_of(tile)] + [jnp.zeros_like(tile)], axis=0)
    shape = (4 * ROWS, 3 * LANES)
    row, lane = rows_and_lanes(shape)
    pick = jnp.where(lax.rem(row, ROWS) == lax.div(lane, LANES), 1.0, 0.0)
    wide = lax.dot_general(
        parts.astype(jnp.bfloat16),
        pick.astype(jnp.bfloat16),
        (((0,), (0,)), ((), ())),
        preferred_element_type=jnp.float32,
    )
    for i in range(3):
        spread[i, pl.ds(first, LANES), :] = wide[:, i * LANES : (i + 1) * LANES]


def scaled_gaussian(u):
    value = ROOT_OF_GAUSS[-1]
    for factor in ROOT_OF_GAUSS[-2::-1]:
        value = value * u + factor
    for _ in range(6):
        value = value * value
    return value


def coefficients(target, source):
    delta = [t - s for t, s in zip(target, source)]
    u = (delta[0] * delta[0] + SOFT_U) + delta[1] * delta[1] + delta[2] * delta[2]
    inv = lax.rsqrt(u)
    tail = (1.0 - lax.erf(u * inv)) * inv
    gauss = scaled_gaussian(u)
    rest = gauss * (u - 1.5)
    return tail + rest, ((tail - rest) - gauss) * (inv * inv)


def velocity_terms(target, source, force, coef_c, coef_d):
    delta = [t - s for t, s in zip(target, source)]
    along = coef_d * (delta[0] * force[0] + delta[1] * force[1] + delta[2] * force[2])
    return [coef_c * f + along * d for f, d in zip(force, delta)]


def all_pairs(n_groups, chunks_of, blocks_of, max_chunks, max_blocks, refs):
    listed, spread, coefs, acc = refs
    components = range(3)

    def targets(first):
        at = pl.ds(pl.multiple_of(first, CHUNK), CHUNK)
        return [spread[i, at, :] for i in components]

    def rows(tile_id, at):
        return [[listed[tile_id + b, i : i + 1, :] for i in at] for b in range(WIDE)]

    total = jnp.int32(0)
    for group in range(n_groups):
        total = total + chunks_of[group] * blocks_of[group]
    acc[...] = jnp.zeros_like(acc)
    coefs[...] = jnp.zeros_like(coefs)

    def one_item(item, state):
        group, chunk, block, old_first, old_tile = state
        new_first = (group * max_chunks + chunk) * CHUNK
        new_tile = (group * max_blocks + block) * WIDE
        old_at = pl.ds(pl.multiple_of(old_first, CHUNK), CHUNK)
        old_coefs = [(coefs[b, 0], coefs[b, 1]) for b in range(WIDE)]
        sums = [acc[i, old_at, :] for i in components]
        old_target, old_source = targets(old_first), rows(old_tile, (0, 1, 2))
        old_force = rows(old_tile, (4, 5, 6))
        new_target, new_source = targets(new_first), rows(new_tile, (0, 1, 2))

        new_coefs = [coefficients(new_target, source) for source in new_source]
        for pair in zip(old_source, old_force, old_coefs):
            terms = velocity_terms(old_target, pair[0], pair[1], *pair[2])
            sums = [s + t for s, t in zip(sums, terms)]

        for i in components:
            acc[i, old_at, :] = sums[i]
        for b in range(WIDE):
            coefs[b, 0], coefs[b, 1] = new_coefs[b]

        end_block = block + 1 == blocks_of[group]
        next_block = jnp.where(end_block, 0, block + 1)
        next_chunk = jnp.where(end_block, chunk + 1, chunk)
        end_chunk = next_chunk == chunks_of[group]
        next_chunk = jnp.where(end_chunk, 0, next_chunk)
        next_group = jnp.where(end_chunk, jnp.minimum(group + 1, n_groups - 1), group)
        return next_group, next_chunk, next_block, new_first, new_tile

    lax.fori_loop(0, total + 1, one_item, (jnp.int32(0),) * 5)


def lane_sums(acc, first):
    row, _ = rows_and_lanes()
    parts = [jnp.concatenate(parts_of(acc[i, pl.ds(first, LANES), :]), axis=1) for i in range(3)]
    sums = lax.dot_general(
        jnp.ones((2 * ROWS, 3 * LANES), jnp.bfloat16),
        jnp.concatenate(parts, axis=0),
        (((1,), (1,)), ((), ())),
        preferred_element_type=jnp.float32,
    )[:ROWS]
    merged = jnp.zeros((ROWS, LANES), jnp.float32)
    for i in range(3):
        merged = jnp.where(row == i, sums[:, i * LANES : (i + 1) * LANES], merged)
    return merged


def inner_kernel(cells, count_ref, own_ref, out_ref, chunks_of, blocks_of, *refs):
    listed, spread, coefs, acc, result = refs
    row, lane = rows_and_lanes()
    n_bins = cells[0] * cells[1] * cells[2]
    bins = [(i, j, k) for i in range(cells[0]) for j in range(cells[1]) for k in range(cells[2])]
    sources, counts = [], []
    for at in bins:
        moved = jnp.zeros((ROWS, LANES), jnp.float32)
        for i in range(3):
            moved = jnp.where(row == i, SPLIT_XI * (at[i] - 0.5 * (cells[i] - 1)), moved)
        counts.append(count_ref[at])
        sources.append((own_ref[at] + moved, counts[-1]))
    filled = compact(listed, 0, sources)
    n_tiles = lax.div(filled + LANES - 1, LANES)
    n_blocks = lax.div(filled + BLOCK - 1, BLOCK)
    blocks_of[0] = n_blocks
    chunks_of[0] = lax.div(filled + CHUNK - 1, CHUNK)

    def prepare(tile_id, carry):
        spread_targets(spread, pl.multiple_of(tile_id * LANES, LANES), listed[tile_id])
        return carry

    lax.fori_loop(0, n_tiles, prepare, 0)
    refs = (listed, spread, coefs, acc)
    all_pairs(1, chunks_of, blocks_of, n_bins * LANES // CHUNK, n_bins // WIDE, refs)

    def finish(tile_id, carry):
        sums = lane_sums(acc, pl.multiple_of(tile_id * LANES, LANES))
        tile = listed[tile_id]
        own = pltpu.roll(tile, ROWS - FORCE_ROW, 0)
        result[tile_id] = (2.0 * STOKES_NORM) * sums - (STOKES_NORM * SELF_C) * own
        return carry

    lax.fori_loop(0, n_tiles, finish, 0)
    before = jnp.int32(0)
    for at, count in zip(bins, counts):
        tile_id = lax.shift_right_logical(before, 7)
        back = LANES - lax.bitwise_and(before, LANES - 1)
        turn = lax.bitwise_and(back, LANES - 1)
        part = jnp.where(
            lane < back, pltpu.roll(result[tile_id], turn, 1), pltpu.roll(result[tile_id + 1], turn, 1)
        )
        out_ref[at] = part
        before = before + count


def outer_kernel(cells, *refs):
    pieces, (inner_ref, out_ref), refs = refs[:6], refs[6:8], refs[8:]
    ext, count_v, count_s, sem, chunks_of, blocks_of = refs[:6]
    listed, spread, coefs, acc = refs[6:]
    own, other, x_lo, x_hi, y_lo, y_hi = pieces
    size_x, size_y, size_z = cells
    n_z = 2 * size_z
    n_bins = size_x * size_y * size_z
    row, lane = rows_and_lanes()

    held = jnp.zeros((ROWS, LANES), jnp.float32)
    for ix in range(size_x + 2):
        for iy in range(size_y + 2):
            for iz in range(n_z):
                if iy == 0:
                    tile = y_lo[ix, 0, iz]
                elif iy == size_y + 1:
                    tile = y_hi[ix, 0, iz]
                elif ix == 0:
                    tile = x_lo[0, iy - 1, iz]
                elif ix == size_x + 1:
                    tile = x_hi[0, iy - 1, iz]
                elif iz < size_z:
                    tile = own[ix - 1, iy - 1, iz]
                else:
                    tile = other[ix - 1, iy - 1, iz - size_z]
                cell = (ix * (size_y + 2) + iy) * n_z + iz
                ext[cell] = tile
                held = jnp.where(lane == cell, tile, held)
    count_v[...] = held.astype(jnp.int32)
    copy = pltpu.make_async_copy(count_v, count_s, sem)
    copy.start()
    copy.wait()

    max_tiles = listed.shape[0] // n_bins
    steps = [
        (a, b, c) for a in (0, -1, 1) for b in (0, -1, 1) for c in (0, -1, 1) if 1 in (a, b, c)
    ]

    def prepare(flat_id, carry):
        at = (flat_id // (size_y * size_z), flat_id // size_z % size_y, flat_id % size_z)
        out = [2 * i - 1 for i in at]
        moves = [
            jnp.where(row == i, (SPLIT_XI * out[i].astype(jnp.float32)), 0.0) for i in range(3)
        ]
        sources = []
        for step in steps:
            moved = sum(s * m for s, m in zip(step, moves) if s != 0)
            x, y, z = (i + s * o for i, s, o in zip(at, step, out))
            cell = ((x + 1) * (size_y + 2) + y + 1) * n_z + lax.rem(z + n_z, n_z)
            sources.append((ext[cell] + moved, count_s[COUNT_ROW, cell]))
        filled = compact(listed, flat_id * max_tiles, sources)
        n_blocks = lax.div(filled + BLOCK - 1, BLOCK)
        own_cell = ((at[0] + 1) * (size_y + 2) + at[1] + 1) * n_z + at[2]
        blocks_of[flat_id] = n_blocks
        chunks_of[flat_id] = lax.div(count_s[COUNT_ROW, own_cell] + CHUNK - 1, CHUNK)

        spread_targets(spread, pl.multiple_of(flat_id * LANES, LANES), ext[own_cell])
        return carry

    lax.fori_loop(0, n_bins, prepare, 0)
    refs = (listed, spread, coefs, acc)
    all_pairs(n_bins, chunks_of, blocks_of, LANES // CHUNK, max_tiles // WIDE, refs)

    slot = lax.broadcasted_iota(jnp.int32, (1, LANES), 1)
    for ix in range(size_x):
        for iy in range(size_y):
            for iz in range(size_z):
                flat_id = (ix * size_y + iy) * size_z + iz
                sums = lane_sums(acc, flat_id * LANES)
                total = (2.0 * STOKES_NORM) * sums + inner_ref[ix, iy, iz]
                count = count_s[COUNT_ROW, ((ix + 1) * (size_y + 2) + iy + 1) * n_z + iz]
                for i in range(3):
                    out_ref[i, ix, iy, iz : iz + 1, :] = jnp.where(
                        slot < count, total[i : i + 1], 0.0
                    )


def shifted(array, axis, dim):
    size, length = lax.axis_size(axis), array.shape[dim]
    up = [(i, (i + 1) % size) for i in range(size)]
    down = [(j, i) for i, j in up]
    before = lax.ppermute(lax.slice_in_dim(array, length - 1, length, axis=dim), axis, up)
    after = lax.ppermute(lax.slice_in_dim(array, 0, 1, axis=dim), axis, down)
    return before, after


def pair_scratch(n_targets, n_tiles):
    return [
        pltpu.VMEM((n_tiles, ROWS, LANES), jnp.float32),
        pltpu.VMEM((3, n_targets, LANES), jnp.float32),
        pltpu.VMEM((WIDE, 2, CHUNK, LANES), jnp.float32),
        pltpu.VMEM((3, n_targets, LANES), jnp.float32),
    ]


def on_device(offsets, forces, counts):
    cells = offsets.shape[1:4]
    slots = offsets.shape[4]
    n_bins = cells[0] * cells[1] * cells[2]
    n_cells = (cells[0] + 2) * (cells[1] + 2) * 2 * cells[2]
    whole = pl.BlockSpec(memory_space=pltpu.VMEM)
    scalars = pl.BlockSpec(memory_space=pltpu.SMEM)
    tiles = jax.ShapeDtypeStruct(cells + (ROWS, slots), jnp.float32)
    own, sent = pl.pallas_call(
        functools.partial(pack_kernel, cells),
        out_shape=[tiles, tiles],
        in_specs=[scalars, whole, whole],
        out_specs=[whole, whole],
        name="pack",
    )(counts, offsets, forces)

    size = lax.axis_size("ha")
    other = lax.ppermute(sent, "ha", [(i, (i + 1) % size) for i in range(size)])
    params = pltpu.CompilerParams(vmem_limit_bytes=24 << 20)
    inner = pl.pallas_call(
        functools.partial(inner_kernel, cells),
        out_shape=tiles,
        in_specs=[scalars, whole],
        out_specs=whole,
        scratch_shapes=[pltpu.SMEM((1,), jnp.int32), pltpu.SMEM((1,), jnp.int32)]
        + pair_scratch(n_bins * LANES, n_bins + WIDE)
        + [pltpu.VMEM((n_bins + 2, ROWS, LANES), jnp.float32)],
        compiler_params=params,
        cost_estimate=pl.CostEstimate(flops=1 << 30, bytes_accessed=1 << 16, transcendentals=1 << 22),
        name="inner",
    )(counts, own)
    other, inner = lax.optimization_barrier((other, inner))
    column = jnp.concatenate([own, other], axis=2)
    x_lo, x_hi = shifted(column, "gx", 0)
    wide = jnp.concatenate([x_lo, column, x_hi], axis=0)
    y_lo, y_hi = shifted(wide, "gy", 1)

    max_tiles = 20 + WIDE
    return pl.pallas_call(
        functools.partial(outer_kernel, cells),
        out_shape=jax.ShapeDtypeStruct((3,) + cells + (slots,), jnp.float32),
        in_specs=[whole] * 7,
        out_specs=whole,
        scratch_shapes=[
            pltpu.VMEM((n_cells, ROWS, LANES), jnp.float32),
            pltpu.VMEM((ROWS, LANES), jnp.int32),
            pltpu.SMEM((ROWS, LANES), jnp.int32),
            pltpu.SemaphoreType.DMA,
            pltpu.SMEM((n_bins,), jnp.int32),
            pltpu.SMEM((n_bins,), jnp.int32),
        ]
        + pair_scratch(n_bins * LANES, n_bins * max_tiles),
        compiler_params=params,
        name="outer",
    )(own, other, x_lo, x_hi, y_lo, y_hi, inner)


def solution(mesh):
    in_specs = (
        P(None, "gx", "gy", "ha", None),
        P(None, "gx", "gy", "ha", None),
        P("gx", "gy", "ha"),
    )
    out_specs = P(None, "gx", "gy", "ha", None)
    return jax.shard_map(on_device, mesh=mesh, in_specs=in_specs, out_specs=out_specs, check_vma=False)
```

```python
import functools
import math

import jax
import jax.numpy as jnp
from jax import lax
from jax.experimental import pallas as pl
from jax.experimental.pallas import tpu as pltpu
from jax.sharding import PartitionSpec as P

SPLIT_XI = 2.0
SOFT_SQ = 0.01
GAUSS_COEF = 2.0 * SPLIT_XI / math.sqrt(math.pi)
STOKES_NORM = 1.0 / (8.0 * math.pi)

SOFT_U = SPLIT_XI * SPLIT_XI * SOFT_SQ
LOG2_E = math.log2(math.e)
LOG2_G = math.log2(GAUSS_COEF)
SELF_C = math.erfc(math.sqrt(SOFT_U)) / math.sqrt(SOFT_SQ) + GAUSS_COEF * (
    2.0 * SOFT_U - 3.0
) * math.exp(-SOFT_U)

LANES = 128
ROWS = 8
CHUNK = 32
WIDE = 2
BLOCK = WIDE * LANES
COUNT_ROW = 3
FORCE_ROW = 4


def rows_and_lanes(shape=(ROWS, LANES)):
    return lax.broadcasted_iota(jnp.int32, shape, 0), lax.broadcasted_iota(jnp.int32, shape, 1)


def pack_kernel(cells, count_ref, offset_ref, force_ref, out_ref, sent_ref):
    slot = lax.broadcasted_iota(jnp.int32, (1, LANES), 1)
    for ix in range(cells[0]):
        for iy in range(cells[1]):
            for iz in range(cells[2]):
                count = count_ref[ix, iy, iz]
                filled = jnp.full((1, LANES), count, jnp.int32).astype(jnp.float32)
                for i in range(3):
                    position = offset_ref[i, ix, iy, iz : iz + 1, :]
                    out_ref[ix, iy, iz, i : i + 1, :] = position * SPLIT_XI - 0.5 * SPLIT_XI
                    force = force_ref[i, ix, iy, iz : iz + 1, :]
                    at = FORCE_ROW + i
                    out_ref[ix, iy, iz, at : at + 1, :] = jnp.where(slot < count, force, 0.0)
                out_ref[ix, iy, iz, 3:4, :] = filled
                out_ref[ix, iy, iz, 7:8, :] = filled
                sent_ref[ix, iy, iz] = out_ref[ix, iy, iz]


def compact(listed, base, sources):
    _, lane = rows_and_lanes()
    filled = jnp.int32(0)
    moved = []
    for tile, count in sources:
        at = lax.bitwise_and(filled, LANES - 1)
        tile_id = base + lax.shift_right_logical(filled, 7)
        moved.append((pltpu.roll(tile, at, 1), lane >= at, tile_id, at + count >= LANES))
        filled = filled + count
    current = jnp.zeros((ROWS, LANES), jnp.float32)
    for tile, behind, tile_id, full in moved:
        current = jnp.where(behind, tile, current)
        spill = jnp.where(behind, 0.0, tile)
        listed[tile_id] = current
        listed[tile_id + 1] = spill
        current = jnp.where(full, spill, current)
    last = base + lax.shift_right_logical(filled, 7)
    for more in range(1, WIDE):
        listed[last + more] = jnp.zeros((ROWS, LANES), jnp.float32)
    return filled


def parts_of(value):
    high = value.astype(jnp.bfloat16)
    rest = value - high.astype(jnp.float32)
    middle = rest.astype(jnp.bfloat16)
    low = rest - middle.astype(jnp.float32)
    return high, middle, low.astype(jnp.bfloat16)


def spread_targets(spread, first, tile):
    parts = jnp.concatenate([p.astype(jnp.float32) for p in parts_of(tile)] + [jnp.zeros_like(tile)], axis=0)
    shape = (4 * ROWS, 3 * LANES)
    row, lane = rows_and_lanes(shape)
    pick = jnp.where(lax.rem(row, ROWS) == lax.div(lane, LANES), 1.0, 0.0)
    wide = lax.dot_general(
        parts.astype(jnp.bfloat16),
        pick.astype(jnp.bfloat16),
        (((0,), (0,)), ((), ())),
        preferred_element_type=jnp.float32,
    )
    for i in range(3):
        spread[i, pl.ds(first, LANES), :] = wide[:, i * LANES : (i + 1) * LANES]


def coefficients(target, source, force):
    delta = [t - s for t, s in zip(target, source)]
    u = (delta[0] * delta[0] + SOFT_U) + delta[1] * delta[1] + delta[2] * delta[2]
    inv = lax.rsqrt(u)
    tail = (1.0 - lax.erf(u * inv)) * inv
    gauss = jnp.exp2(LOG2_G - u * LOG2_E)
    rest = gauss * (u - 1.5)
    coef_d = ((tail - rest) - gauss) * (inv * inv)
    along = coef_d * (delta[0] * force[0] + delta[1] * force[1] + delta[2] * force[2])
    return tail + rest, along


def all_pairs(groups, limits, max_chunks, max_blocks, refs):
    listed, spread, coefs, acc = refs

    def rows(tile_id, at):
        return [[listed[tile_id + b, i : i + 1, :] for i in at] for b in range(WIDE)]

    total = jnp.int32(0)
    for group in range(groups):
        begin, end, blocks = limits(group)
        total = total + (end - begin) * blocks
    coefs[...] = jnp.zeros_like(coefs)

    def one_item(item, state):
        group, chunk, block, old_first, old_tile = state
        new_first = (group * max_chunks + chunk) * CHUNK
        new_tile = (group * max_blocks + block) * WIDE
        old_at = pl.ds(pl.multiple_of(old_first, CHUNK), CHUNK)
        new_at = pl.ds(pl.multiple_of(new_first, CHUNK), CHUNK)
        old_coefs = [(coefs[b, 0], coefs[b, 1]) for b in range(WIDE)]
        sums = [acc[i, old_at, :] for i in range(4)]
        old_source, old_force = rows(old_tile, (0, 1, 2)), rows(old_tile, (4, 5, 6))
        target = [spread[i, new_at, :] for i in range(3)]
        new_source, new_force = rows(new_tile, (0, 1, 2)), rows(new_tile, (4, 5, 6))

        new_coefs = [coefficients(target, *pair) for pair in zip(new_source, new_force)]
        for source, force, (coef_c, along) in zip(old_source, old_force, old_coefs):
            for i in range(3):
                sums[i] = sums[i] + (coef_c * force[i] - along * source[i])
            sums[3] = sums[3] + along

        for i in range(4):
            acc[i, old_at, :] = sums[i]
        for b in range(WIDE):
            coefs[b, 0], coefs[b, 1] = new_coefs[b]

        _, end, blocks = limits(group)
        end_block = block + 1 == blocks
        next_block = jnp.where(end_block, 0, block + 1)
        next_chunk = jnp.where(end_block, chunk + 1, chunk)
        next_group = jnp.where(next_chunk == end, jnp.minimum(group + 1, groups - 1), group)
        next_chunk = jnp.where(next_chunk == end, 0, next_chunk)
        return next_group, next_chunk, next_block, new_first, new_tile

    first = limits(0)[0]
    zero = jnp.int32(0)
    lax.fori_loop(0, total + 1, one_item, (zero, first, zero, first * CHUNK, zero))


def velocities(acc, first, tile):
    row, _ = rows_and_lanes()
    parts = [jnp.concatenate(parts_of(acc[i, pl.ds(first, LANES), :]), axis=1) for i in range(4)]
    sums = lax.dot_general(
        jnp.ones((2 * ROWS, 3 * LANES), jnp.bfloat16),
        jnp.concatenate(parts, axis=0),
        (((1,), (1,)), ((), ())),
        preferred_element_type=jnp.float32,
    )[:ROWS]
    merged = tile * sums[:, 3 * LANES :]
    for i in range(3):
        merged = merged + jnp.where(row == i, sums[:, i * LANES : (i + 1) * LANES], 0.0)
    return (2.0 * STOKES_NORM) * merged


def bins_of(cells):
    return [(i, j, k) for i in range(cells[0]) for j in range(cells[1]) for k in range(cells[2])]


def inner_kernel(cells, part, parts, count_ref, own_ref, out_ref, listed, spread, coefs, acc):
    row, _ = rows_and_lanes()
    sources = []
    for at in bins_of(cells):
        moved = jnp.zeros((ROWS, LANES), jnp.float32)
        for i in range(3):
            moved = jnp.where(row == i, SPLIT_XI * (at[i] - 0.5 * (cells[i] - 1)), moved)
        sources.append((own_ref[at] + moved, count_ref[at]))
    filled = compact(listed, 0, sources)
    n_chunks = lax.div(filled + CHUNK - 1, CHUNK)
    n_blocks = lax.div(filled + BLOCK - 1, BLOCK)
    n_tiles = lax.div(filled + LANES - 1, LANES)
    begin, end = lax.div(n_tiles * part, parts), lax.div(n_tiles * (part + 1), parts)
    per_tile = LANES // CHUNK
    out_ref[...] = jnp.zeros_like(out_ref)

    def prepare(tile_id, carry):
        first = pl.multiple_of(tile_id * LANES, LANES)
        spread_targets(spread, first, listed[tile_id])
        for i in range(4):
            acc[i, pl.ds(first, LANES), :] = jnp.zeros((LANES, LANES), jnp.float32)
        return carry

    lax.fori_loop(begin, end, prepare, 0)
    limits = (begin * per_tile, jnp.minimum(end * per_tile, n_chunks), n_blocks)
    all_pairs(1, lambda group: limits, acc.shape[1] // CHUNK, 0, (listed, spread, coefs, acc))

    def finish(tile_id, carry):
        tile = listed[tile_id]
        total = velocities(acc, pl.multiple_of(tile_id * LANES, LANES), tile)
        own = pltpu.roll(tile, ROWS - FORCE_ROW, 0)
        out_ref[tile_id] = total - (STOKES_NORM * SELF_C) * own
        return carry

    lax.fori_loop(begin, end, finish, 0)


def around(cells, steps, cell_of, refs, targets, ext, count_s, copy):
    listed, spread, coefs, acc, blocks_of, count_ref = refs
    size_x, size_y, size_z = cells
    row, _ = rows_and_lanes()
    bins = bins_of(cells)
    acc[...] = jnp.zeros_like(acc)
    for n, at in enumerate(bins):
        spread_targets(spread, n * LANES, targets[at])
    copy.wait()
    max_tiles = listed.shape[0] // len(bins)

    def prepare(flat_id, carry):
        at = (flat_id // (size_y * size_z), flat_id // size_z % size_y, flat_id % size_z)
        out = [2 * i - 1 for i in at]
        moves = [
            jnp.where(row == i, (SPLIT_XI * out[i].astype(jnp.float32)), 0.0) for i in range(3)
        ]
        sources = []
        for step in steps:
            moved = sum(s * m for s, m in zip(step, moves) if s != 0)
            cell = cell_of(*(i + s * o for i, s, o in zip(at, step, out)))
            sources.append((ext[cell] + moved, count_s[COUNT_ROW, cell]))
        filled = compact(listed, flat_id * max_tiles, sources)
        blocks_of[flat_id] = lax.div(filled + BLOCK - 1, BLOCK)
        return carry

    lax.fori_loop(0, len(bins), prepare, 0)

    def limits(group):
        if isinstance(group, int):
            count = count_ref[bins[group]]
        else:
            count = count_ref[group // (size_y * size_z), group // size_z % size_y, group % size_z]
        return 0, lax.div(count + CHUNK - 1, CHUNK), blocks_of[group]

    all_pairs(
        len(bins), limits, LANES // CHUNK, max_tiles // WIDE, (listed, spread, coefs, acc)
    )
    return [velocities(acc, n * LANES, targets[at]) for n, at in enumerate(bins)]


STEPS = [(a, b, c) for a in (0, -1, 1) for b in (0, -1, 1) for c in (0, -1, 1)]
OUT_Y = [step for step in STEPS if step[1] == 1]
OUT_XZ = [step for step in STEPS if step[1] != 1 and 1 in step]


def start_counts(tiles, count_v, count_s, sem):
    _, lane = rows_and_lanes()
    held = jnp.zeros((ROWS, LANES), jnp.float32)
    for cell, tile in enumerate(tiles):
        held = jnp.where(lane == cell, tile, held)
    count_v[...] = held.astype(jnp.int32)
    copy = pltpu.make_async_copy(count_v, count_s, sem)
    copy.start()
    return copy


def middle_kernel(cells, parts, count_ref, own_ref, wide_ref, *refs):
    results, (out_ref, ext, count_v, count_s, sem), refs = refs[:parts], refs[parts : parts + 5], refs[parts + 5 :]
    result, refs = refs[-1], refs[:-1]
    size_x, size_y, size_z = cells
    n_z = 2 * size_z
    places = [(i, j, k) for i in range(size_x + 2) for j in range(size_y) for k in range(n_z)]
    tiles = [wide_ref[at] for at in places]
    for n, tile in enumerate(tiles):
        ext[n] = tile
    copy = start_counts(tiles, count_v, count_s, sem)

    def cell_of(x, y, z):
        return ((x + 1) * size_y + y) * n_z + lax.rem(z + n_z, n_z)

    totals = around(cells, OUT_XZ, cell_of, refs + (count_ref,), own_ref, ext, count_s, copy)
    for n in range(result.shape[0]):
        result[n] = sum(r[n] for r in results)
    _, lane = rows_and_lanes()
    before = jnp.int32(0)
    for at, total in zip(bins_of(cells), totals):
        tile_id = lax.shift_right_logical(before, 7)
        back = LANES - lax.bitwise_and(before, LANES - 1)
        turn = lax.bitwise_and(back, LANES - 1)
        part = jnp.where(
            lane < back, pltpu.roll(result[tile_id], turn, 1), pltpu.roll(result[tile_id + 1], turn, 1)
        )
        out_ref[at] = total + part
        before = before + count_ref[at]


def last_kernel(cells, count_ref, own_ref, y_lo, y_hi, middle_ref, out_ref, ext, count_v, count_s, sem, *refs):
    size_x, size_y, size_z = cells
    n_z = 2 * size_z
    tiles = []
    for ix in range(size_x + 2):
        for side in (y_lo, y_hi):
            tiles += [side[ix, 0, iz] for iz in range(n_z)]
    for n, tile in enumerate(tiles):
        ext[n] = tile
    copy = start_counts(tiles, count_v, count_s, sem)

    def cell_of(x, y, z):
        return ((x + 1) * 2 + lax.div(y + 1, size_y + 1)) * n_z + lax.rem(z + n_z, n_z)

    totals = around(cells, OUT_Y, cell_of, refs + (count_ref,), own_ref, ext, count_s, copy)
    slot = lax.broadcasted_iota(jnp.int32, (1, LANES), 1)
    for at, total in zip(bins_of(cells), totals):
        total = jnp.where(slot < count_ref[at], total + middle_ref[at], 0.0)
        for i in range(3):
            out_ref[i, at[0], at[1], at[2] : at[2] + 1, :] = total[i : i + 1]


def shifted(array, axis, dim):
    size, length = lax.axis_size(axis), array.shape[dim]
    up = [(i, (i + 1) % size) for i in range(size)]
    down = [(j, i) for i, j in up]
    before = lax.ppermute(lax.slice_in_dim(array, length - 1, length, axis=dim), axis, up)
    after = lax.ppermute(lax.slice_in_dim(array, 0, 1, axis=dim), axis, down)
    return before, after


def pair_scratch(n_targets, n_tiles):
    return [
        pltpu.VMEM((n_tiles, ROWS, LANES), jnp.float32),
        pltpu.VMEM((3, n_targets, LANES), jnp.float32),
        pltpu.VMEM((WIDE, 2, CHUNK, LANES), jnp.float32),
        pltpu.VMEM((4, n_targets, LANES), jnp.float32),
    ]


PARTS = 3


def on_device(offsets, forces, counts):
    cells = offsets.shape[1:4]
    slots = offsets.shape[4]
    n_bins = cells[0] * cells[1] * cells[2]
    whole = pl.BlockSpec(memory_space=pltpu.VMEM)
    scalars = pl.BlockSpec(memory_space=pltpu.SMEM)
    tiles = jax.ShapeDtypeStruct(cells + (ROWS, slots), jnp.float32)
    listed = jax.ShapeDtypeStruct((n_bins + WIDE, ROWS, slots), jnp.float32)

    def params(mib):
        return pltpu.CompilerParams(vmem_limit_bytes=mib << 20)

    own, sent = pl.pallas_call(
        functools.partial(pack_kernel, cells),
        out_shape=[tiles, tiles],
        in_specs=[scalars, whole, whole],
        out_specs=[whole, whole],
        compiler_params=params(4),
        name="pack",
    )(counts, offsets, forces)

    def inner(part, own):
        return pl.pallas_call(
            functools.partial(inner_kernel, cells, part, PARTS),
            out_shape=listed,
            in_specs=[scalars, whole],
            out_specs=whole,
            scratch_shapes=pair_scratch(n_bins * LANES, n_bins + WIDE),
            compiler_params=params(8),
            cost_estimate=pl.CostEstimate(flops=1 << 28, bytes_accessed=1 << 16, transcendentals=1 << 20),
            name="inner%d" % part,
        )(counts, own)

    def around_call(kernel, n_steps, out_shape, name, *args):
        n_tiles = (n_steps + 2 * WIDE - 1) // WIDE * WIDE
        return pl.pallas_call(
            kernel,
            out_shape=out_shape,
            in_specs=[scalars] + [whole] * len(args),
            out_specs=whole,
            scratch_shapes=[
                pltpu.VMEM((2 * (cells[0] + 2) * 2 * cells[2], ROWS, LANES), jnp.float32),
                pltpu.VMEM((ROWS, LANES), jnp.int32),
                pltpu.SMEM((ROWS, LANES), jnp.int32),
                pltpu.SemaphoreType.DMA,
            ]
            + pair_scratch(n_bins * LANES, n_bins * n_tiles)
            + [pltpu.SMEM((n_bins,), jnp.int32)]
            + ([pltpu.VMEM(listed.shape, jnp.float32)] if name == "middle" else []),
            compiler_params=params(8),
            cost_estimate=pl.CostEstimate(flops=1 << 28, bytes_accessed=1 << 16, transcendentals=1 << 20),
            name=name,
        )(counts, *args)

    together = lax.optimization_barrier
    first = inner(0, own)
    sent, own_1, first = together((sent, own, first))
    size = lax.axis_size("ha")
    other = lax.ppermute(sent, "ha", [(i, (i + 1) % size) for i in range(size)])
    second = inner(1, own_1)
    other, own_2, second = together((other, own, second))
    column = jnp.concatenate([own_2, other], axis=2)
    x_lo, x_hi = shifted(column, "gx", 0)
    third = inner(2, own_2)
    x_lo, x_hi, third = together((x_lo, x_hi, third))
    wide = jnp.concatenate([x_lo, column, x_hi], axis=0)
    y_lo, y_hi = shifted(wide, "gy", 1)
    middle = around_call(
        functools.partial(middle_kernel, cells, PARTS),
        len(OUT_XZ),
        tiles,
        "middle",
        own,
        wide,
        first,
        second,
        third,
    )
    y_lo, y_hi, middle = together((y_lo, y_hi, middle))
    out = jax.ShapeDtypeStruct((3,) + cells + (slots,), jnp.float32)
    return around_call(
        functools.partial(last_kernel, cells), len(OUT_Y), out, "last", own, y_lo, y_hi, middle
    )


def solution(mesh):
    in_specs = (
        P(None, "gx", "gy", "ha", None),
        P(None, "gx", "gy", "ha", None),
        P("gx", "gy", "ha"),
    )
    out_specs = P(None, "gx", "gy", "ha", None)
    return jax.shard_map(on_device, mesh=mesh, in_specs=in_specs, out_specs=out_specs, check_vma=False)
```

```python
import functools
import math

import jax
import jax.numpy as jnp
from jax import lax
from jax.experimental import pallas as pl
from jax.experimental.pallas import tpu as pltpu
from jax.sharding import PartitionSpec as P

SPLIT_XI = 2.0
SOFT_SQ = 0.01
GAUSS_COEF = 2.0 * SPLIT_XI / math.sqrt(math.pi)
STOKES_NORM = 1.0 / (8.0 * math.pi)

SOFT_U = SPLIT_XI * SPLIT_XI * SOFT_SQ
LOG2_E = math.log2(math.e)
LOG2_G = math.log2(GAUSS_COEF)
SELF_C = math.erfc(math.sqrt(SOFT_U)) / math.sqrt(SOFT_SQ) + GAUSS_COEF * (
    2.0 * SOFT_U - 3.0
) * math.exp(-SOFT_U)

LANES = 128
ROWS = 8
CHUNK = 32
WIDE = 2
BLOCK = WIDE * LANES
COUNT_ROW = 3
FORCE_ROW = 4


def rows_and_lanes(shape=(ROWS, LANES)):
    return lax.broadcasted_iota(jnp.int32, shape, 0), lax.broadcasted_iota(jnp.int32, shape, 1)


def bins_of(cells):
    return [(i, j, k) for i in range(cells[0]) for j in range(cells[1]) for k in range(cells[2])]


def shift_tile(cells, at):
    row, _ = rows_and_lanes()
    moved = jnp.zeros((ROWS, LANES), jnp.float32)
    for i in range(3):
        moved = jnp.where(row == i, SPLIT_XI * (at[i] - 0.5 * (cells[i] - 1)), moved)
    return moved


def compact(listed, base, sources):
    _, lane = rows_and_lanes()
    filled = jnp.int32(0)
    moved = []
    for tile, count in sources:
        at = lax.bitwise_and(filled, LANES - 1)
        tile_id = base + lax.shift_right_logical(filled, 7)
        moved.append((pltpu.roll(tile, at, 1), lane >= at, tile_id, at + count >= LANES))
        filled = filled + count
    current = jnp.zeros((ROWS, LANES), jnp.float32)
    for tile, behind, tile_id, full in moved:
        current = jnp.where(behind, tile, current)
        spill = jnp.where(behind, 0.0, tile)
        listed[tile_id] = current
        listed[tile_id + 1] = spill
        current = jnp.where(full, spill, current)
    last = base + lax.shift_right_logical(filled, 7)
    for more in range(1, WIDE):
        listed[last + more] = jnp.zeros((ROWS, LANES), jnp.float32)
    return filled


def up_to(count, size):
    return lax.shift_right_logical(count + (size - 1), size.bit_length() - 1)


def parts_of(value, n):
    parts = []
    for _ in range(n):
        part = value.astype(jnp.bfloat16)
        value = value - part.astype(jnp.float32)
        parts.append(part)
    return parts


def spread_targets(spread, first, tile):
    parts = [p.astype(jnp.float32) for p in parts_of(tile, 3)] + [jnp.zeros_like(tile)]
    row, lane = rows_and_lanes((4 * ROWS, 3 * LANES))
    pick = jnp.where(lax.bitwise_and(row, ROWS - 1) == lax.shift_right_logical(lane, 7), 1.0, 0.0)
    wide = lax.dot_general(
        jnp.concatenate(parts, axis=0).astype(jnp.bfloat16),
        pick.astype(jnp.bfloat16),
        (((0,), (0,)), ((), ())),
        preferred_element_type=jnp.float32,
    )
    for i in range(3):
        spread[i, first : first + LANES, :] = wide[:, i * LANES : (i + 1) * LANES]


def pre_kernel(
    cells, count_hbm, offset_hbm, force_hbm, own_ref, listed, spread, count_ref, offset_v, force_v, sems
):
    copies = [
        pltpu.make_async_copy(offset_hbm, offset_v, sems.at[0]),
        pltpu.make_async_copy(force_hbm, force_v, sems.at[1]),
        pltpu.make_async_copy(count_hbm, count_ref, sems.at[2]),
    ]
    for copy in copies:
        copy.start()
    for copy in copies:
        copy.wait()
    slot = lax.broadcasted_iota(jnp.int32, (1, LANES), 1)
    for at in bins_of(cells):
        ix, iy, iz = at
        count = count_ref[at]
        filled = jnp.full((1, LANES), count, jnp.int32).astype(jnp.float32)
        for i in range(3):
            position = offset_v[i, ix, iy, iz : iz + 1, :]
            own_ref[ix, iy, iz, i : i + 1, :] = position * SPLIT_XI - 0.5 * SPLIT_XI
            force = force_v[i, ix, iy, iz : iz + 1, :]
            own_ref[ix, iy, iz, 4 + i : 5 + i, :] = jnp.where(slot < count, force, 0.0)
        own_ref[ix, iy, iz, 3:4, :] = filled
        own_ref[ix, iy, iz, 7:8, :] = filled
    tiles = [own_ref[at] + shift_tile(cells, at) for at in bins_of(cells)]
    compact(listed, 0, [(tile, count_ref[at]) for tile, at in zip(tiles, bins_of(cells))])
    for n, tile in enumerate(tiles):
        spread_targets(spread, n * LANES, tile)


def coefficients(target, source, force):
    delta = [t - s for t, s in zip(target, source)]
    u = (delta[0] * delta[0] + SOFT_U) + delta[1] * delta[1] + delta[2] * delta[2]
    inv = lax.rsqrt(u)
    tail = (1.0 - lax.erf(u * inv)) * inv
    gauss = jnp.exp2(LOG2_G - u * LOG2_E)
    rest = gauss * (u - 1.5)
    coef_d = ((tail - rest) - gauss) * (inv * inv)
    along = coef_d * (delta[0] * force[0] + delta[1] * force[1] + delta[2] * force[2])
    return tail + rest, along


def all_pairs(groups, chunks_of, blocks_of, list_of, listed, spread, coefs, acc):
    n_groups = len(groups)

    def rows(tile_id, at):
        return [[listed[tile_id + b, i : i + 1, :] for i in at] for b in range(WIDE)]

    total = jnp.int32(0)
    for group in range(n_groups):
        total = total + chunks_of[group] * blocks_of[group]
    coefs[...] = jnp.zeros_like(coefs)

    def one_item(item, state):
        group, chunk, block, old_first, old_tile = state
        new_first = group * LANES + chunk * CHUNK
        new_tile = list_of(group) + block * WIDE
        old_at = pl.ds(pl.multiple_of(old_first, CHUNK), CHUNK)
        new_at = pl.ds(pl.multiple_of(new_first + groups.start * LANES, CHUNK), CHUNK)
        old_coefs = [(coefs[b, 0], coefs[b, 1]) for b in range(WIDE)]
        sums = [acc[i, old_at, :] for i in range(4)]
        old_source, old_force = rows(old_tile, (0, 1, 2)), rows(old_tile, (4, 5, 6))
        target = [spread[i, new_at, :] for i in range(3)]
        new_source, new_force = rows(new_tile, (0, 1, 2)), rows(new_tile, (4, 5, 6))

        new_coefs = [coefficients(target, *pair) for pair in zip(new_source, new_force)]
        for source, force, (coef_c, along) in zip(old_source, old_force, old_coefs):
            for i in range(3):
                sums[i] = sums[i] + (coef_c * force[i] - along * source[i])
            sums[3] = sums[3] + along

        for i in range(4):
            acc[i, old_at, :] = sums[i]
        for b in range(WIDE):
            coefs[b, 0], coefs[b, 1] = new_coefs[b]

        end_block = block + 1 == blocks_of[group]
        next_block = jnp.where(end_block, 0, block + 1)
        next_chunk = jnp.where(end_block, chunk + 1, chunk)
        end_chunk = next_chunk == chunks_of[group]
        next_group = jnp.where(end_chunk, jnp.minimum(group + 1, n_groups - 1), group)
        return next_group, jnp.where(end_chunk, 0, next_chunk), next_block, new_first, new_tile

    zero = jnp.int32(0)
    lax.fori_loop(0, total + 1, one_item, (zero, zero, zero, zero, list_of(zero)))


def inner_kernel(cells, groups, count_ref, listed, spread, acc, coefs, chunks_of, blocks_of):
    acc[...] = jnp.zeros_like(acc)
    bins = bins_of(cells)
    filled = jnp.int32(0)
    for at in bins:
        filled = filled + count_ref[at]
    for n, group in enumerate(groups):
        chunks_of[n] = up_to(count_ref[bins[group]], CHUNK)
        blocks_of[n] = up_to(filled, BLOCK)
    all_pairs(groups, chunks_of, blocks_of, lambda group: jnp.int32(0), listed, spread, coefs, acc)


def counts_of(tiles, count_v, count_s, sem):
    _, lane = rows_and_lanes()
    held = jnp.zeros((ROWS, LANES), jnp.float32)
    for cell, tile in enumerate(tiles):
        held = jnp.where(lane == cell, tile, held)
    count_v[...] = held.astype(jnp.int32)
    copy = pltpu.make_async_copy(count_v, count_s, sem)
    copy.start()
    return copy


def middle_kernel(cells, count_ref, wide, spread, acc, listed, coefs, chunks_of, blocks_of, count_v, count_s, sem):
    size_x, size_y, size_z = cells
    n_z = 2 * size_z
    places = [(i, j, k) for i in range(size_x + 2) for j in range(size_y) for k in range(n_z)]
    copy = counts_of([wide[at] for at in places], count_v, count_s, sem)
    acc[...] = jnp.zeros_like(acc)
    n_lists = size_x * size_z
    max_tiles = listed.shape[0] // n_lists
    copy.wait()
    for bx in range(size_x):
        for bz in range(size_z):
            out_x, out_z = (-1, size_x)[bx], (-1, size_z)[bz]
            steps = [(out_x, y, z) for y in range(size_y) for z in (bz - 1, bz, bz + 1)]
            steps += [(x, y, out_z) for x in range(size_x) for y in range(size_y)]
            sources = []
            for x, y, z in steps:
                place = (x + 1, y, z % n_z)
                count = count_s[COUNT_ROW, places.index(place)]
                sources.append((wide[place] + shift_tile(cells, (x, y, z)), count))
            n = bx * size_z + bz
            n_blocks = up_to(compact(listed, n * max_tiles, sources), BLOCK)
            for by in range(size_y):
                group = (bx * size_y + by) * size_z + bz
                blocks_of[group] = n_blocks
                chunks_of[group] = up_to(count_ref[bx, by, bz], CHUNK)

    def list_of(group):
        bx = lax.div(group, size_y * size_z)
        return (bx * size_z + lax.rem(group, size_z)) * max_tiles

    all_pairs(range(size_x * size_y * size_z), chunks_of, blocks_of, list_of, listed, spread, coefs, acc)


def last_kernel(cells, count_ref, own_ref, y_lo, y_hi, spread, *refs):
    sums, (out_ref, acc, listed, coefs, chunks_of, blocks_of, count_v, count_s, sem) = refs[:4], refs[4:]
    size_x, size_y, size_z = cells
    n_z = 2 * size_z
    bins = bins_of(cells)
    places = [(i, j, k) for i in range(size_x + 2) for j in range(2) for k in range(n_z)]
    tiles = [(y_lo, y_hi)[j][i, 0, k] for i, j, k in places]
    copy = counts_of(tiles, count_v, count_s, sem)
    acc[...] = jnp.zeros_like(acc)
    max_tiles = listed.shape[0] // len(bins)
    copy.wait()
    for n, (bx, by, bz) in enumerate(bins):
        sources = []
        for x in (bx - 1, bx, bx + 1):
            for z in (bz - 1, bz, bz + 1):
                cell = places.index((x + 1, by, z % n_z))
                tile = tiles[cell] + shift_tile(cells, (x, (-1, size_y)[by], z))
                sources.append((tile, count_s[COUNT_ROW, cell]))
        blocks_of[n] = up_to(compact(listed, n * max_tiles, sources), BLOCK)
        chunks_of[n] = up_to(count_ref[bx, by, bz], CHUNK)
    list_of = lambda group: group * max_tiles
    all_pairs(range(len(bins)), chunks_of, blocks_of, list_of, listed, spread, coefs, acc)

    middle, inners = sums[0], sums[1:]
    row, lane = rows_and_lanes((2 * LANES, LANES))
    row_8, _ = rows_and_lanes()
    slot = lax.broadcasted_iota(jnp.int32, (1, LANES), 1)
    first_group = 0
    for inner in inners:
        held = inner.shape[1]
        first = first_group * LANES
        merged = jnp.zeros((held, LANES), jnp.float32)
        for i in range(4):
            total = acc[i, first : first + held, :] + middle[i, first : first + held, :] + inner[i]
            merged = merged + jnp.dot(
                jnp.concatenate(parts_of(total, 2), axis=1),
                jnp.where(lane == i, 1.0, 0.0).astype(jnp.bfloat16),
                preferred_element_type=jnp.float32,
            )
        for n in range(held // LANES):
            at = bins[first_group + n]
            by_row = jnp.transpose(merged[n * LANES : (n + 1) * LANES])[:ROWS]
            tile = own_ref[at]
            total = by_row + (tile + shift_tile(cells, at)) * jnp.broadcast_to(by_row[3:4], (ROWS, LANES))
            own = pltpu.roll(tile, ROWS - FORCE_ROW, 0)
            total = (2.0 * STOKES_NORM) * total - (STOKES_NORM * SELF_C) * own
            total = jnp.where(slot < count_ref[at], total, 0.0)
            for i in range(3):
                out_ref[i, at[0], at[1], at[2] : at[2] + 1, :] = total[i : i + 1]
        first_group += held // LANES


def shifted(array, axis, dim):
    size, length = lax.axis_size(axis), array.shape[dim]
    up = [(i, (i + 1) % size) for i in range(size)]
    down = [(j, i) for i, j in up]
    before = lax.ppermute(lax.slice_in_dim(array, length - 1, length, axis=dim), axis, up)
    after = lax.ppermute(lax.slice_in_dim(array, 0, 1, axis=dim), axis, down)
    return before, after


PARTS = (range(0, 3), range(3, 6), range(6, 8))


def on_device(offsets, forces, counts):
    cells = offsets.shape[1:4]
    slots = offsets.shape[4]
    n_bins = cells[0] * cells[1] * cells[2]
    n_targets = n_bins * slots
    whole = pl.BlockSpec(memory_space=pltpu.VMEM)
    scalars = pl.BlockSpec(memory_space=pltpu.SMEM)
    distant = pl.BlockSpec(memory_space=pltpu.HBM)

    def floats(*shape):
        return jax.ShapeDtypeStruct(shape, jnp.float32)

    def params(mib):
        return pltpu.CompilerParams(vmem_limit_bytes=mib << 20)

    own, listed, spread = pl.pallas_call(
        functools.partial(pre_kernel, cells),
        out_shape=[
            floats(*cells, ROWS, slots),
            floats(n_bins + WIDE, ROWS, slots),
            floats(3, n_targets, slots),
        ],
        in_specs=[distant] * 3,
        out_specs=[whole, whole, whole],
        scratch_shapes=[
            pltpu.SMEM(counts.shape, jnp.int32),
            pltpu.VMEM(offsets.shape, jnp.float32),
            pltpu.VMEM(forces.shape, jnp.float32),
            pltpu.SemaphoreType.DMA((3,)),
        ],
        compiler_params=params(8),
        name="pre",
    )(counts, offsets, forces)

    loop_scratch = [
        pltpu.VMEM((WIDE, 2, CHUNK, LANES), jnp.float32),
        pltpu.SMEM((n_bins,), jnp.int32),
        pltpu.SMEM((n_bins,), jnp.int32),
    ]
    count_scratch = [
        pltpu.VMEM((ROWS, LANES), jnp.int32),
        pltpu.SMEM((ROWS, LANES), jnp.int32),
        pltpu.SemaphoreType.DMA,
    ]
    cost = pl.CostEstimate(flops=1 << 28, bytes_accessed=1 << 16, transcendentals=1 << 20)

    def inner(part, listed):
        return pl.pallas_call(
            functools.partial(inner_kernel, cells, PARTS[part]),
            out_shape=floats(4, len(PARTS[part]) * slots, slots),
            in_specs=[scalars, whole, whole],
            out_specs=whole,
            scratch_shapes=loop_scratch,
            compiler_params=params(8),
            cost_estimate=cost,
            name="inner%d" % part,
        )(counts, listed, spread)

    def list_tiles(n_lists, n_steps):
        n_tiles = (n_steps + 2 * WIDE - 1) // WIDE * WIDE
        return pltpu.VMEM((n_lists * n_tiles, ROWS, LANES), jnp.float32)

    together = lax.optimization_barrier
    first = inner(0, listed)
    sent, listed_1, first = together((own, listed, first))
    size = lax.axis_size("ha")
    other = lax.ppermute(sent, "ha", [(i, (i + 1) % size) for i in range(size)])
    second = inner(1, listed_1)
    other, sent, listed_2, second = together((other, sent, listed_1, second))
    column = jnp.concatenate([sent, other], axis=2)
    x_lo, x_hi = shifted(column, "gx", 0)
    third = inner(2, listed_2)
    x_lo, x_hi, third = together((x_lo, x_hi, third))
    wide = jnp.concatenate([x_lo, column, x_hi], axis=0)
    y_lo, y_hi = shifted(wide, "gy", 1)
    middle = pl.pallas_call(
        functools.partial(middle_kernel, cells),
        out_shape=floats(4, n_targets, slots),
        in_specs=[scalars, whole, whole],
        out_specs=whole,
        scratch_shapes=[list_tiles(cells[0] * cells[2], 10)] + loop_scratch + count_scratch,
        compiler_params=params(8),
        cost_estimate=cost,
        name="middle",
    )(counts, wide, spread)
    y_lo, y_hi, middle = together((y_lo, y_hi, middle))
    return pl.pallas_call(
        functools.partial(last_kernel, cells),
        out_shape=floats(3, *cells, slots),
        in_specs=[scalars] + [whole] * 8,
        out_specs=whole,
        scratch_shapes=[pltpu.VMEM((4, n_targets, slots), jnp.float32), list_tiles(n_bins, 9)]
        + loop_scratch
        + count_scratch,
        compiler_params=params(12),
        cost_estimate=cost,
        name="last",
    )(counts, own, y_lo, y_hi, spread, middle, first, second, third)


def solution(mesh):
    in_specs = (
        P(None, "gx", "gy", "ha", None),
        P(None, "gx", "gy", "ha", None),
        P("gx", "gy", "ha"),
    )
    out_specs = P(None, "gx", "gy", "ha", None)
    return jax.shard_map(on_device, mesh=mesh, in_specs=in_specs, out_specs=out_specs, check_vma=False)
```

```python
import functools
import math

import jax
import jax.numpy as jnp
from jax import lax
from jax.experimental import pallas as pl
from jax.experimental.pallas import tpu as pltpu
from jax.sharding import PartitionSpec as P

SPLIT_XI = 2.0
SOFT_SQ = 0.01
GAUSS_COEF = 2.0 * SPLIT_XI / math.sqrt(math.pi)
STOKES_NORM = 1.0 / (8.0 * math.pi)

SOFT_U = SPLIT_XI * SPLIT_XI * SOFT_SQ
LOG2_E = math.log2(math.e)
LOG2_G = math.log2(GAUSS_COEF)
SELF_C = math.erfc(math.sqrt(SOFT_U)) / math.sqrt(SOFT_SQ) + GAUSS_COEF * (
    2.0 * SOFT_U - 3.0
) * math.exp(-SOFT_U)

LANES = 128
ROWS = 8
CHUNK = 32
WIDE = 2
BLOCK = WIDE * LANES
COUNT_ROW = 3
FULL = 640
EARLY = 3
FIRST = (3, 4)
SECOND = (5, 6, 7, 0, 1, 2)
FORCE_ROW = 4


def rows_and_lanes(shape=(ROWS, LANES)):
    return lax.broadcasted_iota(jnp.int32, shape, 0), lax.broadcasted_iota(jnp.int32, shape, 1)


def bins_of(cells):
    return [(i, j, k) for i in range(cells[0]) for j in range(cells[1]) for k in range(cells[2])]


def shift_tile(cells, at):
    row, _ = rows_and_lanes()
    moved = jnp.zeros((ROWS, LANES), jnp.float32)
    for i in range(3):
        moved = jnp.where(row == i, SPLIT_XI * (at[i] - 0.5 * (cells[i] - 1)), moved)
    return moved


def compact(listed, base, sources):
    _, lane = rows_and_lanes()
    filled = jnp.int32(0)
    moved = []
    for tile, count in sources:
        at = lax.bitwise_and(filled, LANES - 1)
        tile_id = base + lax.shift_right_logical(filled, 7)
        moved.append((pltpu.roll(tile, at, 1), lane >= at, tile_id, at + count >= LANES))
        filled = filled + count
    current = jnp.zeros((ROWS, LANES), jnp.float32)
    for tile, behind, tile_id, full in moved:
        current = jnp.where(behind, tile, current)
        spill = jnp.where(behind, 0.0, tile)
        listed[tile_id] = current
        listed[tile_id + 1] = spill
        current = jnp.where(full, spill, current)
    last = base + lax.shift_right_logical(filled, 7)
    for more in range(1, WIDE):
        listed[last + more] = jnp.zeros((ROWS, LANES), jnp.float32)
    return filled


def up_to(count, size):
    return lax.shift_right_logical(count + (size - 1), size.bit_length() - 1)


def parts_of(value, n):
    parts = []
    for _ in range(n):
        part = value.astype(jnp.bfloat16)
        value = value - part.astype(jnp.float32)
        parts.append(part)
    return parts


def spread_targets(spread, first, tile):
    parts = [p.astype(jnp.float32) for p in parts_of(tile, 3)] + [jnp.zeros_like(tile)]
    row, lane = rows_and_lanes((4 * ROWS, 3 * LANES))
    pick = jnp.where(lax.bitwise_and(row, ROWS - 1) == lax.shift_right_logical(lane, 7), 1.0, 0.0)
    wide = lax.dot_general(
        jnp.concatenate(parts, axis=0).astype(jnp.bfloat16),
        pick.astype(jnp.bfloat16),
        (((0,), (0,)), ((), ())),
        preferred_element_type=jnp.float32,
    )
    for i in range(3):
        spread[i, first : first + LANES, :] = wide[:, i * LANES : (i + 1) * LANES]


def coefficients(target, source, force):
    delta = [t - s for t, s in zip(target, source)]
    u = (delta[0] * delta[0] + SOFT_U) + delta[1] * delta[1] + delta[2] * delta[2]
    inv = lax.rsqrt(u)
    tail = (1.0 - lax.erf(u * inv)) * inv
    gauss = jnp.exp2(LOG2_G - u * LOG2_E)
    rest = gauss * (u - 1.5)
    coef_d = ((tail - rest) - gauss) * (inv * inv)
    along = coef_d * (delta[0] * force[0] + delta[1] * force[1] + delta[2] * force[2])
    return tail + rest, along


def all_pairs(n_groups, chunks_of, blocks_of, bin_of, list_of, listed, spread, coefs, acc):
    def rows(tile_id, at):
        return [[listed[tile_id + b, i : i + 1, :] for i in at] for b in range(WIDE)]

    total = jnp.int32(0)
    for group in range(n_groups):
        total = total + chunks_of[group] * blocks_of[group]
    coefs[...] = jnp.zeros_like(coefs)

    def one_item(item, state):
        group, chunk, block, old_first, old_tile = state
        new_first = group * LANES + chunk * CHUNK
        new_tile = list_of(group) + block * WIDE
        old_at = pl.ds(pl.multiple_of(old_first, CHUNK), CHUNK)
        new_at = pl.ds(pl.multiple_of(bin_of(group) * LANES + chunk * CHUNK, CHUNK), CHUNK)
        old_coefs = [(coefs[b, 0], coefs[b, 1]) for b in range(WIDE)]
        sums = [acc[i, old_at, :] for i in range(4)]
        old_source, old_force = rows(old_tile, (0, 1, 2)), rows(old_tile, (4, 5, 6))
        target = [spread[i, new_at, :] for i in range(3)]
        new_source, new_force = rows(new_tile, (0, 1, 2)), rows(new_tile, (4, 5, 6))

        new_coefs = [coefficients(target, *pair) for pair in zip(new_source, new_force)]
        for source, force, (coef_c, along) in zip(old_source, old_force, old_coefs):
            for i in range(3):
                sums[i] = sums[i] + (coef_c * force[i] - along * source[i])
            sums[3] = sums[3] + along

        for i in range(4):
            acc[i, old_at, :] = sums[i]
        for b in range(WIDE):
            coefs[b, 0], coefs[b, 1] = new_coefs[b]

        end_block = block + 1 == blocks_of[group]
        next_block = jnp.where(end_block, 0, block + 1)
        next_chunk = jnp.where(end_block, chunk + 1, chunk)
        end_chunk = next_chunk == chunks_of[group]
        next_group = jnp.where(end_chunk, jnp.minimum(group + 1, n_groups - 1), group)
        return next_group, jnp.where(end_chunk, 0, next_chunk), next_block, new_first, new_tile

    zero = jnp.int32(0)
    lax.fori_loop(0, total + 1, one_item, (zero, zero, zero, zero, list_of(zero)))


def is_full(cells, count_ref):
    filled = jnp.int32(0)
    for at in bins_of(cells):
        filled = filled + count_ref[at]
    return filled, filled > FULL


def list_own(cells, count_ref, own_ref, listed):
    sources = [(own_ref[at] + shift_tile(cells, at), count_ref[at]) for at in bins_of(cells)]
    compact(listed, 0, sources)


def inner_pairs(cells, groups, n_active, bin_of, filled, count_ref, listed, spread, coefs, acc, limits):
    chunks_of, blocks_of = limits
    bins = bins_of(cells)
    for n, group in enumerate(groups):
        n_chunks = up_to(count_ref[bins[group]], CHUNK)
        chunks_of[n] = jnp.where(n < n_active, n_chunks, 0)
        blocks_of[n] = up_to(filled, BLOCK)
    list_of = lambda group: jnp.int32(0)
    all_pairs(len(groups), chunks_of, blocks_of, bin_of, list_of, listed, spread, coefs, acc)


def velocity_rows(cells, group, by_row, tile):
    position = tile + shift_tile(cells, bins_of(cells)[group])
    return (2.0 * STOKES_NORM) * (by_row + position * jnp.broadcast_to(by_row[3:4], (ROWS, LANES)))


def lane_sums(totals):
    _, lane = rows_and_lanes((2 * LANES, LANES))
    merged = jnp.zeros(totals[0].shape, jnp.float32)
    for i, total in enumerate(totals):
        merged = merged + jnp.dot(
            jnp.concatenate(parts_of(total, 2), axis=1),
            jnp.where(lane == i, 1.0, 0.0).astype(jnp.bfloat16),
            preferred_element_type=jnp.float32,
        )
    return merged


def pack_kernel(cells, count_ref, offset_v, force_v, own_ref, early_ref, listed, spread, coefs, acc, *limits):
    slot = lax.broadcasted_iota(jnp.int32, (1, LANES), 1)
    for at in bins_of(cells):
        ix, iy, iz = at
        count = count_ref[at]
        wide = jnp.full((1, LANES), count, jnp.int32).astype(jnp.float32)
        for i in range(3):
            position = offset_v[i, ix, iy, iz : iz + 1, :]
            own_ref[ix, iy, iz, i : i + 1, :] = position * SPLIT_XI - 0.5 * SPLIT_XI
            force = force_v[i, ix, iy, iz : iz + 1, :]
            own_ref[ix, iy, iz, 4 + i : 5 + i, :] = jnp.where(slot < count, force, 0.0)
        own_ref[ix, iy, iz, 3:4, :] = wide
        own_ref[ix, iy, iz, 7:8, :] = wide
    early_ref[...] = jnp.zeros_like(early_ref)
    filled, full = is_full(cells, count_ref)

    @pl.when(full)
    def _():
        list_own(cells, count_ref, own_ref, listed)
        acc[...] = jnp.zeros_like(acc)
        groups = range(EARLY)
        tiles = [own_ref[bins_of(cells)[n]] for n in groups]
        for n in groups:
            spread_targets(spread, n * LANES, tiles[n] + shift_tile(cells, bins_of(cells)[n]))
        same = lambda group: group
        inner_pairs(cells, groups, EARLY, same, filled, count_ref, listed, spread, coefs, acc, limits)
        merged = lane_sums([acc[i] for i in range(4)])
        for n in groups:
            by_row = jnp.transpose(merged[n * LANES : (n + 1) * LANES])[:ROWS]
            early_ref[n] = velocity_rows(cells, n, by_row, tiles[n])


def first_kernel(cells, groups, count_ref, own_ref, listed, spread, acc, coefs, *limits):
    list_own(cells, count_ref, own_ref, listed)
    for n, at in enumerate(bins_of(cells)):
        spread_targets(spread, n * LANES, own_ref[at] + shift_tile(cells, at))
    acc[...] = jnp.zeros_like(acc)
    filled, _ = is_full(cells, count_ref)
    bin_of = lambda group: group + groups[0]
    inner_pairs(cells, groups, len(groups), bin_of, filled, count_ref, listed, spread, coefs, acc, limits)


def second_kernel(cells, groups, count_ref, listed, spread, acc, coefs, *limits):
    acc[...] = jnp.zeros_like(acc)
    filled, full = is_full(cells, count_ref)
    n_active = jnp.where(full, len(groups) - EARLY, len(groups))
    n_bins = len(bins_of(cells))

    def bin_of(group):
        at = group + groups[0]
        return jnp.where(at >= n_bins, at - n_bins, at)

    inner_pairs(cells, groups, n_active, bin_of, filled, count_ref, listed, spread, coefs, acc, limits)


def counts_of(tiles, count_v, count_s, sem):
    _, lane = rows_and_lanes()
    held = jnp.zeros((ROWS, LANES), jnp.float32)
    for cell, tile in enumerate(tiles):
        held = jnp.where(lane == cell, tile, held)
    count_v[...] = held.astype(jnp.int32)
    copy = pltpu.make_async_copy(count_v, count_s, sem)
    copy.start()
    return copy


def middle_kernel(cells, count_ref, wide, spread, acc, listed, coefs, chunks_of, blocks_of, count_v, count_s, sem):
    size_x, size_y, size_z = cells
    n_z = 2 * size_z
    places = [(i, j, k) for i in range(size_x + 2) for j in range(size_y) for k in range(n_z)]
    copy = counts_of([wide[at] for at in places], count_v, count_s, sem)
    acc[...] = jnp.zeros_like(acc)
    n_lists = size_x * size_z
    max_tiles = listed.shape[0] // n_lists
    copy.wait()
    for bx in range(size_x):
        for bz in range(size_z):
            out_x, out_z = (-1, size_x)[bx], (-1, size_z)[bz]
            steps = [(out_x, y, z) for y in range(size_y) for z in (bz - 1, bz, bz + 1)]
            steps += [(x, y, out_z) for x in range(size_x) for y in range(size_y)]
            sources = []
            for x, y, z in steps:
                place = (x + 1, y, z % n_z)
                count = count_s[COUNT_ROW, places.index(place)]
                sources.append((wide[place] + shift_tile(cells, (x, y, z)), count))
            n = bx * size_z + bz
            n_blocks = up_to(compact(listed, n * max_tiles, sources), BLOCK)
            for by in range(size_y):
                group = (bx * size_y + by) * size_z + bz
                blocks_of[group] = n_blocks
                chunks_of[group] = up_to(count_ref[bx, by, bz], CHUNK)

    def list_of(group):
        bx = lax.div(group, size_y * size_z)
        return (bx * size_z + lax.rem(group, size_z)) * max_tiles

    same = lambda group: group
    all_pairs(size_x * size_y * size_z, chunks_of, blocks_of, same, list_of, listed, spread, coefs, acc)


def last_kernel(cells, count_ref, own_ref, y_lo, y_hi, spread, *refs):
    middle, first, second, early = refs[:4]
    out_ref, acc, listed, coefs, chunks_of, blocks_of, count_v, count_s, sem = refs[4:]
    size_x, size_y, size_z = cells
    n_z = 2 * size_z
    bins = bins_of(cells)
    places = [(i, j, k) for i in range(size_x + 2) for j in range(2) for k in range(n_z)]
    tiles = [(y_lo, y_hi)[j][i, 0, k] for i, j, k in places]
    copy = counts_of(tiles, count_v, count_s, sem)
    acc[...] = jnp.zeros_like(acc)
    max_tiles = listed.shape[0] // len(bins)
    copy.wait()
    for n, (bx, by, bz) in enumerate(bins):
        sources = []
        for x in (bx - 1, bx, bx + 1):
            for z in (bz - 1, bz, bz + 1):
                cell = places.index((x + 1, by, z % n_z))
                tile = tiles[cell] + shift_tile(cells, (x, (-1, size_y)[by], z))
                sources.append((tile, count_s[COUNT_ROW, cell]))
        blocks_of[n] = up_to(compact(listed, n * max_tiles, sources), BLOCK)
        chunks_of[n] = up_to(count_ref[bx, by, bz], CHUNK)
    list_of = lambda group: group * max_tiles
    same = lambda group: group
    all_pairs(len(bins), chunks_of, blocks_of, same, list_of, listed, spread, coefs, acc)

    slot = lax.broadcasted_iota(jnp.int32, (1, LANES), 1)
    totals = [[], [], [], []]
    for inner, groups in ((first, FIRST), (second, SECOND)):
        for m, n in enumerate(groups):
            here, there = slice(n * LANES, (n + 1) * LANES), slice(m * LANES, (m + 1) * LANES)
            for i in range(4):
                totals[i].append(acc[i, here, :] + middle[i, here, :] + inner[i, there, :])
    merged = lane_sums([jnp.concatenate(total, axis=0) for total in totals])
    for m, n in enumerate(FIRST + SECOND):
        at = bins[n]
        by_row = jnp.transpose(merged[m * LANES : (m + 1) * LANES])[:ROWS]
        tile = own_ref[at]
        total = velocity_rows(cells, n, by_row, tile)
        total = total - (STOKES_NORM * SELF_C) * pltpu.roll(tile, ROWS - FORCE_ROW, 0)
        if n < EARLY:
            total = total + early[n]
        total = jnp.where(slot < count_ref[at], total, 0.0)
        for i in range(3):
            out_ref[i, at[0], at[1], at[2] : at[2] + 1, :] = total[i : i + 1]


def shifted(array, axis, dim):
    size, length = lax.axis_size(axis), array.shape[dim]
    up = [(i, (i + 1) % size) for i in range(size)]
    down = [(j, i) for i, j in up]
    before = lax.ppermute(lax.slice_in_dim(array, length - 1, length, axis=dim), axis, up)
    after = lax.ppermute(lax.slice_in_dim(array, 0, 1, axis=dim), axis, down)
    return before, after


def on_device(offsets, forces, counts):
    cells = offsets.shape[1:4]
    slots = offsets.shape[4]
    n_bins = cells[0] * cells[1] * cells[2]
    n_targets = n_bins * slots
    whole = pl.BlockSpec(memory_space=pltpu.VMEM)
    scalars = pl.BlockSpec(memory_space=pltpu.SMEM)

    def floats(*shape):
        return jax.ShapeDtypeStruct(shape, jnp.float32)

    def params(mib):
        return pltpu.CompilerParams(vmem_limit_bytes=mib << 20)

    loop_scratch = [
        pltpu.VMEM((WIDE, 2, CHUNK, LANES), jnp.float32),
        pltpu.SMEM((n_bins,), jnp.int32),
        pltpu.SMEM((n_bins,), jnp.int32),
    ]
    count_scratch = [
        pltpu.VMEM((ROWS, LANES), jnp.int32),
        pltpu.SMEM((ROWS, LANES), jnp.int32),
        pltpu.SemaphoreType.DMA,
    ]
    cost = pl.CostEstimate(flops=1 << 28, bytes_accessed=1 << 16, transcendentals=1 << 20)

    def list_tiles(n_lists, n_steps):
        n_tiles = (n_steps + 2 * WIDE - 1) // WIDE * WIDE
        return pltpu.VMEM((n_lists * n_tiles, ROWS, LANES), jnp.float32)

    own_list, all_targets = floats(n_bins + WIDE, ROWS, slots), floats(3, n_targets, slots)
    own, early = pl.pallas_call(
        functools.partial(pack_kernel, cells),
        out_shape=[floats(*cells, ROWS, slots), floats(EARLY, ROWS, slots)],
        in_specs=[scalars, whole, whole],
        out_specs=[whole, whole],
        scratch_shapes=[
            pltpu.VMEM(own_list.shape, jnp.float32),
            pltpu.VMEM((3, EARLY * slots, slots), jnp.float32),
            loop_scratch[0],
            pltpu.VMEM((4, EARLY * slots, slots), jnp.float32),
        ]
        + loop_scratch[1:],
        name="pack",
    )(counts, offsets, forces)

    together = lax.optimization_barrier
    size = lax.axis_size("ha")
    other = lax.ppermute(own, "ha", [(i, (i + 1) % size) for i in range(size)])
    listed, spread, first = pl.pallas_call(
        functools.partial(first_kernel, cells, FIRST),
        out_shape=[own_list, all_targets, floats(4, len(FIRST) * slots, slots)],
        in_specs=[scalars, whole],
        out_specs=[whole] * 3,
        scratch_shapes=loop_scratch,
        compiler_params=params(8),
        cost_estimate=cost,
        name="first",
    )(counts, own)
    other, sent, listed, first = together((other, own, listed, first))
    column = jnp.concatenate([sent, other], axis=2)
    x_lo, x_hi = shifted(column, "gx", 0)
    second = pl.pallas_call(
        functools.partial(second_kernel, cells, SECOND),
        out_shape=floats(4, len(SECOND) * slots, slots),
        in_specs=[scalars, whole, whole],
        out_specs=whole,
        scratch_shapes=loop_scratch,
        compiler_params=params(8),
        cost_estimate=cost,
        name="second",
    )(counts, listed, spread)
    x_lo, x_hi, second = together((x_lo, x_hi, second))
    wide = jnp.concatenate([x_lo, column, x_hi], axis=0)
    y_lo, y_hi = shifted(wide, "gy", 1)
    middle = pl.pallas_call(
        functools.partial(middle_kernel, cells),
        out_shape=floats(4, n_targets, slots),
        in_specs=[scalars, whole, whole],
        out_specs=whole,
        scratch_shapes=[list_tiles(cells[0] * cells[2], 10)] + loop_scratch + count_scratch,
        compiler_params=params(8),
        cost_estimate=cost,
        name="middle",
    )(counts, wide, spread)
    y_lo, y_hi, middle = together((y_lo, y_hi, middle))
    return pl.pallas_call(
        functools.partial(last_kernel, cells),
        out_shape=floats(3, *cells, slots),
        in_specs=[scalars] + [whole] * 8,
        out_specs=whole,
        scratch_shapes=[pltpu.VMEM((4, n_targets, slots), jnp.float32), list_tiles(n_bins, 9)]
        + loop_scratch
        + count_scratch,
        compiler_params=params(12),
        cost_estimate=cost,
        name="last",
    )(counts, own, y_lo, y_hi, spread, middle, first, second, early)


def solution(mesh):
    in_specs = (
        P(None, "gx", "gy", "ha", None),
        P(None, "gx", "gy", "ha", None),
        P("gx", "gy", "ha"),
    )
    out_specs = P(None, "gx", "gy", "ha", None)
    return jax.shard_map(on_device, mesh=mesh, in_specs=in_specs, out_specs=out_specs, check_vma=False)
```

```python
import functools
import math

import jax
import jax.numpy as jnp
from jax import lax
from jax.experimental import pallas as pl
from jax.experimental.pallas import tpu as pltpu
from jax.sharding import PartitionSpec as P

SPLIT_XI = 2.0
SOFT_SQ = 0.01
GAUSS_COEF = 2.0 * SPLIT_XI / math.sqrt(math.pi)
STOKES_NORM = 1.0 / (8.0 * math.pi)

SOFT_U = SPLIT_XI * SPLIT_XI * SOFT_SQ
LOG2_E = math.log2(math.e)
LOG2_G = math.log2(GAUSS_COEF)
SELF_C = math.erfc(math.sqrt(SOFT_U)) / math.sqrt(SOFT_SQ) + GAUSS_COEF * (
    2.0 * SOFT_U - 3.0
) * math.exp(-SOFT_U)

LANES = 128
ROWS = 8
CHUNK = 32
UNITS = 2
COUNT_ROW = 3
FULL = 640
EARLY = 3
FIRST = (3, 4)
SECOND = (5, 6, 7, 0, 1, 2)
FORCE_ROW = 4


def rows_and_lanes(shape=(ROWS, LANES)):
    return lax.broadcasted_iota(jnp.int32, shape, 0), lax.broadcasted_iota(jnp.int32, shape, 1)


def bins_of(cells):
    return [(i, j, k) for i in range(cells[0]) for j in range(cells[1]) for k in range(cells[2])]


def shift_tile(cells, at):
    row, _ = rows_and_lanes()
    moved = jnp.zeros((ROWS, LANES), jnp.float32)
    for i in range(3):
        moved = jnp.where(row == i, SPLIT_XI * (at[i] - 0.5 * (cells[i] - 1)), moved)
    return moved


def compact(listed, base, sources):
    _, lane = rows_and_lanes()
    filled = jnp.int32(0)
    moved = []
    for tile, count in sources:
        at = lax.bitwise_and(filled, LANES - 1)
        tile_id = base + lax.shift_right_logical(filled, 7)
        moved.append((pltpu.roll(tile, at, 1), lane >= at, tile_id, at + count >= LANES))
        filled = filled + count
    current = jnp.zeros((ROWS, LANES), jnp.float32)
    for tile, behind, tile_id, full in moved:
        current = jnp.where(behind, tile, current)
        spill = jnp.where(behind, 0.0, tile)
        listed[tile_id] = current
        listed[tile_id + 1] = spill
        current = jnp.where(full, spill, current)
    return filled


def up_to(count, size):
    return lax.shift_right_logical(count + (size - 1), size.bit_length() - 1)


def parts_of(value, n):
    parts = []
    for _ in range(n):
        part = value.astype(jnp.bfloat16)
        value = value - part.astype(jnp.float32)
        parts.append(part)
    return parts


def spread_targets(spread, first, tile):
    parts = [p.astype(jnp.float32) for p in parts_of(tile, 3)] + [jnp.zeros_like(tile)]
    row, lane = rows_and_lanes((4 * ROWS, 3 * LANES))
    pick = jnp.where(lax.bitwise_and(row, ROWS - 1) == lax.shift_right_logical(lane, 7), 1.0, 0.0)
    wide = lax.dot_general(
        jnp.concatenate(parts, axis=0).astype(jnp.bfloat16),
        pick.astype(jnp.bfloat16),
        (((0,), (0,)), ((), ())),
        preferred_element_type=jnp.float32,
    )
    for i in range(3):
        spread[i, first : first + LANES, :] = wide[:, i * LANES : (i + 1) * LANES]


def coefficients(target, source, force):
    delta = [t - s for t, s in zip(target, source)]
    u = (delta[0] * delta[0] + SOFT_U) + delta[1] * delta[1] + delta[2] * delta[2]
    inv = lax.rsqrt(u)
    tail = (1.0 - lax.erf(u * inv)) * inv
    gauss = jnp.exp2(LOG2_G - u * LOG2_E)
    rest = gauss * (u - 1.5)
    coef_d = ((tail - rest) - gauss) * (inv * inv)
    along = coef_d * (delta[0] * force[0] + delta[1] * force[1] + delta[2] * force[2])
    return tail + rest, along


def all_pairs(n_groups, chunks_of, tiles_of, bin_of, list_of, listed, spread, coefs, acc):
    trash = acc.shape[1] - CHUNK

    def rows(tile_id, at):
        return [listed[tile_id, i : i + 1, :] for i in at]

    total = jnp.int32(0)
    for group in range(n_groups):
        total = total + chunks_of[group] * tiles_of[group]
    coefs[...] = jnp.zeros_like(coefs)

    def advance(group, chunk, tile):
        end_tile = tile + 1 == tiles_of[group]
        next_chunk = jnp.where(end_tile, chunk + 1, chunk)
        end_chunk = next_chunk == chunks_of[group]
        next_group = jnp.where(end_chunk, jnp.minimum(group + 1, n_groups - 1), group)
        return next_group, jnp.where(end_chunk, 0, next_chunk), jnp.where(end_tile, 0, tile + 1)

    def some_units(step, state):
        place, olds = state[:3], state[3:]
        news, targets, sources = [], [], []
        for n in range(UNITS):
            group, chunk, tile = place
            valid = step * UNITS + n < total
            news += [jnp.where(valid, group * LANES + chunk * CHUNK, trash), list_of(group) + tile]
            at = pl.ds(pl.multiple_of(bin_of(group) * LANES + chunk * CHUNK, CHUNK), CHUNK)
            targets.append([spread[i, at, :] for i in range(3)])
            sources.append((rows(news[-1], (0, 1, 2)), rows(news[-1], (4, 5, 6))))
            place = advance(*place)
        old_coefs = [(coefs[n, 0], coefs[n, 1]) for n in range(UNITS)]
        old_sources = [(rows(tile, (0, 1, 2)), rows(tile, (4, 5, 6))) for tile in olds[1::2]]

        new_coefs = [coefficients(target, *source) for target, source in zip(targets, sources)]
        terms = []
        for (source, force), (coef_c, along) in zip(old_sources, old_coefs):
            terms.append([coef_c * force[i] - along * source[i] for i in range(3)] + [along])

        for first, unit in zip(olds[::2], terms):
            at = pl.ds(pl.multiple_of(first, CHUNK), CHUNK)
            for i in range(4):
                acc[i, at, :] = acc[i, at, :] + unit[i]
        for n in range(UNITS):
            coefs[n, 0], coefs[n, 1] = new_coefs[n]
        return place + tuple(news)

    zero = jnp.int32(0)
    start = (zero, zero, zero) + (jnp.int32(trash), list_of(zero)) * UNITS
    lax.fori_loop(0, lax.div(total + UNITS - 1, UNITS) + 1, some_units, start)


def is_full(cells, count_ref):
    filled = jnp.int32(0)
    for at in bins_of(cells):
        filled = filled + count_ref[at]
    return filled, filled > FULL


def list_own(cells, count_ref, own_ref, listed):
    sources = [(own_ref[at] + shift_tile(cells, at), count_ref[at]) for at in bins_of(cells)]
    compact(listed, 0, sources)


def inner_pairs(cells, groups, n_active, bin_of, filled, count_ref, listed, spread, coefs, acc, limits):
    chunks_of, tiles_of = limits
    bins = bins_of(cells)
    for n, group in enumerate(groups):
        n_chunks = up_to(count_ref[bins[group]], CHUNK)
        chunks_of[n] = jnp.where(n < n_active, n_chunks, 0)
        tiles_of[n] = up_to(filled, LANES)
    list_of = lambda group: jnp.int32(0)
    all_pairs(len(groups), chunks_of, tiles_of, bin_of, list_of, listed, spread, coefs, acc)


def velocity_rows(cells, group, by_row, tile):
    position = tile + shift_tile(cells, bins_of(cells)[group])
    return (2.0 * STOKES_NORM) * (by_row + position * jnp.broadcast_to(by_row[3:4], (ROWS, LANES)))


def lane_sums(totals):
    _, lane = rows_and_lanes((2 * LANES, LANES))
    merged = jnp.zeros(totals[0].shape, jnp.float32)
    for i, total in enumerate(totals):
        merged = merged + jnp.dot(
            jnp.concatenate(parts_of(total, 2), axis=1),
            jnp.where(lane == i, 1.0, 0.0).astype(jnp.bfloat16),
            preferred_element_type=jnp.float32,
        )
    return merged


def pack_kernel(cells, count_ref, offset_v, force_v, own_ref, early_ref, listed, spread, coefs, acc, *limits):
    slot = lax.broadcasted_iota(jnp.int32, (1, LANES), 1)
    for at in bins_of(cells):
        ix, iy, iz = at
        count = count_ref[at]
        wide = jnp.full((1, LANES), count, jnp.int32).astype(jnp.float32)
        for i in range(3):
            position = offset_v[i, ix, iy, iz : iz + 1, :]
            own_ref[ix, iy, iz, i : i + 1, :] = position * SPLIT_XI - 0.5 * SPLIT_XI
            force = force_v[i, ix, iy, iz : iz + 1, :]
            own_ref[ix, iy, iz, 4 + i : 5 + i, :] = jnp.where(slot < count, force, 0.0)
        own_ref[ix, iy, iz, 3:4, :] = wide
        own_ref[ix, iy, iz, 7:8, :] = wide
    early_ref[...] = jnp.zeros_like(early_ref)
    filled, full = is_full(cells, count_ref)

    @pl.when(full)
    def _():
        list_own(cells, count_ref, own_ref, listed)
        acc[...] = jnp.zeros_like(acc)
        groups = range(EARLY)
        tiles = [own_ref[bins_of(cells)[n]] for n in groups]
        for n in groups:
            spread_targets(spread, n * LANES, tiles[n] + shift_tile(cells, bins_of(cells)[n]))
        same = lambda group: group
        inner_pairs(cells, groups, EARLY, same, filled, count_ref, listed, spread, coefs, acc, limits)
        merged = lane_sums([acc[i, : EARLY * LANES, :] for i in range(4)])
        for n in groups:
            by_row = jnp.transpose(merged[n * LANES : (n + 1) * LANES])[:ROWS]
            early_ref[n] = velocity_rows(cells, n, by_row, tiles[n])


def first_kernel(cells, groups, own_ref, listed, spread, acc, coefs, chunks_of, tiles_of, count_v, count_s, sem):
    bins = bins_of(cells)
    copy = counts_of([own_ref[at] for at in bins], count_v, count_s, sem)
    for n, at in enumerate(bins):
        spread_targets(spread, n * LANES, own_ref[at] + shift_tile(cells, at))
    acc[...] = jnp.zeros_like(acc)
    copy.wait()
    count_ref = {at: count_s[COUNT_ROW, n] for n, at in enumerate(bins)}
    list_own(cells, count_ref, own_ref, listed)
    filled, _ = is_full(cells, count_ref)
    limits = chunks_of, tiles_of
    bin_of = lambda group: group + groups[0]
    inner_pairs(cells, groups, len(groups), bin_of, filled, count_ref, listed, spread, coefs, acc, limits)


def second_kernel(cells, groups, count_ref, listed, spread, acc, coefs, *limits):
    acc[...] = jnp.zeros_like(acc)
    filled, full = is_full(cells, count_ref)
    n_active = jnp.where(full, len(groups) - EARLY, len(groups))
    n_bins = len(bins_of(cells))

    def bin_of(group):
        at = group + groups[0]
        return jnp.where(at >= n_bins, at - n_bins, at)

    inner_pairs(cells, groups, n_active, bin_of, filled, count_ref, listed, spread, coefs, acc, limits)


def counts_of(tiles, count_v, count_s, sem):
    _, lane = rows_and_lanes()
    held = jnp.zeros((ROWS, LANES), jnp.float32)
    for cell, tile in enumerate(tiles):
        held = jnp.where(lane == cell, tile, held)
    count_v[...] = held.astype(jnp.int32)
    copy = pltpu.make_async_copy(count_v, count_s, sem)
    copy.start()
    return copy


def middle_kernel(cells, count_ref, wide, spread, acc, listed, coefs, chunks_of, tiles_of, count_v, count_s, sem):
    size_x, size_y, size_z = cells
    n_z = 2 * size_z
    places = [(i, j, k) for i in range(size_x + 2) for j in range(size_y) for k in range(n_z)]
    copy = counts_of([wide[at] for at in places], count_v, count_s, sem)
    acc[...] = jnp.zeros_like(acc)
    n_lists = size_x * size_z
    max_tiles = listed.shape[0] // n_lists
    copy.wait()
    for bx in range(size_x):
        for bz in range(size_z):
            out_x, out_z = (-1, size_x)[bx], (-1, size_z)[bz]
            steps = [(out_x, y, z) for y in range(size_y) for z in (bz - 1, bz, bz + 1)]
            steps += [(x, y, out_z) for x in range(size_x) for y in range(size_y)]
            sources = []
            for x, y, z in steps:
                place = (x + 1, y, z % n_z)
                count = count_s[COUNT_ROW, places.index(place)]
                sources.append((wide[place] + shift_tile(cells, (x, y, z)), count))
            n = bx * size_z + bz
            n_tiles = up_to(compact(listed, n * max_tiles, sources), LANES)
            for by in range(size_y):
                group = (bx * size_y + by) * size_z + bz
                tiles_of[group] = n_tiles
                chunks_of[group] = up_to(count_ref[bx, by, bz], CHUNK)

    def list_of(group):
        bx = lax.div(group, size_y * size_z)
        return (bx * size_z + lax.rem(group, size_z)) * max_tiles

    same = lambda group: group
    all_pairs(size_x * size_y * size_z, chunks_of, tiles_of, same, list_of, listed, spread, coefs, acc)


def last_kernel(cells, count_ref, own_ref, y_lo, y_hi, spread, *refs):
    middle, first, second, early = refs[:4]
    out_ref, acc, listed, coefs, chunks_of, tiles_of, count_v, count_s, sem = refs[4:]
    size_x, size_y, size_z = cells
    n_z = 2 * size_z
    bins = bins_of(cells)
    places = [(i, j, k) for i in range(size_x + 2) for j in range(2) for k in range(n_z)]
    tiles = [(y_lo, y_hi)[j][i, 0, k] for i, j, k in places]
    copy = counts_of(tiles, count_v, count_s, sem)
    acc[...] = jnp.zeros_like(acc)
    max_tiles = listed.shape[0] // len(bins)
    copy.wait()
    for n, (bx, by, bz) in enumerate(bins):
        sources = []
        for x in (bx - 1, bx, bx + 1):
            for z in (bz - 1, bz, bz + 1):
                cell = places.index((x + 1, by, z % n_z))
                tile = tiles[cell] + shift_tile(cells, (x, (-1, size_y)[by], z))
                sources.append((tile, count_s[COUNT_ROW, cell]))
        tiles_of[n] = up_to(compact(listed, n * max_tiles, sources), LANES)
        chunks_of[n] = up_to(count_ref[bx, by, bz], CHUNK)
    list_of = lambda group: group * max_tiles
    same = lambda group: group
    all_pairs(len(bins), chunks_of, tiles_of, same, list_of, listed, spread, coefs, acc)

    slot = lax.broadcasted_iota(jnp.int32, (1, LANES), 1)
    totals = [[], [], [], []]
    for inner, groups in ((first, FIRST), (second, SECOND)):
        for m, n in enumerate(groups):
            here, there = slice(n * LANES, (n + 1) * LANES), slice(m * LANES, (m + 1) * LANES)
            for i in range(4):
                totals[i].append(acc[i, here, :] + middle[i, here, :] + inner[i, there, :])
    merged = lane_sums([jnp.concatenate(total, axis=0) for total in totals])
    for m, n in enumerate(FIRST + SECOND):
        at = bins[n]
        by_row = jnp.transpose(merged[m * LANES : (m + 1) * LANES])[:ROWS]
        tile = own_ref[at]
        total = velocity_rows(cells, n, by_row, tile)
        total = total - (STOKES_NORM * SELF_C) * pltpu.roll(tile, ROWS - FORCE_ROW, 0)
        if n < EARLY:
            total = total + early[n]
        total = jnp.where(slot < count_ref[at], total, 0.0)
        for i in range(3):
            out_ref[i, at[0], at[1], at[2] : at[2] + 1, :] = total[i : i + 1]


def shifted(array, axis, dim):
    size, length = lax.axis_size(axis), array.shape[dim]
    up = [(i, (i + 1) % size) for i in range(size)]
    down = [(j, i) for i, j in up]
    before = lax.ppermute(lax.slice_in_dim(array, length - 1, length, axis=dim), axis, up)
    after = lax.ppermute(lax.slice_in_dim(array, 0, 1, axis=dim), axis, down)
    return before, after


def shifted_apart(array, axis, dim):
    size, length = lax.axis_size(axis), array.shape[dim]
    at = lax.axis_index(axis)
    up = [(i, i + 1) for i in range(size - 1)]
    down = [(j, i) for i, j in up]
    last = lax.slice_in_dim(array, length - 1, length, axis=dim)
    first = lax.slice_in_dim(array, 0, 1, axis=dim)
    far = lax.ppermute(jnp.where(at == 0, first, last), axis, [(0, size - 1), (size - 1, 0)])
    before = lax.ppermute(last, axis, up)
    after = lax.ppermute(first, axis, down)
    return before, after, far


def on_device(offsets, forces, counts):
    cells = offsets.shape[1:4]
    slots = offsets.shape[4]
    n_bins = cells[0] * cells[1] * cells[2]
    n_targets = n_bins * slots
    whole = pl.BlockSpec(memory_space=pltpu.VMEM)
    scalars = pl.BlockSpec(memory_space=pltpu.SMEM)

    def floats(*shape):
        return jax.ShapeDtypeStruct(shape, jnp.float32)

    def params(mib):
        return pltpu.CompilerParams(vmem_limit_bytes=mib << 20)

    loop_scratch = [
        pltpu.VMEM((UNITS, 2, CHUNK, LANES), jnp.float32),
        pltpu.SMEM((n_bins,), jnp.int32),
        pltpu.SMEM((n_bins,), jnp.int32),
    ]
    count_scratch = [
        pltpu.VMEM((ROWS, LANES), jnp.int32),
        pltpu.SMEM((ROWS, LANES), jnp.int32),
        pltpu.SemaphoreType.DMA,
    ]
    cost = pl.CostEstimate(flops=1 << 28, bytes_accessed=1 << 16, transcendentals=1 << 20)

    def list_tiles(n_lists, n_steps):
        return pltpu.VMEM((n_lists * (n_steps + 1), ROWS, LANES), jnp.float32)

    own_list, all_targets = floats(n_bins + 1, ROWS, slots), floats(3, n_targets, slots)
    own, early = pl.pallas_call(
        functools.partial(pack_kernel, cells),
        out_shape=[floats(*cells, ROWS, slots), floats(EARLY, ROWS, slots)],
        in_specs=[scalars, whole, whole],
        out_specs=[whole, whole],
        scratch_shapes=[
            pltpu.VMEM(own_list.shape, jnp.float32),
            pltpu.VMEM((3, EARLY * slots, slots), jnp.float32),
            loop_scratch[0],
            pltpu.VMEM((4, EARLY * slots + CHUNK, slots), jnp.float32),
        ]
        + loop_scratch[1:],
        name="pack",
    )(counts, offsets, forces)

    together = lax.optimization_barrier
    size = lax.axis_size("ha")
    other = lax.ppermute(own, "ha", [(i, (i + 1) % size) for i in range(size)])
    listed, spread, first = pl.pallas_call(
        functools.partial(first_kernel, cells, FIRST),
        out_shape=[own_list, all_targets, floats(4, len(FIRST) * slots + CHUNK, slots)],
        in_specs=[whole],
        out_specs=[whole] * 3,
        scratch_shapes=loop_scratch + count_scratch,
        compiler_params=params(8),
        cost_estimate=cost,
        name="first",
    )(own)
    other, sent, listed, first = together((other, own, listed, first))
    column = jnp.concatenate([sent, other], axis=2)
    x_lo, x_hi, x_far = shifted_apart(column, "gx", 0)
    second = pl.pallas_call(
        functools.partial(second_kernel, cells, SECOND),
        out_shape=floats(4, len(SECOND) * slots + CHUNK, slots),
        in_specs=[scalars, whole, whole],
        out_specs=whole,
        scratch_shapes=loop_scratch,
        compiler_params=params(8),
        cost_estimate=cost,
        name="second",
    )(counts, listed, spread)
    x_lo, x_hi, x_far, second = together((x_lo, x_hi, x_far, second))
    at_x = lax.axis_index("gx")
    x_lo = jnp.where(at_x == 0, x_far, x_lo)
    x_hi = jnp.where(at_x == lax.axis_size("gx") - 1, x_far, x_hi)
    wide = jnp.concatenate([x_lo, column, x_hi], axis=0)
    y_lo, y_hi = shifted(wide, "gy", 1)
    middle = pl.pallas_call(
        functools.partial(middle_kernel, cells),
        out_shape=floats(4, n_targets + CHUNK, slots),
        in_specs=[scalars, whole, whole],
        out_specs=whole,
        scratch_shapes=[list_tiles(cells[0] * cells[2], 10)] + loop_scratch + count_scratch,
        compiler_params=params(8),
        cost_estimate=cost,
        name="middle",
    )(counts, wide, spread)
    y_lo, y_hi, middle = together((y_lo, y_hi, middle))
    return pl.pallas_call(
        functools.partial(last_kernel, cells),
        out_shape=floats(3, *cells, slots),
        in_specs=[scalars] + [whole] * 8,
        out_specs=whole,
        scratch_shapes=[pltpu.VMEM((4, n_targets + CHUNK, slots), jnp.float32), list_tiles(n_bins, 9)]
        + loop_scratch
        + count_scratch,
        compiler_params=params(12),
        cost_estimate=cost,
        name="last",
    )(counts, own, y_lo, y_hi, spread, middle, first, second, early)


def solution(mesh):
    in_specs = (
        P(None, "gx", "gy", "ha", None),
        P(None, "gx", "gy", "ha", None),
        P("gx", "gy", "ha"),
    )
    out_specs = P(None, "gx", "gy", "ha", None)
    return jax.shard_map(on_device, mesh=mesh, in_specs=in_specs, out_specs=out_specs, check_vma=False)
```

```python
import functools
import math

import jax
import jax.numpy as jnp
from jax import lax
from jax.experimental import pallas as pl
from jax.experimental.pallas import tpu as pltpu
from jax.sharding import PartitionSpec as P

SPLIT_XI = 2.0
SOFT_SQ = 0.01
GAUSS_COEF = 2.0 * SPLIT_XI / math.sqrt(math.pi)
STOKES_NORM = 1.0 / (8.0 * math.pi)

SOFT_U = SPLIT_XI * SPLIT_XI * SOFT_SQ
LOG2_E = math.log2(math.e)
LOG2_G = math.log2(GAUSS_COEF)
SELF_C = math.erfc(math.sqrt(SOFT_U)) / math.sqrt(SOFT_SQ) + GAUSS_COEF * (
    2.0 * SOFT_U - 3.0
) * math.exp(-SOFT_U)

LANES = 128
ROWS = 8
CHUNK = 32
UNITS = 4
COUNT_ROW = 3
FULL = 640
EARLY = 3
FIRST = (3, 4)
SECOND = (5, 6, 7, 0, 1, 2)
LIST_Z, LIST_X, LIST_Y = 5, 7, 10
FORCE_ROW = 4


def rows_and_lanes(shape=(ROWS, LANES)):
    return lax.broadcasted_iota(jnp.int32, shape, 0), lax.broadcasted_iota(jnp.int32, shape, 1)


def bins_of(cells):
    return [(i, j, k) for i in range(cells[0]) for j in range(cells[1]) for k in range(cells[2])]


def shift_tile(cells, at):
    row, _ = rows_and_lanes()
    moved = jnp.zeros((ROWS, LANES), jnp.float32)
    for i in range(3):
        moved = jnp.where(row == i, SPLIT_XI * (at[i] - 0.5 * (cells[i] - 1)), moved)
    return moved


def compact(listed, base, sources):
    _, lane = rows_and_lanes()
    filled = jnp.int32(0)
    moved = []
    for tile, count in sources:
        at = lax.bitwise_and(filled, LANES - 1)
        tile_id = base + lax.shift_right_logical(filled, 7)
        moved.append((pltpu.roll(tile, at, 1), lane >= at, tile_id, at + count >= LANES))
        filled = filled + count
    current = jnp.zeros((ROWS, LANES), jnp.float32)
    for tile, behind, tile_id, full in moved:
        current = jnp.where(behind, tile, current)
        spill = jnp.where(behind, 0.0, tile)
        listed[tile_id] = current
        listed[tile_id + 1] = spill
        current = jnp.where(full, spill, current)
    return filled


def up_to(count, size):
    return lax.shift_right_logical(count + (size - 1), size.bit_length() - 1)


def parts_of(value, n):
    parts = []
    for _ in range(n):
        part = value.astype(jnp.bfloat16)
        value = value - part.astype(jnp.float32)
        parts.append(part)
    return parts


def spread_targets(spread, first, tile):
    parts = [p.astype(jnp.float32) for p in parts_of(tile, 3)] + [jnp.zeros_like(tile)]
    row, lane = rows_and_lanes((4 * ROWS, 3 * LANES))
    pick = jnp.where(lax.bitwise_and(row, ROWS - 1) == lax.shift_right_logical(lane, 7), 1.0, 0.0)
    wide = lax.dot_general(
        jnp.concatenate(parts, axis=0).astype(jnp.bfloat16),
        pick.astype(jnp.bfloat16),
        (((0,), (0,)), ((), ())),
        preferred_element_type=jnp.float32,
    )
    for i in range(3):
        spread[i, first : first + LANES, :] = wide[:, i * LANES : (i + 1) * LANES]


def coefficients(target, source, force):
    delta = [t - s for t, s in zip(target, source)]
    u = (delta[0] * delta[0] + SOFT_U) + delta[1] * delta[1] + delta[2] * delta[2]
    inv = lax.rsqrt(u)
    tail = (1.0 - lax.erf(u * inv)) * inv
    gauss = jnp.exp2(LOG2_G - u * LOG2_E)
    rest = gauss * (u - 1.5)
    coef_d = ((tail - rest) - gauss) * (inv * inv)
    along = coef_d * (delta[0] * force[0] + delta[1] * force[1] + delta[2] * force[2])
    return tail + rest, along


class Groups:
    def __init__(self, tables):
        self.tables = tables
        self.size = 0
        self.total = jnp.int32(0)

    def add(self, n_chunks, n_tiles, first_tile, spread_row, acc_row):
        for table, value in zip(self.tables, (n_chunks, n_tiles, first_tile, spread_row, acc_row)):
            table[self.size] = jnp.int32(value)
        self.size += 1
        self.total = self.total + n_chunks * n_tiles

    def run(self, listed, spread, coefs, acc):
        chunks_of, tiles_of, list_of, spread_of, acc_of = self.tables
        trash = acc.shape[1] - CHUNK
        coefs[...] = jnp.zeros_like(coefs)

        def rows(tile_id, at):
            return [listed[tile_id, i : i + 1, :] for i in at]

        def advance(group, chunk, tile):
            end_tile = tile + 1 == tiles_of[group]
            next_chunk = jnp.where(end_tile, chunk + CHUNK, chunk)
            end_chunk = next_chunk == chunks_of[group] * CHUNK
            next_group = jnp.where(end_chunk, jnp.minimum(group + 1, self.size - 1), group)
            return next_group, jnp.where(end_chunk, 0, next_chunk), jnp.where(end_tile, 0, tile + 1)

        def some_units(step, state):
            place, olds = state[:3], state[3:]
            news, targets, sources = [], [], []
            for n in range(UNITS):
                group, chunk, tile = place
                valid = step * UNITS + n < self.total
                news += [jnp.where(valid, acc_of[group] + chunk, trash), list_of[group] + tile]
                at = pl.ds(pl.multiple_of(spread_of[group] + chunk, CHUNK), CHUNK)
                targets.append([spread[i, at, :] for i in range(3)])
                sources.append((rows(news[-1], (0, 1, 2)), rows(news[-1], (4, 5, 6))))
                place = advance(*place)
            old_coefs = [(coefs[n, 0], coefs[n, 1]) for n in range(UNITS)]
            old_sources = [(rows(tile, (0, 1, 2)), rows(tile, (4, 5, 6))) for tile in olds[1::2]]

            new_coefs = [coefficients(target, *source) for target, source in zip(targets, sources)]
            terms = []
            for (source, force), (coef_c, along) in zip(old_sources, old_coefs):
                terms.append([coef_c * force[i] - along * source[i] for i in range(3)] + [along])

            for first, unit in zip(olds[::2], terms):
                at = pl.ds(pl.multiple_of(first, CHUNK), CHUNK)
                for i in range(4):
                    acc[i, at, :] = acc[i, at, :] + unit[i]
            for n in range(UNITS):
                coefs[n, 0], coefs[n, 1] = new_coefs[n]
            return place + tuple(news)

        zero = jnp.int32(0)
        start = (zero, zero, zero) + (jnp.int32(trash), list_of[0]) * UNITS
        lax.fori_loop(0, lax.div(self.total + UNITS - 1, UNITS) + 1, some_units, start)


def is_full(cells, count_ref):
    filled = jnp.int32(0)
    for at in bins_of(cells):
        filled = filled + count_ref[at]
    return filled, filled > FULL


def list_own(cells, count_ref, own_ref, listed):
    sources = [(own_ref[at] + shift_tile(cells, at), count_ref[at]) for at in bins_of(cells)]
    compact(listed, 0, sources)


def velocity_rows(cells, group, by_row, tile):
    position = tile + shift_tile(cells, bins_of(cells)[group])
    return (2.0 * STOKES_NORM) * (by_row + position * jnp.broadcast_to(by_row[3:4], (ROWS, LANES)))


def lane_sums(totals):
    _, lane = rows_and_lanes((2 * LANES, LANES))
    merged = jnp.zeros(totals[0].shape, jnp.float32)
    for i, total in enumerate(totals):
        merged = merged + jnp.dot(
            jnp.concatenate(parts_of(total, 2), axis=1),
            jnp.where(lane == i, 1.0, 0.0).astype(jnp.bfloat16),
            preferred_element_type=jnp.float32,
        )
    return merged


def pack_kernel(cells, count_ref, offset_v, force_v, own_ref, early_ref, listed, spread, coefs, acc, *tables):
    slot = lax.broadcasted_iota(jnp.int32, (1, LANES), 1)
    for at in bins_of(cells):
        ix, iy, iz = at
        count = count_ref[at]
        wide = jnp.full((1, LANES), count, jnp.int32).astype(jnp.float32)
        for i in range(3):
            position = offset_v[i, ix, iy, iz : iz + 1, :]
            own_ref[ix, iy, iz, i : i + 1, :] = position * SPLIT_XI - 0.5 * SPLIT_XI
            force = force_v[i, ix, iy, iz : iz + 1, :]
            own_ref[ix, iy, iz, 4 + i : 5 + i, :] = jnp.where(slot < count, force, 0.0)
        own_ref[ix, iy, iz, 3:4, :] = wide
        own_ref[ix, iy, iz, 7:8, :] = wide
    early_ref[...] = jnp.zeros_like(early_ref)
    filled, full = is_full(cells, count_ref)

    @pl.when(full)
    def _():
        list_own(cells, count_ref, own_ref, listed)
        acc[...] = jnp.zeros_like(acc)
        groups = range(EARLY)
        tiles = [own_ref[bins_of(cells)[n]] for n in groups]
        work = Groups(tables)
        for n in groups:
            at = bins_of(cells)[n]
            spread_targets(spread, n * LANES, tiles[n] + shift_tile(cells, at))
            work.add(up_to(count_ref[at], CHUNK), up_to(filled, LANES), 0, n * LANES, n * LANES)
        work.run(listed, spread, coefs, acc)
        merged = lane_sums([acc[i, : EARLY * LANES, :] for i in range(4)])
        for n in groups:
            by_row = jnp.transpose(merged[n * LANES : (n + 1) * LANES])[:ROWS]
            early_ref[n] = velocity_rows(cells, n, by_row, tiles[n])


def counts_of(tiles, count_v, count_s, sem):
    _, lane = rows_and_lanes()
    held = jnp.zeros((ROWS, LANES), jnp.float32)
    for cell, tile in enumerate(tiles):
        held = jnp.where(lane == cell, tile, held)
    count_v[...] = held.astype(jnp.int32)
    copy = pltpu.make_async_copy(count_v, count_s, sem)
    copy.start()
    return copy


def first_kernel(cells, own_ref, listed, spread, acc, coefs, *refs):
    tables, (count_v, count_s, sem) = refs[:5], refs[5:]
    bins = bins_of(cells)
    copy = counts_of([own_ref[at] for at in bins], count_v, count_s, sem)
    for n, at in enumerate(bins):
        spread_targets(spread, n * LANES, own_ref[at] + shift_tile(cells, at))
    acc[...] = jnp.zeros_like(acc)
    copy.wait()
    count_ref = {at: count_s[COUNT_ROW, n] for n, at in enumerate(bins)}
    list_own(cells, count_ref, own_ref, listed)
    filled, _ = is_full(cells, count_ref)
    work = Groups(tables)
    for m, n in enumerate(FIRST):
        work.add(up_to(count_ref[bins[n]], CHUNK), up_to(filled, LANES), 0, n * LANES, m * LANES)
    work.run(listed, spread, coefs, acc)


def second_kernel(cells, count_ref, other, own_list, spread, acc, listed, coefs, *refs):
    tables, (count_v, count_s, sem) = refs[:5], refs[5:]
    bins = bins_of(cells)
    size_x, size_y, size_z = cells
    copy = counts_of([other[at] for at in bins], count_v, count_s, sem)
    acc[...] = jnp.zeros_like(acc)
    n_own = own_list.shape[0]
    for n in range(n_own):
        listed[n] = own_list[n]
    filled, full = is_full(cells, count_ref)
    copy.wait()
    work = Groups(tables)
    for bz in range(size_z):
        z = (-1, size_z)[bz]
        sources = []
        for x in range(size_x):
            for y in range(size_y):
                place = (x, y, z % size_z)
                tile = other[place] + shift_tile(cells, (x, y, z))
                sources.append((tile, count_s[COUNT_ROW, bins.index(place)]))
        first_tile = n_own + bz * LIST_Z
        n_tiles = up_to(compact(listed, first_tile, sources), LANES)
        for n, at in enumerate(bins):
            if at[2] == bz:
                work.add(up_to(count_ref[at], CHUNK), n_tiles, first_tile, n * LANES, n * LANES)
    for n in SECOND:
        n_chunks = up_to(count_ref[bins[n]], CHUNK)
        n_chunks = jnp.where(full, 0, n_chunks) if n < EARLY else n_chunks
        work.add(n_chunks, up_to(filled, LANES), 0, n * LANES, n * LANES)
    work.run(listed, spread, coefs, acc)


def middle_kernel(cells, count_ref, wide, spread, acc, listed, coefs, *refs):
    tables, (count_v, count_s, sem) = refs[:5], refs[5:]
    size_x, size_y, size_z = cells
    n_z = 2 * size_z
    bins = bins_of(cells)
    places = [(i, j, k) for i in (0, size_x + 1) for j in range(size_y) for k in range(n_z)]
    copy = counts_of([wide[at] for at in places], count_v, count_s, sem)
    acc[...] = jnp.zeros_like(acc)
    copy.wait()
    work = Groups(tables)
    for bx in range(size_x):
        for bz in range(size_z):
            x = (-1, size_x)[bx]
            sources = []
            for y in range(size_y):
                for z in (bz - 1, bz, bz + 1):
                    place = (x + 1, y, z % n_z)
                    tile = wide[place] + shift_tile(cells, (x, y, z))
                    sources.append((tile, count_s[COUNT_ROW, places.index(place)]))
            first_tile = (bx * size_z + bz) * LIST_X
            n_tiles = up_to(compact(listed, first_tile, sources), LANES)
            for n, at in enumerate(bins):
                if (at[0], at[2]) == (bx, bz):
                    work.add(up_to(count_ref[at], CHUNK), n_tiles, first_tile, n * LANES, n * LANES)
    work.run(listed, spread, coefs, acc)


def last_kernel(cells, count_ref, own_ref, y_lo, y_hi, spread, *refs):
    (middle, first, second, early, out_ref, acc, listed, coefs), refs = refs[:8], refs[8:]
    tables, (count_v, count_s, sem) = refs[:5], refs[5:]
    size_x, size_y, size_z = cells
    n_z = 2 * size_z
    bins = bins_of(cells)
    places = [(i, j, k) for i in range(size_x + 2) for j in range(2) for k in range(n_z)]
    tiles = [(y_lo, y_hi)[j][i, 0, k] for i, j, k in places]
    copy = counts_of(tiles, count_v, count_s, sem)
    acc[...] = jnp.zeros_like(acc)
    copy.wait()
    work = Groups(tables)
    for n, (bx, by, bz) in enumerate(bins):
        sources = []
        for x in (bx - 1, bx, bx + 1):
            for z in (bz - 1, bz, bz + 1):
                cell = places.index((x + 1, by, z % n_z))
                tile = tiles[cell] + shift_tile(cells, (x, (-1, size_y)[by], z))
                sources.append((tile, count_s[COUNT_ROW, cell]))
        n_tiles = up_to(compact(listed, n * LIST_Y, sources), LANES)
        work.add(up_to(count_ref[bx, by, bz], CHUNK), n_tiles, n * LIST_Y, n * LANES, n * LANES)
    work.run(listed, spread, coefs, acc)

    slot = lax.broadcasted_iota(jnp.int32, (1, LANES), 1)
    totals = [[], [], [], []]
    for n in range(len(bins)):
        here = slice(n * LANES, (n + 1) * LANES)
        for i in range(4):
            total = acc[i, here, :] + middle[i, here, :] + second[i, here, :]
            if n in FIRST:
                m = FIRST.index(n)
                total = total + first[i, m * LANES : (m + 1) * LANES, :]
            totals[i].append(total)
    merged = lane_sums([jnp.concatenate(total, axis=0) for total in totals])
    for n, at in enumerate(bins):
        by_row = jnp.transpose(merged[n * LANES : (n + 1) * LANES])[:ROWS]
        tile = own_ref[at]
        total = velocity_rows(cells, n, by_row, tile)
        total = total - (STOKES_NORM * SELF_C) * pltpu.roll(tile, ROWS - FORCE_ROW, 0)
        if n < EARLY:
            total = total + early[n]
        total = jnp.where(slot < count_ref[at], total, 0.0)
        for i in range(3):
            out_ref[i, at[0], at[1], at[2] : at[2] + 1, :] = total[i : i + 1]


def shifted(array, axis, dim):
    size, length = lax.axis_size(axis), array.shape[dim]
    up = [(i, (i + 1) % size) for i in range(size)]
    down = [(j, i) for i, j in up]
    after = lax.ppermute(lax.slice_in_dim(array, 0, 1, axis=dim), axis, down)
    before = lax.ppermute(lax.slice_in_dim(array, length - 1, length, axis=dim), axis, up)
    return before, after


def on_device(offsets, forces, counts):
    cells = offsets.shape[1:4]
    slots = offsets.shape[4]
    n_bins = cells[0] * cells[1] * cells[2]
    n_targets = n_bins * slots
    whole = pl.BlockSpec(memory_space=pltpu.VMEM)
    scalars = pl.BlockSpec(memory_space=pltpu.SMEM)

    def floats(*shape):
        return jax.ShapeDtypeStruct(shape, jnp.float32)

    def params(mib):
        return pltpu.CompilerParams(vmem_limit_bytes=mib << 20)

    loop_scratch = [pltpu.VMEM((UNITS, 2, CHUNK, LANES), jnp.float32)]
    loop_scratch += [pltpu.SMEM((2 * n_bins,), jnp.int32)] * 5
    count_scratch = [
        pltpu.VMEM((ROWS, LANES), jnp.int32),
        pltpu.SMEM((ROWS, LANES), jnp.int32),
        pltpu.SemaphoreType.DMA,
    ]
    cost = pl.CostEstimate(flops=1 << 28, bytes_accessed=1 << 16, transcendentals=1 << 20)

    def list_scratch(n_tiles):
        return [pltpu.VMEM((n_tiles, ROWS, LANES), jnp.float32)]

    own_list, all_targets = floats(n_bins + 1, ROWS, slots), floats(3, n_targets, slots)
    own, early = pl.pallas_call(
        functools.partial(pack_kernel, cells),
        out_shape=[floats(*cells, ROWS, slots), floats(EARLY, ROWS, slots)],
        in_specs=[scalars, whole, whole],
        out_specs=[whole, whole],
        scratch_shapes=[
            pltpu.VMEM(own_list.shape, jnp.float32),
            pltpu.VMEM((3, EARLY * slots, slots), jnp.float32),
            loop_scratch[0],
            pltpu.VMEM((4, EARLY * slots + CHUNK, slots), jnp.float32),
        ]
        + loop_scratch[1:],
        name="pack",
    )(counts, offsets, forces)

    together = lax.optimization_barrier
    size = lax.axis_size("ha")
    other = lax.ppermute(own, "ha", [(i, (i + 1) % size) for i in range(size)])
    listed, spread, first = pl.pallas_call(
        functools.partial(first_kernel, cells),
        out_shape=[own_list, all_targets, floats(4, len(FIRST) * slots + CHUNK, slots)],
        in_specs=[whole],
        out_specs=[whole] * 3,
        scratch_shapes=loop_scratch + count_scratch,
        compiler_params=params(8),
        cost_estimate=cost,
        name="first",
    )(own)
    other, sent, listed, first = together((other, own, listed, first))
    column = jnp.concatenate([sent, other], axis=2)
    x_lo, x_hi = shifted(column, "gx", 0)
    second = pl.pallas_call(
        functools.partial(second_kernel, cells),
        out_shape=floats(4, n_targets + CHUNK, slots),
        in_specs=[scalars] + [whole] * 3,
        out_specs=whole,
        scratch_shapes=[
            pltpu.VMEM((own_list.shape[0] + cells[2] * LIST_Z, ROWS, LANES), jnp.float32)
        ]
        + loop_scratch
        + count_scratch,
        compiler_params=params(8),
        cost_estimate=cost,
        name="second",
    )(counts, other, listed, spread)
    x_hi, x_lo, second = together((x_hi, x_lo, second))
    wide = jnp.concatenate([x_lo, column, x_hi], axis=0)
    y_lo, y_hi = shifted(wide, "gy", 1)
    middle = pl.pallas_call(
        functools.partial(middle_kernel, cells),
        out_shape=floats(4, n_targets + CHUNK, slots),
        in_specs=[scalars, whole, whole],
        out_specs=whole,
        scratch_shapes=list_scratch(cells[0] * cells[2] * LIST_X) + loop_scratch + count_scratch,
        compiler_params=params(8),
        cost_estimate=cost,
        name="middle",
    )(counts, wide, spread)
    y_lo, y_hi, middle = together((y_lo, y_hi, middle))
    return pl.pallas_call(
        functools.partial(last_kernel, cells),
        out_shape=floats(3, *cells, slots),
        in_specs=[scalars] + [whole] * 8,
        out_specs=whole,
        scratch_shapes=[pltpu.VMEM((4, n_targets + CHUNK, slots), jnp.float32)]
        + list_scratch(n_bins * LIST_Y)
        + loop_scratch
        + count_scratch,
        compiler_params=params(12),
        cost_estimate=cost,
        name="last",
    )(counts, own, y_lo, y_hi, spread, middle, first, second, early)


def solution(mesh):
    in_specs = (
        P(None, "gx", "gy", "ha", None),
        P(None, "gx", "gy", "ha", None),
        P("gx", "gy", "ha"),
    )
    out_specs = P(None, "gx", "gy", "ha", None)
    return jax.shard_map(on_device, mesh=mesh, in_specs=in_specs, out_specs=out_specs, check_vma=False)
```

```python
import functools
import math

import jax
import jax.numpy as jnp
from jax import lax
from jax.experimental import pallas as pl
from jax.experimental.pallas import tpu as pltpu
from jax.sharding import PartitionSpec as P

SPLIT_XI = 2.0
SOFT_SQ = 0.01
GAUSS_COEF = 2.0 * SPLIT_XI / math.sqrt(math.pi)
STOKES_NORM = 1.0 / (8.0 * math.pi)

SOFT_U = SPLIT_XI * SPLIT_XI * SOFT_SQ
LOG2_E = math.log2(math.e)
LOG2_G = math.log2(GAUSS_COEF)
SELF_C = math.erfc(math.sqrt(SOFT_U)) / math.sqrt(SOFT_SQ) + GAUSS_COEF * (
    2.0 * SOFT_U - 3.0
) * math.exp(-SOFT_U)

LANES = 128
ROWS = 8
CHUNK = 32
UNITS = 4
COUNT_ROW = 3
FULL = 640
EARLY = 3
FIRST = (3, 4)
SECOND = (5, 6, 7, 0, 1, 2)
LIST_Z, LIST_X, LIST_Y = 5, 7, 10
FORCE_ROW = 4


def rows_and_lanes(shape=(ROWS, LANES)):
    return lax.broadcasted_iota(jnp.int32, shape, 0), lax.broadcasted_iota(jnp.int32, shape, 1)


def bins_of(cells):
    return [(i, j, k) for i in range(cells[0]) for j in range(cells[1]) for k in range(cells[2])]


def shift_tile(cells, at):
    row, _ = rows_and_lanes()
    moved = jnp.zeros((ROWS, LANES), jnp.float32)
    for i in range(3):
        moved = jnp.where(row == i, SPLIT_XI * (at[i] - 0.5 * (cells[i] - 1)), moved)
    return moved


def compact(listed, base, sources):
    _, lane = rows_and_lanes()
    filled = jnp.int32(0)
    moved = []
    for tile, count in sources:
        at = lax.bitwise_and(filled, LANES - 1)
        tile_id = base + lax.shift_right_logical(filled, 7)
        moved.append((pltpu.roll(tile, at, 1), lane >= at, tile_id, at + count >= LANES))
        filled = filled + count
    current = jnp.zeros((ROWS, LANES), jnp.float32)
    for tile, behind, tile_id, full in moved:
        current = jnp.where(behind, tile, current)
        spill = jnp.where(behind, 0.0, tile)
        listed[tile_id] = current
        listed[tile_id + 1] = spill
        current = jnp.where(full, spill, current)
    return filled


def up_to(count, size):
    return lax.shift_right_logical(count + (size - 1), size.bit_length() - 1)


def parts_of(value, n):
    parts = []
    for _ in range(n):
        part = value.astype(jnp.bfloat16)
        value = value - part.astype(jnp.float32)
        parts.append(part)
    return parts


def spread_targets(spread, first, tile):
    parts = [p.astype(jnp.float32) for p in parts_of(tile, 3)] + [jnp.zeros_like(tile)]
    row, lane = rows_and_lanes((4 * ROWS, 3 * LANES))
    pick = jnp.where(lax.bitwise_and(row, ROWS - 1) == lax.shift_right_logical(lane, 7), 1.0, 0.0)
    wide = lax.dot_general(
        jnp.concatenate(parts, axis=0).astype(jnp.bfloat16),
        pick.astype(jnp.bfloat16),
        (((0,), (0,)), ((), ())),
        preferred_element_type=jnp.float32,
    )
    for i in range(3):
        spread[i, first : first + LANES, :] = wide[:, i * LANES : (i + 1) * LANES]


def coefficients(target, source, force):
    delta = [t - s for t, s in zip(target, source)]
    u = (delta[0] * delta[0] + SOFT_U) + delta[1] * delta[1] + delta[2] * delta[2]
    inv = lax.rsqrt(u)
    tail = (1.0 - lax.erf(u * inv)) * inv
    gauss = jnp.exp2(LOG2_G - u * LOG2_E)
    rest = gauss * (u - 1.5)
    coef_d = ((tail - rest) - gauss) * (inv * inv)
    along = coef_d * (delta[0] * force[0] + delta[1] * force[1] + delta[2] * force[2])
    return tail + rest, along


class Groups:
    def __init__(self, tables):
        self.tables = tables
        self.size = 0
        self.total = jnp.int32(0)

    def add(self, n_chunks, n_tiles, first_tile, spread_row, acc_row):
        for table, value in zip(self.tables, (n_chunks, n_tiles, first_tile, spread_row, acc_row)):
            table[self.size] = jnp.int32(value)
        self.size += 1
        self.total = self.total + n_chunks * n_tiles

    def run(self, listed, spread, coefs, acc):
        chunks_of, tiles_of, list_of, spread_of, acc_of = self.tables
        trash = acc.shape[1] - CHUNK
        coefs[...] = jnp.zeros_like(coefs)

        def rows(tile_id, at):
            return [listed[tile_id, i : i + 1, :] for i in at]

        def advance(group, chunk, tile):
            end_tile = tile + 1 == tiles_of[group]
            next_chunk = jnp.where(end_tile, chunk + CHUNK, chunk)
            end_chunk = next_chunk == chunks_of[group] * CHUNK
            next_group = jnp.where(end_chunk, jnp.minimum(group + 1, self.size - 1), group)
            return next_group, jnp.where(end_chunk, 0, next_chunk), jnp.where(end_tile, 0, tile + 1)

        def some_units(step, state):
            place, olds = state[:3], state[3:]
            news, targets, sources = [], [], []
            for n in range(UNITS):
                group, chunk, tile = place
                valid = step * UNITS + n < self.total
                news += [jnp.where(valid, acc_of[group] + chunk, trash), list_of[group] + tile]
                at = pl.ds(pl.multiple_of(spread_of[group] + chunk, CHUNK), CHUNK)
                targets.append([spread[i, at, :] for i in range(3)])
                sources.append((rows(news[-1], (0, 1, 2)), rows(news[-1], (4, 5, 6))))
                place = advance(*place)
            old_coefs = [(coefs[n, 0], coefs[n, 1]) for n in range(UNITS)]
            old_sources = [(rows(tile, (0, 1, 2)), rows(tile, (4, 5, 6))) for tile in olds[1::2]]

            new_coefs = [coefficients(target, *source) for target, source in zip(targets, sources)]
            terms = []
            for (source, force), (coef_c, along) in zip(old_sources, old_coefs):
                terms.append([coef_c * force[i] - along * source[i] for i in range(3)] + [along])

            for first, unit in zip(olds[::2], terms):
                at = pl.ds(pl.multiple_of(first, CHUNK), CHUNK)
                for i in range(4):
                    acc[i, at, :] = acc[i, at, :] + unit[i]
            for n in range(UNITS):
                coefs[n, 0], coefs[n, 1] = new_coefs[n]
            return place + tuple(news)

        zero = jnp.int32(0)
        start = (zero, zero, zero) + (jnp.int32(trash), list_of[0]) * UNITS
        lax.fori_loop(0, lax.div(self.total + UNITS - 1, UNITS) + 1, some_units, start)


def is_full(cells, count_ref):
    filled = jnp.int32(0)
    for at in bins_of(cells):
        filled = filled + count_ref[at]
    return filled, filled > FULL


def list_own(cells, count_ref, own_ref, listed):
    sources = [(own_ref[at] + shift_tile(cells, at), count_ref[at]) for at in bins_of(cells)]
    compact(listed, 0, sources)


def velocity_rows(cells, group, by_row, tile):
    position = tile + shift_tile(cells, bins_of(cells)[group])
    return (2.0 * STOKES_NORM) * (by_row + position * jnp.broadcast_to(by_row[3:4], (ROWS, LANES)))


def lane_sums(totals):
    _, lane = rows_and_lanes((2 * LANES, LANES))
    merged = jnp.zeros(totals[0].shape, jnp.float32)
    for i, total in enumerate(totals):
        merged = merged + jnp.dot(
            jnp.concatenate(parts_of(total, 2), axis=1),
            jnp.where(lane == i, 1.0, 0.0).astype(jnp.bfloat16),
            preferred_element_type=jnp.float32,
        )
    return merged


def pack_kernel(cells, count_ref, offset_v, force_v, own_ref, early_ref, listed, spread, coefs, acc, *tables):
    slot = lax.broadcasted_iota(jnp.int32, (1, LANES), 1)
    for at in bins_of(cells):
        ix, iy, iz = at
        count = count_ref[at]
        wide = jnp.full((1, LANES), count, jnp.int32).astype(jnp.float32)
        for i in range(3):
            position = offset_v[i, ix, iy, iz : iz + 1, :]
            own_ref[ix, iy, iz, i : i + 1, :] = position * SPLIT_XI - 0.5 * SPLIT_XI
            force = force_v[i, ix, iy, iz : iz + 1, :]
            own_ref[ix, iy, iz, 4 + i : 5 + i, :] = jnp.where(slot < count, force, 0.0)
        own_ref[ix, iy, iz, 3:4, :] = wide
        own_ref[ix, iy, iz, 7:8, :] = wide
    early_ref[...] = jnp.zeros_like(early_ref)
    filled, full = is_full(cells, count_ref)

    @pl.when(full)
    def _():
        list_own(cells, count_ref, own_ref, listed)
        acc[...] = jnp.zeros_like(acc)
        groups = range(EARLY)
        tiles = [own_ref[bins_of(cells)[n]] for n in groups]
        work = Groups(tables)
        for n in groups:
            at = bins_of(cells)[n]
            spread_targets(spread, n * LANES, tiles[n] + shift_tile(cells, at))
            work.add(up_to(count_ref[at], CHUNK), up_to(filled, LANES), 0, n * LANES, n * LANES)
        work.run(listed, spread, coefs, acc)
        merged = lane_sums([acc[i, : EARLY * LANES, :] for i in range(4)])
        for n in groups:
            by_row = jnp.transpose(merged[n * LANES : (n + 1) * LANES])[:ROWS]
            early_ref[n] = velocity_rows(cells, n, by_row, tiles[n])


def counts_of(tiles, count_v, count_s, sem):
    _, lane = rows_and_lanes()
    held = jnp.zeros((ROWS, LANES), jnp.float32)
    for cell, tile in enumerate(tiles):
        held = jnp.where(lane == cell, tile, held)
    count_v[...] = held.astype(jnp.int32)
    copy = pltpu.make_async_copy(count_v, count_s, sem)
    copy.start()
    return copy


def first_kernel(cells, sent_ref, own_ref, listed, spread, acc, coefs, *refs):
    tables, (count_v, count_s, sem) = refs[:5], refs[5:]
    bins = bins_of(cells)
    copy = counts_of([sent_ref[at] for at in bins], count_v, count_s, sem)
    own_ref[...] = sent_ref[...]
    for n, at in enumerate(bins):
        spread_targets(spread, n * LANES, own_ref[at] + shift_tile(cells, at))
    acc[...] = jnp.zeros_like(acc)
    copy.wait()
    count_ref = {at: count_s[COUNT_ROW, n] for n, at in enumerate(bins)}
    list_own(cells, count_ref, own_ref, listed)
    filled, _ = is_full(cells, count_ref)
    work = Groups(tables)
    for m, n in enumerate(FIRST):
        work.add(up_to(count_ref[bins[n]], CHUNK), up_to(filled, LANES), 0, n * LANES, m * LANES)
    work.run(listed, spread, coefs, acc)


def second_kernel(cells, count_ref, other, own_list, spread, first, acc, listed, coefs, *refs):
    tables, (count_v, count_s, sem) = refs[:5], refs[5:]
    bins = bins_of(cells)
    size_x, size_y, size_z = cells
    copy = counts_of([other[at] for at in bins], count_v, count_s, sem)
    for n in range(len(bins)):
        here = slice(n * LANES, (n + 1) * LANES)
        if n in FIRST:
            m = FIRST.index(n)
            acc[:, here, :] = first[:, m * LANES : (m + 1) * LANES, :]
        else:
            acc[:, here, :] = jnp.zeros((4, LANES, LANES), jnp.float32)
    n_own = own_list.shape[0]
    for n in range(n_own):
        listed[n] = own_list[n]
    filled, full = is_full(cells, count_ref)
    copy.wait()
    work = Groups(tables)
    for bz in range(size_z):
        z = (-1, size_z)[bz]
        sources = []
        for x in range(size_x):
            for y in range(size_y):
                place = (x, y, z % size_z)
                tile = other[place] + shift_tile(cells, (x, y, z))
                sources.append((tile, count_s[COUNT_ROW, bins.index(place)]))
        first_tile = n_own + bz * LIST_Z
        n_tiles = up_to(compact(listed, first_tile, sources), LANES)
        for n, at in enumerate(bins):
            if at[2] == bz:
                work.add(up_to(count_ref[at], CHUNK), n_tiles, first_tile, n * LANES, n * LANES)
    for n in SECOND:
        n_chunks = up_to(count_ref[bins[n]], CHUNK)
        n_chunks = jnp.where(full, 0, n_chunks) if n < EARLY else n_chunks
        work.add(n_chunks, up_to(filled, LANES), 0, n * LANES, n * LANES)
    work.run(listed, spread, coefs, acc)


def middle_kernel(cells, count_ref, wide, spread, second, acc, listed, coefs, *refs):
    tables, (count_v, count_s, sem) = refs[:5], refs[5:]
    size_x, size_y, size_z = cells
    n_z = 2 * size_z
    bins = bins_of(cells)
    places = [(i, j, k) for i in (0, size_x + 1) for j in range(size_y) for k in range(n_z)]
    copy = counts_of([wide[at] for at in places], count_v, count_s, sem)
    acc[...] = second[...]
    copy.wait()
    work = Groups(tables)
    for bx in range(size_x):
        for bz in range(size_z):
            x = (-1, size_x)[bx]
            sources = []
            for y in range(size_y):
                for z in (bz - 1, bz, bz + 1):
                    place = (x + 1, y, z % n_z)
                    tile = wide[place] + shift_tile(cells, (x, y, z))
                    sources.append((tile, count_s[COUNT_ROW, places.index(place)]))
            first_tile = (bx * size_z + bz) * LIST_X
            n_tiles = up_to(compact(listed, first_tile, sources), LANES)
            for n, at in enumerate(bins):
                if (at[0], at[2]) == (bx, bz):
                    work.add(up_to(count_ref[at], CHUNK), n_tiles, first_tile, n * LANES, n * LANES)
    work.run(listed, spread, coefs, acc)


def last_kernel(cells, count_ref, own_ref, y_lo, y_hi, spread, *refs):
    (middle, early, out_ref, acc, listed, coefs), refs = refs[:6], refs[6:]
    tables, (count_v, count_s, sem) = refs[:5], refs[5:]
    size_x, size_y, size_z = cells
    n_z = 2 * size_z
    bins = bins_of(cells)
    places = [(i, j, k) for i in range(size_x + 2) for j in range(2) for k in range(n_z)]
    tiles = [(y_lo, y_hi)[j][i, 0, k] for i, j, k in places]
    copy = counts_of(tiles, count_v, count_s, sem)
    acc[...] = middle[...]
    copy.wait()
    work = Groups(tables)
    for n, (bx, by, bz) in enumerate(bins):
        sources = []
        for x in (bx - 1, bx, bx + 1):
            for z in (bz - 1, bz, bz + 1):
                cell = places.index((x + 1, by, z % n_z))
                tile = tiles[cell] + shift_tile(cells, (x, (-1, size_y)[by], z))
                sources.append((tile, count_s[COUNT_ROW, cell]))
        n_tiles = up_to(compact(listed, n * LIST_Y, sources), LANES)
        work.add(up_to(count_ref[bx, by, bz], CHUNK), n_tiles, n * LIST_Y, n * LANES, n * LANES)
    work.run(listed, spread, coefs, acc)

    slot = lax.broadcasted_iota(jnp.int32, (1, LANES), 1)
    merged = lane_sums([acc[i, : len(bins) * LANES, :] for i in range(4)])
    for n, at in enumerate(bins):
        by_row = jnp.transpose(merged[n * LANES : (n + 1) * LANES])[:ROWS]
        tile = own_ref[at]
        total = velocity_rows(cells, n, by_row, tile)
        total = total - (STOKES_NORM * SELF_C) * pltpu.roll(tile, ROWS - FORCE_ROW, 0)
        if n < EARLY:
            total = total + early[n]
        total = jnp.where(slot < count_ref[at], total, 0.0)
        for i in range(3):
            out_ref[i, at[0], at[1], at[2] : at[2] + 1, :] = total[i : i + 1]


def shifted(array, axis, dim):
    size, length = lax.axis_size(axis), array.shape[dim]
    up = [(i, (i + 1) % size) for i in range(size)]
    down = [(j, i) for i, j in up]
    after = lax.ppermute(lax.slice_in_dim(array, 0, 1, axis=dim), axis, down)
    before = lax.ppermute(lax.slice_in_dim(array, length - 1, length, axis=dim), axis, up)
    return before, after


def on_device(offsets, forces, counts):
    cells = offsets.shape[1:4]
    slots = offsets.shape[4]
    n_bins = cells[0] * cells[1] * cells[2]
    n_targets = n_bins * slots
    whole = pl.BlockSpec(memory_space=pltpu.VMEM)
    scalars = pl.BlockSpec(memory_space=pltpu.SMEM)

    def floats(*shape):
        return jax.ShapeDtypeStruct(shape, jnp.float32)

    def params(mib):
        return pltpu.CompilerParams(vmem_limit_bytes=mib << 20)

    loop_scratch = [pltpu.VMEM((UNITS, 2, CHUNK, LANES), jnp.float32)]
    loop_scratch += [pltpu.SMEM((2 * n_bins,), jnp.int32)] * 5
    count_scratch = [
        pltpu.VMEM((ROWS, LANES), jnp.int32),
        pltpu.SMEM((ROWS, LANES), jnp.int32),
        pltpu.SemaphoreType.DMA,
    ]
    cost = pl.CostEstimate(flops=1 << 28, bytes_accessed=1 << 16, transcendentals=1 << 20)

    def list_scratch(n_tiles):
        return [pltpu.VMEM((n_tiles, ROWS, LANES), jnp.float32)]

    own_list, all_targets = floats(n_bins + 1, ROWS, slots), floats(3, n_targets, slots)
    sent, early = pl.pallas_call(
        functools.partial(pack_kernel, cells),
        out_shape=[floats(*cells, ROWS, slots), floats(EARLY, ROWS, slots)],
        in_specs=[scalars, whole, whole],
        out_specs=[whole, whole],
        scratch_shapes=[
            pltpu.VMEM(own_list.shape, jnp.float32),
            pltpu.VMEM((3, EARLY * slots, slots), jnp.float32),
            loop_scratch[0],
            pltpu.VMEM((4, EARLY * slots + CHUNK, slots), jnp.float32),
        ]
        + loop_scratch[1:],
        name="pack",
    )(counts, offsets, forces)

    together = lax.optimization_barrier
    size = lax.axis_size("ha")
    other = lax.ppermute(sent, "ha", [(i, (i + 1) % size) for i in range(size)])
    own, listed, spread, first = pl.pallas_call(
        functools.partial(first_kernel, cells),
        out_shape=[sent, own_list, all_targets, floats(4, len(FIRST) * slots + CHUNK, slots)],
        in_specs=[whole],
        out_specs=[whole] * 4,
        scratch_shapes=loop_scratch + count_scratch,
        compiler_params=params(8),
        cost_estimate=cost,
        name="first",
    )(sent)
    other, own, listed, first = together((other, own, listed, first))
    column = jnp.concatenate([own, other], axis=2)
    x_lo, x_hi = shifted(column, "gx", 0)
    second = pl.pallas_call(
        functools.partial(second_kernel, cells),
        out_shape=floats(4, n_targets + CHUNK, slots),
        in_specs=[scalars] + [whole] * 4,
        out_specs=whole,
        scratch_shapes=[
            pltpu.VMEM((own_list.shape[0] + cells[2] * LIST_Z, ROWS, LANES), jnp.float32)
        ]
        + loop_scratch
        + count_scratch,
        compiler_params=params(8),
        cost_estimate=cost,
        name="second",
    )(counts, other, listed, spread, first)
    x_lo, x_hi, second = together((x_lo, x_hi, second))
    wide = jnp.concatenate([x_lo, column, x_hi], axis=0)
    y_lo, y_hi = shifted(wide, "gy", 1)
    middle = pl.pallas_call(
        functools.partial(middle_kernel, cells),
        out_shape=floats(4, n_targets + CHUNK, slots),
        in_specs=[scalars] + [whole] * 3,
        out_specs=whole,
        scratch_shapes=list_scratch(cells[0] * cells[2] * LIST_X) + loop_scratch + count_scratch,
        compiler_params=params(8),
        cost_estimate=cost,
        name="middle",
    )(counts, wide, spread, second)
    y_lo, y_hi, middle = together((y_lo, y_hi, middle))
    return pl.pallas_call(
        functools.partial(last_kernel, cells),
        out_shape=floats(3, *cells, slots),
        in_specs=[scalars] + [whole] * 6,
        out_specs=whole,
        scratch_shapes=[pltpu.VMEM((4, n_targets + CHUNK, slots), jnp.float32)]
        + list_scratch(n_bins * LIST_Y)
        + loop_scratch
        + count_scratch,
        compiler_params=params(12),
        cost_estimate=cost,
        name="last",
    )(counts, own, y_lo, y_hi, spread, middle, early)


def solution(mesh):
    in_specs = (
        P(None, "gx", "gy", "ha", None),
        P(None, "gx", "gy", "ha", None),
        P("gx", "gy", "ha"),
    )
    out_specs = P(None, "gx", "gy", "ha", None)
    return jax.shard_map(on_device, mesh=mesh, in_specs=in_specs, out_specs=out_specs, check_vma=False)
```

```python
import functools
import math

import jax
import jax.numpy as jnp
from jax import lax
from jax.experimental import pallas as pl
from jax.experimental.pallas import tpu as pltpu
from jax.sharding import PartitionSpec as P

SPLIT_XI = 2.0
SOFT_SQ = 0.01
GAUSS_COEF = 2.0 * SPLIT_XI / math.sqrt(math.pi)
STOKES_NORM = 1.0 / (8.0 * math.pi)

SOFT_U = SPLIT_XI * SPLIT_XI * SOFT_SQ
LOG2_E = math.log2(math.e)
LOG2_G = math.log2(GAUSS_COEF)
SELF_C = math.erfc(math.sqrt(SOFT_U)) / math.sqrt(SOFT_SQ) + GAUSS_COEF * (
    2.0 * SOFT_U - 3.0
) * math.exp(-SOFT_U)

LANES = 128
ROWS = 8
CHUNK = 32
UNITS = 4
COUNT_ROW = 3
FULL = 640
EARLY = 3
LIST_X, LIST_Z, LIST_Y = 5, 7, 10
FORCE_ROW = 4


def rows_and_lanes(shape=(ROWS, LANES)):
    return lax.broadcasted_iota(jnp.int32, shape, 0), lax.broadcasted_iota(jnp.int32, shape, 1)


def bins_of(cells):
    return [(i, j, k) for i in range(cells[0]) for j in range(cells[1]) for k in range(cells[2])]


def shift_tile(cells, at):
    row, _ = rows_and_lanes()
    moved = jnp.zeros((ROWS, LANES), jnp.float32)
    for i in range(3):
        moved = jnp.where(row == i, SPLIT_XI * (at[i] - 0.5 * (cells[i] - 1)), moved)
    return moved


def compact(listed, base, sources):
    _, lane = rows_and_lanes()
    filled = jnp.int32(0)
    moved = []
    for tile, count in sources:
        at = lax.bitwise_and(filled, LANES - 1)
        tile_id = base + lax.shift_right_logical(filled, 7)
        moved.append((pltpu.roll(tile, at, 1), lane >= at, tile_id, at + count >= LANES))
        filled = filled + count
    current = jnp.zeros((ROWS, LANES), jnp.float32)
    for tile, behind, tile_id, full in moved:
        current = jnp.where(behind, tile, current)
        spill = jnp.where(behind, 0.0, tile)
        listed[tile_id] = current
        listed[tile_id + 1] = spill
        current = jnp.where(full, spill, current)
    return filled


def up_to(count, size):
    return lax.shift_right_logical(count + (size - 1), size.bit_length() - 1)


def parts_of(value, n):
    parts = []
    for _ in range(n):
        part = value.astype(jnp.bfloat16)
        value = value - part.astype(jnp.float32)
        parts.append(part)
    return parts


def spread_targets(spread, first, tile):
    parts = [p.astype(jnp.float32) for p in parts_of(tile, 3)] + [jnp.zeros_like(tile)]
    row, lane = rows_and_lanes((4 * ROWS, 3 * LANES))
    pick = jnp.where(lax.bitwise_and(row, ROWS - 1) == lax.shift_right_logical(lane, 7), 1.0, 0.0)
    wide = lax.dot_general(
        jnp.concatenate(parts, axis=0).astype(jnp.bfloat16),
        pick.astype(jnp.bfloat16),
        (((0,), (0,)), ((), ())),
        preferred_element_type=jnp.float32,
    )
    for i in range(3):
        spread[i, first : first + LANES, :] = wide[:, i * LANES : (i + 1) * LANES]


def coefficients(target, source, force):
    delta = [t - s for t, s in zip(target, source)]
    u = (delta[0] * delta[0] + SOFT_U) + delta[1] * delta[1] + delta[2] * delta[2]
    inv = lax.rsqrt(u)
    tail = (1.0 - lax.erf(u * inv)) * inv
    gauss = jnp.exp2(LOG2_G - u * LOG2_E)
    rest = gauss * (u - 1.5)
    coef_d = ((tail - rest) - gauss) * (inv * inv)
    along = coef_d * (delta[0] * force[0] + delta[1] * force[1] + delta[2] * force[2])
    return tail + rest, along


class Groups:
    def __init__(self, tables):
        self.tables = tables
        self.size = 0
        self.total = jnp.int32(0)

    def add(self, n_chunks, n_tiles, first_tile, spread_row, acc_row):
        for table, value in zip(self.tables, (n_chunks, n_tiles, first_tile, spread_row, acc_row)):
            table[self.size] = jnp.int32(value)
        self.size += 1
        self.total = self.total + n_chunks * n_tiles

    def run(self, listed, spread, coefs, acc):
        chunks_of, tiles_of, list_of, spread_of, acc_of = self.tables
        trash = acc.shape[1] - CHUNK
        coefs[...] = jnp.zeros_like(coefs)

        def rows(tile_id, at):
            return [listed[tile_id, i : i + 1, :] for i in at]

        def advance(group, chunk, tile):
            end_tile = tile + 1 == tiles_of[group]
            next_chunk = jnp.where(end_tile, chunk + CHUNK, chunk)
            end_chunk = next_chunk == chunks_of[group] * CHUNK
            next_group = jnp.where(end_chunk, jnp.minimum(group + 1, self.size - 1), group)
            return next_group, jnp.where(end_chunk, 0, next_chunk), jnp.where(end_tile, 0, tile + 1)

        def some_units(step, state):
            place, olds = state[:3], state[3:]
            news, targets, sources = [], [], []
            for n in range(UNITS):
                group, chunk, tile = place
                valid = step * UNITS + n < self.total
                news += [jnp.where(valid, acc_of[group] + chunk, trash), list_of[group] + tile]
                at = pl.ds(pl.multiple_of(spread_of[group] + chunk, CHUNK), CHUNK)
                targets.append([spread[i, at, :] for i in range(3)])
                sources.append((rows(news[-1], (0, 1, 2)), rows(news[-1], (4, 5, 6))))
                place = advance(*place)
            old_coefs = [(coefs[n, 0], coefs[n, 1]) for n in range(UNITS)]
            old_sources = [(rows(tile, (0, 1, 2)), rows(tile, (4, 5, 6))) for tile in olds[1::2]]

            new_coefs = [coefficients(target, *source) for target, source in zip(targets, sources)]
            terms = []
            for (source, force), (coef_c, along) in zip(old_sources, old_coefs):
                terms.append([coef_c * force[i] - along * source[i] for i in range(3)] + [along])

            for first, unit in zip(olds[::2], terms):
                at = pl.ds(pl.multiple_of(first, CHUNK), CHUNK)
                for i in range(4):
                    acc[i, at, :] = acc[i, at, :] + unit[i]
            for n in range(UNITS):
                coefs[n, 0], coefs[n, 1] = new_coefs[n]
            return place + tuple(news)

        zero = jnp.int32(0)
        start = (zero, zero, zero) + (jnp.int32(trash), list_of[0]) * UNITS
        lax.fori_loop(0, lax.div(self.total + UNITS - 1, UNITS) + 1, some_units, start)


def is_full(cells, count_ref):
    filled = jnp.int32(0)
    for at in bins_of(cells):
        filled = filled + count_ref[at]
    return filled, filled > FULL


def list_own(cells, count_ref, own_ref, listed):
    sources = [(own_ref[at] + shift_tile(cells, at), count_ref[at]) for at in bins_of(cells)]
    compact(listed, 0, sources)


def velocity_rows(cells, group, by_row, tile):
    position = tile + shift_tile(cells, bins_of(cells)[group])
    return (2.0 * STOKES_NORM) * (by_row + position * jnp.broadcast_to(by_row[3:4], (ROWS, LANES)))


def lane_sums(totals):
    _, lane = rows_and_lanes((2 * LANES, LANES))
    merged = jnp.zeros(totals[0].shape, jnp.float32)
    for i, total in enumerate(totals):
        merged = merged + jnp.dot(
            jnp.concatenate(parts_of(total, 2), axis=1),
            jnp.where(lane == i, 1.0, 0.0).astype(jnp.bfloat16),
            preferred_element_type=jnp.float32,
        )
    return merged


def pack_kernel(
    cells, count_ref, offset_v, force_v, own_ref, low_ref, high_ref, early_ref, listed, spread, coefs, acc, *tables
):
    slot = lax.broadcasted_iota(jnp.int32, (1, LANES), 1)
    for at in bins_of(cells):
        ix, iy, iz = at
        count = count_ref[at]
        wide = jnp.full((1, LANES), count, jnp.int32).astype(jnp.float32)
        for i in range(3):
            position = offset_v[i, ix, iy, iz : iz + 1, :]
            own_ref[ix, iy, iz, i : i + 1, :] = position * SPLIT_XI - 0.5 * SPLIT_XI
            force = force_v[i, ix, iy, iz : iz + 1, :]
            own_ref[ix, iy, iz, 4 + i : 5 + i, :] = jnp.where(slot < count, force, 0.0)
        own_ref[ix, iy, iz, 3:4, :] = wide
        own_ref[ix, iy, iz, 7:8, :] = wide
    low_ref[...] = own_ref[:1]
    high_ref[...] = own_ref[cells[0] - 1 :]
    early_ref[...] = jnp.zeros_like(early_ref)
    filled, full = is_full(cells, count_ref)

    @pl.when(full)
    def _():
        list_own(cells, count_ref, own_ref, listed)
        acc[...] = jnp.zeros_like(acc)
        groups = range(EARLY)
        tiles = [own_ref[bins_of(cells)[n]] for n in groups]
        work = Groups(tables)
        for n in groups:
            at = bins_of(cells)[n]
            spread_targets(spread, n * LANES, tiles[n] + shift_tile(cells, at))
            work.add(up_to(count_ref[at], CHUNK), up_to(filled, LANES), 0, n * LANES, n * LANES)
        work.run(listed, spread, coefs, acc)
        merged = lane_sums([acc[i, : EARLY * LANES, :] for i in range(4)])
        for n in groups:
            by_row = jnp.transpose(merged[n * LANES : (n + 1) * LANES])[:ROWS]
            early_ref[n] = velocity_rows(cells, n, by_row, tiles[n])


def counts_of(tiles, count_v, count_s, sem):
    _, lane = rows_and_lanes()
    held = jnp.zeros((ROWS, LANES), jnp.float32)
    for cell, tile in enumerate(tiles):
        held = jnp.where(lane == cell, tile, held)
    count_v[...] = held.astype(jnp.int32)
    copy = pltpu.make_async_copy(count_v, count_s, sem)
    copy.start()
    return copy


def first_kernel(cells, sent_ref, own_ref, spread, acc, listed, coefs, *refs):
    tables, (count_v, count_s, sem) = refs[:5], refs[5:]
    bins = bins_of(cells)
    copy = counts_of([sent_ref[at] for at in bins], count_v, count_s, sem)
    own_ref[...] = sent_ref[...]
    for n, at in enumerate(bins):
        spread_targets(spread, n * LANES, own_ref[at] + shift_tile(cells, at))
    acc[...] = jnp.zeros_like(acc)
    copy.wait()
    count_ref = {at: count_s[COUNT_ROW, n] for n, at in enumerate(bins)}
    list_own(cells, count_ref, own_ref, listed)
    filled, full = is_full(cells, count_ref)
    work = Groups(tables)
    for n in reversed(range(len(bins))):
        n_chunks = up_to(count_ref[bins[n]], CHUNK)
        n_chunks = jnp.where(full, 0, n_chunks) if n < EARLY else n_chunks
        work.add(n_chunks, up_to(filled, LANES), 0, n * LANES, n * LANES)
    work.run(listed, spread, coefs, acc)


def second_kernel(cells, count_ref, x_lo, x_hi, spread, first, acc, listed, coefs, *refs):
    tables, (count_v, count_s, sem) = refs[:5], refs[5:]
    bins = bins_of(cells)
    size_x, size_y, size_z = cells
    layer = [(y, z) for y in range(size_y) for z in range(size_z)]
    copy = counts_of([side[0, y, z] for side in (x_lo, x_hi) for y, z in layer], count_v, count_s, sem)
    acc[...] = first[...]
    copy.wait()
    work = Groups(tables)
    for bx, side in enumerate((x_lo, x_hi)):
        sources = []
        for n, (y, z) in enumerate(layer):
            tile = side[0, y, z] + shift_tile(cells, ((-1, size_x)[bx], y, z))
            sources.append((tile, count_s[COUNT_ROW, bx * len(layer) + n]))
        n_tiles = up_to(compact(listed, bx * LIST_X, sources), LANES)
        for n, at in enumerate(bins):
            if at[0] == bx:
                work.add(up_to(count_ref[at], CHUNK), n_tiles, bx * LIST_X, n * LANES, n * LANES)
    work.run(listed, spread, coefs, acc)


def middle_kernel(cells, count_ref, other, spread, second, acc, listed, coefs, *refs):
    tables, (count_v, count_s, sem) = refs[:5], refs[5:]
    size_x, size_y, size_z = cells
    bins = bins_of(cells)
    places = [(i, j, k) for i in range(size_x + 2) for j in range(size_y) for k in range(size_z)]
    copy = counts_of([other[at] for at in places], count_v, count_s, sem)
    acc[...] = second[...]
    copy.wait()
    work = Groups(tables)
    for bx in range(size_x):
        for bz in range(size_z):
            z = (-1, size_z)[bz]
            sources = []
            for x in (bx - 1, bx, bx + 1):
                for y in range(size_y):
                    place = (x + 1, y, z % size_z)
                    tile = other[place] + shift_tile(cells, (x, y, z))
                    sources.append((tile, count_s[COUNT_ROW, places.index(place)]))
            first_tile = (bx * size_z + bz) * LIST_Z
            n_tiles = up_to(compact(listed, first_tile, sources), LANES)
            for n, at in enumerate(bins):
                if (at[0], at[2]) == (bx, bz):
                    work.add(up_to(count_ref[at], CHUNK), n_tiles, first_tile, n * LANES, n * LANES)
    work.run(listed, spread, coefs, acc)


def last_kernel(cells, count_ref, own_ref, y_lo, y_hi, spread, *refs):
    (middle, early, out_ref, acc, listed, coefs), refs = refs[:6], refs[6:]
    tables, (count_v, count_s, sem) = refs[:5], refs[5:]
    size_x, size_y, size_z = cells
    n_z = 2 * size_z
    bins = bins_of(cells)
    places = [(i, j, k) for i in range(size_x + 2) for j in range(2) for k in range(n_z)]
    tiles = [(y_lo, y_hi)[j][i, 0, k] for i, j, k in places]
    copy = counts_of(tiles, count_v, count_s, sem)
    acc[...] = middle[...]
    copy.wait()
    work = Groups(tables)
    for n, (bx, by, bz) in enumerate(bins):
        sources = []
        for x in (bx - 1, bx, bx + 1):
            for z in (bz - 1, bz, bz + 1):
                cell = places.index((x + 1, by, z % n_z))
                tile = tiles[cell] + shift_tile(cells, (x, (-1, size_y)[by], z))
                sources.append((tile, count_s[COUNT_ROW, cell]))
        n_tiles = up_to(compact(listed, n * LIST_Y, sources), LANES)
        work.add(up_to(count_ref[bx, by, bz], CHUNK), n_tiles, n * LIST_Y, n * LANES, n * LANES)
    work.run(listed, spread, coefs, acc)

    slot = lax.broadcasted_iota(jnp.int32, (1, LANES), 1)
    merged = lane_sums([acc[i, : len(bins) * LANES, :] for i in range(4)])
    for n, at in enumerate(bins):
        by_row = jnp.transpose(merged[n * LANES : (n + 1) * LANES])[:ROWS]
        tile = own_ref[at]
        total = velocity_rows(cells, n, by_row, tile)
        total = total - (STOKES_NORM * SELF_C) * pltpu.roll(tile, ROWS - FORCE_ROW, 0)
        if n < EARLY:
            total = total + early[n]
        total = jnp.where(slot < count_ref[at], total, 0.0)
        for i in range(3):
            out_ref[i, at[0], at[1], at[2] : at[2] + 1, :] = total[i : i + 1]


def shifted(first, last, axis):
    size = lax.axis_size(axis)
    up = [(i, (i + 1) % size) for i in range(size)]
    down = [(j, i) for i, j in up]
    after = lax.ppermute(first, axis, down)
    before = lax.ppermute(last, axis, up)
    return before, after


def on_device(offsets, forces, counts):
    cells = offsets.shape[1:4]
    slots = offsets.shape[4]
    n_bins = cells[0] * cells[1] * cells[2]
    n_targets = n_bins * slots
    whole = pl.BlockSpec(memory_space=pltpu.VMEM)
    scalars = pl.BlockSpec(memory_space=pltpu.SMEM)

    def floats(*shape):
        return jax.ShapeDtypeStruct(shape, jnp.float32)

    def params(mib):
        return pltpu.CompilerParams(vmem_limit_bytes=mib << 20)

    loop_scratch = [pltpu.VMEM((UNITS, 2, CHUNK, LANES), jnp.float32)]
    loop_scratch += [pltpu.SMEM((2 * n_bins,), jnp.int32)] * 5
    count_scratch = [
        pltpu.VMEM((ROWS, LANES), jnp.int32),
        pltpu.SMEM((ROWS, LANES), jnp.int32),
        pltpu.SemaphoreType.DMA,
    ]
    cost = pl.CostEstimate(flops=1 << 28, bytes_accessed=1 << 16, transcendentals=1 << 20)

    def list_scratch(n_tiles):
        return [pltpu.VMEM((n_tiles, ROWS, LANES), jnp.float32)]

    sent, low, high, early = pl.pallas_call(
        functools.partial(pack_kernel, cells),
        out_shape=[
            floats(*cells, ROWS, slots),
            floats(1, *cells[1:], ROWS, slots),
            floats(1, *cells[1:], ROWS, slots),
            floats(EARLY, ROWS, slots),
        ],
        in_specs=[scalars, whole, whole],
        out_specs=[whole] * 4,
        scratch_shapes=list_scratch(n_bins + 1)
        + [
            pltpu.VMEM((3, EARLY * slots, slots), jnp.float32),
            loop_scratch[0],
            pltpu.VMEM((4, EARLY * slots + CHUNK, slots), jnp.float32),
        ]
        + loop_scratch[1:],
        name="pack",
    )(counts, offsets, forces)

    together = lax.optimization_barrier
    sums = floats(4, n_targets + CHUNK, slots)

    def add_pairs(kernel, list_tiles, name, *args):
        return pl.pallas_call(
            functools.partial(kernel, cells),
            out_shape=sums,
            in_specs=[scalars] + [whole] * len(args),
            out_specs=whole,
            scratch_shapes=list_scratch(list_tiles) + loop_scratch + count_scratch,
            compiler_params=params(8),
            cost_estimate=cost,
            name=name,
        )(counts, *args)

    x_lo, x_hi = shifted(low, high, "gx")
    own, spread, first = pl.pallas_call(
        functools.partial(first_kernel, cells),
        out_shape=[sent, floats(3, n_targets, slots), sums],
        in_specs=[whole],
        out_specs=[whole] * 3,
        scratch_shapes=list_scratch(n_bins + 1) + loop_scratch + count_scratch,
        compiler_params=params(8),
        cost_estimate=cost,
        name="first",
    )(sent)
    x_hi, x_lo, own, first = together((x_hi, x_lo, own, first))
    slab = jnp.concatenate([x_lo, own, x_hi], axis=0)
    size = lax.axis_size("ha")
    other = lax.ppermute(slab, "ha", [(i, (i + 1) % size) for i in range(size)])
    second = add_pairs(second_kernel, cells[0] * LIST_X, "second", x_lo, x_hi, spread, first)
    other, slab, second = together((other, slab, second))
    wide = jnp.concatenate([slab, other], axis=2)
    y_lo, y_hi = shifted(wide[:, :1], wide[:, cells[1] - 1 :], "gy")
    middle = add_pairs(middle_kernel, cells[0] * cells[2] * LIST_Z, "middle", other, spread, second)
    y_lo, y_hi, middle = together((y_lo, y_hi, middle))
    return pl.pallas_call(
        functools.partial(last_kernel, cells),
        out_shape=floats(3, *cells, slots),
        in_specs=[scalars] + [whole] * 6,
        out_specs=whole,
        scratch_shapes=[pltpu.VMEM((4, n_targets + CHUNK, slots), jnp.float32)]
        + list_scratch(n_bins * LIST_Y)
        + loop_scratch
        + count_scratch,
        compiler_params=params(12),
        cost_estimate=cost,
        name="last",
    )(counts, own, y_lo, y_hi, spread, middle, early)


def solution(mesh):
    in_specs = (
        P(None, "gx", "gy", "ha", None),
        P(None, "gx", "gy", "ha", None),
        P("gx", "gy", "ha"),
    )
    out_specs = P(None, "gx", "gy", "ha", None)
    return jax.shard_map(on_device, mesh=mesh, in_specs=in_specs, out_specs=out_specs, check_vma=False)
```

```python
import functools
import math

import jax
import jax.numpy as jnp
from jax import lax
from jax.experimental import pallas as pl
from jax.experimental.pallas import tpu as pltpu
from jax.sharding import PartitionSpec as P

SPLIT_XI = 2.0
SOFT_SQ = 0.01
GAUSS_COEF = 2.0 * SPLIT_XI / math.sqrt(math.pi)
STOKES_NORM = 1.0 / (8.0 * math.pi)

SOFT_U = SPLIT_XI * SPLIT_XI * SOFT_SQ
LOG2_E = math.log2(math.e)
LOG2_G = math.log2(GAUSS_COEF)
SELF_C = math.erfc(math.sqrt(SOFT_U)) / math.sqrt(SOFT_SQ) + GAUSS_COEF * (
    2.0 * SOFT_U - 3.0
) * math.exp(-SOFT_U)

LANES = 128
ROWS = 8
CHUNK = 32
UNITS = 8
COUNT_ROW = 3
FULL = 640
EARLY = 3
FIRST = (3, 4)
SECOND = (5, 6, 7, 3, 4, 0, 1, 2)
LIST_Z, LIST_X, LIST_Y = 5, 7, 10
FORCE_ROW = 4


def rows_and_lanes(shape=(ROWS, LANES)):
    return lax.broadcasted_iota(jnp.int32, shape, 0), lax.broadcasted_iota(jnp.int32, shape, 1)


def bins_of(cells):
    return [(i, j, k) for i in range(cells[0]) for j in range(cells[1]) for k in range(cells[2])]


def shift_tile(cells, at):
    row, _ = rows_and_lanes()
    moved = jnp.zeros((ROWS, LANES), jnp.float32)
    for i in range(3):
        moved = jnp.where(row == i, SPLIT_XI * (at[i] - 0.5 * (cells[i] - 1)), moved)
    return moved


def compact(listed, base, sources):
    _, lane = rows_and_lanes()
    filled = jnp.int32(0)
    moved = []
    for tile, count in sources:
        at = lax.bitwise_and(filled, LANES - 1)
        tile_id = base + lax.shift_right_logical(filled, 7)
        moved.append((pltpu.roll(tile, at, 1), lane >= at, tile_id, at + count >= LANES))
        filled = filled + count
    current = jnp.zeros((ROWS, LANES), jnp.float32)
    for tile, behind, tile_id, full in moved:
        current = jnp.where(behind, tile, current)
        spill = jnp.where(behind, 0.0, tile)
        listed[tile_id] = current
        listed[tile_id + 1] = spill
        current = jnp.where(full, spill, current)
    return filled


def up_to(count, size):
    return lax.shift_right_logical(count + (size - 1), size.bit_length() - 1)


def parts_of(value, n):
    parts = []
    for _ in range(n):
        part = value.astype(jnp.bfloat16)
        value = value - part.astype(jnp.float32)
        parts.append(part)
    return parts


def spread_targets(spread, first, tile):
    parts = [p.astype(jnp.float32) for p in parts_of(tile, 3)] + [jnp.zeros_like(tile)]
    row, lane = rows_and_lanes((4 * ROWS, 3 * LANES))
    pick = jnp.where(lax.bitwise_and(row, ROWS - 1) == lax.shift_right_logical(lane, 7), 1.0, 0.0)
    wide = lax.dot_general(
        jnp.concatenate(parts, axis=0).astype(jnp.bfloat16),
        pick.astype(jnp.bfloat16),
        (((0,), (0,)), ((), ())),
        preferred_element_type=jnp.float32,
    )
    for i in range(3):
        spread[i, first : first + LANES, :] = wide[:, i * LANES : (i + 1) * LANES]


def coefficients(target, source, force):
    delta = [t - s for t, s in zip(target, source)]
    u = (delta[0] * delta[0] + SOFT_U) + delta[1] * delta[1] + delta[2] * delta[2]
    inv = lax.rsqrt(u)
    tail = (1.0 - lax.erf(u * inv)) * inv
    gauss = jnp.exp2(LOG2_G - u * LOG2_E)
    rest = gauss * (u - 1.5)
    coef_d = ((tail - rest) - gauss) * (inv * inv)
    along = coef_d * (delta[0] * force[0] + delta[1] * force[1] + delta[2] * force[2])
    return tail + rest, along


class Groups:
    def __init__(self, tables):
        self.tables = tables
        self.size = 0
        self.total = jnp.int32(0)

    def add(self, n_chunks, n_tiles, first_tile, spread_row, acc_row):
        for table, value in zip(self.tables, (n_chunks, n_tiles, first_tile, spread_row, acc_row)):
            table[self.size] = jnp.int32(value)
        self.size += 1
        self.total = self.total + n_chunks * n_tiles

    def run(self, listed, spread, coefs, acc):
        chunks_of, tiles_of, list_of, spread_of, acc_of = self.tables
        trash = acc.shape[1] - CHUNK
        coefs[...] = jnp.zeros_like(coefs)

        def rows(tile_id, at):
            return [listed[tile_id, i : i + 1, :] for i in at]

        def advance(group, chunk, tile):
            end_tile = tile + 1 == tiles_of[group]
            next_chunk = jnp.where(end_tile, chunk + CHUNK, chunk)
            end_chunk = next_chunk == chunks_of[group] * CHUNK
            next_group = jnp.where(end_chunk, jnp.minimum(group + 1, self.size - 1), group)
            return next_group, jnp.where(end_chunk, 0, next_chunk), jnp.where(end_tile, 0, tile + 1)

        def some_units(step, state):
            place, olds = state[:3], state[3:]
            news, targets, sources = [], [], []
            for n in range(UNITS):
                group, chunk, tile = place
                valid = step * UNITS + n < self.total
                news += [jnp.where(valid, acc_of[group] + chunk, trash), list_of[group] + tile]
                at = pl.ds(pl.multiple_of(spread_of[group] + chunk, CHUNK), CHUNK)
                targets.append([spread[i, at, :] for i in range(3)])
                sources.append((rows(news[-1], (0, 1, 2)), rows(news[-1], (4, 5, 6))))
                place = advance(*place)
            old_coefs = [(coefs[n, 0], coefs[n, 1]) for n in range(UNITS)]
            old_sources = [(rows(tile, (0, 1, 2)), rows(tile, (4, 5, 6))) for tile in olds[1::2]]

            new_coefs = [coefficients(target, *source) for target, source in zip(targets, sources)]
            terms = []
            for (source, force), (coef_c, along) in zip(old_sources, old_coefs):
                terms.append([coef_c * force[i] - along * source[i] for i in range(3)] + [along])

            for first, unit in zip(olds[::2], terms):
                at = pl.ds(pl.multiple_of(first, CHUNK), CHUNK)
                for i in range(4):
                    acc[i, at, :] = acc[i, at, :] + unit[i]
            for n in range(UNITS):
                coefs[n, 0], coefs[n, 1] = new_coefs[n]
            return place + tuple(news)

        zero = jnp.int32(0)
        start = (zero, zero, zero) + (jnp.int32(trash), list_of[0]) * UNITS
        lax.fori_loop(0, lax.div(self.total + UNITS - 1, UNITS) + 1, some_units, start)


def is_full(cells, count_ref):
    filled = jnp.int32(0)
    for at in bins_of(cells):
        filled = filled + count_ref[at]
    return filled, filled > FULL


def list_own(cells, count_ref, own_ref, listed):
    sources = [(own_ref[at] + shift_tile(cells, at), count_ref[at]) for at in bins_of(cells)]
    compact(listed, 0, sources)


def velocity_rows(cells, group, by_row, tile):
    position = tile + shift_tile(cells, bins_of(cells)[group])
    return (2.0 * STOKES_NORM) * (by_row + position * jnp.broadcast_to(by_row[3:4], (ROWS, LANES)))


def lane_sums(totals):
    _, lane = rows_and_lanes((2 * LANES, LANES))
    merged = jnp.zeros(totals[0].shape, jnp.float32)
    for i, total in enumerate(totals):
        merged = merged + jnp.dot(
            jnp.concatenate(parts_of(total, 2), axis=1),
            jnp.where(lane == i, 1.0, 0.0).astype(jnp.bfloat16),
            preferred_element_type=jnp.float32,
        )
    return merged


def pack_kernel(cells, count_ref, offset_v, force_v, own_ref, early_ref, listed, spread, coefs, acc, *tables):
    slot = lax.broadcasted_iota(jnp.int32, (1, LANES), 1)
    for at in bins_of(cells):
        ix, iy, iz = at
        count = count_ref[at]
        wide = jnp.full((1, LANES), count, jnp.int32).astype(jnp.float32)
        for i in range(3):
            position = offset_v[i, ix, iy, iz : iz + 1, :]
            own_ref[ix, iy, iz, i : i + 1, :] = position * SPLIT_XI - 0.5 * SPLIT_XI
            force = force_v[i, ix, iy, iz : iz + 1, :]
            own_ref[ix, iy, iz, 4 + i : 5 + i, :] = jnp.where(slot < count, force, 0.0)
        own_ref[ix, iy, iz, 3:4, :] = wide
        own_ref[ix, iy, iz, 7:8, :] = wide
    early_ref[...] = jnp.zeros_like(early_ref)
    filled, full = is_full(cells, count_ref)

    @pl.when(full)
    def _():
        list_own(cells, count_ref, own_ref, listed)
        acc[...] = jnp.zeros_like(acc)
        groups = range(EARLY)
        tiles = [own_ref[bins_of(cells)[n]] for n in groups]
        work = Groups(tables)
        for n in groups:
            at = bins_of(cells)[n]
            spread_targets(spread, n * LANES, tiles[n] + shift_tile(cells, at))
            work.add(up_to(count_ref[at], CHUNK), up_to(filled, LANES), 0, n * LANES, n * LANES)
        work.run(listed, spread, coefs, acc)
        merged = lane_sums([acc[i, : EARLY * LANES, :] for i in range(4)])
        for n in groups:
            by_row = jnp.transpose(merged[n * LANES : (n + 1) * LANES])[:ROWS]
            early_ref[n] = velocity_rows(cells, n, by_row, tiles[n])


def counts_of(tiles, count_v, count_s, sem):
    _, lane = rows_and_lanes()
    held = jnp.zeros((ROWS, LANES), jnp.float32)
    for cell, tile in enumerate(tiles):
        held = jnp.where(lane == cell, tile, held)
    count_v[...] = held.astype(jnp.int32)
    copy = pltpu.make_async_copy(count_v, count_s, sem)
    copy.start()
    return copy


def first_kernel(cells, sent_ref, own_ref, listed, spread, acc, coefs, *refs):
    tables, (count_v, count_s, sem) = refs[:5], refs[5:]
    bins = bins_of(cells)
    copy = counts_of([sent_ref[at] for at in bins], count_v, count_s, sem)
    own_ref[...] = sent_ref[...]
    for n, at in enumerate(bins):
        spread_targets(spread, n * LANES, own_ref[at] + shift_tile(cells, at))
    acc[...] = jnp.zeros_like(acc)
    copy.wait()
    count_ref = {at: count_s[COUNT_ROW, n] for n, at in enumerate(bins)}
    list_own(cells, count_ref, own_ref, listed)
    filled, full = is_full(cells, count_ref)
    work = Groups(tables)
    for m, n in enumerate(FIRST):
        n_chunks = jnp.where(full, up_to(count_ref[bins[n]], CHUNK), 0)
        work.add(n_chunks, up_to(filled, LANES), 0, n * LANES, m * LANES)
    work.run(listed, spread, coefs, acc)


def second_kernel(cells, count_ref, other, own_list, spread, first, acc, listed, coefs, *refs):
    tables, (count_v, count_s, sem) = refs[:5], refs[5:]
    bins = bins_of(cells)
    size_x, size_y, size_z = cells
    copy = counts_of([other[at] for at in bins], count_v, count_s, sem)
    for n in range(len(bins)):
        here = slice(n * LANES, (n + 1) * LANES)
        if n in FIRST:
            m = FIRST.index(n)
            acc[:, here, :] = first[:, m * LANES : (m + 1) * LANES, :]
        else:
            acc[:, here, :] = jnp.zeros((4, LANES, LANES), jnp.float32)
    n_own = own_list.shape[0]
    for n in range(n_own):
        listed[n] = own_list[n]
    filled, full = is_full(cells, count_ref)
    copy.wait()
    work = Groups(tables)
    for bz in range(size_z):
        z = (-1, size_z)[bz]
        sources = []
        for x in range(size_x):
            for y in range(size_y):
                place = (x, y, z % size_z)
                tile = other[place] + shift_tile(cells, (x, y, z))
                sources.append((tile, count_s[COUNT_ROW, bins.index(place)]))
        first_tile = n_own + bz * LIST_Z
        n_tiles = up_to(compact(listed, first_tile, sources), LANES)
        for n, at in enumerate(bins):
            if at[2] == bz:
                work.add(up_to(count_ref[at], CHUNK), n_tiles, first_tile, n * LANES, n * LANES)
    for n in SECOND:
        n_chunks = up_to(count_ref[bins[n]], CHUNK)
        n_chunks = jnp.where(full, 0, n_chunks) if n < EARLY or n in FIRST else n_chunks
        work.add(n_chunks, up_to(filled, LANES), 0, n * LANES, n * LANES)
    work.run(listed, spread, coefs, acc)


def middle_kernel(cells, count_ref, wide, spread, second, acc, listed, coefs, *refs):
    tables, (count_v, count_s, sem) = refs[:5], refs[5:]
    size_x, size_y, size_z = cells
    n_z = 2 * size_z
    bins = bins_of(cells)
    places = [(i, j, k) for i in (0, size_x + 1) for j in range(size_y) for k in range(n_z)]
    copy = counts_of([wide[at] for at in places], count_v, count_s, sem)
    acc[...] = second[...]
    copy.wait()
    work = Groups(tables)
    for bx in range(size_x):
        for bz in range(size_z):
            x = (-1, size_x)[bx]
            sources = []
            for y in range(size_y):
                for z in (bz - 1, bz, bz + 1):
                    place = (x + 1, y, z % n_z)
                    tile = wide[place] + shift_tile(cells, (x, y, z))
                    sources.append((tile, count_s[COUNT_ROW, places.index(place)]))
            first_tile = (bx * size_z + bz) * LIST_X
            n_tiles = up_to(compact(listed, first_tile, sources), LANES)
            for n, at in enumerate(bins):
                if (at[0], at[2]) == (bx, bz):
                    work.add(up_to(count_ref[at], CHUNK), n_tiles, first_tile, n * LANES, n * LANES)
    work.run(listed, spread, coefs, acc)


def last_kernel(cells, count_ref, own_ref, y_lo, y_hi, spread, *refs):
    (middle, early, out_ref, acc, listed, coefs), refs = refs[:6], refs[6:]
    tables, (count_v, count_s, sem) = refs[:5], refs[5:]
    size_x, size_y, size_z = cells
    n_z = 2 * size_z
    bins = bins_of(cells)
    places = [(i, j, k) for i in range(size_x + 2) for j in range(2) for k in range(n_z)]
    tiles = [(y_lo, y_hi)[j][i, 0, k] for i, j, k in places]
    copy = counts_of(tiles, count_v, count_s, sem)
    acc[...] = middle[...]
    copy.wait()
    work = Groups(tables)
    for n, (bx, by, bz) in enumerate(bins):
        sources = []
        for x in (bx - 1, bx, bx + 1):
            for z in (bz - 1, bz, bz + 1):
                cell = places.index((x + 1, by, z % n_z))
                tile = tiles[cell] + shift_tile(cells, (x, (-1, size_y)[by], z))
                sources.append((tile, count_s[COUNT_ROW, cell]))
        n_tiles = up_to(compact(listed, n * LIST_Y, sources), LANES)
        work.add(up_to(count_ref[bx, by, bz], CHUNK), n_tiles, n * LIST_Y, n * LANES, n * LANES)
    work.run(listed, spread, coefs, acc)

    slot = lax.broadcasted_iota(jnp.int32, (1, LANES), 1)
    merged = lane_sums([acc[i, : len(bins) * LANES, :] for i in range(4)])
    for n, at in enumerate(bins):
        by_row = jnp.transpose(merged[n * LANES : (n + 1) * LANES])[:ROWS]
        tile = own_ref[at]
        total = velocity_rows(cells, n, by_row, tile)
        total = total - (STOKES_NORM * SELF_C) * pltpu.roll(tile, ROWS - FORCE_ROW, 0)
        if n < EARLY:
            total = total + early[n]
        total = jnp.where(slot < count_ref[at], total, 0.0)
        for i in range(3):
            out_ref[i, at[0], at[1], at[2] : at[2] + 1, :] = total[i : i + 1]


def shifted(array, axis, dim):
    size, length = lax.axis_size(axis), array.shape[dim]
    up = [(i, (i + 1) % size) for i in range(size)]
    down = [(j, i) for i, j in up]
    after = lax.ppermute(lax.slice_in_dim(array, 0, 1, axis=dim), axis, down)
    before = lax.ppermute(lax.slice_in_dim(array, length - 1, length, axis=dim), axis, up)
    return before, after


def on_device(offsets, forces, counts):
    cells = offsets.shape[1:4]
    slots = offsets.shape[4]
    n_bins = cells[0] * cells[1] * cells[2]
    n_targets = n_bins * slots
    whole = pl.BlockSpec(memory_space=pltpu.VMEM)
    scalars = pl.BlockSpec(memory_space=pltpu.SMEM)

    def floats(*shape):
        return jax.ShapeDtypeStruct(shape, jnp.float32)

    def params(mib):
        return pltpu.CompilerParams(vmem_limit_bytes=mib << 20)

    loop_scratch = [pltpu.VMEM((UNITS, 2, CHUNK, LANES), jnp.float32)]
    loop_scratch += [pltpu.SMEM((2 * n_bins,), jnp.int32)] * 5
    count_scratch = [
        pltpu.VMEM((ROWS, LANES), jnp.int32),
        pltpu.SMEM((ROWS, LANES), jnp.int32),
        pltpu.SemaphoreType.DMA,
    ]
    cost = pl.CostEstimate(flops=1 << 28, bytes_accessed=1 << 16, transcendentals=1 << 20)

    def list_scratch(n_tiles):
        return [pltpu.VMEM((n_tiles, ROWS, LANES), jnp.float32)]

    own_list, all_targets = floats(n_bins + 1, ROWS, slots), floats(3, n_targets, slots)
    sent, early = pl.pallas_call(
        functools.partial(pack_kernel, cells),
        out_shape=[floats(*cells, ROWS, slots), floats(EARLY, ROWS, slots)],
        in_specs=[scalars, whole, whole],
        out_specs=[whole, whole],
        scratch_shapes=[
            pltpu.VMEM(own_list.shape, jnp.float32),
            pltpu.VMEM((3, EARLY * slots, slots), jnp.float32),
            loop_scratch[0],
            pltpu.VMEM((4, EARLY * slots + CHUNK, slots), jnp.float32),
        ]
        + loop_scratch[1:],
        name="pack",
    )(counts, offsets, forces)

    together = lax.optimization_barrier
    size = lax.axis_size("ha")
    other = lax.ppermute(sent, "ha", [(i, (i + 1) % size) for i in range(size)])
    own, listed, spread, first = pl.pallas_call(
        functools.partial(first_kernel, cells),
        out_shape=[sent, own_list, all_targets, floats(4, len(FIRST) * slots + CHUNK, slots)],
        in_specs=[whole],
        out_specs=[whole] * 4,
        scratch_shapes=loop_scratch + count_scratch,
        compiler_params=params(8),
        cost_estimate=cost,
        name="first",
    )(sent)
    other, own, listed, first = together((other, own, listed, first))
    column = jnp.concatenate([own, other], axis=2)
    x_lo, x_hi = shifted(column, "gx", 0)
    second = pl.pallas_call(
        functools.partial(second_kernel, cells),
        out_shape=floats(4, n_targets + CHUNK, slots),
        in_specs=[scalars] + [whole] * 4,
        out_specs=whole,
        scratch_shapes=[
            pltpu.VMEM((own_list.shape[0] + cells[2] * LIST_Z, ROWS, LANES), jnp.float32)
        ]
        + loop_scratch
        + count_scratch,
        compiler_params=params(8),
        cost_estimate=cost,
        name="second",
    )(counts, other, listed, spread, first)
    x_lo, x_hi, second = together((x_lo, x_hi, second))
    wide = jnp.concatenate([x_lo, column, x_hi], axis=0)
    y_lo, y_hi = shifted(wide, "gy", 1)
    middle = pl.pallas_call(
        functools.partial(middle_kernel, cells),
        out_shape=floats(4, n_targets + CHUNK, slots),
        in_specs=[scalars] + [whole] * 3,
        out_specs=whole,
        scratch_shapes=list_scratch(cells[0] * cells[2] * LIST_X) + loop_scratch + count_scratch,
        compiler_params=params(8),
        cost_estimate=cost,
        name="middle",
    )(counts, wide, spread, second)
    y_lo, y_hi, middle = together((y_lo, y_hi, middle))
    return pl.pallas_call(
        functools.partial(last_kernel, cells),
        out_shape=floats(3, *cells, slots),
        in_specs=[scalars] + [whole] * 6,
        out_specs=whole,
        scratch_shapes=[pltpu.VMEM((4, n_targets + CHUNK, slots), jnp.float32)]
        + list_scratch(n_bins * LIST_Y)
        + loop_scratch
        + count_scratch,
        compiler_params=params(12),
        cost_estimate=cost,
        name="last",
    )(counts, own, y_lo, y_hi, spread, middle, early)


def solution(mesh):
    in_specs = (
        P(None, "gx", "gy", "ha", None),
        P(None, "gx", "gy", "ha", None),
        P("gx", "gy", "ha"),
    )
    out_specs = P(None, "gx", "gy", "ha", None)
    return jax.shard_map(on_device, mesh=mesh, in_specs=in_specs, out_specs=out_specs, check_vma=False)
```

```python
import functools
import math

import jax
import jax.numpy as jnp
from jax import lax
from jax.experimental import pallas as pl
from jax.experimental.pallas import tpu as pltpu
from jax.sharding import PartitionSpec as P

SPLIT_XI = 2.0
SOFT_SQ = 0.01
GAUSS_COEF = 2.0 * SPLIT_XI / math.sqrt(math.pi)
STOKES_NORM = 1.0 / (8.0 * math.pi)

SOFT_U = SPLIT_XI * SPLIT_XI * SOFT_SQ
LOG2_E = math.log2(math.e)
LOG2_G = math.log2(GAUSS_COEF)
SELF_C = math.erfc(math.sqrt(SOFT_U)) / math.sqrt(SOFT_SQ) + GAUSS_COEF * (
    2.0 * SOFT_U - 3.0
) * math.exp(-SOFT_U)

LANES = 128
ROWS = 8
CHUNK = 32
UNITS = 8
COUNT_ROW = 3
FULL = 640
MANY = 440
EARLY = 3
FIRST = (3, 4)
SECOND = (5, 6, 7, 0, 1, 2, 3, 4)
LIST_Z, LIST_X, LIST_Y = 5, 7, 10
FORCE_ROW = 4


def rows_and_lanes(shape=(ROWS, LANES)):
    return lax.broadcasted_iota(jnp.int32, shape, 0), lax.broadcasted_iota(jnp.int32, shape, 1)


def bins_of(cells):
    return [(i, j, k) for i in range(cells[0]) for j in range(cells[1]) for k in range(cells[2])]


def shift_tile(cells, at):
    row, _ = rows_and_lanes()
    moved = jnp.zeros((ROWS, LANES), jnp.float32)
    for i in range(3):
        moved = jnp.where(row == i, SPLIT_XI * (at[i] - 0.5 * (cells[i] - 1)), moved)
    return moved


def compact(listed, base, sources):
    _, lane = rows_and_lanes()
    filled = jnp.int32(0)
    moved = []
    for tile, count in sources:
        at = lax.bitwise_and(filled, LANES - 1)
        tile_id = base + lax.shift_right_logical(filled, 7)
        moved.append((pltpu.roll(tile, at, 1), lane >= at, tile_id, at + count >= LANES))
        filled = filled + count
    current = jnp.zeros((ROWS, LANES), jnp.float32)
    for tile, behind, tile_id, full in moved:
        current = jnp.where(behind, tile, current)
        spill = jnp.where(behind, 0.0, tile)
        listed[tile_id] = current
        listed[tile_id + 1] = spill
        current = jnp.where(full, spill, current)
    return filled


def up_to(count, size):
    return lax.shift_right_logical(count + (size - 1), size.bit_length() - 1)


def parts_of(value, n):
    parts = []
    for _ in range(n):
        part = value.astype(jnp.bfloat16)
        value = value - part.astype(jnp.float32)
        parts.append(part)
    return parts


def spread_targets(spread, first, tile):
    parts = [p.astype(jnp.float32) for p in parts_of(tile, 3)] + [jnp.zeros_like(tile)]
    row, lane = rows_and_lanes((4 * ROWS, 3 * LANES))
    pick = jnp.where(lax.bitwise_and(row, ROWS - 1) == lax.shift_right_logical(lane, 7), 1.0, 0.0)
    wide = lax.dot_general(
        jnp.concatenate(parts, axis=0).astype(jnp.bfloat16),
        pick.astype(jnp.bfloat16),
        (((0,), (0,)), ((), ())),
        preferred_element_type=jnp.float32,
    )
    for i in range(3):
        spread[i, first : first + LANES, :] = wide[:, i * LANES : (i + 1) * LANES]


def coefficients(target, source, force):
    delta = [t - s for t, s in zip(target, source)]
    u = (delta[0] * delta[0] + SOFT_U) + delta[1] * delta[1] + delta[2] * delta[2]
    inv = lax.rsqrt(u)
    tail = (1.0 - lax.erf(u * inv)) * inv
    gauss = jnp.exp2(LOG2_G - u * LOG2_E)
    rest = gauss * (u - 1.5)
    coef_d = ((tail - rest) - gauss) * (inv * inv)
    along = coef_d * (delta[0] * force[0] + delta[1] * force[1] + delta[2] * force[2])
    return tail + rest, along


class Groups:
    def __init__(self, tables):
        self.tables = tables
        self.size = 0
        self.total = jnp.int32(0)

    def add(self, n_chunks, n_tiles, first_tile, spread_row, acc_row):
        for table, value in zip(self.tables, (n_chunks, n_tiles, first_tile, spread_row, acc_row)):
            table[self.size] = jnp.int32(value)
        self.size += 1
        self.total = self.total + n_chunks * n_tiles

    def run(self, listed, spread, coefs, acc):
        chunks_of, tiles_of, list_of, spread_of, acc_of = self.tables
        trash = acc.shape[1] - CHUNK
        coefs[...] = jnp.zeros_like(coefs)

        def rows(tile_id, at):
            return [listed[tile_id, i : i + 1, :] for i in at]

        def advance(group, chunk, tile):
            end_tile = tile + 1 == tiles_of[group]
            next_chunk = jnp.where(end_tile, chunk + CHUNK, chunk)
            end_chunk = next_chunk == chunks_of[group] * CHUNK
            next_group = jnp.where(end_chunk, jnp.minimum(group + 1, self.size - 1), group)
            return next_group, jnp.where(end_chunk, 0, next_chunk), jnp.where(end_tile, 0, tile + 1)

        def some_units(step, state):
            place, olds = state[:3], state[3:]
            news, targets, sources = [], [], []
            for n in range(UNITS):
                group, chunk, tile = place
                valid = step * UNITS + n < self.total
                news += [jnp.where(valid, acc_of[group] + chunk, trash), list_of[group] + tile]
                at = pl.ds(pl.multiple_of(spread_of[group] + chunk, CHUNK), CHUNK)
                targets.append([spread[i, at, :] for i in range(3)])
                sources.append((rows(news[-1], (0, 1, 2)), rows(news[-1], (4, 5, 6))))
                place = advance(*place)
            old_coefs = [(coefs[n, 0], coefs[n, 1]) for n in range(UNITS)]
            old_sources = [(rows(tile, (0, 1, 2)), rows(tile, (4, 5, 6))) for tile in olds[1::2]]

            new_coefs = [coefficients(target, *source) for target, source in zip(targets, sources)]
            terms = []
            for (source, force), (coef_c, along) in zip(old_sources, old_coefs):
                terms.append([coef_c * force[i] - along * source[i] for i in range(3)] + [along])

            for first, unit in zip(olds[::2], terms):
                at = pl.ds(pl.multiple_of(first, CHUNK), CHUNK)
                for i in range(4):
                    acc[i, at, :] = acc[i, at, :] + unit[i]
            for n in range(UNITS):
                coefs[n, 0], coefs[n, 1] = new_coefs[n]
            return place + tuple(news)

        zero = jnp.int32(0)
        start = (zero, zero, zero) + (jnp.int32(trash), list_of[0]) * UNITS
        lax.fori_loop(0, lax.div(self.total + UNITS - 1, UNITS) + 1, some_units, start)


def is_full(cells, count_ref):
    filled = jnp.int32(0)
    for at in bins_of(cells):
        filled = filled + count_ref[at]
    return filled, filled > FULL, filled > MANY


def list_own(cells, count_ref, own_ref, listed):
    sources = [(own_ref[at] + shift_tile(cells, at), count_ref[at]) for at in bins_of(cells)]
    compact(listed, 0, sources)


def velocity_rows(cells, group, by_row, tile):
    position = tile + shift_tile(cells, bins_of(cells)[group])
    return (2.0 * STOKES_NORM) * (by_row + position * jnp.broadcast_to(by_row[3:4], (ROWS, LANES)))


def lane_sums(totals):
    _, lane = rows_and_lanes((2 * LANES, LANES))
    merged = jnp.zeros(totals[0].shape, jnp.float32)
    for i, total in enumerate(totals):
        merged = merged + jnp.dot(
            jnp.concatenate(parts_of(total, 2), axis=1),
            jnp.where(lane == i, 1.0, 0.0).astype(jnp.bfloat16),
            preferred_element_type=jnp.float32,
        )
    return merged


def pack_kernel(cells, count_hbm, offset_hbm, force_hbm, own_ref, early_ref, *refs):
    (count_ref, offset_v, force_v, sems, listed, spread, coefs, acc), tables = refs[:8], refs[8:]
    copies = [
        pltpu.make_async_copy(source, target, sems.at[n])
        for n, (source, target) in enumerate(
            ((count_hbm, count_ref), (offset_hbm, offset_v), (force_hbm, force_v))
        )
    ]
    for copy in copies:
        copy.start()
    for copy in copies:
        copy.wait()
    slot = lax.broadcasted_iota(jnp.int32, (1, LANES), 1)
    for at in bins_of(cells):
        ix, iy, iz = at
        count = count_ref[at]
        wide = jnp.full((1, LANES), count, jnp.int32).astype(jnp.float32)
        for i in range(3):
            position = offset_v[i, ix, iy, iz : iz + 1, :]
            own_ref[ix, iy, iz, i : i + 1, :] = position * SPLIT_XI - 0.5 * SPLIT_XI
            force = force_v[i, ix, iy, iz : iz + 1, :]
            own_ref[ix, iy, iz, 4 + i : 5 + i, :] = jnp.where(slot < count, force, 0.0)
        own_ref[ix, iy, iz, 3:4, :] = wide
        own_ref[ix, iy, iz, 7:8, :] = wide
    early_ref[...] = jnp.zeros_like(early_ref)
    filled, full, _ = is_full(cells, count_ref)

    @pl.when(full)
    def _():
        list_own(cells, count_ref, own_ref, listed)
        acc[...] = jnp.zeros_like(acc)
        groups = range(EARLY)
        tiles = [own_ref[bins_of(cells)[n]] for n in groups]
        work = Groups(tables)
        for n in groups:
            at = bins_of(cells)[n]
            spread_targets(spread, n * LANES, tiles[n] + shift_tile(cells, at))
            work.add(up_to(count_ref[at], CHUNK), up_to(filled, LANES), 0, n * LANES, n * LANES)
        work.run(listed, spread, coefs, acc)
        merged = lane_sums([acc[i, : EARLY * LANES, :] for i in range(4)])
        for n in groups:
            by_row = jnp.transpose(merged[n * LANES : (n + 1) * LANES])[:ROWS]
            early_ref[n] = velocity_rows(cells, n, by_row, tiles[n])


def counts_of(tiles, count_v, count_s, sem):
    _, lane = rows_and_lanes()
    held = jnp.zeros((ROWS, LANES), jnp.float32)
    for cell, tile in enumerate(tiles):
        held = jnp.where(lane == cell, tile, held)
    count_v[...] = held.astype(jnp.int32)
    copy = pltpu.make_async_copy(count_v, count_s, sem)
    copy.start()
    return copy


def first_kernel(cells, sent_ref, own_ref, listed, spread, acc, coefs, *refs):
    tables, (count_v, count_s, sem) = refs[:5], refs[5:]
    bins = bins_of(cells)
    copy = counts_of([sent_ref[at] for at in bins], count_v, count_s, sem)
    own_ref[...] = sent_ref[...]
    for n, at in enumerate(bins):
        spread_targets(spread, n * LANES, own_ref[at] + shift_tile(cells, at))
    acc[...] = jnp.zeros_like(acc)
    copy.wait()
    count_ref = {at: count_s[COUNT_ROW, n] for n, at in enumerate(bins)}
    list_own(cells, count_ref, own_ref, listed)
    filled, _, many = is_full(cells, count_ref)
    work = Groups(tables)
    for m, n in enumerate(FIRST):
        n_chunks = jnp.where(many, up_to(count_ref[bins[n]], CHUNK), 0)
        work.add(n_chunks, up_to(filled, LANES), 0, n * LANES, m * LANES)
    work.run(listed, spread, coefs, acc)


def second_kernel(cells, count_ref, other, own_list, spread, first, acc, listed, coefs, *refs):
    tables, (count_v, count_s, sem) = refs[:5], refs[5:]
    bins = bins_of(cells)
    size_x, size_y, size_z = cells
    copy = counts_of([other[at] for at in bins], count_v, count_s, sem)
    for n in range(len(bins)):
        here = slice(n * LANES, (n + 1) * LANES)
        if n in FIRST:
            m = FIRST.index(n)
            acc[:, here, :] = first[:, m * LANES : (m + 1) * LANES, :]
        else:
            acc[:, here, :] = jnp.zeros((4, LANES, LANES), jnp.float32)
    n_own = own_list.shape[0]
    for n in range(n_own):
        listed[n] = own_list[n]
    filled, full, many = is_full(cells, count_ref)
    copy.wait()
    work = Groups(tables)
    for bz in range(size_z):
        z = (-1, size_z)[bz]
        sources = []
        for x in range(size_x):
            for y in range(size_y):
                place = (x, y, z % size_z)
                tile = other[place] + shift_tile(cells, (x, y, z))
                sources.append((tile, count_s[COUNT_ROW, bins.index(place)]))
        first_tile = n_own + bz * LIST_Z
        n_tiles = up_to(compact(listed, first_tile, sources), LANES)
        for n, at in enumerate(bins):
            if at[2] == bz:
                work.add(up_to(count_ref[at], CHUNK), n_tiles, first_tile, n * LANES, n * LANES)
    for n in SECOND:
        n_chunks = up_to(count_ref[bins[n]], CHUNK)
        if n < EARLY or n in FIRST:
            n_chunks = jnp.where(full if n < EARLY else many, 0, n_chunks)
        work.add(n_chunks, up_to(filled, LANES), 0, n * LANES, n * LANES)
    work.run(listed, spread, coefs, acc)


def middle_kernel(cells, count_ref, wide, spread, second, acc, listed, coefs, *refs):
    tables, (count_v, count_s, sem) = refs[:5], refs[5:]
    size_x, size_y, size_z = cells
    n_z = 2 * size_z
    bins = bins_of(cells)
    places = [(i, j, k) for i in (0, size_x + 1) for j in range(size_y) for k in range(n_z)]
    copy = counts_of([wide[at] for at in places], count_v, count_s, sem)
    acc[...] = second[...]
    copy.wait()
    work = Groups(tables)
    for bx in range(size_x):
        for bz in range(size_z):
            x = (-1, size_x)[bx]
            sources = []
            for y in range(size_y):
                for z in (bz - 1, bz, bz + 1):
                    place = (x + 1, y, z % n_z)
                    tile = wide[place] + shift_tile(cells, (x, y, z))
                    sources.append((tile, count_s[COUNT_ROW, places.index(place)]))
            first_tile = (bx * size_z + bz) * LIST_X
            n_tiles = up_to(compact(listed, first_tile, sources), LANES)
            for n, at in enumerate(bins):
                if (at[0], at[2]) == (bx, bz):
                    work.add(up_to(count_ref[at], CHUNK), n_tiles, first_tile, n * LANES, n * LANES)
    work.run(listed, spread, coefs, acc)


def last_kernel(cells, count_ref, own_ref, y_lo, y_hi, spread, *refs):
    (middle, early, out_ref, acc, listed, coefs), refs = refs[:6], refs[6:]
    tables, (count_v, count_s, sem) = refs[:5], refs[5:]
    size_x, size_y, size_z = cells
    n_z = 2 * size_z
    bins = bins_of(cells)
    places = [(i, j, k) for i in range(size_x + 2) for j in range(2) for k in range(n_z)]
    tiles = [(y_lo, y_hi)[j][i, 0, k] for i, j, k in places]
    copy = counts_of(tiles, count_v, count_s, sem)
    acc[...] = middle[...]
    copy.wait()
    work = Groups(tables)
    for n, (bx, by, bz) in enumerate(bins):
        sources = []
        for x in (bx - 1, bx, bx + 1):
            for z in (bz - 1, bz, bz + 1):
                cell = places.index((x + 1, by, z % n_z))
                tile = tiles[cell] + shift_tile(cells, (x, (-1, size_y)[by], z))
                sources.append((tile, count_s[COUNT_ROW, cell]))
        n_tiles = up_to(compact(listed, n * LIST_Y, sources), LANES)
        work.add(up_to(count_ref[bx, by, bz], CHUNK), n_tiles, n * LIST_Y, n * LANES, n * LANES)
    work.run(listed, spread, coefs, acc)

    slot = lax.broadcasted_iota(jnp.int32, (1, LANES), 1)
    merged = lane_sums([acc[i, : len(bins) * LANES, :] for i in range(4)])
    for n, at in enumerate(bins):
        by_row = jnp.transpose(merged[n * LANES : (n + 1) * LANES])[:ROWS]
        tile = own_ref[at]
        total = velocity_rows(cells, n, by_row, tile)
        total = total - (STOKES_NORM * SELF_C) * pltpu.roll(tile, ROWS - FORCE_ROW, 0)
        if n < EARLY:
            total = total + early[n]
        total = jnp.where(slot < count_ref[at], total, 0.0)
        for i in range(3):
            out_ref[i, at[0], at[1], at[2] : at[2] + 1, :] = total[i : i + 1]


def shifted(array, axis, dim):
    size, length = lax.axis_size(axis), array.shape[dim]
    up = [(i, (i + 1) % size) for i in range(size)]
    down = [(j, i) for i, j in up]
    after = lax.ppermute(lax.slice_in_dim(array, 0, 1, axis=dim), axis, down)
    before = lax.ppermute(lax.slice_in_dim(array, length - 1, length, axis=dim), axis, up)
    return before, after


def on_device(offsets, forces, counts):
    cells = offsets.shape[1:4]
    slots = offsets.shape[4]
    n_bins = cells[0] * cells[1] * cells[2]
    n_targets = n_bins * slots
    whole = pl.BlockSpec(memory_space=pltpu.VMEM)
    scalars = pl.BlockSpec(memory_space=pltpu.SMEM)

    def floats(*shape):
        return jax.ShapeDtypeStruct(shape, jnp.float32)

    def params(mib):
        return pltpu.CompilerParams(vmem_limit_bytes=mib << 20)

    loop_scratch = [pltpu.VMEM((UNITS, 2, CHUNK, LANES), jnp.float32)]
    loop_scratch += [pltpu.SMEM((2 * n_bins,), jnp.int32)] * 5
    count_scratch = [
        pltpu.VMEM((ROWS, LANES), jnp.int32),
        pltpu.SMEM((ROWS, LANES), jnp.int32),
        pltpu.SemaphoreType.DMA,
    ]
    cost = pl.CostEstimate(flops=1 << 28, bytes_accessed=1 << 16, transcendentals=1 << 20)

    def list_scratch(n_tiles):
        return [pltpu.VMEM((n_tiles, ROWS, LANES), jnp.float32)]

    own_list, all_targets = floats(n_bins + 1, ROWS, slots), floats(3, n_targets, slots)
    arguments = [pltpu.with_memory_space_constraint(x, pltpu.HBM) for x in (counts, offsets, forces)]
    sent, early = pl.pallas_call(
        functools.partial(pack_kernel, cells),
        out_shape=[floats(*cells, ROWS, slots), floats(EARLY, ROWS, slots)],
        in_specs=[pl.BlockSpec(memory_space=pltpu.HBM)] * 3,
        out_specs=[whole, whole],
        scratch_shapes=[
            pltpu.SMEM(counts.shape, jnp.int32),
            pltpu.VMEM(offsets.shape, jnp.float32),
            pltpu.VMEM(forces.shape, jnp.float32),
            pltpu.SemaphoreType.DMA((3,)),
            pltpu.VMEM(own_list.shape, jnp.float32),
            pltpu.VMEM((3, EARLY * slots, slots), jnp.float32),
            loop_scratch[0],
            pltpu.VMEM((4, EARLY * slots + CHUNK, slots), jnp.float32),
        ]
        + loop_scratch[1:],
        compiler_params=params(8),
        name="pack",
    )(*arguments)

    together = lax.optimization_barrier
    size = lax.axis_size("ha")
    other = lax.ppermute(sent, "ha", [(i, (i + 1) % size) for i in range(size)])
    own, listed, spread, first = pl.pallas_call(
        functools.partial(first_kernel, cells),
        out_shape=[sent, own_list, all_targets, floats(4, len(FIRST) * slots + CHUNK, slots)],
        in_specs=[whole],
        out_specs=[whole] * 4,
        scratch_shapes=loop_scratch + count_scratch,
        compiler_params=params(8),
        cost_estimate=cost,
        name="first",
    )(sent)
    other, own, listed, first = together((other, own, listed, first))
    column = jnp.concatenate([own, other], axis=2)
    x_lo, x_hi = shifted(column, "gx", 0)
    second = pl.pallas_call(
        functools.partial(second_kernel, cells),
        out_shape=floats(4, n_targets + CHUNK, slots),
        in_specs=[scalars] + [whole] * 4,
        out_specs=whole,
        scratch_shapes=[
            pltpu.VMEM((own_list.shape[0] + cells[2] * LIST_Z, ROWS, LANES), jnp.float32)
        ]
        + loop_scratch
        + count_scratch,
        compiler_params=params(8),
        cost_estimate=cost,
        name="second",
    )(counts, other, listed, spread, first)
    x_lo, x_hi, second = together((x_lo, x_hi, second))
    wide = jnp.concatenate([x_lo, column, x_hi], axis=0)
    y_lo, y_hi = shifted(wide, "gy", 1)
    middle = pl.pallas_call(
        functools.partial(middle_kernel, cells),
        out_shape=floats(4, n_targets + CHUNK, slots),
        in_specs=[scalars] + [whole] * 3,
        out_specs=whole,
        scratch_shapes=list_scratch(cells[0] * cells[2] * LIST_X) + loop_scratch + count_scratch,
        compiler_params=params(8),
        cost_estimate=cost,
        name="middle",
    )(counts, wide, spread, second)
    y_lo, y_hi, middle = together((y_lo, y_hi, middle))
    return pl.pallas_call(
        functools.partial(last_kernel, cells),
        out_shape=floats(3, *cells, slots),
        in_specs=[scalars] + [whole] * 6,
        out_specs=whole,
        scratch_shapes=[pltpu.VMEM((4, n_targets + CHUNK, slots), jnp.float32)]
        + list_scratch(n_bins * LIST_Y)
        + loop_scratch
        + count_scratch,
        compiler_params=params(12),
        cost_estimate=cost,
        name="last",
    )(counts, own, y_lo, y_hi, spread, middle, early)


def solution(mesh):
    in_specs = (
        P(None, "gx", "gy", "ha", None),
        P(None, "gx", "gy", "ha", None),
        P("gx", "gy", "ha"),
    )
    out_specs = P(None, "gx", "gy", "ha", None)
    return jax.shard_map(on_device, mesh=mesh, in_specs=in_specs, out_specs=out_specs, check_vma=False)
```

```python
import functools
import math

import jax
import jax.numpy as jnp
from jax import lax
from jax.experimental import pallas as pl
from jax.experimental.pallas import tpu as pltpu
from jax.sharding import PartitionSpec as P

SPLIT_XI = 2.0
SOFT_SQ = 0.01
GAUSS_COEF = 2.0 * SPLIT_XI / math.sqrt(math.pi)
STOKES_NORM = 1.0 / (8.0 * math.pi)

SOFT_U = SPLIT_XI * SPLIT_XI * SOFT_SQ
LOG2_E = math.log2(math.e)
LOG2_G = math.log2(GAUSS_COEF)
SELF_C = math.erfc(math.sqrt(SOFT_U)) / math.sqrt(SOFT_SQ) + GAUSS_COEF * (
    2.0 * SOFT_U - 3.0
) * math.exp(-SOFT_U)

LANES = 128
ROWS = 8
CHUNK = 32
UNITS = 8
COUNT_ROW = 3
FULL = 640
MANY = 440
EARLY = 3
FIRST = (3, 4)
SECOND = (5, 6, 7, 0, 1, 2, 3, 4)
LIST_Z, LIST_X, LIST_Y = 5, 7, 10
FORCE_ROW = 4


def rows_and_lanes(shape=(ROWS, LANES)):
    return lax.broadcasted_iota(jnp.int32, shape, 0), lax.broadcasted_iota(jnp.int32, shape, 1)


def bins_of(cells):
    return [(i, j, k) for i in range(cells[0]) for j in range(cells[1]) for k in range(cells[2])]


def shift_tile(cells, at):
    row, _ = rows_and_lanes()
    moved = jnp.zeros((ROWS, LANES), jnp.float32)
    for i in range(3):
        moved = jnp.where(row == i, SPLIT_XI * (at[i] - 0.5 * (cells[i] - 1)), moved)
    return moved


def compact(listed, base, sources):
    _, lane = rows_and_lanes()
    filled = jnp.int32(0)
    moved = []
    for tile, count in sources:
        at = lax.bitwise_and(filled, LANES - 1)
        tile_id = base + lax.shift_right_logical(filled, 7)
        moved.append((pltpu.roll(tile, at, 1), lane >= at, tile_id, at + count >= LANES))
        filled = filled + count
    current = jnp.zeros((ROWS, LANES), jnp.float32)
    for tile, behind, tile_id, full in moved:
        current = jnp.where(behind, tile, current)
        spill = jnp.where(behind, 0.0, tile)
        listed[tile_id] = current
        listed[tile_id + 1] = spill
        current = jnp.where(full, spill, current)
    return filled


def spread_rows(lists, to, listed, base, n_tiles, most):
    def some(tiles):
        for n in tiles:
            for i, row in enumerate((0, 1, 2, 4, 5, 6)):
                lists[to + n, i] = jnp.broadcast_to(listed[base + n, row : row + 1, :], (ROWS, LANES))

    likely = min(5, most)
    some(range(likely))

    @pl.when(n_tiles > likely)
    def _():
        some(range(likely, most))


def up_to(count, size):
    return lax.shift_right_logical(count + (size - 1), size.bit_length() - 1)


def parts_of(value, n):
    parts = []
    for _ in range(n):
        part = value.astype(jnp.bfloat16)
        value = value - part.astype(jnp.float32)
        parts.append(part)
    return parts


def spread_targets(spread, first, tile):
    parts = [p.astype(jnp.float32) for p in parts_of(tile, 3)] + [jnp.zeros_like(tile)]
    row, lane = rows_and_lanes((4 * ROWS, 3 * LANES))
    pick = jnp.where(lax.bitwise_and(row, ROWS - 1) == lax.shift_right_logical(lane, 7), 1.0, 0.0)
    wide = lax.dot_general(
        jnp.concatenate(parts, axis=0).astype(jnp.bfloat16),
        pick.astype(jnp.bfloat16),
        (((0,), (0,)), ((), ())),
        preferred_element_type=jnp.float32,
    )
    for i in range(3):
        spread[i, first : first + LANES, :] = wide[:, i * LANES : (i + 1) * LANES]


def coefficients(target, source, force):
    delta = [t - s for t, s in zip(target, source)]
    u = (delta[0] * delta[0] + SOFT_U) + delta[1] * delta[1] + delta[2] * delta[2]
    inv = lax.rsqrt(u)
    tail = (1.0 - lax.erf(u * inv)) * inv
    gauss = jnp.exp2(LOG2_G - u * LOG2_E)
    rest = gauss * (u - 1.5)
    coef_d = ((tail - rest) - gauss) * (inv * inv)
    along = coef_d * (delta[0] * force[0] + delta[1] * force[1] + delta[2] * force[2])
    return tail + rest, along


class Groups:
    def __init__(self, tables):
        self.tables = tables
        self.size = 0
        self.total = jnp.int32(0)

    def add(self, n_chunks, n_tiles, first_tile, spread_row, acc_row):
        for table, value in zip(self.tables, (n_chunks, n_tiles, first_tile, spread_row, acc_row)):
            table[self.size] = jnp.int32(value)
        self.size += 1
        self.total = self.total + n_chunks * n_tiles

    def run(self, lists, spread, coefs, acc):
        chunks_of, tiles_of, list_of, spread_of, acc_of = self.tables
        trash = acc.shape[1] - CHUNK

        def rows(tile_id):
            wide = [jnp.concatenate([lists[tile_id, i]] * (CHUNK // ROWS), axis=0) for i in range(6)]
            return wide[:3], wide[3:]

        def advance(group, chunk, tile):
            end_tile = tile + 1 == tiles_of[group]
            next_chunk = jnp.where(end_tile, chunk + CHUNK, chunk)
            end_chunk = next_chunk == chunks_of[group] * CHUNK
            next_group = jnp.where(end_chunk, jnp.minimum(group + 1, self.size - 1), group)
            return next_group, jnp.where(end_chunk, 0, next_chunk), jnp.where(end_tile, 0, tile + 1)

        def find(step, place):
            units, found = [], []
            for n in range(UNITS):
                group, chunk, tile = place
                valid = step * UNITS + n < self.total
                units += [jnp.where(valid, acc_of[group] + chunk, trash), list_of[group] + tile]
                at = pl.ds(pl.multiple_of(spread_of[group] + chunk, CHUNK), CHUNK)
                target = [spread[i, at, :] for i in range(3)]
                found.append(coefficients(target, *rows(units[-1])))
                place = advance(*place)
            return found, tuple(units), place

        def use(units):
            terms = []
            for n, tile in enumerate(units[1::2]):
                coef_c, along = coefs[n, 0], coefs[n, 1]
                source, force = rows(tile)
                terms.append([coef_c * force[i] - along * source[i] for i in range(3)] + [along])
            return terms

        def keep(found):
            for n, pair in enumerate(found):
                coefs[n, 0], coefs[n, 1] = pair

        def add(units, terms):
            for first, unit in zip(units[::2], terms):
                at = pl.ds(pl.multiple_of(first, CHUNK), CHUNK)
                for i in range(4):
                    acc[i, at, :] = acc[i, at, :] + unit[i]

        def body(step, state):
            place, olds = state[:3], state[3:]
            terms = use(olds)
            found, news, place = find(step, place)
            add(olds, terms)
            keep(found)
            return place + news

        zero = jnp.int32(0)
        found, units, place = find(0, (zero, zero, zero))
        keep(found)
        state = lax.fori_loop(1, lax.div(self.total + UNITS - 1, UNITS), body, place + units)
        add(state[3:], use(state[3:]))


def is_full(cells, count_ref):
    filled = jnp.int32(0)
    for at in bins_of(cells):
        filled = filled + count_ref[at]
    return filled, filled > FULL, filled > MANY


def list_own(cells, count_ref, own_ref, listed):
    sources = [(own_ref[at] + shift_tile(cells, at), count_ref[at]) for at in bins_of(cells)]
    compact(listed, 0, sources)


def velocity_rows(cells, group, by_row, tile):
    position = tile + shift_tile(cells, bins_of(cells)[group])
    return (2.0 * STOKES_NORM) * (by_row + position * jnp.broadcast_to(by_row[3:4], (ROWS, LANES)))


def lane_sums(totals):
    _, lane = rows_and_lanes((2 * LANES, LANES))
    merged = jnp.zeros(totals[0].shape, jnp.float32)
    for i, total in enumerate(totals):
        merged = merged + jnp.dot(
            jnp.concatenate(parts_of(total, 2), axis=1),
            jnp.where(lane == i, 1.0, 0.0).astype(jnp.bfloat16),
            preferred_element_type=jnp.float32,
        )
    return merged


def pack_kernel(cells, count_hbm, offset_hbm, force_hbm, own_ref, early_ref, *refs):
    (count_ref, offset_v, force_v, sems, listed, lists, spread, coefs, acc), tables = refs[:9], refs[9:]
    copies = [
        pltpu.make_async_copy(source, target, sems.at[n])
        for n, (source, target) in enumerate(
            ((count_hbm, count_ref), (offset_hbm, offset_v), (force_hbm, force_v))
        )
    ]
    for copy in copies:
        copy.start()
    for copy in copies:
        copy.wait()
    slot = lax.broadcasted_iota(jnp.int32, (1, LANES), 1)
    for at in bins_of(cells):
        ix, iy, iz = at
        count = count_ref[at]
        wide = jnp.full((1, LANES), count, jnp.int32).astype(jnp.float32)
        for i in range(3):
            position = offset_v[i, ix, iy, iz : iz + 1, :]
            own_ref[ix, iy, iz, i : i + 1, :] = position * SPLIT_XI - 0.5 * SPLIT_XI
            force = force_v[i, ix, iy, iz : iz + 1, :]
            own_ref[ix, iy, iz, 4 + i : 5 + i, :] = jnp.where(slot < count, force, 0.0)
        own_ref[ix, iy, iz, 3:4, :] = wide
        own_ref[ix, iy, iz, 7:8, :] = wide
    early_ref[...] = jnp.zeros_like(early_ref)
    filled, full, _ = is_full(cells, count_ref)

    @pl.when(full)
    def _():
        list_own(cells, count_ref, own_ref, listed)
        spread_rows(lists, 0, listed, 0, up_to(filled, LANES), len(bins_of(cells)))
        acc[...] = jnp.zeros_like(acc)
        groups = range(EARLY)
        tiles = [own_ref[bins_of(cells)[n]] for n in groups]
        work = Groups(tables)
        for n in groups:
            at = bins_of(cells)[n]
            spread_targets(spread, n * LANES, tiles[n] + shift_tile(cells, at))
            work.add(up_to(count_ref[at], CHUNK), up_to(filled, LANES), 0, n * LANES, n * LANES)
        work.run(lists, spread, coefs, acc)
        merged = lane_sums([acc[i, : EARLY * LANES, :] for i in range(4)])
        for n in groups:
            by_row = jnp.transpose(merged[n * LANES : (n + 1) * LANES])[:ROWS]
            early_ref[n] = velocity_rows(cells, n, by_row, tiles[n])


def counts_of(tiles, count_v, count_s, sem):
    _, lane = rows_and_lanes()
    held = jnp.zeros((ROWS, LANES), jnp.float32)
    for cell, tile in enumerate(tiles):
        held = jnp.where(lane == cell, tile, held)
    count_v[...] = held.astype(jnp.int32)
    copy = pltpu.make_async_copy(count_v, count_s, sem)
    copy.start()
    return copy


def first_kernel(cells, sent_ref, own_ref, lists, spread, acc, listed, coefs, *refs):
    tables, (count_v, count_s, sem) = refs[:5], refs[5:]
    bins = bins_of(cells)
    copy = counts_of([sent_ref[at] for at in bins], count_v, count_s, sem)
    own_ref[...] = sent_ref[...]
    for n, at in enumerate(bins):
        spread_targets(spread, n * LANES, own_ref[at] + shift_tile(cells, at))
    acc[...] = jnp.zeros_like(acc)
    copy.wait()
    count_ref = {at: count_s[COUNT_ROW, n] for n, at in enumerate(bins)}
    list_own(cells, count_ref, own_ref, listed)
    filled, _, many = is_full(cells, count_ref)
    spread_rows(lists, 0, listed, 0, up_to(filled, LANES), len(bins))
    work = Groups(tables)
    for m, n in enumerate(FIRST):
        n_chunks = jnp.where(many, up_to(count_ref[bins[n]], CHUNK), 0)
        work.add(n_chunks, up_to(filled, LANES), 0, n * LANES, m * LANES)
    work.run(lists, spread, coefs, acc)


def second_kernel(cells, count_ref, other, own_lists, spread, first, acc, listed, lists, coefs, *refs):
    tables, (count_v, count_s, sem) = refs[:5], refs[5:]
    bins = bins_of(cells)
    size_x, size_y, size_z = cells
    copy = counts_of([other[at] for at in bins], count_v, count_s, sem)
    for n in range(len(bins)):
        here = slice(n * LANES, (n + 1) * LANES)
        if n in FIRST:
            m = FIRST.index(n)
            acc[:, here, :] = first[:, m * LANES : (m + 1) * LANES, :]
        else:
            acc[:, here, :] = jnp.zeros((4, LANES, LANES), jnp.float32)
    n_own = own_lists.shape[0]
    for n in range(n_own):
        lists[n] = own_lists[n]
    filled, full, many = is_full(cells, count_ref)
    copy.wait()
    work = Groups(tables)
    for bz in range(size_z):
        z = (-1, size_z)[bz]
        sources = []
        for x in range(size_x):
            for y in range(size_y):
                place = (x, y, z % size_z)
                tile = other[place] + shift_tile(cells, (x, y, z))
                sources.append((tile, count_s[COUNT_ROW, bins.index(place)]))
        n_tiles = up_to(compact(listed, bz * LIST_Z, sources), LANES)
        first_tile = n_own + bz * (LIST_Z - 1)
        spread_rows(lists, first_tile, listed, bz * LIST_Z, n_tiles, LIST_Z - 1)
        for n, at in enumerate(bins):
            if at[2] == bz:
                work.add(up_to(count_ref[at], CHUNK), n_tiles, first_tile, n * LANES, n * LANES)
    for n in SECOND:
        n_chunks = up_to(count_ref[bins[n]], CHUNK)
        if n < EARLY or n in FIRST:
            n_chunks = jnp.where(full if n < EARLY else many, 0, n_chunks)
        work.add(n_chunks, up_to(filled, LANES), 0, n * LANES, n * LANES)
    work.run(lists, spread, coefs, acc)


def middle_kernel(cells, count_ref, wide, spread, second, acc, listed, lists, coefs, *refs):
    tables, (count_v, count_s, sem) = refs[:5], refs[5:]
    size_x, size_y, size_z = cells
    n_z = 2 * size_z
    bins = bins_of(cells)
    places = [(i, j, k) for i in (0, size_x + 1) for j in range(size_y) for k in range(n_z)]
    copy = counts_of([wide[at] for at in places], count_v, count_s, sem)
    acc[...] = second[...]
    copy.wait()
    work = Groups(tables)
    for bx in range(size_x):
        for bz in range(size_z):
            x = (-1, size_x)[bx]
            sources = []
            for y in range(size_y):
                for z in (bz - 1, bz, bz + 1):
                    place = (x + 1, y, z % n_z)
                    tile = wide[place] + shift_tile(cells, (x, y, z))
                    sources.append((tile, count_s[COUNT_ROW, places.index(place)]))
            n_list = bx * size_z + bz
            n_tiles = up_to(compact(listed, n_list * LIST_X, sources), LANES)
            first_tile = n_list * (LIST_X - 1)
            spread_rows(lists, first_tile, listed, n_list * LIST_X, n_tiles, LIST_X - 1)
            for n, at in enumerate(bins):
                if (at[0], at[2]) == (bx, bz):
                    work.add(up_to(count_ref[at], CHUNK), n_tiles, first_tile, n * LANES, n * LANES)
    work.run(lists, spread, coefs, acc)


def last_kernel(cells, count_ref, own_ref, y_lo, y_hi, spread, *refs):
    (middle, early, out_ref, acc, listed, lists, coefs), refs = refs[:7], refs[7:]
    tables, (count_v, count_s, sem) = refs[:5], refs[5:]
    size_x, size_y, size_z = cells
    n_z = 2 * size_z
    bins = bins_of(cells)
    places = [(i, j, k) for i in range(size_x + 2) for j in range(2) for k in range(n_z)]
    tiles = [(y_lo, y_hi)[j][i, 0, k] for i, j, k in places]
    copy = counts_of(tiles, count_v, count_s, sem)
    acc[...] = middle[...]
    copy.wait()
    work = Groups(tables)
    for n, (bx, by, bz) in enumerate(bins):
        sources = []
        for x in (bx - 1, bx, bx + 1):
            for z in (bz - 1, bz, bz + 1):
                cell = places.index((x + 1, by, z % n_z))
                tile = tiles[cell] + shift_tile(cells, (x, (-1, size_y)[by], z))
                sources.append((tile, count_s[COUNT_ROW, cell]))
        n_tiles = up_to(compact(listed, n * LIST_Y, sources), LANES)
        first_tile = n * (LIST_Y - 1)
        spread_rows(lists, first_tile, listed, n * LIST_Y, n_tiles, LIST_Y - 1)
        work.add(up_to(count_ref[bx, by, bz], CHUNK), n_tiles, first_tile, n * LANES, n * LANES)
    work.run(lists, spread, coefs, acc)

    slot = lax.broadcasted_iota(jnp.int32, (1, LANES), 1)
    merged = lane_sums([acc[i, : len(bins) * LANES, :] for i in range(4)])
    for n, at in enumerate(bins):
        by_row = jnp.transpose(merged[n * LANES : (n + 1) * LANES])[:ROWS]
        tile = own_ref[at]
        total = velocity_rows(cells, n, by_row, tile)
        total = total - (STOKES_NORM * SELF_C) * pltpu.roll(tile, ROWS - FORCE_ROW, 0)
        if n < EARLY:
            total = total + early[n]
        total = jnp.where(slot < count_ref[at], total, 0.0)
        for i in range(3):
            out_ref[i, at[0], at[1], at[2] : at[2] + 1, :] = total[i : i + 1]


def shifted(array, axis, dim):
    size, length = lax.axis_size(axis), array.shape[dim]
    up = [(i, (i + 1) % size) for i in range(size)]
    down = [(j, i) for i, j in up]
    after = lax.ppermute(lax.slice_in_dim(array, 0, 1, axis=dim), axis, down)
    before = lax.ppermute(lax.slice_in_dim(array, length - 1, length, axis=dim), axis, up)
    return before, after


def on_device(offsets, forces, counts):
    cells = offsets.shape[1:4]
    slots = offsets.shape[4]
    n_bins = cells[0] * cells[1] * cells[2]
    n_targets = n_bins * slots
    whole = pl.BlockSpec(memory_space=pltpu.VMEM)
    scalars = pl.BlockSpec(memory_space=pltpu.SMEM)

    def floats(*shape):
        return jax.ShapeDtypeStruct(shape, jnp.float32)

    def params(mib):
        return pltpu.CompilerParams(vmem_limit_bytes=mib << 20)

    loop_scratch = [pltpu.VMEM((UNITS, 2, CHUNK, LANES), jnp.float32)]
    loop_scratch += [pltpu.SMEM((2 * n_bins,), jnp.int32)] * 5
    count_scratch = [
        pltpu.VMEM((ROWS, LANES), jnp.int32),
        pltpu.SMEM((ROWS, LANES), jnp.int32),
        pltpu.SemaphoreType.DMA,
    ]
    cost = pl.CostEstimate(flops=1 << 28, bytes_accessed=1 << 16, transcendentals=1 << 20)

    def list_scratch(n_lists, n_tiles, more=0):
        return [
            pltpu.VMEM((n_lists * n_tiles, ROWS, LANES), jnp.float32),
            pltpu.VMEM((n_lists * (n_tiles - 1) + more, 6, ROWS, LANES), jnp.float32),
        ]

    own_lists, all_targets = floats(n_bins, 6, ROWS, slots), floats(3, n_targets, slots)
    arguments = [pltpu.with_memory_space_constraint(x, pltpu.HBM) for x in (counts, offsets, forces)]
    sent, early = pl.pallas_call(
        functools.partial(pack_kernel, cells),
        out_shape=[floats(*cells, ROWS, slots), floats(EARLY, ROWS, slots)],
        in_specs=[pl.BlockSpec(memory_space=pltpu.HBM)] * 3,
        out_specs=[whole, whole],
        scratch_shapes=[
            pltpu.SMEM(counts.shape, jnp.int32),
            pltpu.VMEM(offsets.shape, jnp.float32),
            pltpu.VMEM(forces.shape, jnp.float32),
            pltpu.SemaphoreType.DMA((3,)),
            pltpu.VMEM((n_bins + 1, ROWS, LANES), jnp.float32),
            pltpu.VMEM(own_lists.shape, jnp.float32),
            pltpu.VMEM((3, EARLY * slots, slots), jnp.float32),
            loop_scratch[0],
            pltpu.VMEM((4, EARLY * slots + CHUNK, slots), jnp.float32),
        ]
        + loop_scratch[1:],
        compiler_params=params(8),
        name="pack",
    )(*arguments)

    together = lax.optimization_barrier
    size = lax.axis_size("ha")
    other = lax.ppermute(sent, "ha", [(i, (i + 1) % size) for i in range(size)])
    own, listed, spread, first = pl.pallas_call(
        functools.partial(first_kernel, cells),
        out_shape=[sent, own_lists, all_targets, floats(4, len(FIRST) * slots + CHUNK, slots)],
        in_specs=[whole],
        out_specs=[whole] * 4,
        scratch_shapes=[pltpu.VMEM((n_bins + 1, ROWS, LANES), jnp.float32)]
        + loop_scratch
        + count_scratch,
        compiler_params=params(8),
        cost_estimate=cost,
        name="first",
    )(sent)
    other, own, listed, first = together((other, own, listed, first))
    column = jnp.concatenate([own, other], axis=2)
    x_lo, x_hi = shifted(column, "gx", 0)
    second = pl.pallas_call(
        functools.partial(second_kernel, cells),
        out_shape=floats(4, n_targets + CHUNK, slots),
        in_specs=[scalars] + [whole] * 4,
        out_specs=whole,
        scratch_shapes=list_scratch(cells[2], LIST_Z, n_bins)
        + loop_scratch
        + count_scratch,
        compiler_params=params(8),
        cost_estimate=cost,
        name="second",
    )(counts, other, listed, spread, first)
    x_lo, x_hi, second = together((x_lo, x_hi, second))
    wide = jnp.concatenate([x_lo, column, x_hi], axis=0)
    y_lo, y_hi = shifted(wide, "gy", 1)
    middle = pl.pallas_call(
        functools.partial(middle_kernel, cells),
        out_shape=floats(4, n_targets + CHUNK, slots),
        in_specs=[scalars] + [whole] * 3,
        out_specs=whole,
        scratch_shapes=list_scratch(cells[0] * cells[2], LIST_X) + loop_scratch + count_scratch,
        compiler_params=params(8),
        cost_estimate=cost,
        name="middle",
    )(counts, wide, spread, second)
    y_lo, y_hi, middle = together((y_lo, y_hi, middle))
    return pl.pallas_call(
        functools.partial(last_kernel, cells),
        out_shape=floats(3, *cells, slots),
        in_specs=[scalars] + [whole] * 6,
        out_specs=whole,
        scratch_shapes=[pltpu.VMEM((4, n_targets + CHUNK, slots), jnp.float32)]
        + list_scratch(n_bins, LIST_Y)
        + loop_scratch
        + count_scratch,
        compiler_params=params(12),
        cost_estimate=cost,
        name="last",
    )(counts, own, y_lo, y_hi, spread, middle, early)


def solution(mesh):
    in_specs = (
        P(None, "gx", "gy", "ha", None),
        P(None, "gx", "gy", "ha", None),
        P("gx", "gy", "ha"),
    )
    out_specs = P(None, "gx", "gy", "ha", None)
    return jax.shard_map(on_device, mesh=mesh, in_specs=in_specs, out_specs=out_specs, check_vma=False)
```

```python
import functools
import math

import jax
import jax.numpy as jnp
from jax import lax
from jax.experimental import pallas as pl
from jax.experimental.pallas import tpu as pltpu
from jax.sharding import PartitionSpec as P

SPLIT_XI = 2.0
SOFT_SQ = 0.01
GAUSS_COEF = 2.0 * SPLIT_XI / math.sqrt(math.pi)
STOKES_NORM = 1.0 / (8.0 * math.pi)

SOFT_U = SPLIT_XI * SPLIT_XI * SOFT_SQ
LOG2_E = math.log2(math.e)
LOG2_G = math.log2(GAUSS_COEF)
SELF_C = math.erfc(math.sqrt(SOFT_U)) / math.sqrt(SOFT_SQ) + GAUSS_COEF * (
    2.0 * SOFT_U - 3.0
) * math.exp(-SOFT_U)

LANES = 128
ROWS = 8
CHUNK = 32
UNITS = 8
COUNT_ROW = 3
FULL = 640
MANY = 440
EARLY = 3
FIRST = (3, 4)
SECOND = (5, 6, 7, 0, 1, 2, 3, 4)
LIST_Z, LIST_X, LIST_Y = 5, 7, 10
FORCE_ROW = 4


def rows_and_lanes(shape=(ROWS, LANES)):
    return lax.broadcasted_iota(jnp.int32, shape, 0), lax.broadcasted_iota(jnp.int32, shape, 1)


def bins_of(cells):
    return [(i, j, k) for i in range(cells[0]) for j in range(cells[1]) for k in range(cells[2])]


def shift_tile(cells, at):
    row, _ = rows_and_lanes()
    moved = jnp.zeros((ROWS, LANES), jnp.float32)
    for i in range(3):
        moved = jnp.where(row == i, SPLIT_XI * (at[i] - 0.5 * (cells[i] - 1)), moved)
    return moved


def compact(listed, base, sources):
    _, lane = rows_and_lanes()
    filled = jnp.int32(0)
    moved = []
    for tile, count in sources:
        at = lax.bitwise_and(filled, LANES - 1)
        tile_id = base + lax.shift_right_logical(filled, 7)
        moved.append((pltpu.roll(tile, at, 1), lane >= at, tile_id, at + count >= LANES))
        filled = filled + count
    current = jnp.zeros((ROWS, LANES), jnp.float32)
    for tile, behind, tile_id, full in moved:
        current = jnp.where(behind, tile, current)
        spill = jnp.where(behind, 0.0, tile)
        listed[tile_id] = current
        listed[tile_id + 1] = spill
        current = jnp.where(full, spill, current)
    return filled


def spread_rows(lists, to, listed, base, n_tiles, most):
    def some(tiles):
        for n in tiles:
            for i, row in enumerate((0, 1, 2, 4, 5, 6)):
                lists[to + n, i] = jnp.broadcast_to(listed[base + n, row : row + 1, :], (ROWS, LANES))

    likely = min(5, most)
    some(range(likely))

    @pl.when(n_tiles > likely)
    def _():
        some(range(likely, most))


def up_to(count, size):
    return lax.shift_right_logical(count + (size - 1), size.bit_length() - 1)


def parts_of(value, n):
    parts = []
    for _ in range(n):
        part = value.astype(jnp.bfloat16)
        value = value - part.astype(jnp.float32)
        parts.append(part)
    return parts


def spread_targets(spread, first, tile):
    parts = [p.astype(jnp.float32) for p in parts_of(tile, 3)] + [jnp.zeros_like(tile)]
    row, lane = rows_and_lanes((4 * ROWS, 3 * LANES))
    pick = jnp.where(lax.bitwise_and(row, ROWS - 1) == lax.shift_right_logical(lane, 7), 1.0, 0.0)
    wide = lax.dot_general(
        jnp.concatenate(parts, axis=0).astype(jnp.bfloat16),
        pick.astype(jnp.bfloat16),
        (((0,), (0,)), ((), ())),
        preferred_element_type=jnp.float32,
    )
    for i in range(3):
        spread[i, first : first + LANES, :] = wide[:, i * LANES : (i + 1) * LANES]


def coefficients(target, source, force):
    delta = [t - s for t, s in zip(target, source)]
    u = (delta[0] * delta[0] + SOFT_U) + delta[1] * delta[1] + delta[2] * delta[2]
    inv = lax.rsqrt(u)
    tail = (1.0 - lax.erf(u * inv)) * inv
    gauss = jnp.exp2(LOG2_G - u * LOG2_E)
    rest = gauss * (u - 1.5)
    coef_d = ((tail - rest) - gauss) * pl.reciprocal(u, approx=True)
    along = coef_d * (delta[0] * force[0] + delta[1] * force[1] + delta[2] * force[2])
    return tail + rest, along


class Groups:
    def __init__(self, tables):
        self.tables = tables
        self.size = 0
        self.total = jnp.int32(0)

    def add(self, n_chunks, n_tiles, first_tile, spread_row, acc_row):
        for table, value in zip(self.tables, (n_chunks, n_tiles, first_tile, spread_row, acc_row)):
            table[self.size] = jnp.int32(value)
        self.size += 1
        self.total = self.total + n_chunks * n_tiles

    def run(self, lists, spread, coefs, acc):
        chunks_of, tiles_of, list_of, spread_of, acc_of = self.tables
        trash = acc.shape[1] - CHUNK

        def rows(tile_id):
            wide = [jnp.concatenate([lists[tile_id, i]] * (CHUNK // ROWS), axis=0) for i in range(6)]
            return wide[:3], wide[3:]

        def advance(group, chunk, tile):
            end_tile = tile + 1 == tiles_of[group]
            next_chunk = jnp.where(end_tile, chunk + CHUNK, chunk)
            end_chunk = next_chunk == chunks_of[group] * CHUNK
            next_group = jnp.where(end_chunk, jnp.minimum(group + 1, self.size - 1), group)
            return next_group, jnp.where(end_chunk, 0, next_chunk), jnp.where(end_tile, 0, tile + 1)

        def find(step, place):
            units, found = [], []
            for n in range(UNITS):
                group, chunk, tile = place
                valid = step * UNITS + n < self.total
                units += [jnp.where(valid, acc_of[group] + chunk, trash), list_of[group] + tile]
                at = pl.ds(pl.multiple_of(spread_of[group] + chunk, CHUNK), CHUNK)
                target = [spread[i, at, :] for i in range(3)]
                found.append(coefficients(target, *rows(units[-1])))
                place = advance(*place)
            return found, tuple(units), place

        def use(units):
            terms = []
            for n, tile in enumerate(units[1::2]):
                coef_c, along = coefs[n, 0], coefs[n, 1]
                source, force = rows(tile)
                terms.append([coef_c * force[i] - along * source[i] for i in range(3)] + [along])
            return terms

        def keep(found):
            for n, pair in enumerate(found):
                coefs[n, 0], coefs[n, 1] = pair

        def add(units, terms):
            for first, unit in zip(units[::2], terms):
                at = pl.ds(pl.multiple_of(first, CHUNK), CHUNK)
                for i in range(4):
                    acc[i, at, :] = acc[i, at, :] + unit[i]

        def body(step, state):
            place, olds = state[:3], state[3:]
            terms = use(olds)
            found, news, place = find(step, place)
            add(olds, terms)
            keep(found)
            return place + news

        zero = jnp.int32(0)
        found, units, place = find(0, (zero, zero, zero))
        keep(found)
        state = lax.fori_loop(1, lax.div(self.total + UNITS - 1, UNITS), body, place + units)
        add(state[3:], use(state[3:]))


def is_full(cells, count_ref):
    filled = jnp.int32(0)
    for at in bins_of(cells):
        filled = filled + count_ref[at]
    return filled, filled > FULL, filled > MANY


def list_own(cells, count_ref, own_ref, listed):
    sources = [(own_ref[at] + shift_tile(cells, at), count_ref[at]) for at in bins_of(cells)]
    compact(listed, 0, sources)


def velocity_rows(cells, group, by_row, tile):
    position = tile + shift_tile(cells, bins_of(cells)[group])
    return (2.0 * STOKES_NORM) * (by_row + position * jnp.broadcast_to(by_row[3:4], (ROWS, LANES)))


def lane_sums(sums):
    shape = sums[0].shape
    row, _ = rows_and_lanes()
    _, lane = rows_and_lanes(shape)
    half, quarter = LANES // 2, LANES // 4
    low = lane < half

    def folded(a, b):
        return jnp.where(low, a, b) + pltpu.roll(jnp.where(low, b, a), half, 1)

    first, second = folded(sums[0], sums[1]), folded(sums[2], sums[3])
    quarters = jnp.where(
        lax.bitwise_and(lane, quarter) == 0,
        first + pltpu.roll(first, LANES - quarter, 1),
        second + pltpu.roll(second, quarter, 1),
    )
    turned = jnp.transpose(quarters)
    merged = jnp.zeros((ROWS, LANES), jnp.float32)
    for n, i in enumerate((0, 2, 1, 3)):
        total = jnp.sum(turned[n * quarter : (n + 1) * quarter], axis=0, keepdims=True)
        merged = jnp.where(row == i, total, merged)
    return merged


def pack_kernel(cells, count_hbm, offset_hbm, force_hbm, own_ref, early_ref, *refs):
    (count_ref, offset_v, force_v, sems, listed, lists, spread, coefs, acc), tables = refs[:9], refs[9:]
    copies = [
        pltpu.make_async_copy(source, target, sems.at[n])
        for n, (source, target) in enumerate(
            ((count_hbm, count_ref), (offset_hbm, offset_v), (force_hbm, force_v))
        )
    ]
    for copy in copies:
        copy.start()
    for copy in copies:
        copy.wait()
    slot = lax.broadcasted_iota(jnp.int32, (1, LANES), 1)
    for at in bins_of(cells):
        ix, iy, iz = at
        count = count_ref[at]
        wide = jnp.full((1, LANES), count, jnp.int32).astype(jnp.float32)
        for i in range(3):
            position = offset_v[i, ix, iy, iz : iz + 1, :]
            own_ref[ix, iy, iz, i : i + 1, :] = position * SPLIT_XI - 0.5 * SPLIT_XI
            force = force_v[i, ix, iy, iz : iz + 1, :]
            own_ref[ix, iy, iz, 4 + i : 5 + i, :] = jnp.where(slot < count, force, 0.0)
        own_ref[ix, iy, iz, 3:4, :] = wide
        own_ref[ix, iy, iz, 7:8, :] = wide
    early_ref[...] = jnp.zeros_like(early_ref)
    filled, full, _ = is_full(cells, count_ref)

    @pl.when(full)
    def _():
        list_own(cells, count_ref, own_ref, listed)
        spread_rows(lists, 0, listed, 0, up_to(filled, LANES), len(bins_of(cells)))
        acc[...] = jnp.zeros_like(acc)
        groups = range(EARLY)
        tiles = [own_ref[bins_of(cells)[n]] for n in groups]
        work = Groups(tables)
        for n in groups:
            at = bins_of(cells)[n]
            spread_targets(spread, n * LANES, tiles[n] + shift_tile(cells, at))
            work.add(up_to(count_ref[at], CHUNK), up_to(filled, LANES), 0, n * LANES, n * LANES)
        work.run(lists, spread, coefs, acc)
        for n in groups:
            by_row = lane_sums([acc[i, n * LANES : (n + 1) * LANES, :] for i in range(4)])
            early_ref[n] = velocity_rows(cells, n, by_row, tiles[n])


def counts_of(tiles, count_v, count_s, sem):
    _, lane = rows_and_lanes()
    held = jnp.zeros((ROWS, LANES), jnp.float32)
    for cell, tile in enumerate(tiles):
        held = jnp.where(lane == cell, tile, held)
    count_v[...] = held.astype(jnp.int32)
    copy = pltpu.make_async_copy(count_v, count_s, sem)
    copy.start()
    return copy


def first_kernel(cells, sent_ref, own_ref, lists, spread, acc, listed, coefs, *refs):
    tables, (count_v, count_s, sem) = refs[:5], refs[5:]
    bins = bins_of(cells)
    copy = counts_of([sent_ref[at] for at in bins], count_v, count_s, sem)
    own_ref[...] = sent_ref[...]
    for n, at in enumerate(bins):
        spread_targets(spread, n * LANES, own_ref[at] + shift_tile(cells, at))
    acc[...] = jnp.zeros_like(acc)
    copy.wait()
    count_ref = {at: count_s[COUNT_ROW, n] for n, at in enumerate(bins)}
    list_own(cells, count_ref, own_ref, listed)
    filled, _, many = is_full(cells, count_ref)
    spread_rows(lists, 0, listed, 0, up_to(filled, LANES), len(bins))
    work = Groups(tables)
    for m, n in enumerate(FIRST):
        n_chunks = jnp.where(many, up_to(count_ref[bins[n]], CHUNK), 0)
        work.add(n_chunks, up_to(filled, LANES), 0, n * LANES, m * LANES)
    work.run(lists, spread, coefs, acc)


def second_kernel(cells, count_ref, other, own_lists, spread, first, acc, listed, lists, coefs, *refs):
    tables, (count_v, count_s, sem) = refs[:5], refs[5:]
    bins = bins_of(cells)
    size_x, size_y, size_z = cells
    copy = counts_of([other[at] for at in bins], count_v, count_s, sem)
    for n in range(len(bins)):
        here = slice(n * LANES, (n + 1) * LANES)
        if n in FIRST:
            m = FIRST.index(n)
            acc[:, here, :] = first[:, m * LANES : (m + 1) * LANES, :]
        else:
            acc[:, here, :] = jnp.zeros((4, LANES, LANES), jnp.float32)
    n_own = own_lists.shape[0]
    for n in range(n_own):
        lists[n] = own_lists[n]
    filled, full, many = is_full(cells, count_ref)
    copy.wait()
    work = Groups(tables)
    for bz in range(size_z):
        z = (-1, size_z)[bz]
        sources = []
        for x in range(size_x):
            for y in range(size_y):
                place = (x, y, z % size_z)
                tile = other[place] + shift_tile(cells, (x, y, z))
                sources.append((tile, count_s[COUNT_ROW, bins.index(place)]))
        n_tiles = up_to(compact(listed, bz * LIST_Z, sources), LANES)
        first_tile = n_own + bz * (LIST_Z - 1)
        spread_rows(lists, first_tile, listed, bz * LIST_Z, n_tiles, LIST_Z - 1)
        for n, at in enumerate(bins):
            if at[2] == bz:
                work.add(up_to(count_ref[at], CHUNK), n_tiles, first_tile, n * LANES, n * LANES)
    for n in SECOND:
        n_chunks = up_to(count_ref[bins[n]], CHUNK)
        if n < EARLY or n in FIRST:
            n_chunks = jnp.where(full if n < EARLY else many, 0, n_chunks)
        work.add(n_chunks, up_to(filled, LANES), 0, n * LANES, n * LANES)
    work.run(lists, spread, coefs, acc)


def middle_kernel(cells, count_ref, wide, spread, second, acc, listed, lists, coefs, *refs):
    tables, (count_v, count_s, sem) = refs[:5], refs[5:]
    size_x, size_y, size_z = cells
    n_z = 2 * size_z
    bins = bins_of(cells)
    places = [(i, j, k) for i in (0, size_x + 1) for j in range(size_y) for k in range(n_z)]
    copy = counts_of([wide[at] for at in places], count_v, count_s, sem)
    acc[...] = second[...]
    copy.wait()
    work = Groups(tables)
    for bx in range(size_x):
        for bz in range(size_z):
            x = (-1, size_x)[bx]
            sources = []
            for y in range(size_y):
                for z in (bz - 1, bz, bz + 1):
                    place = (x + 1, y, z % n_z)
                    tile = wide[place] + shift_tile(cells, (x, y, z))
                    sources.append((tile, count_s[COUNT_ROW, places.index(place)]))
            n_list = bx * size_z + bz
            n_tiles = up_to(compact(listed, n_list * LIST_X, sources), LANES)
            first_tile = n_list * (LIST_X - 1)
            spread_rows(lists, first_tile, listed, n_list * LIST_X, n_tiles, LIST_X - 1)
            for n, at in enumerate(bins):
                if (at[0], at[2]) == (bx, bz):
                    work.add(up_to(count_ref[at], CHUNK), n_tiles, first_tile, n * LANES, n * LANES)
    work.run(lists, spread, coefs, acc)


def last_kernel(cells, count_ref, own_ref, y_lo, y_hi, spread, *refs):
    (middle, early, out_ref, acc, listed, lists, coefs), refs = refs[:7], refs[7:]
    tables, (count_v, count_s, sem) = refs[:5], refs[5:]
    size_x, size_y, size_z = cells
    n_z = 2 * size_z
    bins = bins_of(cells)
    places = [(i, j, k) for i in range(size_x + 2) for j in range(2) for k in range(n_z)]
    tiles = [(y_lo, y_hi)[j][i, 0, k] for i, j, k in places]
    copy = counts_of(tiles, count_v, count_s, sem)
    acc[...] = middle[...]
    copy.wait()
    work = Groups(tables)
    for n, (bx, by, bz) in enumerate(bins):
        sources = []
        for x in (bx - 1, bx, bx + 1):
            for z in (bz - 1, bz, bz + 1):
                cell = places.index((x + 1, by, z % n_z))
                tile = tiles[cell] + shift_tile(cells, (x, (-1, size_y)[by], z))
                sources.append((tile, count_s[COUNT_ROW, cell]))
        n_tiles = up_to(compact(listed, n * LIST_Y, sources), LANES)
        first_tile = n * (LIST_Y - 1)
        spread_rows(lists, first_tile, listed, n * LIST_Y, n_tiles, LIST_Y - 1)
        work.add(up_to(count_ref[bx, by, bz], CHUNK), n_tiles, first_tile, n * LANES, n * LANES)
    work.run(lists, spread, coefs, acc)

    slot = lax.broadcasted_iota(jnp.int32, (1, LANES), 1)
    for n, at in enumerate(bins):
        by_row = lane_sums([acc[i, n * LANES : (n + 1) * LANES, :] for i in range(4)])
        tile = own_ref[at]
        total = velocity_rows(cells, n, by_row, tile)
        total = total - (STOKES_NORM * SELF_C) * pltpu.roll(tile, ROWS - FORCE_ROW, 0)
        if n < EARLY:
            total = total + early[n]
        total = jnp.where(slot < count_ref[at], total, 0.0)
        for i in range(3):
            out_ref[i, at[0], at[1], at[2] : at[2] + 1, :] = total[i : i + 1]


def shifted(array, axis, dim):
    size, length = lax.axis_size(axis), array.shape[dim]
    up = [(i, (i + 1) % size) for i in range(size)]
    down = [(j, i) for i, j in up]
    after = lax.ppermute(lax.slice_in_dim(array, 0, 1, axis=dim), axis, down)
    before = lax.ppermute(lax.slice_in_dim(array, length - 1, length, axis=dim), axis, up)
    return before, after


def on_device(offsets, forces, counts):
    cells = offsets.shape[1:4]
    slots = offsets.shape[4]
    n_bins = cells[0] * cells[1] * cells[2]
    n_targets = n_bins * slots
    whole = pl.BlockSpec(memory_space=pltpu.VMEM)
    scalars = pl.BlockSpec(memory_space=pltpu.SMEM)

    def floats(*shape):
        return jax.ShapeDtypeStruct(shape, jnp.float32)

    def params(mib):
        return pltpu.CompilerParams(vmem_limit_bytes=mib << 20)

    loop_scratch = [pltpu.VMEM((UNITS, 2, CHUNK, LANES), jnp.float32)]
    loop_scratch += [pltpu.SMEM((2 * n_bins,), jnp.int32)] * 5
    count_scratch = [
        pltpu.VMEM((ROWS, LANES), jnp.int32),
        pltpu.SMEM((ROWS, LANES), jnp.int32),
        pltpu.SemaphoreType.DMA,
    ]
    cost = pl.CostEstimate(flops=1 << 28, bytes_accessed=1 << 16, transcendentals=1 << 20)

    def list_scratch(n_lists, n_tiles, more=0):
        return [
            pltpu.VMEM((n_lists * n_tiles, ROWS, LANES), jnp.float32),
            pltpu.VMEM((n_lists * (n_tiles - 1) + more, 6, ROWS, LANES), jnp.float32),
        ]

    own_lists, all_targets = floats(n_bins, 6, ROWS, slots), floats(3, n_targets, slots)
    arguments = [pltpu.with_memory_space_constraint(x, pltpu.HBM) for x in (counts, offsets, forces)]
    sent, early = pl.pallas_call(
        functools.partial(pack_kernel, cells),
        out_shape=[floats(*cells, ROWS, slots), floats(EARLY, ROWS, slots)],
        in_specs=[pl.BlockSpec(memory_space=pltpu.HBM)] * 3,
        out_specs=[whole, whole],
        scratch_shapes=[
            pltpu.SMEM(counts.shape, jnp.int32),
            pltpu.VMEM(offsets.shape, jnp.float32),
            pltpu.VMEM(forces.shape, jnp.float32),
            pltpu.SemaphoreType.DMA((3,)),
            pltpu.VMEM((n_bins + 1, ROWS, LANES), jnp.float32),
            pltpu.VMEM(own_lists.shape, jnp.float32),
            pltpu.VMEM((3, EARLY * slots, slots), jnp.float32),
            loop_scratch[0],
            pltpu.VMEM((4, EARLY * slots + CHUNK, slots), jnp.float32),
        ]
        + loop_scratch[1:],
        compiler_params=params(8),
        name="pack",
    )(*arguments)

    together = lax.optimization_barrier
    size = lax.axis_size("ha")
    other = lax.ppermute(sent, "ha", [(i, (i + 1) % size) for i in range(size)])
    own, listed, spread, first = pl.pallas_call(
        functools.partial(first_kernel, cells),
        out_shape=[sent, own_lists, all_targets, floats(4, len(FIRST) * slots + CHUNK, slots)],
        in_specs=[whole],
        out_specs=[whole] * 4,
        scratch_shapes=[pltpu.VMEM((n_bins + 1, ROWS, LANES), jnp.float32)]
        + loop_scratch
        + count_scratch,
        compiler_params=params(8),
        cost_estimate=cost,
        name="first",
    )(sent)
    other, own, listed, first = together((other, own, listed, first))
    column = jnp.concatenate([own, other], axis=2)
    x_lo, x_hi = shifted(column, "gx", 0)
    second = pl.pallas_call(
        functools.partial(second_kernel, cells),
        out_shape=floats(4, n_targets + CHUNK, slots),
        in_specs=[scalars] + [whole] * 4,
        out_specs=whole,
        scratch_shapes=list_scratch(cells[2], LIST_Z, n_bins)
        + loop_scratch
        + count_scratch,
        compiler_params=params(8),
        cost_estimate=cost,
        name="second",
    )(counts, other, listed, spread, first)
    x_lo, x_hi, second = together((x_lo, x_hi, second))
    wide = jnp.concatenate([x_lo, column, x_hi], axis=0)
    y_lo, y_hi = shifted(wide, "gy", 1)
    middle = pl.pallas_call(
        functools.partial(middle_kernel, cells),
        out_shape=floats(4, n_targets + CHUNK, slots),
        in_specs=[scalars] + [whole] * 3,
        out_specs=whole,
        scratch_shapes=list_scratch(cells[0] * cells[2], LIST_X) + loop_scratch + count_scratch,
        compiler_params=params(8),
        cost_estimate=cost,
        name="middle",
    )(counts, wide, spread, second)
    y_lo, y_hi, middle = together((y_lo, y_hi, middle))
    return pl.pallas_call(
        functools.partial(last_kernel, cells),
        out_shape=floats(3, *cells, slots),
        in_specs=[scalars] + [whole] * 6,
        out_specs=whole,
        scratch_shapes=[pltpu.VMEM((4, n_targets + CHUNK, slots), jnp.float32)]
        + list_scratch(n_bins, LIST_Y)
        + loop_scratch
        + count_scratch,
        compiler_params=params(12),
        cost_estimate=cost,
        name="last",
    )(counts, own, y_lo, y_hi, spread, middle, early)


def solution(mesh):
    in_specs = (
        P(None, "gx", "gy", "ha", None),
        P(None, "gx", "gy", "ha", None),
        P("gx", "gy", "ha"),
    )
    out_specs = P(None, "gx", "gy", "ha", None)
    return jax.shard_map(on_device, mesh=mesh, in_specs=in_specs, out_specs=out_specs, check_vma=False)
```

```python
import functools
import math

import jax
import jax.numpy as jnp
from jax import lax
from jax.experimental import pallas as pl
from jax.experimental.pallas import tpu as pltpu
from jax.sharding import PartitionSpec as P

SPLIT_XI = 2.0
SOFT_SQ = 0.01
GAUSS_COEF = 2.0 * SPLIT_XI / math.sqrt(math.pi)
STOKES_NORM = 1.0 / (8.0 * math.pi)

SOFT_U = SPLIT_XI * SPLIT_XI * SOFT_SQ
LOG2_E = math.log2(math.e)
LOG2_G = math.log2(GAUSS_COEF)
SELF_C = math.erfc(math.sqrt(SOFT_U)) / math.sqrt(SOFT_SQ) + GAUSS_COEF * (
    2.0 * SOFT_U - 3.0
) * math.exp(-SOFT_U)

LANES = 128
ROWS = 8
CHUNK = 32
UNITS = 8
COUNT_ROW = 3
FULL = 640
MANY = 440
EARLY = 3
FIRST = (3, 4, 5)
SECOND = (6, 7, 5, 0, 1, 2, 3, 4)
FIRST_IF_MANY = (3, 4)
LIST_Z, LIST_X, LIST_Y = 5, 7, 10
FORCE_ROW = 4


def rows_and_lanes(shape=(ROWS, LANES)):
    return lax.broadcasted_iota(jnp.int32, shape, 0), lax.broadcasted_iota(jnp.int32, shape, 1)


def bins_of(cells):
    return [(i, j, k) for i in range(cells[0]) for j in range(cells[1]) for k in range(cells[2])]


def shift_tile(cells, at):
    row, _ = rows_and_lanes()
    moved = jnp.zeros((ROWS, LANES), jnp.float32)
    for i in range(3):
        moved = jnp.where(row == i, SPLIT_XI * (at[i] - 0.5 * (cells[i] - 1)), moved)
    return moved


def compact(listed, base, sources):
    _, lane = rows_and_lanes()
    filled = jnp.int32(0)
    moved = []
    for tile, count in sources:
        at = lax.bitwise_and(filled, LANES - 1)
        tile_id = base + lax.shift_right_logical(filled, 7)
        moved.append((pltpu.roll(tile, at, 1), lane >= at, tile_id, at + count >= LANES))
        filled = filled + count
    current = jnp.zeros((ROWS, LANES), jnp.float32)
    for tile, behind, tile_id, full in moved:
        current = jnp.where(behind, tile, current)
        spill = jnp.where(behind, 0.0, tile)
        listed[tile_id] = current
        listed[tile_id + 1] = spill
        current = jnp.where(full, spill, current)
    return filled


def spread_rows(lists, to, listed, base, n_tiles, most):
    def some(tiles):
        for n in tiles:
            for i, row in enumerate((0, 1, 2, 4, 5, 6)):
                lists[to + n, i] = jnp.broadcast_to(listed[base + n, row : row + 1, :], (ROWS, LANES))

    likely = min(5, most)
    some(range(likely))

    @pl.when(n_tiles > likely)
    def _():
        some(range(likely, most))


def up_to(count, size):
    return lax.shift_right_logical(count + (size - 1), size.bit_length() - 1)


def parts_of(value, n):
    parts = []
    for _ in range(n):
        part = value.astype(jnp.bfloat16)
        value = value - part.astype(jnp.float32)
        parts.append(part)
    return parts


def spread_targets(spread, first, tile):
    parts = [p.astype(jnp.float32) for p in parts_of(tile, 3)] + [jnp.zeros_like(tile)]
    row, lane = rows_and_lanes((4 * ROWS, 3 * LANES))
    pick = jnp.where(lax.bitwise_and(row, ROWS - 1) == lax.shift_right_logical(lane, 7), 1.0, 0.0)
    wide = lax.dot_general(
        jnp.concatenate(parts, axis=0).astype(jnp.bfloat16),
        pick.astype(jnp.bfloat16),
        (((0,), (0,)), ((), ())),
        preferred_element_type=jnp.float32,
    )
    for i in range(3):
        spread[i, first : first + LANES, :] = wide[:, i * LANES : (i + 1) * LANES]


def coefficients(target, source, force):
    delta = [t - s for t, s in zip(target, source)]
    u = (delta[0] * delta[0] + SOFT_U) + delta[1] * delta[1] + delta[2] * delta[2]
    inv = lax.rsqrt(u)
    tail = (1.0 - lax.erf(u * inv)) * inv
    gauss = jnp.exp2(LOG2_G - u * LOG2_E)
    rest = gauss * (u - 1.5)
    coef_d = ((tail - rest) - gauss) * pl.reciprocal(u, approx=True)
    along = coef_d * (delta[0] * force[0] + delta[1] * force[1] + delta[2] * force[2])
    return tail + rest, along


class Groups:
    def __init__(self, tables):
        self.tables = tables
        self.size = 0
        self.total = jnp.int32(0)

    def add(self, n_chunks, n_tiles, first_tile, spread_row, acc_row):
        for table, value in zip(self.tables, (n_chunks, n_tiles, first_tile, spread_row, acc_row)):
            table[self.size] = jnp.int32(value)
        self.size += 1
        self.total = self.total + n_chunks * n_tiles

    def run(self, lists, spread, coefs, acc):
        chunks_of, tiles_of, list_of, spread_of, acc_of = self.tables
        trash = acc.shape[1] - CHUNK

        def rows(tile_id):
            wide = [jnp.concatenate([lists[tile_id, i]] * (CHUNK // ROWS), axis=0) for i in range(6)]
            return wide[:3], wide[3:]

        def advance(group, chunk, tile):
            end_tile = tile + 1 == tiles_of[group]
            next_chunk = jnp.where(end_tile, chunk + CHUNK, chunk)
            end_chunk = next_chunk == chunks_of[group] * CHUNK
            next_group = jnp.where(end_chunk, jnp.minimum(group + 1, self.size - 1), group)
            return next_group, jnp.where(end_chunk, 0, next_chunk), jnp.where(end_tile, 0, tile + 1)

        def find(step, place):
            units, found = [], []
            for n in range(UNITS):
                group, chunk, tile = place
                valid = step * UNITS + n < self.total
                units += [jnp.where(valid, acc_of[group] + chunk, trash), list_of[group] + tile]
                at = pl.ds(pl.multiple_of(spread_of[group] + chunk, CHUNK), CHUNK)
                target = [spread[i, at, :] for i in range(3)]
                found.append(coefficients(target, *rows(units[-1])))
                place = advance(*place)
            return found, tuple(units), place

        def use(units):
            terms = []
            for n, tile in enumerate(units[1::2]):
                coef_c, along = coefs[n, 0], coefs[n, 1]
                source, force = rows(tile)
                terms.append([coef_c * force[i] - along * source[i] for i in range(3)] + [along])
            return terms

        def keep(found):
            for n, pair in enumerate(found):
                coefs[n, 0], coefs[n, 1] = pair

        def add(units, terms):
            for first, unit in zip(units[::2], terms):
                at = pl.ds(pl.multiple_of(first, CHUNK), CHUNK)
                for i in range(4):
                    acc[i, at, :] = acc[i, at, :] + unit[i]

        def body(step, state):
            place, olds = state[:3], state[3:]
            terms = use(olds)
            found, news, place = find(step, place)
            add(olds, terms)
            keep(found)
            return place + news

        zero = jnp.int32(0)
        found, units, place = find(0, (zero, zero, zero))
        keep(found)
        state = lax.fori_loop(1, lax.div(self.total + UNITS - 1, UNITS), body, place + units)
        add(state[3:], use(state[3:]))


def is_full(cells, count_ref):
    filled = jnp.int32(0)
    for at in bins_of(cells):
        filled = filled + count_ref[at]
    return filled, filled > FULL, filled > MANY


def list_own(cells, count_ref, own_ref, listed):
    sources = [(own_ref[at] + shift_tile(cells, at), count_ref[at]) for at in bins_of(cells)]
    compact(listed, 0, sources)


def velocity_rows(cells, group, by_row, tile):
    position = tile + shift_tile(cells, bins_of(cells)[group])
    return (2.0 * STOKES_NORM) * (by_row + position * jnp.broadcast_to(by_row[3:4], (ROWS, LANES)))


def lane_sums(sums, n_bins):
    row, lane = rows_and_lanes((2 * LANES, LANES))
    merged = jnp.zeros(sums[0].shape, jnp.float32)
    for i, part in enumerate(sums):
        merged = merged + jnp.dot(
            jnp.concatenate(parts_of(part, 2), axis=1),
            jnp.where(lax.bitwise_and(lane, ROWS - 1) == i, 1.0, 0.0).astype(jnp.bfloat16),
            preferred_element_type=jnp.float32,
        )
    _, lane = rows_and_lanes((LANES, LANES))
    chosen = merged[:LANES]
    for n in range(1, n_bins):
        chosen = jnp.where(lane >= n * ROWS, merged[n * LANES : (n + 1) * LANES], chosen)
    turned = jnp.transpose(chosen)
    return [turned[n * ROWS : (n + 1) * ROWS] for n in range(n_bins)]


def pack_kernel(cells, count_hbm, offset_hbm, force_hbm, own_ref, early_ref, *refs):
    (count_ref, offset_v, force_v, sems, listed, lists, spread, coefs, acc), tables = refs[:9], refs[9:]
    copies = [
        pltpu.make_async_copy(source, target, sems.at[n])
        for n, (source, target) in enumerate(
            ((count_hbm, count_ref), (offset_hbm, offset_v), (force_hbm, force_v))
        )
    ]
    for copy in copies:
        copy.start()
    for copy in copies:
        copy.wait()
    slot = lax.broadcasted_iota(jnp.int32, (1, LANES), 1)
    for at in bins_of(cells):
        ix, iy, iz = at
        count = count_ref[at]
        wide = jnp.full((1, LANES), count, jnp.int32).astype(jnp.float32)
        for i in range(3):
            position = offset_v[i, ix, iy, iz : iz + 1, :]
            own_ref[ix, iy, iz, i : i + 1, :] = position * SPLIT_XI - 0.5 * SPLIT_XI
            force = force_v[i, ix, iy, iz : iz + 1, :]
            own_ref[ix, iy, iz, 4 + i : 5 + i, :] = jnp.where(slot < count, force, 0.0)
        own_ref[ix, iy, iz, 3:4, :] = wide
        own_ref[ix, iy, iz, 7:8, :] = wide
    early_ref[...] = jnp.zeros_like(early_ref)
    filled, full, _ = is_full(cells, count_ref)

    @pl.when(full)
    def _():
        list_own(cells, count_ref, own_ref, listed)
        spread_rows(lists, 0, listed, 0, up_to(filled, LANES), len(bins_of(cells)))
        acc[...] = jnp.zeros_like(acc)
        groups = range(EARLY)
        tiles = [own_ref[bins_of(cells)[n]] for n in groups]
        work = Groups(tables)
        for n in groups:
            at = bins_of(cells)[n]
            spread_targets(spread, n * LANES, tiles[n] + shift_tile(cells, at))
            work.add(up_to(count_ref[at], CHUNK), up_to(filled, LANES), 0, n * LANES, n * LANES)
        work.run(lists, spread, coefs, acc)
        by_rows = lane_sums([acc[i, : EARLY * LANES, :] for i in range(4)], EARLY)
        for n, by_row in enumerate(by_rows):
            early_ref[n] = velocity_rows(cells, n, by_row, tiles[n])


def counts_of(tiles, count_v, count_s, sem):
    _, lane = rows_and_lanes()
    held = jnp.zeros((ROWS, LANES), jnp.float32)
    for cell, tile in enumerate(tiles):
        held = jnp.where(lane == cell, tile, held)
    count_v[...] = held.astype(jnp.int32)
    copy = pltpu.make_async_copy(count_v, count_s, sem)
    copy.start()
    return copy


def first_kernel(cells, sent_ref, own_ref, lists, spread, acc, listed, coefs, *refs):
    tables, (count_v, count_s, sem) = refs[:5], refs[5:]
    bins = bins_of(cells)
    copy = counts_of([sent_ref[at] for at in bins], count_v, count_s, sem)
    own_ref[...] = sent_ref[...]
    for n, at in enumerate(bins):
        spread_targets(spread, n * LANES, own_ref[at] + shift_tile(cells, at))
    acc[...] = jnp.zeros_like(acc)
    copy.wait()
    count_ref = {at: count_s[COUNT_ROW, n] for n, at in enumerate(bins)}
    list_own(cells, count_ref, own_ref, listed)
    filled, full, many = is_full(cells, count_ref)
    spread_rows(lists, 0, listed, 0, up_to(filled, LANES), len(bins))
    work = Groups(tables)
    for m, n in enumerate(FIRST):
        n_chunks = jnp.where(many if n in FIRST_IF_MANY else full, up_to(count_ref[bins[n]], CHUNK), 0)
        work.add(n_chunks, up_to(filled, LANES), 0, n * LANES, m * LANES)
    work.run(lists, spread, coefs, acc)


def second_kernel(cells, count_ref, other, own_lists, spread, first, acc, listed, lists, coefs, *refs):
    tables, (count_v, count_s, sem) = refs[:5], refs[5:]
    bins = bins_of(cells)
    size_x, size_y, size_z = cells
    copy = counts_of([other[at] for at in bins], count_v, count_s, sem)
    for n in range(len(bins)):
        here = slice(n * LANES, (n + 1) * LANES)
        if n in FIRST:
            m = FIRST.index(n)
            acc[:, here, :] = first[:, m * LANES : (m + 1) * LANES, :]
        else:
            acc[:, here, :] = jnp.zeros((4, LANES, LANES), jnp.float32)
    n_own = own_lists.shape[0]
    for n in range(n_own):
        lists[n] = own_lists[n]
    filled, full, many = is_full(cells, count_ref)
    copy.wait()
    work = Groups(tables)
    for bz in range(size_z):
        z = (-1, size_z)[bz]
        sources = []
        for x in range(size_x):
            for y in range(size_y):
                place = (x, y, z % size_z)
                tile = other[place] + shift_tile(cells, (x, y, z))
                sources.append((tile, count_s[COUNT_ROW, bins.index(place)]))
        n_tiles = up_to(compact(listed, bz * LIST_Z, sources), LANES)
        first_tile = n_own + bz * (LIST_Z - 1)
        spread_rows(lists, first_tile, listed, bz * LIST_Z, n_tiles, LIST_Z - 1)
        for n, at in enumerate(bins):
            if at[2] == bz:
                work.add(up_to(count_ref[at], CHUNK), n_tiles, first_tile, n * LANES, n * LANES)
    for n in SECOND:
        n_chunks = up_to(count_ref[bins[n]], CHUNK)
        if n < EARLY or n in FIRST:
            n_chunks = jnp.where(many if n in FIRST_IF_MANY else full, 0, n_chunks)
        work.add(n_chunks, up_to(filled, LANES), 0, n * LANES, n * LANES)
    work.run(lists, spread, coefs, acc)


def middle_kernel(cells, count_ref, wide, spread, second, acc, listed, lists, coefs, *refs):
    tables, (count_v, count_s, sem) = refs[:5], refs[5:]
    size_x, size_y, size_z = cells
    n_z = 2 * size_z
    bins = bins_of(cells)
    places = [(i, j, k) for i in (0, size_x + 1) for j in range(size_y) for k in range(n_z)]
    copy = counts_of([wide[at] for at in places], count_v, count_s, sem)
    acc[...] = second[...]
    copy.wait()
    work = Groups(tables)
    for bx in range(size_x):
        for bz in range(size_z):
            x = (-1, size_x)[bx]
            sources = []
            for y in range(size_y):
                for z in (bz - 1, bz, bz + 1):
                    place = (x + 1, y, z % n_z)
                    tile = wide[place] + shift_tile(cells, (x, y, z))
                    sources.append((tile, count_s[COUNT_ROW, places.index(place)]))
            n_list = bx * size_z + bz
            n_tiles = up_to(compact(listed, n_list * LIST_X, sources), LANES)
            first_tile = n_list * (LIST_X - 1)
            spread_rows(lists, first_tile, listed, n_list * LIST_X, n_tiles, LIST_X - 1)
            for n, at in enumerate(bins):
                if (at[0], at[2]) == (bx, bz):
                    work.add(up_to(count_ref[at], CHUNK), n_tiles, first_tile, n * LANES, n * LANES)
    work.run(lists, spread, coefs, acc)


def last_kernel(cells, count_ref, own_ref, y_lo, y_hi, spread, *refs):
    (middle, early, out_ref, acc, listed, lists, coefs), refs = refs[:7], refs[7:]
    tables, (count_v, count_s, sem) = refs[:5], refs[5:]
    size_x, size_y, size_z = cells
    n_z = 2 * size_z
    bins = bins_of(cells)
    places = [(i, j, k) for i in range(size_x + 2) for j in range(2) for k in range(n_z)]
    tiles = [(y_lo, y_hi)[j][i, 0, k] for i, j, k in places]
    copy = counts_of(tiles, count_v, count_s, sem)
    acc[...] = middle[...]
    copy.wait()
    work = Groups(tables)
    for n, (bx, by, bz) in enumerate(bins):
        sources = []
        for x in (bx - 1, bx, bx + 1):
            for z in (bz - 1, bz, bz + 1):
                cell = places.index((x + 1, by, z % n_z))
                tile = tiles[cell] + shift_tile(cells, (x, (-1, size_y)[by], z))
                sources.append((tile, count_s[COUNT_ROW, cell]))
        n_tiles = up_to(compact(listed, n * LIST_Y, sources), LANES)
        first_tile = n * (LIST_Y - 1)
        spread_rows(lists, first_tile, listed, n * LIST_Y, n_tiles, LIST_Y - 1)
        work.add(up_to(count_ref[bx, by, bz], CHUNK), n_tiles, first_tile, n * LANES, n * LANES)
    work.run(lists, spread, coefs, acc)

    slot = lax.broadcasted_iota(jnp.int32, (1, LANES), 1)
    by_rows = lane_sums([acc[i, : len(bins) * LANES, :] for i in range(4)], len(bins))
    for n, (at, by_row) in enumerate(zip(bins, by_rows)):
        tile = own_ref[at]
        total = velocity_rows(cells, n, by_row, tile)
        total = total - (STOKES_NORM * SELF_C) * pltpu.roll(tile, ROWS - FORCE_ROW, 0)
        if n < EARLY:
            total = total + early[n]
        total = jnp.where(slot < count_ref[at], total, 0.0)
        for i in range(3):
            out_ref[i, at[0], at[1], at[2] : at[2] + 1, :] = total[i : i + 1]


def shifted(first, last, axis):
    size = lax.axis_size(axis)
    up = [(i, (i + 1) % size) for i in range(size)]
    if size % 2:
        down = [(j, i) for i, j in up]
        return lax.ppermute(last, axis, up), lax.ppermute(first, axis, down)
    odd = lax.rem(lax.axis_index(axis), 2) == 1
    got = []
    for parity in (0, 1):
        pairs = [pair for i, j in up if i % 2 == parity for pair in ((i, j), (j, i))]
        got.append(lax.ppermute(jnp.where(odd == bool(parity), last, first), axis, pairs))
    return jnp.where(odd, got[0], got[1]), jnp.where(odd, got[1], got[0])


def on_device(offsets, forces, counts):
    cells = offsets.shape[1:4]
    slots = offsets.shape[4]
    n_bins = cells[0] * cells[1] * cells[2]
    n_targets = n_bins * slots
    whole = pl.BlockSpec(memory_space=pltpu.VMEM)
    scalars = pl.BlockSpec(memory_space=pltpu.SMEM)

    def floats(*shape):
        return jax.ShapeDtypeStruct(shape, jnp.float32)

    def params(mib):
        return pltpu.CompilerParams(vmem_limit_bytes=mib << 20)

    loop_scratch = [pltpu.VMEM((UNITS, 2, CHUNK, LANES), jnp.float32)]
    loop_scratch += [pltpu.SMEM((2 * n_bins,), jnp.int32)] * 5
    count_scratch = [
        pltpu.VMEM((ROWS, LANES), jnp.int32),
        pltpu.SMEM((ROWS, LANES), jnp.int32),
        pltpu.SemaphoreType.DMA,
    ]
    cost = pl.CostEstimate(flops=1 << 28, bytes_accessed=1 << 16, transcendentals=1 << 20)

    def list_scratch(n_lists, n_tiles, more=0):
        return [
            pltpu.VMEM((n_lists * n_tiles, ROWS, LANES), jnp.float32),
            pltpu.VMEM((n_lists * (n_tiles - 1) + more, 6, ROWS, LANES), jnp.float32),
        ]

    own_lists, all_targets = floats(n_bins, 6, ROWS, slots), floats(3, n_targets, slots)
    arguments = [pltpu.with_memory_space_constraint(x, pltpu.HBM) for x in (counts, offsets, forces)]
    sent, early = pl.pallas_call(
        functools.partial(pack_kernel, cells),
        out_shape=[floats(*cells, ROWS, slots), floats(EARLY, ROWS, slots)],
        in_specs=[pl.BlockSpec(memory_space=pltpu.HBM)] * 3,
        out_specs=[whole, whole],
        scratch_shapes=[
            pltpu.SMEM(counts.shape, jnp.int32),
            pltpu.VMEM(offsets.shape, jnp.float32),
            pltpu.VMEM(forces.shape, jnp.float32),
            pltpu.SemaphoreType.DMA((3,)),
            pltpu.VMEM((n_bins + 1, ROWS, LANES), jnp.float32),
            pltpu.VMEM(own_lists.shape, jnp.float32),
            pltpu.VMEM((3, EARLY * slots, slots), jnp.float32),
            loop_scratch[0],
            pltpu.VMEM((4, EARLY * slots + CHUNK, slots), jnp.float32),
        ]
        + loop_scratch[1:],
        compiler_params=params(8),
        name="pack",
    )(*arguments)

    together = lax.optimization_barrier
    size = lax.axis_size("ha")
    other = lax.ppermute(sent, "ha", [(i, (i + 1) % size) for i in range(size)])
    own, listed, spread, first = pl.pallas_call(
        functools.partial(first_kernel, cells),
        out_shape=[sent, own_lists, all_targets, floats(4, len(FIRST) * slots + CHUNK, slots)],
        in_specs=[whole],
        out_specs=[whole] * 4,
        scratch_shapes=[pltpu.VMEM((n_bins + 1, ROWS, LANES), jnp.float32)]
        + loop_scratch
        + count_scratch,
        compiler_params=params(8),
        cost_estimate=cost,
        name="first",
    )(sent)
    other, own, listed, first = together((other, own, listed, first))
    column = jnp.concatenate([own, other], axis=2)
    x_lo, x_hi = shifted(column[:1], column[cells[0] - 1 :], "gx")
    second = pl.pallas_call(
        functools.partial(second_kernel, cells),
        out_shape=floats(4, n_targets + CHUNK, slots),
        in_specs=[scalars] + [whole] * 4,
        out_specs=whole,
        scratch_shapes=list_scratch(cells[2], LIST_Z, n_bins)
        + loop_scratch
        + count_scratch,
        compiler_params=params(8),
        cost_estimate=cost,
        name="second",
    )(counts, other, listed, spread, first)
    x_hi, x_lo, second = together((x_hi, x_lo, second))
    wide = jnp.concatenate([x_lo, column, x_hi], axis=0)
    y_lo, y_hi = shifted(wide[:, :1], wide[:, cells[1] - 1 :], "gy")
    middle = pl.pallas_call(
        functools.partial(middle_kernel, cells),
        out_shape=floats(4, n_targets + CHUNK, slots),
        in_specs=[scalars] + [whole] * 3,
        out_specs=whole,
        scratch_shapes=list_scratch(cells[0] * cells[2], LIST_X) + loop_scratch + count_scratch,
        compiler_params=params(8),
        cost_estimate=cost,
        name="middle",
    )(counts, wide, spread, second)
    y_lo, y_hi, middle = together((y_lo, y_hi, middle))
    return pl.pallas_call(
        functools.partial(last_kernel, cells),
        out_shape=floats(3, *cells, slots),
        in_specs=[scalars] + [whole] * 6,
        out_specs=whole,
        scratch_shapes=[pltpu.VMEM((4, n_targets + CHUNK, slots), jnp.float32)]
        + list_scratch(n_bins, LIST_Y)
        + loop_scratch
        + count_scratch,
        compiler_params=params(12),
        cost_estimate=cost,
        name="last",
    )(counts, own, y_lo, y_hi, spread, middle, early)


def solution(mesh):
    in_specs = (
        P(None, "gx", "gy", "ha", None),
        P(None, "gx", "gy", "ha", None),
        P("gx", "gy", "ha"),
    )
    out_specs = P(None, "gx", "gy", "ha", None)
    return jax.shard_map(on_device, mesh=mesh, in_specs=in_specs, out_specs=out_specs, check_vma=False)
```

```python
import functools
import math

import jax
import jax.numpy as jnp
from jax import lax
from jax.experimental import pallas as pl
from jax.experimental.pallas import tpu as pltpu
from jax.sharding import PartitionSpec as P

SPLIT_XI = 2.0
SOFT_SQ = 0.01
GAUSS_COEF = 2.0 * SPLIT_XI / math.sqrt(math.pi)
STOKES_NORM = 1.0 / (8.0 * math.pi)

SOFT_U = SPLIT_XI * SPLIT_XI * SOFT_SQ
LOG2_E = math.log2(math.e)
LOG2_G = math.log2(GAUSS_COEF)
SELF_C = math.erfc(math.sqrt(SOFT_U)) / math.sqrt(SOFT_SQ) + GAUSS_COEF * (
    2.0 * SOFT_U - 3.0
) * math.exp(-SOFT_U)

LANES = 128
ROWS = 8
CHUNK = 32
UNITS = 8
COUNT_ROW = 3
FULL = 700
MANY = 440
EARLY = 3
FIRST = (3, 4, 5)
SECOND = (6, 7, 5, 0, 1, 2, 3, 4)
FIRST_IF_MANY = (3, 4)
LIST_Z, LIST_X, LIST_Y = 5, 7, 10
FORCE_ROW = 4


def rows_and_lanes(shape=(ROWS, LANES)):
    return lax.broadcasted_iota(jnp.int32, shape, 0), lax.broadcasted_iota(jnp.int32, shape, 1)


def bins_of(cells):
    return [(i, j, k) for i in range(cells[0]) for j in range(cells[1]) for k in range(cells[2])]


def shift_tile(cells, at):
    row, _ = rows_and_lanes()
    moved = jnp.zeros((ROWS, LANES), jnp.float32)
    for i in range(3):
        moved = jnp.where(row == i, SPLIT_XI * (at[i] - 0.5 * (cells[i] - 1)), moved)
    return moved


def compact(listed, base, sources):
    _, lane = rows_and_lanes()
    filled = jnp.int32(0)
    moved = []
    for tile, count in sources:
        at = lax.bitwise_and(filled, LANES - 1)
        tile_id = base + lax.shift_right_logical(filled, 7)
        moved.append((pltpu.roll(tile, at, 1), lane >= at, tile_id, at + count >= LANES))
        filled = filled + count
    current = jnp.zeros((ROWS, LANES), jnp.float32)
    for tile, behind, tile_id, full in moved:
        current = jnp.where(behind, tile, current)
        spill = jnp.where(behind, 0.0, tile)
        listed[tile_id] = current
        listed[tile_id + 1] = spill
        current = jnp.where(full, spill, current)
    return filled


def up_to(count, size):
    return lax.shift_right_logical(count + (size - 1), size.bit_length() - 1)


def parts_of(value, n):
    parts = []
    for _ in range(n):
        part = value.astype(jnp.bfloat16)
        value = value - part.astype(jnp.float32)
        parts.append(part)
    return parts


def spread_targets(spread, first, tile):
    parts = [p.astype(jnp.float32) for p in parts_of(tile, 3)] + [jnp.zeros_like(tile)]
    row, lane = rows_and_lanes((4 * ROWS, 3 * LANES))
    pick = jnp.where(lax.bitwise_and(row, ROWS - 1) == lax.shift_right_logical(lane, 7), 1.0, 0.0)
    wide = lax.dot_general(
        jnp.concatenate(parts, axis=0).astype(jnp.bfloat16),
        pick.astype(jnp.bfloat16),
        (((0,), (0,)), ((), ())),
        preferred_element_type=jnp.float32,
    )
    for i in range(3):
        spread[i, first : first + LANES, :] = wide[:, i * LANES : (i + 1) * LANES]


def coefficients(target, source, force):
    delta = [t - s for t, s in zip(target, source)]
    u = (delta[0] * delta[0] + SOFT_U) + delta[1] * delta[1] + delta[2] * delta[2]
    inv = lax.rsqrt(u)
    tail = (1.0 - lax.erf(u * inv)) * inv
    gauss = jnp.exp2(LOG2_G - u * LOG2_E)
    rest = gauss * (u - 1.5)
    coef_d = ((tail - rest) - gauss) * pl.reciprocal(u, approx=True)
    along = coef_d * (delta[0] * force[0] + delta[1] * force[1] + delta[2] * force[2])
    return tail + rest, along


class Groups:
    def __init__(self, tables):
        self.tables = tables
        self.size = 0
        self.total = jnp.int32(0)

    def add(self, n_chunks, n_tiles, first_tile, spread_row, acc_row):
        for table, value in zip(self.tables, (n_chunks, n_tiles, first_tile, spread_row, acc_row)):
            table[self.size] = jnp.int32(value)
        self.size += 1
        self.total = self.total + n_chunks * n_tiles

    def run(self, listed, spread, coefs, acc):
        chunks_of, tiles_of, list_of, spread_of, acc_of = self.tables
        trash = acc.shape[1] - CHUNK

        def rows(tile_id):
            single = [listed[tile_id, i : i + 1, :] for i in (0, 1, 2, 4, 5, 6)]
            return single[:3], single[3:]

        def advance(group, chunk, tile):
            end_tile = tile + 1 == tiles_of[group]
            next_chunk = jnp.where(end_tile, chunk + CHUNK, chunk)
            end_chunk = next_chunk == chunks_of[group] * CHUNK
            next_group = jnp.where(end_chunk, jnp.minimum(group + 1, self.size - 1), group)
            return next_group, jnp.where(end_chunk, 0, next_chunk), jnp.where(end_tile, 0, tile + 1)

        def find(step, place):
            units, found = [], []
            for n in range(UNITS):
                group, chunk, tile = place
                valid = step * UNITS + n < self.total
                units += [jnp.where(valid, acc_of[group] + chunk, trash), list_of[group] + tile]
                at = pl.ds(pl.multiple_of(spread_of[group] + chunk, CHUNK), CHUNK)
                target = [spread[i, at, :] for i in range(3)]
                found.append(coefficients(target, *rows(units[-1])))
                place = advance(*place)
            return found, tuple(units), place

        def use(units):
            terms = []
            for n, tile in enumerate(units[1::2]):
                coef_c, along = coefs[n, 0], coefs[n, 1]
                source, force = rows(tile)
                terms.append([coef_c * force[i] - along * source[i] for i in range(3)] + [along])
            return terms

        def keep(found):
            for n, pair in enumerate(found):
                coefs[n, 0], coefs[n, 1] = pair

        def add(units, terms):
            for first, unit in zip(units[::2], terms):
                at = pl.ds(pl.multiple_of(first, CHUNK), CHUNK)
                for i in range(4):
                    acc[i, at, :] = acc[i, at, :] + unit[i]

        def body(step, state):
            place, olds = state[:3], state[3:]
            terms = use(olds)
            found, news, place = find(step, place)
            add(olds, terms)
            keep(found)
            return place + news

        zero = jnp.int32(0)
        found, units, place = find(0, (zero, zero, zero))
        keep(found)
        state = lax.fori_loop(1, lax.div(self.total + UNITS - 1, UNITS), body, place + units)
        add(state[3:], use(state[3:]))


def is_full(cells, count_ref):
    filled = jnp.int32(0)
    for at in bins_of(cells):
        filled = filled + count_ref[at]
    return filled, filled > FULL, filled > MANY


def list_own(cells, count_ref, own_ref, listed):
    sources = [(own_ref[at] + shift_tile(cells, at), count_ref[at]) for at in bins_of(cells)]
    compact(listed, 0, sources)


def velocity_rows(cells, group, by_row, tile):
    position = tile + shift_tile(cells, bins_of(cells)[group])
    return (2.0 * STOKES_NORM) * (by_row + position * jnp.broadcast_to(by_row[3:4], (ROWS, LANES)))


def lane_sums(sums, n_bins):
    row, lane = rows_and_lanes((2 * LANES, LANES))
    merged = jnp.zeros(sums[0].shape, jnp.float32)
    for i, part in enumerate(sums):
        merged = merged + jnp.dot(
            jnp.concatenate(parts_of(part, 2), axis=1),
            jnp.where(lax.bitwise_and(lane, ROWS - 1) == i, 1.0, 0.0).astype(jnp.bfloat16),
            preferred_element_type=jnp.float32,
        )
    _, lane = rows_and_lanes((LANES, LANES))
    chosen = merged[:LANES]
    for n in range(1, n_bins):
        chosen = jnp.where(lane >= n * ROWS, merged[n * LANES : (n + 1) * LANES], chosen)
    turned = jnp.transpose(chosen)
    return [turned[n * ROWS : (n + 1) * ROWS] for n in range(n_bins)]


def pack_kernel(cells, count_hbm, offset_hbm, force_hbm, own_ref, early_ref, *refs):
    (count_ref, offset_v, force_v, sems, listed, spread, coefs, acc), tables = refs[:8], refs[8:]
    copies = [
        pltpu.make_async_copy(source, target, sems.at[n])
        for n, (source, target) in enumerate(
            ((count_hbm, count_ref), (offset_hbm, offset_v), (force_hbm, force_v))
        )
    ]
    for copy in copies:
        copy.start()
    for copy in copies:
        copy.wait()
    slot = lax.broadcasted_iota(jnp.int32, (1, LANES), 1)
    for at in bins_of(cells):
        ix, iy, iz = at
        count = count_ref[at]
        wide = jnp.full((1, LANES), count, jnp.int32).astype(jnp.float32)
        for i in range(3):
            position = offset_v[i, ix, iy, iz : iz + 1, :]
            own_ref[ix, iy, iz, i : i + 1, :] = position * SPLIT_XI - 0.5 * SPLIT_XI
            force = force_v[i, ix, iy, iz : iz + 1, :]
            own_ref[ix, iy, iz, 4 + i : 5 + i, :] = jnp.where(slot < count, force, 0.0)
        own_ref[ix, iy, iz, 3:4, :] = wide
        own_ref[ix, iy, iz, 7:8, :] = wide
    early_ref[...] = jnp.zeros_like(early_ref)
    filled, full, _ = is_full(cells, count_ref)

    @pl.when(full)
    def _():
        list_own(cells, count_ref, own_ref, listed)
        acc[...] = jnp.zeros_like(acc)
        groups = range(EARLY)
        tiles = [own_ref[bins_of(cells)[n]] for n in groups]
        work = Groups(tables)
        for n in groups:
            at = bins_of(cells)[n]
            spread_targets(spread, n * LANES, tiles[n] + shift_tile(cells, at))
            work.add(up_to(count_ref[at], CHUNK), up_to(filled, LANES), 0, n * LANES, n * LANES)
        work.run(listed, spread, coefs, acc)
        by_rows = lane_sums([acc[i, : EARLY * LANES, :] for i in range(4)], EARLY)
        for n, by_row in enumerate(by_rows):
            early_ref[n] = velocity_rows(cells, n, by_row, tiles[n])


def counts_of(tiles):
    return [tile[COUNT_ROW, 0].astype(jnp.int32) for tile in tiles]


def first_kernel(cells, sent_ref, own_ref, listed, spread, acc, coefs, *tables):
    bins = bins_of(cells)
    count_s = counts_of([sent_ref[at] for at in bins])
    own_ref[...] = sent_ref[...]
    for n, at in enumerate(bins):
        spread_targets(spread, n * LANES, own_ref[at] + shift_tile(cells, at))
    acc[...] = jnp.zeros_like(acc)
    count_ref = {at: count_s[n] for n, at in enumerate(bins)}
    list_own(cells, count_ref, own_ref, listed)
    filled, full, many = is_full(cells, count_ref)
    work = Groups(tables)
    for m, n in enumerate(FIRST):
        n_chunks = jnp.where(many if n in FIRST_IF_MANY else full, up_to(count_ref[bins[n]], CHUNK), 0)
        work.add(n_chunks, up_to(filled, LANES), 0, n * LANES, m * LANES)
    work.run(listed, spread, coefs, acc)


def second_kernel(cells, count_ref, other, own_list, spread, first, acc, listed, coefs, *tables):
    bins = bins_of(cells)
    size_x, size_y, size_z = cells
    count_s = counts_of([other[at] for at in bins])
    for n in range(len(bins)):
        here = slice(n * LANES, (n + 1) * LANES)
        if n in FIRST:
            m = FIRST.index(n)
            acc[:, here, :] = first[:, m * LANES : (m + 1) * LANES, :]
        else:
            acc[:, here, :] = jnp.zeros((4, LANES, LANES), jnp.float32)
    n_own = own_list.shape[0]
    for n in range(n_own):
        listed[n] = own_list[n]
    filled, full, many = is_full(cells, count_ref)
    work = Groups(tables)
    for bz in range(size_z):
        z = (-1, size_z)[bz]
        sources = []
        for x in range(size_x):
            for y in range(size_y):
                place = (x, y, z % size_z)
                tile = other[place] + shift_tile(cells, (x, y, z))
                sources.append((tile, count_s[bins.index(place)]))
        first_tile = n_own + bz * LIST_Z
        n_tiles = up_to(compact(listed, first_tile, sources), LANES)
        for n, at in enumerate(bins):
            if at[2] == bz:
                work.add(up_to(count_ref[at], CHUNK), n_tiles, first_tile, n * LANES, n * LANES)
    for n in SECOND:
        n_chunks = up_to(count_ref[bins[n]], CHUNK)
        if n < EARLY or n in FIRST:
            n_chunks = jnp.where(many if n in FIRST_IF_MANY else full, 0, n_chunks)
        work.add(n_chunks, up_to(filled, LANES), 0, n * LANES, n * LANES)
    work.run(listed, spread, coefs, acc)


def middle_kernel(cells, count_ref, wide, spread, second, acc, listed, coefs, *tables):
    size_x, size_y, size_z = cells
    n_z = 2 * size_z
    bins = bins_of(cells)
    places = [(i, j, k) for i in (0, size_x + 1) for j in range(size_y) for k in range(n_z)]
    count_s = counts_of([wide[at] for at in places])
    acc[...] = second[...]
    work = Groups(tables)
    for bx in range(size_x):
        for bz in range(size_z):
            x = (-1, size_x)[bx]
            sources = []
            for y in range(size_y):
                for z in (bz - 1, bz, bz + 1):
                    place = (x + 1, y, z % n_z)
                    tile = wide[place] + shift_tile(cells, (x, y, z))
                    sources.append((tile, count_s[places.index(place)]))
            first_tile = (bx * size_z + bz) * LIST_X
            n_tiles = up_to(compact(listed, first_tile, sources), LANES)
            for n, at in enumerate(bins):
                if (at[0], at[2]) == (bx, bz):
                    work.add(up_to(count_ref[at], CHUNK), n_tiles, first_tile, n * LANES, n * LANES)
    work.run(listed, spread, coefs, acc)


def last_kernel(cells, count_ref, own_ref, y_lo, y_hi, spread, *refs):
    (middle, early, out_ref, acc, listed, coefs), tables = refs[:6], refs[6:]
    size_x, size_y, size_z = cells
    n_z = 2 * size_z
    bins = bins_of(cells)
    places = [(i, j, k) for i in range(size_x + 2) for j in range(2) for k in range(n_z)]
    tiles = [(y_lo, y_hi)[j][i, 0, k] for i, j, k in places]
    count_s = counts_of(tiles)
    acc[...] = middle[...]
    work = Groups(tables)
    for n, (bx, by, bz) in enumerate(bins):
        sources = []
        for x in (bx - 1, bx, bx + 1):
            for z in (bz - 1, bz, bz + 1):
                cell = places.index((x + 1, by, z % n_z))
                tile = tiles[cell] + shift_tile(cells, (x, (-1, size_y)[by], z))
                sources.append((tile, count_s[cell]))
        n_tiles = up_to(compact(listed, n * LIST_Y, sources), LANES)
        first_tile = n * LIST_Y
        work.add(up_to(count_ref[bx, by, bz], CHUNK), n_tiles, first_tile, n * LANES, n * LANES)
    work.run(listed, spread, coefs, acc)

    slot = lax.broadcasted_iota(jnp.int32, (1, LANES), 1)
    by_rows = lane_sums([acc[i, : len(bins) * LANES, :] for i in range(4)], len(bins))
    for n, (at, by_row) in enumerate(zip(bins, by_rows)):
        tile = own_ref[at]
        total = velocity_rows(cells, n, by_row, tile)
        total = total - (STOKES_NORM * SELF_C) * pltpu.roll(tile, ROWS - FORCE_ROW, 0)
        if n < EARLY:
            total = total + early[n]
        total = jnp.where(slot < count_ref[at], total, 0.0)
        for i in range(3):
            out_ref[i, at[0], at[1], at[2] : at[2] + 1, :] = total[i : i + 1]


def shifted(first, last, axis):
    size = lax.axis_size(axis)
    up = [(i, (i + 1) % size) for i in range(size)]
    if size % 2:
        down = [(j, i) for i, j in up]
        return lax.ppermute(last, axis, up), lax.ppermute(first, axis, down)
    odd = lax.rem(lax.axis_index(axis), 2) == 1
    got = []
    for parity in (0, 1):
        pairs = [pair for i, j in up if i % 2 == parity for pair in ((i, j), (j, i))]
        got.append(lax.ppermute(jnp.where(odd == bool(parity), last, first), axis, pairs))
    return jnp.where(odd, got[0], got[1]), jnp.where(odd, got[1], got[0])


def on_device(offsets, forces, counts):
    cells = offsets.shape[1:4]
    slots = offsets.shape[4]
    n_bins = cells[0] * cells[1] * cells[2]
    n_targets = n_bins * slots
    whole = pl.BlockSpec(memory_space=pltpu.VMEM)
    scalars = pl.BlockSpec(memory_space=pltpu.SMEM)

    def floats(*shape):
        return jax.ShapeDtypeStruct(shape, jnp.float32)

    def params(mib):
        return pltpu.CompilerParams(vmem_limit_bytes=mib << 20)

    loop_scratch = [pltpu.VMEM((UNITS, 2, CHUNK, LANES), jnp.float32)]
    loop_scratch += [pltpu.SMEM((2 * n_bins,), jnp.int32)] * 5
    cost = pl.CostEstimate(flops=1 << 28, bytes_accessed=1 << 16, transcendentals=1 << 20)

    def list_scratch(n_tiles):
        return [pltpu.VMEM((n_tiles, ROWS, LANES), jnp.float32)]

    own_list, all_targets = floats(n_bins + 1, ROWS, slots), floats(3, n_targets, slots)
    arguments = [pltpu.with_memory_space_constraint(x, pltpu.HBM) for x in (counts, offsets, forces)]
    sent, early = pl.pallas_call(
        functools.partial(pack_kernel, cells),
        out_shape=[floats(*cells, ROWS, slots), floats(EARLY, ROWS, slots)],
        in_specs=[pl.BlockSpec(memory_space=pltpu.HBM)] * 3,
        out_specs=[whole, whole],
        scratch_shapes=[
            pltpu.SMEM(counts.shape, jnp.int32),
            pltpu.VMEM(offsets.shape, jnp.float32),
            pltpu.VMEM(forces.shape, jnp.float32),
            pltpu.SemaphoreType.DMA((3,)),
            pltpu.VMEM(own_list.shape, jnp.float32),
            pltpu.VMEM((3, EARLY * slots, slots), jnp.float32),
            loop_scratch[0],
            pltpu.VMEM((4, EARLY * slots + CHUNK, slots), jnp.float32),
        ]
        + loop_scratch[1:],
        compiler_params=params(8),
        name="pack",
    )(*arguments)

    together = lax.optimization_barrier
    size = lax.axis_size("ha")
    other = lax.ppermute(sent, "ha", [(i, (i + 1) % size) for i in range(size)])
    own, listed, spread, first = pl.pallas_call(
        functools.partial(first_kernel, cells),
        out_shape=[sent, own_list, all_targets, floats(4, len(FIRST) * slots + CHUNK, slots)],
        in_specs=[whole],
        out_specs=[whole] * 4,
        scratch_shapes=loop_scratch,
        compiler_params=params(8),
        cost_estimate=cost,
        name="first",
    )(sent)
    other, own, listed, first = together((other, own, listed, first))
    column = jnp.concatenate([own, other], axis=2)
    x_lo, x_hi = shifted(column[:1], column[cells[0] - 1 :], "gx")
    second = pl.pallas_call(
        functools.partial(second_kernel, cells),
        out_shape=floats(4, n_targets + CHUNK, slots),
        in_specs=[scalars] + [whole] * 4,
        out_specs=whole,
        scratch_shapes=list_scratch(cells[2] * LIST_Z + n_bins + 1)
        + loop_scratch,
        compiler_params=params(8),
        cost_estimate=cost,
        name="second",
    )(counts, other, listed, spread, first)
    x_hi, x_lo, second = together((x_hi, x_lo, second))
    wide = jnp.concatenate([x_lo, column, x_hi], axis=0)
    y_lo, y_hi = shifted(wide[:, :1], wide[:, cells[1] - 1 :], "gy")
    middle = pl.pallas_call(
        functools.partial(middle_kernel, cells),
        out_shape=floats(4, n_targets + CHUNK, slots),
        in_specs=[scalars] + [whole] * 3,
        out_specs=whole,
        scratch_shapes=list_scratch(cells[0] * cells[2] * LIST_X) + loop_scratch,
        compiler_params=params(8),
        cost_estimate=cost,
        name="middle",
    )(counts, wide, spread, second)
    y_lo, y_hi, middle = together((y_lo, y_hi, middle))
    return pl.pallas_call(
        functools.partial(last_kernel, cells),
        out_shape=floats(3, *cells, slots),
        in_specs=[scalars] + [whole] * 6,
        out_specs=whole,
        scratch_shapes=[pltpu.VMEM((4, n_targets + CHUNK, slots), jnp.float32)]
        + list_scratch(n_bins * LIST_Y)
        + loop_scratch,
        compiler_params=params(12),
        cost_estimate=cost,
        name="last",
    )(counts, own, y_lo, y_hi, spread, middle, early)


def solution(mesh):
    in_specs = (
        P(None, "gx", "gy", "ha", None),
        P(None, "gx", "gy", "ha", None),
        P("gx", "gy", "ha"),
    )
    out_specs = P(None, "gx", "gy", "ha", None)
    return jax.shard_map(on_device, mesh=mesh, in_specs=in_specs, out_specs=out_specs, check_vma=False)
```

```python
import functools
import math

import jax
import jax.numpy as jnp
from jax import lax
from jax.experimental import pallas as pl
from jax.experimental.pallas import tpu as pltpu
from jax.sharding import PartitionSpec as P

SPLIT_XI = 2.0
SOFT_SQ = 0.01
GAUSS_COEF = 2.0 * SPLIT_XI / math.sqrt(math.pi)
STOKES_NORM = 1.0 / (8.0 * math.pi)

SOFT_U = SPLIT_XI * SPLIT_XI * SOFT_SQ
LOG2_E = math.log2(math.e)
LOG2_G = math.log2(GAUSS_COEF)
SELF_C = math.erfc(math.sqrt(SOFT_U)) / math.sqrt(SOFT_SQ) + GAUSS_COEF * (
    2.0 * SOFT_U - 3.0
) * math.exp(-SOFT_U)

LANES = 128
ROWS = 8
CHUNK = 16
UNITS = 16
COUNT_ROW = 3
FULL = 700
MANY = 440
EARLY = 3
FIRST = (3, 4, 5)
SECOND = (6, 7, 5, 0, 1, 2, 3, 4)
FIRST_IF_MANY = (3, 4)
LIST_Z, LIST_X, LIST_Y = 5, 7, 10
FORCE_ROW = 4


def rows_and_lanes(shape=(ROWS, LANES)):
    return lax.broadcasted_iota(jnp.int32, shape, 0), lax.broadcasted_iota(jnp.int32, shape, 1)


def bins_of(cells):
    return [(i, j, k) for i in range(cells[0]) for j in range(cells[1]) for k in range(cells[2])]


def shift_tile(cells, at):
    row, _ = rows_and_lanes()
    moved = jnp.zeros((ROWS, LANES), jnp.float32)
    for i in range(3):
        moved = jnp.where(row == i, SPLIT_XI * (at[i] - 0.5 * (cells[i] - 1)), moved)
    return moved


def compact(listed, base, sources):
    _, lane = rows_and_lanes()
    filled = jnp.int32(0)
    moved = []
    for tile, count in sources:
        at = lax.bitwise_and(filled, LANES - 1)
        tile_id = base + lax.shift_right_logical(filled, 7)
        moved.append((pltpu.roll(tile, at, 1), lane >= at, tile_id, at + count >= LANES))
        filled = filled + count
    current = jnp.zeros((ROWS, LANES), jnp.float32)
    for tile, behind, tile_id, full in moved:
        current = jnp.where(behind, tile, current)
        spill = jnp.where(behind, 0.0, tile)
        listed[tile_id] = current
        listed[tile_id + 1] = spill
        current = jnp.where(full, spill, current)
    return filled


def up_to(count, size):
    return lax.shift_right_logical(count + (size - 1), size.bit_length() - 1)


def parts_of(value, n):
    parts = []
    for _ in range(n):
        part = value.astype(jnp.bfloat16)
        value = value - part.astype(jnp.float32)
        parts.append(part)
    return parts


def spread_targets(spread, first, tile):
    parts = [p.astype(jnp.float32) for p in parts_of(tile, 3)] + [jnp.zeros_like(tile)]
    row, lane = rows_and_lanes((4 * ROWS, 3 * LANES))
    pick = jnp.where(lax.bitwise_and(row, ROWS - 1) == lax.shift_right_logical(lane, 7), 1.0, 0.0)
    wide = lax.dot_general(
        jnp.concatenate(parts, axis=0).astype(jnp.bfloat16),
        pick.astype(jnp.bfloat16),
        (((0,), (0,)), ((), ())),
        preferred_element_type=jnp.float32,
    )
    for i in range(3):
        spread[i, first : first + LANES, :] = wide[:, i * LANES : (i + 1) * LANES]


def coefficients(target, source, force):
    delta = [t - s for t, s in zip(target, source)]
    u = (delta[0] * delta[0] + SOFT_U) + delta[1] * delta[1] + delta[2] * delta[2]
    inv = lax.rsqrt(u)
    tail = (1.0 - lax.erf(u * inv)) * inv
    gauss = jnp.exp2(LOG2_G - u * LOG2_E)
    rest = gauss * (u - 1.5)
    coef_d = ((tail - rest) - gauss) * pl.reciprocal(u, approx=True)
    along = coef_d * (delta[0] * force[0] + delta[1] * force[1] + delta[2] * force[2])
    return tail + rest, along


class Groups:
    def __init__(self, tables):
        self.tables = tables
        self.size = 0
        self.total = jnp.int32(0)

    def add(self, n_chunks, n_tiles, first_tile, spread_row, acc_row):
        for table, value in zip(self.tables, (n_chunks, n_tiles, first_tile, spread_row, acc_row)):
            table[self.size] = jnp.int32(value)
        self.size += 1
        self.total = self.total + n_chunks * n_tiles

    def run(self, listed, spread, coefs, acc):
        chunks_of, tiles_of, list_of, spread_of, acc_of = self.tables
        trash = acc.shape[1] - CHUNK

        def rows(tile_id):
            single = [listed[tile_id, i : i + 1, :] for i in (0, 1, 2, 4, 5, 6)]
            return single[:3], single[3:]

        def advance(group, chunk, tile):
            end_tile = tile + 1 == tiles_of[group]
            next_chunk = jnp.where(end_tile, chunk + CHUNK, chunk)
            end_chunk = next_chunk == chunks_of[group] * CHUNK
            next_group = jnp.where(end_chunk, jnp.minimum(group + 1, self.size - 1), group)
            return next_group, jnp.where(end_chunk, 0, next_chunk), jnp.where(end_tile, 0, tile + 1)

        def find(step, place):
            units, found = [], []
            for n in range(UNITS):
                group, chunk, tile = place
                valid = step * UNITS + n < self.total
                units += [jnp.where(valid, acc_of[group] + chunk, trash), list_of[group] + tile]
                at = pl.ds(pl.multiple_of(spread_of[group] + chunk, CHUNK), CHUNK)
                target = [spread[i, at, :] for i in range(3)]
                found.append(coefficients(target, *rows(units[-1])))
                place = advance(*place)
            return found, tuple(units), place

        def use(units):
            terms = []
            for n, tile in enumerate(units[1::2]):
                coef_c, along = coefs[n, 0], coefs[n, 1]
                source, force = rows(tile)
                terms.append([coef_c * force[i] - along * source[i] for i in range(3)] + [along])
            return terms

        def keep(found):
            for n, pair in enumerate(found):
                coefs[n, 0], coefs[n, 1] = pair

        def add(units, terms):
            for first, unit in zip(units[::2], terms):
                at = pl.ds(pl.multiple_of(first, CHUNK), CHUNK)
                for i in range(4):
                    acc[i, at, :] = acc[i, at, :] + unit[i]

        def body(step, state):
            place, olds = state[:3], state[3:]
            terms = use(olds)
            found, news, place = find(step, place)
            add(olds, terms)
            keep(found)
            return place + news

        zero = jnp.int32(0)
        found, units, place = find(0, (zero, zero, zero))
        keep(found)
        state = lax.fori_loop(1, lax.div(self.total + UNITS - 1, UNITS), body, place + units)
        add(state[3:], use(state[3:]))


def is_full(cells, count_ref):
    filled = jnp.int32(0)
    for at in bins_of(cells):
        filled = filled + count_ref[at]
    return filled, filled > FULL, filled > MANY


def list_own(cells, count_ref, own_ref, listed):
    sources = [(own_ref[at] + shift_tile(cells, at), count_ref[at]) for at in bins_of(cells)]
    compact(listed, 0, sources)


def velocity_rows(cells, group, by_row, tile):
    position = tile + shift_tile(cells, bins_of(cells)[group])
    return (2.0 * STOKES_NORM) * (by_row + position * jnp.broadcast_to(by_row[3:4], (ROWS, LANES)))


def lane_sums(sums, n_bins):
    row, lane = rows_and_lanes((2 * LANES, LANES))
    merged = jnp.zeros(sums[0].shape, jnp.float32)
    for i, part in enumerate(sums):
        merged = merged + jnp.dot(
            jnp.concatenate(parts_of(part, 2), axis=1),
            jnp.where(lax.bitwise_and(lane, ROWS - 1) == i, 1.0, 0.0).astype(jnp.bfloat16),
            preferred_element_type=jnp.float32,
        )
    _, lane = rows_and_lanes((LANES, LANES))
    chosen = merged[:LANES]
    for n in range(1, n_bins):
        chosen = jnp.where(lane >= n * ROWS, merged[n * LANES : (n + 1) * LANES], chosen)
    turned = jnp.transpose(chosen)
    return [turned[n * ROWS : (n + 1) * ROWS] for n in range(n_bins)]


def pack_kernel(cells, count_hbm, offset_hbm, force_hbm, own_ref, early_ref, *refs):
    (count_ref, offset_v, force_v, sems, listed, spread, coefs, acc), tables = refs[:8], refs[8:]
    copies = [
        pltpu.make_async_copy(source, target, sems.at[n])
        for n, (source, target) in enumerate(
            ((count_hbm, count_ref), (offset_hbm, offset_v), (force_hbm, force_v))
        )
    ]
    for copy in copies:
        copy.start()
    for copy in copies:
        copy.wait()
    slot = lax.broadcasted_iota(jnp.int32, (1, LANES), 1)
    for at in bins_of(cells):
        ix, iy, iz = at
        count = count_ref[at]
        wide = jnp.full((1, LANES), count, jnp.int32).astype(jnp.float32)
        for i in range(3):
            position = offset_v[i, ix, iy, iz : iz + 1, :]
            own_ref[ix, iy, iz, i : i + 1, :] = position * SPLIT_XI - 0.5 * SPLIT_XI
            force = force_v[i, ix, iy, iz : iz + 1, :]
            own_ref[ix, iy, iz, 4 + i : 5 + i, :] = jnp.where(slot < count, force, 0.0)
        own_ref[ix, iy, iz, 3:4, :] = wide
        own_ref[ix, iy, iz, 7:8, :] = wide
    early_ref[...] = jnp.zeros_like(early_ref)
    filled, full, _ = is_full(cells, count_ref)

    @pl.when(full)
    def _():
        list_own(cells, count_ref, own_ref, listed)
        acc[...] = jnp.zeros_like(acc)
        groups = range(EARLY)
        tiles = [own_ref[bins_of(cells)[n]] for n in groups]
        work = Groups(tables)
        for n in groups:
            at = bins_of(cells)[n]
            spread_targets(spread, n * LANES, tiles[n] + shift_tile(cells, at))
            work.add(up_to(count_ref[at], CHUNK), up_to(filled, LANES), 0, n * LANES, n * LANES)
        work.run(listed, spread, coefs, acc)
        by_rows = lane_sums([acc[i, : EARLY * LANES, :] for i in range(4)], EARLY)
        for n, by_row in enumerate(by_rows):
            early_ref[n] = velocity_rows(cells, n, by_row, tiles[n])


def counts_of(tiles):
    return [tile[COUNT_ROW, 0].astype(jnp.int32) for tile in tiles]


def first_kernel(cells, sent_ref, own_ref, listed, spread, acc, coefs, *tables):
    bins = bins_of(cells)
    count_s = counts_of([sent_ref[at] for at in bins])
    own_ref[...] = sent_ref[...]
    for n, at in enumerate(bins):
        spread_targets(spread, n * LANES, own_ref[at] + shift_tile(cells, at))
    acc[...] = jnp.zeros_like(acc)
    count_ref = {at: count_s[n] for n, at in enumerate(bins)}
    list_own(cells, count_ref, own_ref, listed)
    filled, full, many = is_full(cells, count_ref)
    work = Groups(tables)
    for m, n in enumerate(FIRST):
        n_chunks = jnp.where(many if n in FIRST_IF_MANY else full, up_to(count_ref[bins[n]], CHUNK), 0)
        work.add(n_chunks, up_to(filled, LANES), 0, n * LANES, m * LANES)
    work.run(listed, spread, coefs, acc)


def second_kernel(cells, count_ref, other, own_list, spread, first, acc, listed, coefs, *tables):
    bins = bins_of(cells)
    size_x, size_y, size_z = cells
    count_s = counts_of([other[at] for at in bins])
    for n in range(len(bins)):
        here = slice(n * LANES, (n + 1) * LANES)
        if n in FIRST:
            m = FIRST.index(n)
            acc[:, here, :] = first[:, m * LANES : (m + 1) * LANES, :]
        else:
            acc[:, here, :] = jnp.zeros((4, LANES, LANES), jnp.float32)
    n_own = own_list.shape[0]
    for n in range(n_own):
        listed[n] = own_list[n]
    filled, full, many = is_full(cells, count_ref)
    work = Groups(tables)
    for bz in range(size_z):
        z = (-1, size_z)[bz]
        sources = []
        for x in range(size_x):
            for y in range(size_y):
                place = (x, y, z % size_z)
                tile = other[place] + shift_tile(cells, (x, y, z))
                sources.append((tile, count_s[bins.index(place)]))
        first_tile = n_own + bz * LIST_Z
        n_tiles = up_to(compact(listed, first_tile, sources), LANES)
        for n, at in enumerate(bins):
            if at[2] == bz:
                work.add(up_to(count_ref[at], CHUNK), n_tiles, first_tile, n * LANES, n * LANES)
    for n in SECOND:
        n_chunks = up_to(count_ref[bins[n]], CHUNK)
        if n < EARLY or n in FIRST:
            n_chunks = jnp.where(many if n in FIRST_IF_MANY else full, 0, n_chunks)
        work.add(n_chunks, up_to(filled, LANES), 0, n * LANES, n * LANES)
    work.run(listed, spread, coefs, acc)


def middle_kernel(cells, count_ref, wide, spread, second, acc, listed, coefs, *tables):
    size_x, size_y, size_z = cells
    n_z = 2 * size_z
    bins = bins_of(cells)
    places = [(i, j, k) for i in (0, size_x + 1) for j in range(size_y) for k in range(n_z)]
    count_s = counts_of([wide[at] for at in places])
    acc[...] = second[...]
    work = Groups(tables)
    for bx in range(size_x):
        for bz in range(size_z):
            x = (-1, size_x)[bx]
            sources = []
            for y in range(size_y):
                for z in (bz - 1, bz, bz + 1):
                    place = (x + 1, y, z % n_z)
                    tile = wide[place] + shift_tile(cells, (x, y, z))
                    sources.append((tile, count_s[places.index(place)]))
            first_tile = (bx * size_z + bz) * LIST_X
            n_tiles = up_to(compact(listed, first_tile, sources), LANES)
            for n, at in enumerate(bins):
                if (at[0], at[2]) == (bx, bz):
                    work.add(up_to(count_ref[at], CHUNK), n_tiles, first_tile, n * LANES, n * LANES)
    work.run(listed, spread, coefs, acc)


def last_kernel(cells, count_ref, own_ref, y_lo, y_hi, spread, *refs):
    (middle, early, out_ref, acc, listed, coefs), tables = refs[:6], refs[6:]
    size_x, size_y, size_z = cells
    n_z = 2 * size_z
    bins = bins_of(cells)
    places = [(i, j, k) for i in range(size_x + 2) for j in range(2) for k in range(n_z)]
    tiles = [(y_lo, y_hi)[j][i, 0, k] for i, j, k in places]
    count_s = counts_of(tiles)
    acc[...] = middle[...]
    work = Groups(tables)
    for n, (bx, by, bz) in enumerate(bins):
        sources = []
        for x in (bx - 1, bx, bx + 1):
            for z in (bz - 1, bz, bz + 1):
                cell = places.index((x + 1, by, z % n_z))
                tile = tiles[cell] + shift_tile(cells, (x, (-1, size_y)[by], z))
                sources.append((tile, count_s[cell]))
        n_tiles = up_to(compact(listed, n * LIST_Y, sources), LANES)
        first_tile = n * LIST_Y
        work.add(up_to(count_ref[bx, by, bz], CHUNK), n_tiles, first_tile, n * LANES, n * LANES)
    work.run(listed, spread, coefs, acc)

    slot = lax.broadcasted_iota(jnp.int32, (1, LANES), 1)
    by_rows = lane_sums([acc[i, : len(bins) * LANES, :] for i in range(4)], len(bins))
    for n, (at, by_row) in enumerate(zip(bins, by_rows)):
        tile = own_ref[at]
        total = velocity_rows(cells, n, by_row, tile)
        total = total - (STOKES_NORM * SELF_C) * pltpu.roll(tile, ROWS - FORCE_ROW, 0)
        if n < EARLY:
            total = total + early[n]
        total = jnp.where(slot < count_ref[at], total, 0.0)
        for i in range(3):
            out_ref[i, at[0], at[1], at[2] : at[2] + 1, :] = total[i : i + 1]


def shifted(first, last, axis):
    size = lax.axis_size(axis)
    up = [(i, (i + 1) % size) for i in range(size)]
    if size % 2:
        down = [(j, i) for i, j in up]
        return lax.ppermute(last, axis, up), lax.ppermute(first, axis, down)
    odd = lax.rem(lax.axis_index(axis), 2) == 1
    got = []
    for parity in (0, 1):
        pairs = [pair for i, j in up if i % 2 == parity for pair in ((i, j), (j, i))]
        got.append(lax.ppermute(jnp.where(odd == bool(parity), last, first), axis, pairs))
    return jnp.where(odd, got[0], got[1]), jnp.where(odd, got[1], got[0])


def on_device(offsets, forces, counts):
    cells = offsets.shape[1:4]
    slots = offsets.shape[4]
    n_bins = cells[0] * cells[1] * cells[2]
    n_targets = n_bins * slots
    whole = pl.BlockSpec(memory_space=pltpu.VMEM)
    scalars = pl.BlockSpec(memory_space=pltpu.SMEM)

    def floats(*shape):
        return jax.ShapeDtypeStruct(shape, jnp.float32)

    def params(mib):
        return pltpu.CompilerParams(vmem_limit_bytes=mib << 20)

    loop_scratch = [pltpu.VMEM((UNITS, 2, CHUNK, LANES), jnp.float32)]
    loop_scratch += [pltpu.SMEM((2 * n_bins,), jnp.int32)] * 5
    cost = pl.CostEstimate(flops=1 << 28, bytes_accessed=1 << 16, transcendentals=1 << 20)

    def list_scratch(n_tiles):
        return [pltpu.VMEM((n_tiles, ROWS, LANES), jnp.float32)]

    own_list, all_targets = floats(n_bins + 1, ROWS, slots), floats(3, n_targets, slots)
    arguments = [pltpu.with_memory_space_constraint(x, pltpu.HBM) for x in (counts, offsets, forces)]
    sent, early = pl.pallas_call(
        functools.partial(pack_kernel, cells),
        out_shape=[floats(*cells, ROWS, slots), floats(EARLY, ROWS, slots)],
        in_specs=[pl.BlockSpec(memory_space=pltpu.HBM)] * 3,
        out_specs=[whole, whole],
        scratch_shapes=[
            pltpu.SMEM(counts.shape, jnp.int32),
            pltpu.VMEM(offsets.shape, jnp.float32),
            pltpu.VMEM(forces.shape, jnp.float32),
            pltpu.SemaphoreType.DMA((3,)),
            pltpu.VMEM(own_list.shape, jnp.float32),
            pltpu.VMEM((3, EARLY * slots, slots), jnp.float32),
            loop_scratch[0],
            pltpu.VMEM((4, EARLY * slots + CHUNK, slots), jnp.float32),
        ]
        + loop_scratch[1:],
        compiler_params=params(8),
        name="pack",
    )(*arguments)

    together = lax.optimization_barrier
    size = lax.axis_size("ha")
    other = lax.ppermute(sent, "ha", [(i, (i + 1) % size) for i in range(size)])
    own, listed, spread, first = pl.pallas_call(
        functools.partial(first_kernel, cells),
        out_shape=[sent, own_list, all_targets, floats(4, len(FIRST) * slots + CHUNK, slots)],
        in_specs=[whole],
        out_specs=[whole] * 4,
        scratch_shapes=loop_scratch,
        compiler_params=params(8),
        cost_estimate=cost,
        name="first",
    )(sent)
    other, own, listed, first = together((other, own, listed, first))
    column = jnp.concatenate([own, other], axis=2)
    x_lo, x_hi = shifted(column[:1], column[cells[0] - 1 :], "gx")
    second = pl.pallas_call(
        functools.partial(second_kernel, cells),
        out_shape=floats(4, n_targets + CHUNK, slots),
        in_specs=[scalars] + [whole] * 4,
        out_specs=whole,
        scratch_shapes=list_scratch(cells[2] * LIST_Z + n_bins + 1)
        + loop_scratch,
        compiler_params=params(8),
        cost_estimate=cost,
        name="second",
    )(counts, other, listed, spread, first)
    x_hi, x_lo, second = together((x_hi, x_lo, second))
    wide = jnp.concatenate([x_lo, column, x_hi], axis=0)
    y_lo, y_hi = shifted(wide[:, :1], wide[:, cells[1] - 1 :], "gy")
    middle = pl.pallas_call(
        functools.partial(middle_kernel, cells),
        out_shape=floats(4, n_targets + CHUNK, slots),
        in_specs=[scalars] + [whole] * 3,
        out_specs=whole,
        scratch_shapes=list_scratch(cells[0] * cells[2] * LIST_X) + loop_scratch,
        compiler_params=params(8),
        cost_estimate=cost,
        name="middle",
    )(counts, wide, spread, second)
    y_lo, y_hi, middle = together((y_lo, y_hi, middle))
    return pl.pallas_call(
        functools.partial(last_kernel, cells),
        out_shape=floats(3, *cells, slots),
        in_specs=[scalars] + [whole] * 6,
        out_specs=whole,
        scratch_shapes=[pltpu.VMEM((4, n_targets + CHUNK, slots), jnp.float32)]
        + list_scratch(n_bins * LIST_Y)
        + loop_scratch,
        compiler_params=params(12),
        cost_estimate=cost,
        name="last",
    )(counts, own, y_lo, y_hi, spread, middle, early)


def solution(mesh):
    in_specs = (
        P(None, "gx", "gy", "ha", None),
        P(None, "gx", "gy", "ha", None),
        P("gx", "gy", "ha"),
    )
    out_specs = P(None, "gx", "gy", "ha", None)
    return jax.shard_map(on_device, mesh=mesh, in_specs=in_specs, out_specs=out_specs, check_vma=False)
```

```python
import functools
import math

import jax
import jax.numpy as jnp
from jax import lax
from jax.experimental import pallas as pl
from jax.experimental.pallas import tpu as pltpu
from jax.sharding import PartitionSpec as P

SPLIT_XI = 2.0
SOFT_SQ = 0.01
GAUSS_COEF = 2.0 * SPLIT_XI / math.sqrt(math.pi)
STOKES_NORM = 1.0 / (8.0 * math.pi)

SOFT_U = SPLIT_XI * SPLIT_XI * SOFT_SQ
LOG2_E = math.log2(math.e)
LOG2_G = math.log2(GAUSS_COEF)
SELF_C = math.erfc(math.sqrt(SOFT_U)) / math.sqrt(SOFT_SQ) + GAUSS_COEF * (
    2.0 * SOFT_U - 3.0
) * math.exp(-SOFT_U)

LANES = 128
ROWS = 8
CHUNK = 32
UNITS = 8
COUNT_ROW = 3
FULL = 700
MANY = 440
EARLY = 3
FIRST = (3, 4, 5)
SECOND = (6, 7, 5, 0, 1, 2, 3, 4)
FIRST_IF_MANY = (3, 4)
LIST_Z, LIST_X, LIST_Y = 5, 7, 10
FORCE_ROW = 4


def rows_and_lanes(shape=(ROWS, LANES)):
    return lax.broadcasted_iota(jnp.int32, shape, 0), lax.broadcasted_iota(jnp.int32, shape, 1)


def bins_of(cells):
    return [(i, j, k) for i in range(cells[0]) for j in range(cells[1]) for k in range(cells[2])]


def shift_tile(cells, at):
    row, _ = rows_and_lanes()
    moved = jnp.zeros((ROWS, LANES), jnp.float32)
    for i in range(3):
        moved = jnp.where(row == i, SPLIT_XI * (at[i] - 0.5 * (cells[i] - 1)), moved)
    return moved


def compact(listed, base, sources):
    _, lane = rows_and_lanes()
    filled = jnp.int32(0)
    moved = []
    for tile, count in sources:
        at = lax.bitwise_and(filled, LANES - 1)
        tile_id = base + lax.shift_right_logical(filled, 7)
        moved.append((pltpu.roll(tile, at, 1), lane >= at, tile_id, at + count >= LANES))
        filled = filled + count
    current = jnp.zeros((ROWS, LANES), jnp.float32)
    for tile, behind, tile_id, full in moved:
        current = jnp.where(behind, tile, current)
        spill = jnp.where(behind, 0.0, tile)
        listed[tile_id] = current
        listed[tile_id + 1] = spill
        current = jnp.where(full, spill, current)
    return filled


def up_to(count, size):
    return lax.shift_right_logical(count + (size - 1), size.bit_length() - 1)


def parts_of(value, n):
    parts = []
    for _ in range(n):
        part = value.astype(jnp.bfloat16)
        value = value - part.astype(jnp.float32)
        parts.append(part)
    return parts


def spread_targets(spread, first, tile):
    parts = [p.astype(jnp.float32) for p in parts_of(tile, 3)] + [jnp.zeros_like(tile)]
    row, lane = rows_and_lanes((4 * ROWS, 3 * LANES))
    pick = jnp.where(lax.bitwise_and(row, ROWS - 1) == lax.shift_right_logical(lane, 7), 1.0, 0.0)
    wide = lax.dot_general(
        jnp.concatenate(parts, axis=0).astype(jnp.bfloat16),
        pick.astype(jnp.bfloat16),
        (((0,), (0,)), ((), ())),
        preferred_element_type=jnp.float32,
    )
    for i in range(3):
        spread[i, first : first + LANES, :] = wide[:, i * LANES : (i + 1) * LANES]


def separations(target, source, force):
    delta = [t - s for t, s in zip(target, source)]
    u = (delta[0] * delta[0] + SOFT_U) + delta[1] * delta[1] + delta[2] * delta[2]
    return u, delta[0] * force[0] + delta[1] * force[1] + delta[2] * force[2]


def coefficients(u, dot):
    inv = lax.rsqrt(u)
    tail = (1.0 - lax.erf(u * inv)) * inv
    gauss = jnp.exp2(LOG2_G - u * LOG2_E)
    rest = gauss * (u - 1.5)
    coef_d = ((tail - rest) - gauss) * pl.reciprocal(u, approx=True)
    return tail + rest, coef_d * dot


class Groups:
    def __init__(self, tables):
        self.tables = tables
        self.size = 0
        self.total = jnp.int32(0)

    def add(self, n_chunks, n_tiles, first_tile, spread_row, acc_row):
        for table, value in zip(self.tables, (n_chunks, n_tiles, first_tile, spread_row, acc_row)):
            table[self.size] = jnp.int32(value)
        self.size += 1
        self.total = self.total + n_chunks * n_tiles

    def run(self, listed, spread, coefs, acc):
        chunks_of, tiles_of, list_of, spread_of, acc_of = self.tables
        trash = acc.shape[1] - CHUNK

        def rows(tile_id):
            single = [listed[tile_id, i : i + 1, :] for i in (0, 1, 2, 4, 5, 6)]
            return single[:3], single[3:]

        def advance(group, chunk, tile):
            end_tile = tile + 1 == tiles_of[group]
            next_chunk = jnp.where(end_tile, chunk + CHUNK, chunk)
            end_chunk = next_chunk == chunks_of[group] * CHUNK
            next_group = jnp.where(end_chunk, jnp.minimum(group + 1, self.size - 1), group)
            return next_group, jnp.where(end_chunk, 0, next_chunk), jnp.where(end_tile, 0, tile + 1)

        def find(step, place):
            units, found = [], []
            for n in range(UNITS):
                group, chunk, tile = place
                valid = step * UNITS + n < self.total
                units += [jnp.where(valid, acc_of[group] + chunk, trash), list_of[group] + tile]
                at = pl.ds(pl.multiple_of(spread_of[group] + chunk, CHUNK), CHUNK)
                target = [spread[i, at, :] for i in range(3)]
                found.append(separations(target, *rows(units[-1])))
                place = advance(*place)
            return found, tuple(units), place

        def weigh():
            return [coefficients(coefs[n, 0], coefs[n, 1]) for n in range(UNITS)]

        def use(units):
            terms = []
            for n, tile in enumerate(units[1::2]):
                coef_c, along = coefs[n, 2], coefs[n, 3]
                source, force = rows(tile)
                terms.append([coef_c * force[i] - along * source[i] for i in range(3)] + [along])
            return terms

        def keep(pairs, at):
            for n, pair in enumerate(pairs):
                coefs[n, at], coefs[n, at + 1] = pair

        def add(units, terms):
            for first, unit in zip(units[::2], terms):
                at = pl.ds(pl.multiple_of(first, CHUNK), CHUNK)
                for i in range(4):
                    acc[i, at, :] = acc[i, at, :] + unit[i]

        def body(step, state):
            place, middle, old = state[:3], state[3 : 3 + 2 * UNITS], state[3 + 2 * UNITS :]
            terms = use(old)
            weighed = weigh()
            found, new, place = find(step, place)
            add(old, terms)
            keep(weighed, 2)
            keep(found, 0)
            return place + new + middle

        zero = jnp.int32(0)
        found, old, place = find(0, (zero, zero, zero))
        keep(found, 0)
        weighed = weigh()
        found, new, place = find(1, place)
        keep(weighed, 2)
        keep(found, 0)
        steps = lax.shift_right_logical(self.total + (UNITS - 1), UNITS.bit_length() - 1)
        state = lax.fori_loop(2, steps, body, place + new + old)
        middle, old = state[3 : 3 + 2 * UNITS], state[3 + 2 * UNITS :]
        terms = use(old)
        weighed = weigh()
        add(old, terms)
        keep(weighed, 2)
        add(middle, use(middle))


def is_full(cells, count_ref):
    filled = jnp.int32(0)
    for at in bins_of(cells):
        filled = filled + count_ref[at]
    return filled, filled > FULL, filled > MANY


def list_own(cells, count_ref, own_ref, listed):
    sources = [(own_ref[at] + shift_tile(cells, at), count_ref[at]) for at in bins_of(cells)]
    compact(listed, 0, sources)


def velocity_rows(cells, group, by_row, tile):
    position = tile + shift_tile(cells, bins_of(cells)[group])
    return (2.0 * STOKES_NORM) * (by_row + position * jnp.broadcast_to(by_row[3:4], (ROWS, LANES)))


def lane_sums(sums, n_bins):
    row, lane = rows_and_lanes((2 * LANES, LANES))
    merged = jnp.zeros(sums[0].shape, jnp.float32)
    for i, part in enumerate(sums):
        merged = merged + jnp.dot(
            jnp.concatenate(parts_of(part, 2), axis=1),
            jnp.where(lax.bitwise_and(lane, ROWS - 1) == i, 1.0, 0.0).astype(jnp.bfloat16),
            preferred_element_type=jnp.float32,
        )
    _, lane = rows_and_lanes((LANES, LANES))
    chosen = merged[:LANES]
    for n in range(1, n_bins):
        chosen = jnp.where(lane >= n * ROWS, merged[n * LANES : (n + 1) * LANES], chosen)
    turned = jnp.transpose(chosen)
    return [turned[n * ROWS : (n + 1) * ROWS] for n in range(n_bins)]


def pack_kernel(cells, count_hbm, offset_hbm, force_hbm, own_ref, early_ref, *refs):
    (count_ref, offset_v, force_v, sems, listed, spread, coefs, acc), tables = refs[:8], refs[8:]
    copies = [
        pltpu.make_async_copy(source, target, sems.at[n])
        for n, (source, target) in enumerate(
            ((count_hbm, count_ref), (offset_hbm, offset_v), (force_hbm, force_v))
        )
    ]
    for copy in copies:
        copy.start()
    for copy in copies:
        copy.wait()
    slot = lax.broadcasted_iota(jnp.int32, (1, LANES), 1)
    for at in bins_of(cells):
        ix, iy, iz = at
        count = count_ref[at]
        wide = jnp.full((1, LANES), count, jnp.int32).astype(jnp.float32)
        for i in range(3):
            position = offset_v[i, ix, iy, iz : iz + 1, :]
            own_ref[ix, iy, iz, i : i + 1, :] = position * SPLIT_XI - 0.5 * SPLIT_XI
            force = force_v[i, ix, iy, iz : iz + 1, :]
            own_ref[ix, iy, iz, 4 + i : 5 + i, :] = jnp.where(slot < count, force, 0.0)
        own_ref[ix, iy, iz, 3:4, :] = wide
        own_ref[ix, iy, iz, 7:8, :] = wide
    early_ref[...] = jnp.zeros_like(early_ref)
    filled, full, _ = is_full(cells, count_ref)

    @pl.when(full)
    def _():
        list_own(cells, count_ref, own_ref, listed)
        acc[...] = jnp.zeros_like(acc)
        groups = range(EARLY)
        tiles = [own_ref[bins_of(cells)[n]] for n in groups]
        work = Groups(tables)
        for n in groups:
            at = bins_of(cells)[n]
            spread_targets(spread, n * LANES, tiles[n] + shift_tile(cells, at))
            work.add(up_to(count_ref[at], CHUNK), up_to(filled, LANES), 0, n * LANES, n * LANES)
        work.run(listed, spread, coefs, acc)
        by_rows = lane_sums([acc[i, : EARLY * LANES, :] for i in range(4)], EARLY)
        for n, by_row in enumerate(by_rows):
            early_ref[n] = velocity_rows(cells, n, by_row, tiles[n])


def counts_of(tiles):
    return [tile[COUNT_ROW, 0].astype(jnp.int32) for tile in tiles]


def first_kernel(cells, sent_ref, own_ref, listed, spread, acc, coefs, *tables):
    bins = bins_of(cells)
    count_s = counts_of([sent_ref[at] for at in bins])
    own_ref[...] = sent_ref[...]
    for n, at in enumerate(bins):
        spread_targets(spread, n * LANES, own_ref[at] + shift_tile(cells, at))
    acc[...] = jnp.zeros_like(acc)
    count_ref = {at: count_s[n] for n, at in enumerate(bins)}
    list_own(cells, count_ref, own_ref, listed)
    filled, full, many = is_full(cells, count_ref)
    work = Groups(tables)
    for m, n in enumerate(FIRST):
        n_chunks = jnp.where(many if n in FIRST_IF_MANY else full, up_to(count_ref[bins[n]], CHUNK), 0)
        work.add(n_chunks, up_to(filled, LANES), 0, n * LANES, m * LANES)
    work.run(listed, spread, coefs, acc)


def second_kernel(cells, count_ref, other, own_list, spread, first, acc, listed, coefs, *tables):
    bins = bins_of(cells)
    size_x, size_y, size_z = cells
    count_s = counts_of([other[at] for at in bins])
    for n in range(len(bins)):
        here = slice(n * LANES, (n + 1) * LANES)
        if n in FIRST:
            m = FIRST.index(n)
            acc[:, here, :] = first[:, m * LANES : (m + 1) * LANES, :]
        else:
            acc[:, here, :] = jnp.zeros((4, LANES, LANES), jnp.float32)
    n_own = own_list.shape[0]
    for n in range(n_own):
        listed[n] = own_list[n]
    filled, full, many = is_full(cells, count_ref)
    work = Groups(tables)
    for bz in range(size_z):
        z = (-1, size_z)[bz]
        sources = []
        for x in range(size_x):
            for y in range(size_y):
                place = (x, y, z % size_z)
                tile = other[place] + shift_tile(cells, (x, y, z))
                sources.append((tile, count_s[bins.index(place)]))
        first_tile = n_own + bz * LIST_Z
        n_tiles = up_to(compact(listed, first_tile, sources), LANES)
        for n, at in enumerate(bins):
            if at[2] == bz:
                work.add(up_to(count_ref[at], CHUNK), n_tiles, first_tile, n * LANES, n * LANES)
    for n in SECOND:
        n_chunks = up_to(count_ref[bins[n]], CHUNK)
        if n < EARLY or n in FIRST:
            n_chunks = jnp.where(many if n in FIRST_IF_MANY else full, 0, n_chunks)
        work.add(n_chunks, up_to(filled, LANES), 0, n * LANES, n * LANES)
    work.run(listed, spread, coefs, acc)


def middle_kernel(cells, count_ref, wide, spread, second, acc, listed, coefs, *tables):
    size_x, size_y, size_z = cells
    n_z = 2 * size_z
    bins = bins_of(cells)
    places = [(i, j, k) for i in (0, size_x + 1) for j in range(size_y) for k in range(n_z)]
    count_s = counts_of([wide[at] for at in places])
    acc[...] = second[...]
    work = Groups(tables)
    for bx in range(size_x):
        for bz in range(size_z):
            x = (-1, size_x)[bx]
            sources = []
            for y in range(size_y):
                for z in (bz - 1, bz, bz + 1):
                    place = (x + 1, y, z % n_z)
                    tile = wide[place] + shift_tile(cells, (x, y, z))
                    sources.append((tile, count_s[places.index(place)]))
            first_tile = (bx * size_z + bz) * LIST_X
            n_tiles = up_to(compact(listed, first_tile, sources), LANES)
            for n, at in enumerate(bins):
                if (at[0], at[2]) == (bx, bz):
                    work.add(up_to(count_ref[at], CHUNK), n_tiles, first_tile, n * LANES, n * LANES)
    work.run(listed, spread, coefs, acc)


def last_kernel(cells, count_ref, own_ref, y_lo, y_hi, spread, *refs):
    (middle, early, out_ref, acc, listed, coefs), tables = refs[:6], refs[6:]
    size_x, size_y, size_z = cells
    n_z = 2 * size_z
    bins = bins_of(cells)
    places = [(i, j, k) for i in range(size_x + 2) for j in range(2) for k in range(n_z)]
    tiles = [(y_lo, y_hi)[j][i, 0, k] for i, j, k in places]
    count_s = counts_of(tiles)
    acc[...] = middle[...]
    work = Groups(tables)
    for n, (bx, by, bz) in enumerate(bins):
        sources = []
        for x in (bx - 1, bx, bx + 1):
            for z in (bz - 1, bz, bz + 1):
                cell = places.index((x + 1, by, z % n_z))
                tile = tiles[cell] + shift_tile(cells, (x, (-1, size_y)[by], z))
                sources.append((tile, count_s[cell]))
        n_tiles = up_to(compact(listed, n * LIST_Y, sources), LANES)
        first_tile = n * LIST_Y
        work.add(up_to(count_ref[bx, by, bz], CHUNK), n_tiles, first_tile, n * LANES, n * LANES)
    work.run(listed, spread, coefs, acc)

    slot = lax.broadcasted_iota(jnp.int32, (1, LANES), 1)
    by_rows = lane_sums([acc[i, : len(bins) * LANES, :] for i in range(4)], len(bins))
    for n, (at, by_row) in enumerate(zip(bins, by_rows)):
        tile = own_ref[at]
        total = velocity_rows(cells, n, by_row, tile)
        total = total - (STOKES_NORM * SELF_C) * pltpu.roll(tile, ROWS - FORCE_ROW, 0)
        if n < EARLY:
            total = total + early[n]
        total = jnp.where(slot < count_ref[at], total, 0.0)
        for i in range(3):
            out_ref[i, at[0], at[1], at[2] : at[2] + 1, :] = total[i : i + 1]


def shifted(first, last, axis):
    size = lax.axis_size(axis)
    up = [(i, (i + 1) % size) for i in range(size)]
    if size % 2:
        down = [(j, i) for i, j in up]
        return lax.ppermute(last, axis, up), lax.ppermute(first, axis, down)
    odd = lax.rem(lax.axis_index(axis), 2) == 1
    got = []
    for parity in (0, 1):
        pairs = [pair for i, j in up if i % 2 == parity for pair in ((i, j), (j, i))]
        got.append(lax.ppermute(jnp.where(odd == bool(parity), last, first), axis, pairs))
    return jnp.where(odd, got[0], got[1]), jnp.where(odd, got[1], got[0])


def on_device(offsets, forces, counts):
    cells = offsets.shape[1:4]
    slots = offsets.shape[4]
    n_bins = cells[0] * cells[1] * cells[2]
    n_targets = n_bins * slots
    whole = pl.BlockSpec(memory_space=pltpu.VMEM)
    scalars = pl.BlockSpec(memory_space=pltpu.SMEM)

    def floats(*shape):
        return jax.ShapeDtypeStruct(shape, jnp.float32)

    def params(mib):
        return pltpu.CompilerParams(vmem_limit_bytes=mib << 20)

    loop_scratch = [pltpu.VMEM((UNITS, 4, CHUNK, LANES), jnp.float32)]
    loop_scratch += [pltpu.SMEM((2 * n_bins,), jnp.int32)] * 5
    cost = pl.CostEstimate(flops=1 << 28, bytes_accessed=1 << 16, transcendentals=1 << 20)

    def list_scratch(n_tiles):
        return [pltpu.VMEM((n_tiles, ROWS, LANES), jnp.float32)]

    own_list, all_targets = floats(n_bins + 1, ROWS, slots), floats(3, n_targets, slots)
    arguments = [pltpu.with_memory_space_constraint(x, pltpu.HBM) for x in (counts, offsets, forces)]
    sent, early = pl.pallas_call(
        functools.partial(pack_kernel, cells),
        out_shape=[floats(*cells, ROWS, slots), floats(EARLY, ROWS, slots)],
        in_specs=[pl.BlockSpec(memory_space=pltpu.HBM)] * 3,
        out_specs=[whole, whole],
        scratch_shapes=[
            pltpu.SMEM(counts.shape, jnp.int32),
            pltpu.VMEM(offsets.shape, jnp.float32),
            pltpu.VMEM(forces.shape, jnp.float32),
            pltpu.SemaphoreType.DMA((3,)),
            pltpu.VMEM(own_list.shape, jnp.float32),
            pltpu.VMEM((3, EARLY * slots, slots), jnp.float32),
            loop_scratch[0],
            pltpu.VMEM((4, EARLY * slots + CHUNK, slots), jnp.float32),
        ]
        + loop_scratch[1:],
        compiler_params=params(8),
        name="pack",
    )(*arguments)

    together = lax.optimization_barrier
    size = lax.axis_size("ha")
    other = lax.ppermute(sent, "ha", [(i, (i + 1) % size) for i in range(size)])
    own, listed, spread, first = pl.pallas_call(
        functools.partial(first_kernel, cells),
        out_shape=[sent, own_list, all_targets, floats(4, len(FIRST) * slots + CHUNK, slots)],
        in_specs=[whole],
        out_specs=[whole] * 4,
        scratch_shapes=loop_scratch,
        compiler_params=params(8),
        cost_estimate=cost,
        name="first",
    )(sent)
    other, own, listed, first = together((other, own, listed, first))
    column = jnp.concatenate([own, other], axis=2)
    x_lo, x_hi = shifted(column[:1], column[cells[0] - 1 :], "gx")
    second = pl.pallas_call(
        functools.partial(second_kernel, cells),
        out_shape=floats(4, n_targets + CHUNK, slots),
        in_specs=[scalars] + [whole] * 4,
        out_specs=whole,
        scratch_shapes=list_scratch(cells[2] * LIST_Z + n_bins + 1)
        + loop_scratch,
        compiler_params=params(8),
        cost_estimate=cost,
        name="second",
    )(counts, other, listed, spread, first)
    x_hi, x_lo, second = together((x_hi, x_lo, second))
    wide = jnp.concatenate([x_lo, column, x_hi], axis=0)
    y_lo, y_hi = shifted(wide[:, :1], wide[:, cells[1] - 1 :], "gy")
    middle = pl.pallas_call(
        functools.partial(middle_kernel, cells),
        out_shape=floats(4, n_targets + CHUNK, slots),
        in_specs=[scalars] + [whole] * 3,
        out_specs=whole,
        scratch_shapes=list_scratch(cells[0] * cells[2] * LIST_X) + loop_scratch,
        compiler_params=params(8),
        cost_estimate=cost,
        name="middle",
    )(counts, wide, spread, second)
    y_lo, y_hi, middle = together((y_lo, y_hi, middle))
    return pl.pallas_call(
        functools.partial(last_kernel, cells),
        out_shape=floats(3, *cells, slots),
        in_specs=[scalars] + [whole] * 6,
        out_specs=whole,
        scratch_shapes=[pltpu.VMEM((4, n_targets + CHUNK, slots), jnp.float32)]
        + list_scratch(n_bins * LIST_Y)
        + loop_scratch,
        compiler_params=params(12),
        cost_estimate=cost,
        name="last",
    )(counts, own, y_lo, y_hi, spread, middle, early)


def solution(mesh):
    in_specs = (
        P(None, "gx", "gy", "ha", None),
        P(None, "gx", "gy", "ha", None),
        P("gx", "gy", "ha"),
    )
    out_specs = P(None, "gx", "gy", "ha", None)
    return jax.shard_map(on_device, mesh=mesh, in_specs=in_specs, out_specs=out_specs, check_vma=False)
```

```python
import functools
import math

import jax
import jax.numpy as jnp
from jax import lax
from jax.experimental import pallas as pl
from jax.experimental.pallas import tpu as pltpu
from jax.sharding import PartitionSpec as P

SPLIT_XI = 2.0
SOFT_SQ = 0.01
GAUSS_COEF = 2.0 * SPLIT_XI / math.sqrt(math.pi)
STOKES_NORM = 1.0 / (8.0 * math.pi)

SOFT_U = SPLIT_XI * SPLIT_XI * SOFT_SQ
LOG2_E = math.log2(math.e)
LOG2_G = math.log2(GAUSS_COEF)
SELF_C = math.erfc(math.sqrt(SOFT_U)) / math.sqrt(SOFT_SQ) + GAUSS_COEF * (
    2.0 * SOFT_U - 3.0
) * math.exp(-SOFT_U)

LANES = 128
ROWS = 8
CHUNK = 32
UNITS = 8
COUNT_ROW = 3
FULL = 700
MANY = 440
EARLY = 3
FIRST = (3, 4, 5)
SECOND = (6, 7, 5, 0, 1, 2, 3, 4)
FIRST_IF_MANY = (3, 4)
LIST_Z, LIST_X, LIST_Y = 5, 7, 10
FORCE_ROW = 4


def rows_and_lanes(shape=(ROWS, LANES)):
    return lax.broadcasted_iota(jnp.int32, shape, 0), lax.broadcasted_iota(jnp.int32, shape, 1)


def bins_of(cells):
    return [(i, j, k) for i in range(cells[0]) for j in range(cells[1]) for k in range(cells[2])]


def shift_tile(cells, at):
    row, _ = rows_and_lanes()
    moved = jnp.zeros((ROWS, LANES), jnp.float32)
    for i in range(3):
        moved = jnp.where(row == i, SPLIT_XI * (at[i] - 0.5 * (cells[i] - 1)), moved)
    return moved


def compact(listed, base, sources):
    _, lane = rows_and_lanes()
    filled = jnp.int32(0)
    moved = []
    for tile, count in sources:
        at = lax.bitwise_and(filled, LANES - 1)
        tile_id = base + lax.shift_right_logical(filled, 7)
        moved.append((pltpu.roll(tile, at, 1), lane >= at, tile_id, at + count >= LANES))
        filled = filled + count
    current = jnp.zeros((ROWS, LANES), jnp.float32)
    for tile, behind, tile_id, full in moved:
        current = jnp.where(behind, tile, current)
        spill = jnp.where(behind, 0.0, tile)
        listed[tile_id] = current
        listed[tile_id + 1] = spill
        current = jnp.where(full, spill, current)
    return filled


def up_to(count, size):
    return lax.shift_right_logical(count + (size - 1), size.bit_length() - 1)


def parts_of(value, n):
    parts = []
    for _ in range(n):
        part = value.astype(jnp.bfloat16)
        value = value - part.astype(jnp.float32)
        parts.append(part)
    return parts


def spread_targets(spread, first, tile):
    parts = [p.astype(jnp.float32) for p in parts_of(tile, 3)] + [jnp.zeros_like(tile)]
    row, lane = rows_and_lanes((4 * ROWS, 3 * LANES))
    pick = jnp.where(lax.bitwise_and(row, ROWS - 1) == lax.shift_right_logical(lane, 7), 1.0, 0.0)
    wide = lax.dot_general(
        jnp.concatenate(parts, axis=0).astype(jnp.bfloat16),
        pick.astype(jnp.bfloat16),
        (((0,), (0,)), ((), ())),
        preferred_element_type=jnp.float32,
    )
    for i in range(3):
        spread[i, first : first + LANES, :] = wide[:, i * LANES : (i + 1) * LANES]


def coefficients(target, source, force):
    delta = [t - s for t, s in zip(target, source)]
    u = (delta[0] * delta[0] + SOFT_U) + delta[1] * delta[1] + delta[2] * delta[2]
    inv = lax.rsqrt(u)
    tail = (1.0 - lax.erf(u * inv)) * inv
    gauss = jnp.exp2(LOG2_G - u * LOG2_E)
    rest = gauss * (u - 1.5)
    coef_d = ((tail - rest) - gauss) * pl.reciprocal(u, approx=True)
    along = coef_d * (delta[0] * force[0] + delta[1] * force[1] + delta[2] * force[2])
    return tail + rest, along


class Groups:
    def __init__(self, tables):
        self.tables = tables
        self.size = 0
        self.total = jnp.int32(0)

    def add(self, n_chunks, n_tiles, first_tile, spread_row, acc_row):
        for table, value in zip(self.tables, (n_chunks, n_tiles, first_tile, spread_row, acc_row)):
            table[self.size] = jnp.int32(value)
        self.size += 1
        self.total = self.total + n_chunks * n_tiles

    def run(self, listed, spread, coefs, acc):
        chunks_of, tiles_of, list_of, spread_of, acc_of = self.tables
        trash = acc.shape[1] - CHUNK

        def rows(tile_id):
            single = [listed[tile_id, i : i + 1, :] for i in (0, 1, 2, 4, 5, 6)]
            return single[:3], single[3:]

        def advance(group, chunk, tile):
            end_tile = tile + 1 == tiles_of[group]
            next_chunk = jnp.where(end_tile, chunk + CHUNK, chunk)
            end_chunk = next_chunk == chunks_of[group] * CHUNK
            next_group = jnp.where(end_chunk, jnp.minimum(group + 1, self.size - 1), group)
            return next_group, jnp.where(end_chunk, 0, next_chunk), jnp.where(end_tile, 0, tile + 1)

        def find(step, place):
            units, found = [], []
            for n in range(UNITS):
                group, chunk, tile = place
                valid = step * UNITS + n < self.total
                units += [jnp.where(valid, acc_of[group] + chunk, trash), list_of[group] + tile]
                at = pl.ds(pl.multiple_of(spread_of[group] + chunk, CHUNK), CHUNK)
                target = [spread[i, at, :] for i in range(3)]
                found.append(coefficients(target, *rows(units[-1])))
                place = advance(*place)
            return found, tuple(units), place

        def use(units):
            terms = []
            for n, tile in enumerate(units[1::2]):
                coef_c, along = coefs[n, 0], coefs[n, 1]
                source, force = rows(tile)
                terms.append([coef_c * force[i] - along * source[i] for i in range(3)] + [along])
            return terms

        def keep(found):
            for n, pair in enumerate(found):
                coefs[n, 0], coefs[n, 1] = pair

        def add(units, terms):
            for first, unit in zip(units[::2], terms):
                at = pl.ds(pl.multiple_of(first, CHUNK), CHUNK)
                for i in range(4):
                    acc[i, at, :] = acc[i, at, :] + unit[i]

        def body(step, state):
            place, olds = state[:3], state[3:]
            terms = use(olds)
            found, news, place = find(step, place)
            add(olds, terms)
            keep(found)
            return place + news

        zero = jnp.int32(0)
        found, units, place = find(0, (zero, zero, zero))
        keep(found)
        state = lax.fori_loop(1, lax.div(self.total + UNITS - 1, UNITS), body, place + units)
        add(state[3:], use(state[3:]))


def is_full(cells, count_ref):
    filled = jnp.int32(0)
    for at in bins_of(cells):
        filled = filled + count_ref[at]
    return filled, filled > FULL, filled > MANY


def list_own(cells, count_ref, own_ref, listed):
    sources = [(own_ref[at] + shift_tile(cells, at), count_ref[at]) for at in bins_of(cells)]
    compact(listed, 0, sources)


def velocity_rows(cells, group, by_row, tile):
    position = tile + shift_tile(cells, bins_of(cells)[group])
    return (2.0 * STOKES_NORM) * (by_row + position * jnp.broadcast_to(by_row[3:4], (ROWS, LANES)))


def lane_sums(sums, n_bins):
    row, lane = rows_and_lanes((2 * LANES, LANES))
    merged = jnp.zeros(sums[0].shape, jnp.float32)
    for i, part in enumerate(sums):
        merged = merged + jnp.dot(
            jnp.concatenate(parts_of(part, 2), axis=1),
            jnp.where(lax.bitwise_and(lane, ROWS - 1) == i, 1.0, 0.0).astype(jnp.bfloat16),
            preferred_element_type=jnp.float32,
        )
    _, lane = rows_and_lanes((LANES, LANES))
    chosen = merged[:LANES]
    for n in range(1, n_bins):
        chosen = jnp.where(lane >= n * ROWS, merged[n * LANES : (n + 1) * LANES], chosen)
    turned = jnp.transpose(chosen)
    return [turned[n * ROWS : (n + 1) * ROWS] for n in range(n_bins)]


def pack_kernel(cells, count_hbm, offset_hbm, force_hbm, own_ref, early_ref, *refs):
    (count_ref, offset_v, force_v, sems, listed, spread, coefs, acc), tables = refs[:8], refs[8:]
    copies = [
        pltpu.make_async_copy(source, target, sems.at[n])
        for n, (source, target) in enumerate(
            ((count_hbm, count_ref), (offset_hbm, offset_v), (force_hbm, force_v))
        )
    ]
    for copy in copies:
        copy.start()
    for copy in copies:
        copy.wait()
    slot = lax.broadcasted_iota(jnp.int32, (1, LANES), 1)
    for at in bins_of(cells):
        ix, iy, iz = at
        count = count_ref[at]
        wide = jnp.full((1, LANES), count, jnp.int32).astype(jnp.float32)
        for i in range(3):
            position = offset_v[i, ix, iy, iz : iz + 1, :]
            own_ref[ix, iy, iz, i : i + 1, :] = position * SPLIT_XI - 0.5 * SPLIT_XI
            force = force_v[i, ix, iy, iz : iz + 1, :]
            own_ref[ix, iy, iz, 4 + i : 5 + i, :] = jnp.where(slot < count, force, 0.0)
        own_ref[ix, iy, iz, 3:4, :] = wide
        own_ref[ix, iy, iz, 7:8, :] = wide
    early_ref[...] = jnp.zeros_like(early_ref)
    filled, full, _ = is_full(cells, count_ref)

    @pl.when(full)
    def _():
        list_own(cells, count_ref, own_ref, listed)
        acc[...] = jnp.zeros_like(acc)
        groups = range(EARLY)
        tiles = [own_ref[bins_of(cells)[n]] for n in groups]
        work = Groups(tables)
        for n in groups:
            at = bins_of(cells)[n]
            spread_targets(spread, n * LANES, tiles[n] + shift_tile(cells, at))
            work.add(up_to(count_ref[at], CHUNK), up_to(filled, LANES), 0, n * LANES, n * LANES)
        work.run(listed, spread, coefs, acc)
        by_rows = lane_sums([acc[i, : EARLY * LANES, :] for i in range(4)], EARLY)
        for n, by_row in enumerate(by_rows):
            early_ref[n] = velocity_rows(cells, n, by_row, tiles[n])


def counts_of(tiles):
    return [tile[COUNT_ROW, 0].astype(jnp.int32) for tile in tiles]


def first_kernel(cells, sent_ref, own_ref, listed, spread, acc, coefs, *tables):
    bins = bins_of(cells)
    count_s = counts_of([sent_ref[at] for at in bins])
    own_ref[...] = sent_ref[...]
    for n, at in enumerate(bins):
        spread_targets(spread, n * LANES, own_ref[at] + shift_tile(cells, at))
    acc[...] = jnp.zeros_like(acc)
    count_ref = {at: count_s[n] for n, at in enumerate(bins)}
    list_own(cells, count_ref, own_ref, listed)
    filled, full, many = is_full(cells, count_ref)
    work = Groups(tables)
    for m, n in enumerate(FIRST):
        n_chunks = jnp.where(many if n in FIRST_IF_MANY else full, up_to(count_ref[bins[n]], CHUNK), 0)
        work.add(n_chunks, up_to(filled, LANES), 0, n * LANES, m * LANES)
    work.run(listed, spread, coefs, acc)


def second_kernel(cells, count_ref, other, own_list, spread, first, acc, listed, coefs, *tables):
    bins = bins_of(cells)
    size_x, size_y, size_z = cells
    count_s = counts_of([other[at] for at in bins])
    for n in range(len(bins)):
        here = slice(n * LANES, (n + 1) * LANES)
        if n in FIRST:
            m = FIRST.index(n)
            acc[:, here, :] = first[:, m * LANES : (m + 1) * LANES, :]
        else:
            acc[:, here, :] = jnp.zeros((4, LANES, LANES), jnp.float32)
    n_own = own_list.shape[0]
    for n in range(n_own):
        listed[n] = own_list[n]
    filled, full, many = is_full(cells, count_ref)
    work = Groups(tables)
    for bz in range(size_z):
        z = (-1, size_z)[bz]
        sources = []
        for x in range(size_x):
            for y in range(size_y):
                place = (x, y, z % size_z)
                tile = other[place] + shift_tile(cells, (x, y, z))
                sources.append((tile, count_s[bins.index(place)]))
        first_tile = n_own + bz * LIST_Z
        n_tiles = up_to(compact(listed, first_tile, sources), LANES)
        for n, at in enumerate(bins):
            if at[2] == bz:
                work.add(up_to(count_ref[at], CHUNK), n_tiles, first_tile, n * LANES, n * LANES)
    for n in SECOND:
        n_chunks = up_to(count_ref[bins[n]], CHUNK)
        if n < EARLY or n in FIRST:
            n_chunks = jnp.where(many if n in FIRST_IF_MANY else full, 0, n_chunks)
        work.add(n_chunks, up_to(filled, LANES), 0, n * LANES, n * LANES)
    work.run(listed, spread, coefs, acc)


def middle_kernel(cells, count_ref, wide, spread, _, acc, listed, coefs, *tables):
    size_x, size_y, size_z = cells
    n_z = 2 * size_z
    bins = bins_of(cells)
    places = [(i, j, k) for i in (0, size_x + 1) for j in range(size_y) for k in range(n_z)]
    count_s = counts_of([wide[at] for at in places])
    work = Groups(tables)
    for bx in range(size_x):
        for bz in range(size_z):
            x = (-1, size_x)[bx]
            sources = []
            for y in range(size_y):
                for z in (bz - 1, bz, bz + 1):
                    place = (x + 1, y, z % n_z)
                    tile = wide[place] + shift_tile(cells, (x, y, z))
                    sources.append((tile, count_s[places.index(place)]))
            first_tile = (bx * size_z + bz) * LIST_X
            n_tiles = up_to(compact(listed, first_tile, sources), LANES)
            for n, at in enumerate(bins):
                if (at[0], at[2]) == (bx, bz):
                    work.add(up_to(count_ref[at], CHUNK), n_tiles, first_tile, n * LANES, n * LANES)
    work.run(listed, spread, coefs, acc)


def last_kernel(cells, count_ref, own_ref, y_lo, y_hi, spread, *refs):
    (_, early, out_ref, acc, listed, coefs), tables = refs[:6], refs[6:]
    size_x, size_y, size_z = cells
    n_z = 2 * size_z
    bins = bins_of(cells)
    places = [(i, j, k) for i in range(size_x + 2) for j in range(2) for k in range(n_z)]
    tiles = [(y_lo, y_hi)[j][i, 0, k] for i, j, k in places]
    count_s = counts_of(tiles)
    work = Groups(tables)
    for n, (bx, by, bz) in enumerate(bins):
        sources = []
        for x in (bx - 1, bx, bx + 1):
            for z in (bz - 1, bz, bz + 1):
                cell = places.index((x + 1, by, z % n_z))
                tile = tiles[cell] + shift_tile(cells, (x, (-1, size_y)[by], z))
                sources.append((tile, count_s[cell]))
        n_tiles = up_to(compact(listed, n * LIST_Y, sources), LANES)
        first_tile = n * LIST_Y
        work.add(up_to(count_ref[bx, by, bz], CHUNK), n_tiles, first_tile, n * LANES, n * LANES)
    work.run(listed, spread, coefs, acc)

    slot = lax.broadcasted_iota(jnp.int32, (1, LANES), 1)
    by_rows = lane_sums([acc[i, : len(bins) * LANES, :] for i in range(4)], len(bins))
    for n, (at, by_row) in enumerate(zip(bins, by_rows)):
        tile = own_ref[at]
        total = velocity_rows(cells, n, by_row, tile)
        total = total - (STOKES_NORM * SELF_C) * pltpu.roll(tile, ROWS - FORCE_ROW, 0)
        if n < EARLY:
            total = total + early[n]
        total = jnp.where(slot < count_ref[at], total, 0.0)
        for i in range(3):
            out_ref[i, at[0], at[1], at[2] : at[2] + 1, :] = total[i : i + 1]


def shifted(first, last, axis):
    size = lax.axis_size(axis)
    up = [(i, (i + 1) % size) for i in range(size)]
    if size % 2:
        down = [(j, i) for i, j in up]
        return lax.ppermute(last, axis, up), lax.ppermute(first, axis, down)
    odd = lax.rem(lax.axis_index(axis), 2) == 1
    got = []
    for parity in (0, 1):
        pairs = [pair for i, j in up if i % 2 == parity for pair in ((i, j), (j, i))]
        got.append(lax.ppermute(jnp.where(odd == bool(parity), last, first), axis, pairs))
    return jnp.where(odd, got[0], got[1]), jnp.where(odd, got[1], got[0])


def on_device(offsets, forces, counts):
    cells = offsets.shape[1:4]
    slots = offsets.shape[4]
    n_bins = cells[0] * cells[1] * cells[2]
    n_targets = n_bins * slots
    whole = pl.BlockSpec(memory_space=pltpu.VMEM)
    scalars = pl.BlockSpec(memory_space=pltpu.SMEM)

    def floats(*shape):
        return jax.ShapeDtypeStruct(shape, jnp.float32)

    def params(mib):
        return pltpu.CompilerParams(vmem_limit_bytes=mib << 20)

    loop_scratch = [pltpu.VMEM((UNITS, 2, CHUNK, LANES), jnp.float32)]
    loop_scratch += [pltpu.SMEM((2 * n_bins,), jnp.int32)] * 5
    cost = pl.CostEstimate(flops=1 << 28, bytes_accessed=1 << 16, transcendentals=1 << 20)

    def in_place(sums):
        return pltpu.with_memory_space_constraint(sums, pltpu.VMEM)

    def list_scratch(n_tiles):
        return [pltpu.VMEM((n_tiles, ROWS, LANES), jnp.float32)]

    own_list, all_targets = floats(n_bins + 1, ROWS, slots), floats(3, n_targets, slots)
    arguments = [pltpu.with_memory_space_constraint(x, pltpu.HBM) for x in (counts, offsets, forces)]
    sent, early = pl.pallas_call(
        functools.partial(pack_kernel, cells),
        out_shape=[floats(*cells, ROWS, slots), floats(EARLY, ROWS, slots)],
        in_specs=[pl.BlockSpec(memory_space=pltpu.HBM)] * 3,
        out_specs=[whole, whole],
        scratch_shapes=[
            pltpu.SMEM(counts.shape, jnp.int32),
            pltpu.VMEM(offsets.shape, jnp.float32),
            pltpu.VMEM(forces.shape, jnp.float32),
            pltpu.SemaphoreType.DMA((3,)),
            pltpu.VMEM(own_list.shape, jnp.float32),
            pltpu.VMEM((3, EARLY * slots, slots), jnp.float32),
            loop_scratch[0],
            pltpu.VMEM((4, EARLY * slots + CHUNK, slots), jnp.float32),
        ]
        + loop_scratch[1:],
        compiler_params=params(8),
        name="pack",
    )(*arguments)

    together = lax.optimization_barrier
    size = lax.axis_size("ha")
    other = lax.ppermute(sent, "ha", [(i, (i + 1) % size) for i in range(size)])
    own, listed, spread, first = pl.pallas_call(
        functools.partial(first_kernel, cells),
        out_shape=[sent, own_list, all_targets, floats(4, len(FIRST) * slots + CHUNK, slots)],
        in_specs=[whole],
        out_specs=[whole] * 4,
        scratch_shapes=loop_scratch,
        compiler_params=params(8),
        cost_estimate=cost,
        name="first",
    )(sent)
    other, own, listed, first = together((other, own, listed, first))
    column = jnp.concatenate([own, other], axis=2)
    x_lo, x_hi = shifted(column[:1], column[cells[0] - 1 :], "gx")
    second = pl.pallas_call(
        functools.partial(second_kernel, cells),
        out_shape=floats(4, n_targets + CHUNK, slots),
        in_specs=[scalars] + [whole] * 4,
        out_specs=whole,
        scratch_shapes=list_scratch(cells[2] * LIST_Z + n_bins + 1)
        + loop_scratch,
        compiler_params=params(8),
        cost_estimate=cost,
        name="second",
    )(counts, other, listed, spread, first)
    x_hi, x_lo, second = together((x_hi, x_lo, second))
    wide = jnp.concatenate([x_lo, column, x_hi], axis=0)
    y_lo, y_hi = shifted(wide[:, :1], wide[:, cells[1] - 1 :], "gy")
    middle = pl.pallas_call(
        functools.partial(middle_kernel, cells),
        out_shape=floats(4, n_targets + CHUNK, slots),
        in_specs=[scalars] + [whole] * 3,
        out_specs=whole,
        scratch_shapes=list_scratch(cells[0] * cells[2] * LIST_X) + loop_scratch,
        input_output_aliases={3: 0},
        compiler_params=params(8),
        cost_estimate=cost,
        name="middle",
    )(counts, wide, spread, in_place(second))
    y_lo, y_hi, middle = together((y_lo, y_hi, middle))
    return pl.pallas_call(
        functools.partial(last_kernel, cells),
        out_shape=[floats(3, *cells, slots), floats(4, n_targets + CHUNK, slots)],
        in_specs=[scalars] + [whole] * 6,
        out_specs=[whole, whole],
        scratch_shapes=list_scratch(n_bins * LIST_Y)
        + loop_scratch,
        input_output_aliases={5: 1},
        compiler_params=params(12),
        cost_estimate=cost,
        name="last",
    )(counts, own, y_lo, y_hi, spread, in_place(middle), early)[0]


def solution(mesh):
    in_specs = (
        P(None, "gx", "gy", "ha", None),
        P(None, "gx", "gy", "ha", None),
        P("gx", "gy", "ha"),
    )
    out_specs = P(None, "gx", "gy", "ha", None)
    return jax.shard_map(on_device, mesh=mesh, in_specs=in_specs, out_specs=out_specs, check_vma=False)
```

```python
import functools
import math

import jax
import jax.numpy as jnp
from jax import lax
from jax.experimental import pallas as pl
from jax.experimental.pallas import tpu as pltpu
from jax.sharding import PartitionSpec as P

SPLIT_XI = 2.0
SOFT_SQ = 0.01
GAUSS_COEF = 2.0 * SPLIT_XI / math.sqrt(math.pi)
STOKES_NORM = 1.0 / (8.0 * math.pi)

SOFT_U = SPLIT_XI * SPLIT_XI * SOFT_SQ
LOG2_E = math.log2(math.e)
LOG2_G = math.log2(GAUSS_COEF)
SELF_C = math.erfc(math.sqrt(SOFT_U)) / math.sqrt(SOFT_SQ) + GAUSS_COEF * (
    2.0 * SOFT_U - 3.0
) * math.exp(-SOFT_U)

LANES = 128
ROWS = 8
CHUNK = 32
UNITS = 8
COUNT_ROW = 3
FULL = 700
MANY = 440
EARLY = 3
FIRST = (3, 4, 5)
SECOND = (6, 7, 5, 0, 1, 2, 3, 4)
FIRST_IF_MANY = (3, 4)
LIST_Z, LIST_X, LIST_Y = 5, 7, 10
FORCE_ROW = 4


def rows_and_lanes(shape=(ROWS, LANES)):
    return lax.broadcasted_iota(jnp.int32, shape, 0), lax.broadcasted_iota(jnp.int32, shape, 1)


def bins_of(cells):
    return [(i, j, k) for i in range(cells[0]) for j in range(cells[1]) for k in range(cells[2])]


def shift_tile(cells, at):
    row, _ = rows_and_lanes()
    moved = jnp.zeros((ROWS, LANES), jnp.float32)
    for i in range(3):
        moved = jnp.where(row == i, SPLIT_XI * (at[i] - 0.5 * (cells[i] - 1)), moved)
    return moved


def compact(listed, base, sources):
    _, lane = rows_and_lanes()
    filled = jnp.int32(0)
    moved = []
    for tile, count in sources:
        at = lax.bitwise_and(filled, LANES - 1)
        tile_id = base + lax.shift_right_logical(filled, 7)
        moved.append((pltpu.roll(tile, at, 1), lane >= at, tile_id, at + count >= LANES))
        filled = filled + count
    current = jnp.zeros((ROWS, LANES), jnp.float32)
    for tile, behind, tile_id, full in moved:
        current = jnp.where(behind, tile, current)
        spill = jnp.where(behind, 0.0, tile)
        listed[tile_id] = current
        listed[tile_id + 1] = spill
        current = jnp.where(full, spill, current)
    return filled


def up_to(count, size):
    return lax.shift_right_logical(count + (size - 1), size.bit_length() - 1)


def parts_of(value, n):
    parts = []
    for _ in range(n):
        part = value.astype(jnp.bfloat16)
        value = value - part.astype(jnp.float32)
        parts.append(part)
    return parts


def spread_targets(spread, first, tile):
    parts = [p.astype(jnp.float32) for p in parts_of(tile, 3)] + [jnp.zeros_like(tile)]
    row, lane = rows_and_lanes((4 * ROWS, 3 * LANES))
    pick = jnp.where(lax.bitwise_and(row, ROWS - 1) == lax.shift_right_logical(lane, 7), 1.0, 0.0)
    wide = lax.dot_general(
        jnp.concatenate(parts, axis=0).astype(jnp.bfloat16),
        pick.astype(jnp.bfloat16),
        (((0,), (0,)), ((), ())),
        preferred_element_type=jnp.float32,
    )
    for i in range(3):
        spread[i, first : first + LANES, :] = wide[:, i * LANES : (i + 1) * LANES]


def coefficients(target, source, force):
    delta = [t - s for t, s in zip(target, source)]
    u = (delta[0] * delta[0] + SOFT_U) + delta[1] * delta[1] + delta[2] * delta[2]
    inv = lax.rsqrt(u)
    tail = (1.0 - lax.erf(u * inv)) * inv
    gauss = jnp.exp2(LOG2_G - u * LOG2_E)
    rest = gauss * (u - 1.5)
    coef_d = ((tail - rest) - gauss) * pl.reciprocal(u, approx=True)
    along = coef_d * (delta[0] * force[0] + delta[1] * force[1] + delta[2] * force[2])
    return tail + rest, along


class Groups:
    def __init__(self, tables):
        self.tables = tables
        self.size = 0
        self.total = jnp.int32(0)

    def add(self, n_chunks, n_tiles, first_tile, spread_row, acc_row):
        for table, value in zip(self.tables, (n_chunks, n_tiles, first_tile, spread_row, acc_row)):
            table[self.size] = jnp.int32(value)
        self.size += 1
        self.total = self.total + n_chunks * n_tiles

    def run(self, listed, spread, coefs, acc):
        chunks_of, tiles_of, list_of, spread_of, acc_of = self.tables
        trash = acc.shape[1] - CHUNK

        def rows(tile_id):
            single = [listed[tile_id, i : i + 1, :] for i in (0, 1, 2, 4, 5, 6)]
            return single[:3], single[3:]

        def advance(group, chunk, tile):
            end_tile = tile + 1 == tiles_of[group]
            next_chunk = jnp.where(end_tile, chunk + CHUNK, chunk)
            end_chunk = next_chunk == chunks_of[group] * CHUNK
            next_group = jnp.where(end_chunk, jnp.minimum(group + 1, self.size - 1), group)
            return next_group, jnp.where(end_chunk, 0, next_chunk), jnp.where(end_tile, 0, tile + 1)

        def find(step, place):
            units, found = [], []
            for n in range(UNITS):
                group, chunk, tile = place
                valid = step * UNITS + n < self.total
                units += [jnp.where(valid, acc_of[group] + chunk, trash), list_of[group] + tile]
                at = pl.ds(pl.multiple_of(spread_of[group] + chunk, CHUNK), CHUNK)
                target = [spread[i, at, :] for i in range(3)]
                found.append(coefficients(target, *rows(units[-1])))
                place = advance(*place)
            return found, tuple(units), place

        def use(units):
            terms = []
            for n, tile in enumerate(units[1::2]):
                coef_c, along = coefs[n, 0], coefs[n, 1]
                source, force = rows(tile)
                terms.append([coef_c * force[i] - along * source[i] for i in range(3)] + [along])
            return terms

        def keep(found):
            for n, pair in enumerate(found):
                coefs[n, 0], coefs[n, 1] = pair

        def add(units, terms):
            for first, unit in zip(units[::2], terms):
                at = pl.ds(pl.multiple_of(first, CHUNK), CHUNK)
                for i in range(4):
                    acc[i, at, :] = acc[i, at, :] + unit[i]

        def body(step, state):
            place, olds = state[:3], state[3:]
            terms = use(olds)
            found, news, place = find(step, place)
            add(olds, terms)
            keep(found)
            return place + news

        zero = jnp.int32(0)
        found, units, place = find(0, (zero, zero, zero))
        keep(found)
        state = lax.fori_loop(1, lax.div(self.total + UNITS - 1, UNITS), body, place + units)
        add(state[3:], use(state[3:]))


def is_full(cells, count_ref):
    filled = jnp.int32(0)
    for at in bins_of(cells):
        filled = filled + count_ref[at]
    return filled, filled > FULL, filled > MANY


def list_own(cells, count_ref, own_ref, listed):
    sources = [(own_ref[at] + shift_tile(cells, at), count_ref[at]) for at in bins_of(cells)]
    compact(listed, 0, sources)


def velocity_rows(cells, group, by_row, tile):
    position = tile + shift_tile(cells, bins_of(cells)[group])
    return (2.0 * STOKES_NORM) * (by_row + position * jnp.broadcast_to(by_row[3:4], (ROWS, LANES)))


def lane_sums(sums, n_bins):
    row, lane = rows_and_lanes((2 * LANES * len(sums), LANES))
    pick = lax.bitwise_and(lane, ROWS - 1) == lax.shift_right_logical(row, (2 * LANES).bit_length() - 1)
    merged = jnp.dot(
        jnp.concatenate([p for part in sums for p in parts_of(part, 2)], axis=1),
        jnp.where(pick, 1.0, 0.0).astype(jnp.bfloat16),
        preferred_element_type=jnp.float32,
    )
    _, lane = rows_and_lanes((LANES, LANES))
    chosen = merged[:LANES]
    for n in range(1, n_bins):
        chosen = jnp.where(lane >= n * ROWS, merged[n * LANES : (n + 1) * LANES], chosen)
    turned = jnp.transpose(chosen)
    return [turned[n * ROWS : (n + 1) * ROWS] for n in range(n_bins)]


def pack_kernel(cells, count_hbm, offset_hbm, force_hbm, own_ref, early_ref, *refs):
    (count_ref, offset_v, force_v, sems, listed, spread, coefs, acc), tables = refs[:8], refs[8:]
    copies = [
        pltpu.make_async_copy(source, target, sems.at[n])
        for n, (source, target) in enumerate(
            ((count_hbm, count_ref), (offset_hbm, offset_v), (force_hbm, force_v))
        )
    ]
    for copy in copies:
        copy.start()
    for copy in copies:
        copy.wait()
    slot = lax.broadcasted_iota(jnp.int32, (1, LANES), 1)
    for at in bins_of(cells):
        ix, iy, iz = at
        count = count_ref[at]
        wide = jnp.full((1, LANES), count, jnp.int32).astype(jnp.float32)
        for i in range(3):
            position = offset_v[i, ix, iy, iz : iz + 1, :]
            own_ref[ix, iy, iz, i : i + 1, :] = position * SPLIT_XI - 0.5 * SPLIT_XI
            force = force_v[i, ix, iy, iz : iz + 1, :]
            own_ref[ix, iy, iz, 4 + i : 5 + i, :] = jnp.where(slot < count, force, 0.0)
        own_ref[ix, iy, iz, 3:4, :] = wide
        own_ref[ix, iy, iz, 7:8, :] = wide
    early_ref[...] = jnp.zeros_like(early_ref)
    filled, full, _ = is_full(cells, count_ref)

    @pl.when(full)
    def _():
        list_own(cells, count_ref, own_ref, listed)
        acc[...] = jnp.zeros_like(acc)
        groups = range(EARLY)
        tiles = [own_ref[bins_of(cells)[n]] for n in groups]
        work = Groups(tables)
        for n in groups:
            at = bins_of(cells)[n]
            spread_targets(spread, n * LANES, tiles[n] + shift_tile(cells, at))
            work.add(up_to(count_ref[at], CHUNK), up_to(filled, LANES), 0, n * LANES, n * LANES)
        work.run(listed, spread, coefs, acc)
        by_rows = lane_sums([acc[i, : EARLY * LANES, :] for i in range(4)], EARLY)
        for n, by_row in enumerate(by_rows):
            early_ref[n] = velocity_rows(cells, n, by_row, tiles[n])


def counts_of(tiles):
    return [tile[COUNT_ROW, 0].astype(jnp.int32) for tile in tiles]


def first_kernel(cells, sent_ref, own_ref, listed, spread, acc, coefs, *tables):
    bins = bins_of(cells)
    count_s = counts_of([sent_ref[at] for at in bins])
    own_ref[...] = sent_ref[...]
    for n, at in enumerate(bins):
        spread_targets(spread, n * LANES, own_ref[at] + shift_tile(cells, at))
    acc[...] = jnp.zeros_like(acc)
    count_ref = {at: count_s[n] for n, at in enumerate(bins)}
    list_own(cells, count_ref, own_ref, listed)
    filled, full, many = is_full(cells, count_ref)
    work = Groups(tables)
    for m, n in enumerate(FIRST):
        n_chunks = jnp.where(many if n in FIRST_IF_MANY else full, up_to(count_ref[bins[n]], CHUNK), 0)
        work.add(n_chunks, up_to(filled, LANES), 0, n * LANES, m * LANES)
    work.run(listed, spread, coefs, acc)


def second_kernel(cells, count_ref, other, own_list, spread, first, acc, listed, coefs, *tables):
    bins = bins_of(cells)
    size_x, size_y, size_z = cells
    count_s = counts_of([other[at] for at in bins])
    for n in range(len(bins)):
        here = slice(n * LANES, (n + 1) * LANES)
        if n in FIRST:
            m = FIRST.index(n)
            acc[:, here, :] = first[:, m * LANES : (m + 1) * LANES, :]
        else:
            acc[:, here, :] = jnp.zeros((4, LANES, LANES), jnp.float32)
    n_own = own_list.shape[0]
    for n in range(n_own):
        listed[n] = own_list[n]
    filled, full, many = is_full(cells, count_ref)
    work = Groups(tables)
    for bz in range(size_z):
        z = (-1, size_z)[bz]
        sources = []
        for x in range(size_x):
            for y in range(size_y):
                place = (x, y, z % size_z)
                tile = other[place] + shift_tile(cells, (x, y, z))
                sources.append((tile, count_s[bins.index(place)]))
        first_tile = n_own + bz * LIST_Z
        n_tiles = up_to(compact(listed, first_tile, sources), LANES)
        for n, at in enumerate(bins):
            if at[2] == bz:
                work.add(up_to(count_ref[at], CHUNK), n_tiles, first_tile, n * LANES, n * LANES)
    for n in SECOND:
        n_chunks = up_to(count_ref[bins[n]], CHUNK)
        if n < EARLY or n in FIRST:
            n_chunks = jnp.where(many if n in FIRST_IF_MANY else full, 0, n_chunks)
        work.add(n_chunks, up_to(filled, LANES), 0, n * LANES, n * LANES)
    work.run(listed, spread, coefs, acc)


def middle_kernel(cells, count_ref, wide, spread, _, acc, listed, coefs, *tables):
    size_x, size_y, size_z = cells
    n_z = 2 * size_z
    bins = bins_of(cells)
    places = [(i, j, k) for i in (0, size_x + 1) for j in range(size_y) for k in range(n_z)]
    count_s = counts_of([wide[at] for at in places])
    work = Groups(tables)
    for bx in range(size_x):
        for bz in range(size_z):
            x = (-1, size_x)[bx]
            sources = []
            for y in range(size_y):
                for z in (bz - 1, bz, bz + 1):
                    place = (x + 1, y, z % n_z)
                    tile = wide[place] + shift_tile(cells, (x, y, z))
                    sources.append((tile, count_s[places.index(place)]))
            first_tile = (bx * size_z + bz) * LIST_X
            n_tiles = up_to(compact(listed, first_tile, sources), LANES)
            for n, at in enumerate(bins):
                if (at[0], at[2]) == (bx, bz):
                    work.add(up_to(count_ref[at], CHUNK), n_tiles, first_tile, n * LANES, n * LANES)
    work.run(listed, spread, coefs, acc)


def last_kernel(cells, count_ref, own_ref, y_lo, y_hi, spread, *refs):
    (_, early, out_ref, acc, listed, coefs), tables = refs[:6], refs[6:]
    size_x, size_y, size_z = cells
    n_z = 2 * size_z
    bins = bins_of(cells)
    places = [(i, j, k) for i in range(size_x + 2) for j in range(2) for k in range(n_z)]
    tiles = [(y_lo, y_hi)[j][i, 0, k] for i, j, k in places]
    count_s = counts_of(tiles)
    work = Groups(tables)
    for n, (bx, by, bz) in enumerate(bins):
        sources = []
        for x in (bx - 1, bx, bx + 1):
            for z in (bz - 1, bz, bz + 1):
                cell = places.index((x + 1, by, z % n_z))
                tile = tiles[cell] + shift_tile(cells, (x, (-1, size_y)[by], z))
                sources.append((tile, count_s[cell]))
        n_tiles = up_to(compact(listed, n * LIST_Y, sources), LANES)
        first_tile = n * LIST_Y
        work.add(up_to(count_ref[bx, by, bz], CHUNK), n_tiles, first_tile, n * LANES, n * LANES)
    work.run(listed, spread, coefs, acc)

    slot = lax.broadcasted_iota(jnp.int32, (1, LANES), 1)
    by_rows = lane_sums([acc[i, : len(bins) * LANES, :] for i in range(4)], len(bins))
    for n, (at, by_row) in enumerate(zip(bins, by_rows)):
        tile = own_ref[at]
        total = velocity_rows(cells, n, by_row, tile)
        total = total - (STOKES_NORM * SELF_C) * pltpu.roll(tile, ROWS - FORCE_ROW, 0)
        if n < EARLY:
            total = total + early[n]
        total = jnp.where(slot < count_ref[at], total, 0.0)
        for i in range(3):
            out_ref[i, at[0], at[1], at[2] : at[2] + 1, :] = total[i : i + 1]


def shifted(first, last, axis):
    size = lax.axis_size(axis)
    up = [(i, (i + 1) % size) for i in range(size)]
    if size % 2:
        down = [(j, i) for i, j in up]
        return lax.ppermute(last, axis, up), lax.ppermute(first, axis, down)
    odd = lax.rem(lax.axis_index(axis), 2) == 1
    got = []
    for parity in (0, 1):
        pairs = [pair for i, j in up if i % 2 == parity for pair in ((i, j), (j, i))]
        got.append(lax.ppermute(jnp.where(odd == bool(parity), last, first), axis, pairs))
    return jnp.where(odd, got[0], got[1]), jnp.where(odd, got[1], got[0])


def on_device(offsets, forces, counts):
    cells = offsets.shape[1:4]
    slots = offsets.shape[4]
    n_bins = cells[0] * cells[1] * cells[2]
    n_targets = n_bins * slots
    whole = pl.BlockSpec(memory_space=pltpu.VMEM)
    scalars = pl.BlockSpec(memory_space=pltpu.SMEM)

    def floats(*shape):
        return jax.ShapeDtypeStruct(shape, jnp.float32)

    def params(mib):
        return pltpu.CompilerParams(vmem_limit_bytes=mib << 20)

    loop_scratch = [pltpu.VMEM((UNITS, 2, CHUNK, LANES), jnp.float32)]
    loop_scratch += [pltpu.SMEM((2 * n_bins,), jnp.int32)] * 5
    cost = pl.CostEstimate(flops=1 << 28, bytes_accessed=1 << 16, transcendentals=1 << 20)

    def in_place(sums):
        return pltpu.with_memory_space_constraint(sums, pltpu.VMEM)

    def list_scratch(n_tiles):
        return [pltpu.VMEM((n_tiles, ROWS, LANES), jnp.float32)]

    own_list, all_targets = floats(n_bins + 1, ROWS, slots), floats(3, n_targets, slots)
    arguments = [pltpu.with_memory_space_constraint(x, pltpu.HBM) for x in (counts, offsets, forces)]
    sent, early = pl.pallas_call(
        functools.partial(pack_kernel, cells),
        out_shape=[floats(*cells, ROWS, slots), floats(EARLY, ROWS, slots)],
        in_specs=[pl.BlockSpec(memory_space=pltpu.HBM)] * 3,
        out_specs=[whole, whole],
        scratch_shapes=[
            pltpu.SMEM(counts.shape, jnp.int32),
            pltpu.VMEM(offsets.shape, jnp.float32),
            pltpu.VMEM(forces.shape, jnp.float32),
            pltpu.SemaphoreType.DMA((3,)),
            pltpu.VMEM(own_list.shape, jnp.float32),
            pltpu.VMEM((3, EARLY * slots, slots), jnp.float32),
            loop_scratch[0],
            pltpu.VMEM((4, EARLY * slots + CHUNK, slots), jnp.float32),
        ]
        + loop_scratch[1:],
        compiler_params=params(8),
        name="pack",
    )(*arguments)

    together = lax.optimization_barrier
    size = lax.axis_size("ha")
    other = lax.ppermute(sent, "ha", [(i, (i + 1) % size) for i in range(size)])
    own, listed, spread, first = pl.pallas_call(
        functools.partial(first_kernel, cells),
        out_shape=[sent, own_list, all_targets, floats(4, len(FIRST) * slots + CHUNK, slots)],
        in_specs=[whole],
        out_specs=[whole] * 4,
        scratch_shapes=loop_scratch,
        compiler_params=params(8),
        cost_estimate=cost,
        name="first",
    )(sent)
    other, own, listed, first = together((other, own, listed, first))
    column = jnp.concatenate([own, other], axis=2)
    x_lo, x_hi = shifted(column[:1], column[cells[0] - 1 :], "gx")
    second = pl.pallas_call(
        functools.partial(second_kernel, cells),
        out_shape=floats(4, n_targets + CHUNK, slots),
        in_specs=[scalars] + [whole] * 4,
        out_specs=whole,
        scratch_shapes=list_scratch(cells[2] * LIST_Z + n_bins + 1)
        + loop_scratch,
        compiler_params=params(8),
        cost_estimate=cost,
        name="second",
    )(counts, other, listed, spread, first)
    x_lo, x_hi, second = together((x_lo, x_hi, second))
    wide = jnp.concatenate([x_lo, column, x_hi], axis=0)
    y_lo, y_hi = shifted(wide[:, :1], wide[:, cells[1] - 1 :], "gy")
    middle = pl.pallas_call(
        functools.partial(middle_kernel, cells),
        out_shape=floats(4, n_targets + CHUNK, slots),
        in_specs=[scalars] + [whole] * 3,
        out_specs=whole,
        scratch_shapes=list_scratch(cells[0] * cells[2] * LIST_X) + loop_scratch,
        input_output_aliases={3: 0},
        compiler_params=params(8),
        cost_estimate=cost,
        name="middle",
    )(counts, wide, spread, in_place(second))
    y_lo, y_hi, middle = together((y_lo, y_hi, middle))
    return pl.pallas_call(
        functools.partial(last_kernel, cells),
        out_shape=[floats(3, *cells, slots), floats(4, n_targets + CHUNK, slots)],
        in_specs=[scalars] + [whole] * 6,
        out_specs=[whole, whole],
        scratch_shapes=list_scratch(n_bins * LIST_Y)
        + loop_scratch,
        input_output_aliases={5: 1},
        compiler_params=params(12),
        cost_estimate=cost,
        name="last",
    )(counts, own, y_lo, y_hi, spread, in_place(middle), early)[0]


def solution(mesh):
    in_specs = (
        P(None, "gx", "gy", "ha", None),
        P(None, "gx", "gy", "ha", None),
        P("gx", "gy", "ha"),
    )
    out_specs = P(None, "gx", "gy", "ha", None)
    return jax.shard_map(on_device, mesh=mesh, in_specs=in_specs, out_specs=out_specs, check_vma=False)
```

```python
import functools
import math

import jax
import jax.numpy as jnp
from jax import lax
from jax.experimental import pallas as pl
from jax.experimental.pallas import tpu as pltpu
from jax.sharding import PartitionSpec as P

SPLIT_XI = 2.0
SOFT_SQ = 0.01
GAUSS_COEF = 2.0 * SPLIT_XI / math.sqrt(math.pi)
STOKES_NORM = 1.0 / (8.0 * math.pi)

SOFT_U = SPLIT_XI * SPLIT_XI * SOFT_SQ
LOG2_E = math.log2(math.e)
LOG2_G = math.log2(GAUSS_COEF)
SELF_C = math.erfc(math.sqrt(SOFT_U)) / math.sqrt(SOFT_SQ) + GAUSS_COEF * (
    2.0 * SOFT_U - 3.0
) * math.exp(-SOFT_U)

LANES = 128
ROWS = 8
CHUNK = 32
UNITS = 8
COUNT_ROW = 3
MANY = 440
EARLY = 3
FIRST = (3, 4, 5)
SECOND = (6, 7, 5, 0, 1, 2, 3, 4)
FIRST_IF_MANY = (3, 4)
LIST_Z, LIST_X, LIST_Y = 5, 7, 10
FORCE_ROW = 4


def rows_and_lanes(shape=(ROWS, LANES)):
    return lax.broadcasted_iota(jnp.int32, shape, 0), lax.broadcasted_iota(jnp.int32, shape, 1)


def bins_of(cells):
    return [(i, j, k) for i in range(cells[0]) for j in range(cells[1]) for k in range(cells[2])]


def shift_tile(cells, at):
    row, _ = rows_and_lanes()
    moved = jnp.zeros((ROWS, LANES), jnp.float32)
    for i in range(3):
        moved = jnp.where(row == i, SPLIT_XI * (at[i] - 0.5 * (cells[i] - 1)), moved)
    return moved


def compact(listed, base, sources):
    _, lane = rows_and_lanes()
    filled = jnp.int32(0)
    moved = []
    for tile, count in sources:
        at = lax.bitwise_and(filled, LANES - 1)
        tile_id = base + lax.shift_right_logical(filled, 7)
        moved.append((pltpu.roll(tile, at, 1), lane >= at, tile_id, at + count >= LANES))
        filled = filled + count
    current = jnp.zeros((ROWS, LANES), jnp.float32)
    for tile, behind, tile_id, full in moved:
        current = jnp.where(behind, tile, current)
        spill = jnp.where(behind, 0.0, tile)
        listed[tile_id] = current
        listed[tile_id + 1] = spill
        current = jnp.where(full, spill, current)
    return filled


def up_to(count, size):
    return lax.shift_right_logical(count + (size - 1), size.bit_length() - 1)


def parts_of(value, n):
    parts = []
    for _ in range(n):
        part = value.astype(jnp.bfloat16)
        value = value - part.astype(jnp.float32)
        parts.append(part)
    return parts


def spread_targets(spread, first, tile):
    parts = [p.astype(jnp.float32) for p in parts_of(tile, 3)] + [jnp.zeros_like(tile)]
    row, lane = rows_and_lanes((4 * ROWS, 3 * LANES))
    pick = jnp.where(lax.bitwise_and(row, ROWS - 1) == lax.shift_right_logical(lane, 7), 1.0, 0.0)
    wide = lax.dot_general(
        jnp.concatenate(parts, axis=0).astype(jnp.bfloat16),
        pick.astype(jnp.bfloat16),
        (((0,), (0,)), ((), ())),
        preferred_element_type=jnp.float32,
    )
    for i in range(3):
        spread[i, first : first + LANES, :] = wide[:, i * LANES : (i + 1) * LANES]


def coefficients(target, source, force):
    delta = [t - s for t, s in zip(target, source)]
    u = (delta[0] * delta[0] + SOFT_U) + delta[1] * delta[1] + delta[2] * delta[2]
    inv = lax.rsqrt(u)
    tail = (1.0 - lax.erf(u * inv)) * inv
    gauss = jnp.exp2(LOG2_G - u * LOG2_E)
    rest = gauss * (u - 1.5)
    coef_d = ((tail - rest) - gauss) * pl.reciprocal(u, approx=True)
    along = coef_d * (delta[0] * force[0] + delta[1] * force[1] + delta[2] * force[2])
    return tail + rest, along


class Groups:
    def __init__(self, tables):
        self.tables = tables
        self.size = 0
        self.total = jnp.int32(0)

    def add(self, n_chunks, n_tiles, first_tile, spread_row, acc_row):
        for table, value in zip(self.tables, (n_chunks, n_tiles, first_tile, spread_row, acc_row)):
            table[self.size] = jnp.int32(value)
        self.size += 1
        self.total = self.total + n_chunks * n_tiles

    def run(self, listed, spread, coefs, acc):
        chunks_of, tiles_of, list_of, spread_of, acc_of = self.tables
        trash = acc.shape[1] - CHUNK

        def rows(tile_id):
            single = [listed[tile_id, i : i + 1, :] for i in (0, 1, 2, 4, 5, 6)]
            return single[:3], single[3:]

        def advance(group, chunk, tile):
            end_tile = tile + 1 == tiles_of[group]
            next_chunk = jnp.where(end_tile, chunk + CHUNK, chunk)
            end_chunk = next_chunk == chunks_of[group] * CHUNK
            next_group = jnp.where(end_chunk, jnp.minimum(group + 1, self.size - 1), group)
            return next_group, jnp.where(end_chunk, 0, next_chunk), jnp.where(end_tile, 0, tile + 1)

        def find(step, place):
            units, found = [], []
            for n in range(UNITS):
                group, chunk, tile = place
                valid = step * UNITS + n < self.total
                units += [jnp.where(valid, acc_of[group] + chunk, trash), list_of[group] + tile]
                at = pl.ds(pl.multiple_of(spread_of[group] + chunk, CHUNK), CHUNK)
                target = [spread[i, at, :] for i in range(3)]
                found.append(coefficients(target, *rows(units[-1])))
                place = advance(*place)
            return found, tuple(units), place

        def use(units):
            terms = []
            for n, tile in enumerate(units[1::2]):
                coef_c, along = coefs[n, 0], coefs[n, 1]
                source, force = rows(tile)
                terms.append([coef_c * force[i] - along * source[i] for i in range(3)] + [along])
            return terms

        def keep(found):
            for n, pair in enumerate(found):
                coefs[n, 0], coefs[n, 1] = pair

        def add(units, terms):
            for first, unit in zip(units[::2], terms):
                at = pl.ds(pl.multiple_of(first, CHUNK), CHUNK)
                for i in range(4):
                    acc[i, at, :] = acc[i, at, :] + unit[i]

        def body(step, state):
            place, olds = state[:3], state[3:]
            terms = use(olds)
            found, news, place = find(step, place)
            add(olds, terms)
            keep(found)
            return place + news

        zero = jnp.int32(0)
        found, units, place = find(0, (zero, zero, zero))
        keep(found)
        state = lax.fori_loop(1, lax.div(self.total + UNITS - 1, UNITS), body, place + units)
        add(state[3:], use(state[3:]))


def is_full(cells, count_ref):
    filled = jnp.int32(0)
    heavy = jnp.int32(0)
    for at in bins_of(cells):
        count = count_ref[at]
        filled = filled + count
        heavy = heavy + jnp.where(count > LANES // 2, 1, 0)
    return filled, heavy == len(bins_of(cells)), filled > MANY


def list_own(cells, count_ref, own_ref, listed):
    sources = [(own_ref[at] + shift_tile(cells, at), count_ref[at]) for at in bins_of(cells)]
    compact(listed, 0, sources)


def velocity_rows(cells, group, by_row, tile):
    position = tile + shift_tile(cells, bins_of(cells)[group])
    return (2.0 * STOKES_NORM) * (by_row + position * jnp.broadcast_to(by_row[3:4], (ROWS, LANES)))


def lane_sums(sums, n_bins):
    row, lane = rows_and_lanes((2 * LANES * len(sums), LANES))
    pick = lax.bitwise_and(lane, ROWS - 1) == lax.shift_right_logical(row, (2 * LANES).bit_length() - 1)
    merged = jnp.dot(
        jnp.concatenate([p for part in sums for p in parts_of(part, 2)], axis=1),
        jnp.where(pick, 1.0, 0.0).astype(jnp.bfloat16),
        preferred_element_type=jnp.float32,
    )
    _, lane = rows_and_lanes((LANES, LANES))
    chosen = merged[:LANES]
    for n in range(1, n_bins):
        chosen = jnp.where(lane >= n * ROWS, merged[n * LANES : (n + 1) * LANES], chosen)
    turned = jnp.transpose(chosen)
    return [turned[n * ROWS : (n + 1) * ROWS] for n in range(n_bins)]


def pack_kernel(cells, count_hbm, offset_hbm, force_hbm, own_ref, early_ref, *refs):
    (count_ref, offset_v, force_v, sems, listed, spread, coefs, acc), tables = refs[:8], refs[8:]
    copies = [
        pltpu.make_async_copy(source, target, sems.at[n])
        for n, (source, target) in enumerate(
            ((count_hbm, count_ref), (offset_hbm, offset_v), (force_hbm, force_v))
        )
    ]
    for copy in copies:
        copy.start()
    for copy in copies:
        copy.wait()
    slot = lax.broadcasted_iota(jnp.int32, (1, LANES), 1)
    for at in bins_of(cells):
        ix, iy, iz = at
        count = count_ref[at]
        wide = jnp.full((1, LANES), count, jnp.int32).astype(jnp.float32)
        for i in range(3):
            position = offset_v[i, ix, iy, iz : iz + 1, :]
            own_ref[ix, iy, iz, i : i + 1, :] = position * SPLIT_XI - 0.5 * SPLIT_XI
            force = force_v[i, ix, iy, iz : iz + 1, :]
            own_ref[ix, iy, iz, 4 + i : 5 + i, :] = jnp.where(slot < count, force, 0.0)
        own_ref[ix, iy, iz, 3:4, :] = wide
        own_ref[ix, iy, iz, 7:8, :] = wide
    early_ref[...] = jnp.zeros_like(early_ref)
    filled, full, _ = is_full(cells, count_ref)

    @pl.when(full)
    def _():
        list_own(cells, count_ref, own_ref, listed)
        acc[...] = jnp.zeros_like(acc)
        groups = range(EARLY)
        tiles = [own_ref[bins_of(cells)[n]] for n in groups]
        work = Groups(tables)
        for n in groups:
            at = bins_of(cells)[n]
            spread_targets(spread, n * LANES, tiles[n] + shift_tile(cells, at))
            work.add(up_to(count_ref[at], CHUNK), up_to(filled, LANES), 0, n * LANES, n * LANES)
        work.run(listed, spread, coefs, acc)
        by_rows = lane_sums([acc[i, : EARLY * LANES, :] for i in range(4)], EARLY)
        for n, by_row in enumerate(by_rows):
            early_ref[n] = velocity_rows(cells, n, by_row, tiles[n])


def counts_of(tiles):
    return [tile[COUNT_ROW, 0].astype(jnp.int32) for tile in tiles]


def first_kernel(cells, sent_ref, own_ref, listed, spread, acc, coefs, *tables):
    bins = bins_of(cells)
    count_s = counts_of([sent_ref[at] for at in bins])
    own_ref[...] = sent_ref[...]
    for n, at in enumerate(bins):
        spread_targets(spread, n * LANES, own_ref[at] + shift_tile(cells, at))
    acc[...] = jnp.zeros_like(acc)
    count_ref = {at: count_s[n] for n, at in enumerate(bins)}
    list_own(cells, count_ref, own_ref, listed)
    filled, full, many = is_full(cells, count_ref)
    work = Groups(tables)
    for m, n in enumerate(FIRST):
        n_chunks = jnp.where(many if n in FIRST_IF_MANY else full, up_to(count_ref[bins[n]], CHUNK), 0)
        work.add(n_chunks, up_to(filled, LANES), 0, n * LANES, m * LANES)
    work.run(listed, spread, coefs, acc)


def second_kernel(cells, count_ref, other, own_list, spread, first, acc, listed, coefs, *tables):
    bins = bins_of(cells)
    size_x, size_y, size_z = cells
    count_s = counts_of([other[at] for at in bins])
    for n in range(len(bins)):
        here = slice(n * LANES, (n + 1) * LANES)
        if n in FIRST:
            m = FIRST.index(n)
            acc[:, here, :] = first[:, m * LANES : (m + 1) * LANES, :]
        else:
            acc[:, here, :] = jnp.zeros((4, LANES, LANES), jnp.float32)
    n_own = own_list.shape[0]
    for n in range(n_own):
        listed[n] = own_list[n]
    filled, full, many = is_full(cells, count_ref)
    work = Groups(tables)
    for bz in range(size_z):
        z = (-1, size_z)[bz]
        sources = []
        for x in range(size_x):
            for y in range(size_y):
                place = (x, y, z % size_z)
                tile = other[place] + shift_tile(cells, (x, y, z))
                sources.append((tile, count_s[bins.index(place)]))
        first_tile = n_own + bz * LIST_Z
        n_tiles = up_to(compact(listed, first_tile, sources), LANES)
        for n, at in enumerate(bins):
            if at[2] == bz:
                work.add(up_to(count_ref[at], CHUNK), n_tiles, first_tile, n * LANES, n * LANES)
    for n in SECOND:
        n_chunks = up_to(count_ref[bins[n]], CHUNK)
        if n < EARLY or n in FIRST:
            n_chunks = jnp.where(many if n in FIRST_IF_MANY else full, 0, n_chunks)
        work.add(n_chunks, up_to(filled, LANES), 0, n * LANES, n * LANES)
    work.run(listed, spread, coefs, acc)


def middle_kernel(cells, count_ref, wide, spread, _, acc, listed, coefs, *tables):
    size_x, size_y, size_z = cells
    n_z = 2 * size_z
    bins = bins_of(cells)
    places = [(i, j, k) for i in (0, size_x + 1) for j in range(size_y) for k in range(n_z)]
    count_s = counts_of([wide[at] for at in places])
    work = Groups(tables)
    for bx in range(size_x):
        for bz in range(size_z):
            x = (-1, size_x)[bx]
            sources = []
            for y in range(size_y):
                for z in (bz - 1, bz, bz + 1):
                    place = (x + 1, y, z % n_z)
                    tile = wide[place] + shift_tile(cells, (x, y, z))
                    sources.append((tile, count_s[places.index(place)]))
            first_tile = (bx * size_z + bz) * LIST_X
            n_tiles = up_to(compact(listed, first_tile, sources), LANES)
            for n, at in enumerate(bins):
                if (at[0], at[2]) == (bx, bz):
                    work.add(up_to(count_ref[at], CHUNK), n_tiles, first_tile, n * LANES, n * LANES)
    work.run(listed, spread, coefs, acc)


def last_kernel(cells, count_ref, own_ref, y_lo, y_hi, spread, *refs):
    (_, early, out_ref, acc, listed, coefs), tables = refs[:6], refs[6:]
    size_x, size_y, size_z = cells
    n_z = 2 * size_z
    bins = bins_of(cells)
    places = [(i, j, k) for i in range(size_x + 2) for j in range(2) for k in range(n_z)]
    tiles = [(y_lo, y_hi)[j][i, 0, k] for i, j, k in places]
    count_s = counts_of(tiles)
    work = Groups(tables)
    for n, (bx, by, bz) in enumerate(bins):
        sources = []
        for x in (bx - 1, bx, bx + 1):
            for z in (bz - 1, bz, bz + 1):
                cell = places.index((x + 1, by, z % n_z))
                tile = tiles[cell] + shift_tile(cells, (x, (-1, size_y)[by], z))
                sources.append((tile, count_s[cell]))
        n_tiles = up_to(compact(listed, n * LIST_Y, sources), LANES)
        first_tile = n * LIST_Y
        work.add(up_to(count_ref[bx, by, bz], CHUNK), n_tiles, first_tile, n * LANES, n * LANES)
    work.run(listed, spread, coefs, acc)

    slot = lax.broadcasted_iota(jnp.int32, (1, LANES), 1)
    by_rows = lane_sums([acc[i, : len(bins) * LANES, :] for i in range(4)], len(bins))
    for n, (at, by_row) in enumerate(zip(bins, by_rows)):
        tile = own_ref[at]
        total = velocity_rows(cells, n, by_row, tile)
        total = total - (STOKES_NORM * SELF_C) * pltpu.roll(tile, ROWS - FORCE_ROW, 0)
        if n < EARLY:
            total = total + early[n]
        total = jnp.where(slot < count_ref[at], total, 0.0)
        for i in range(3):
            out_ref[i, at[0], at[1], at[2] : at[2] + 1, :] = total[i : i + 1]


def shifted(first, last, axis):
    size = lax.axis_size(axis)
    up = [(i, (i + 1) % size) for i in range(size)]
    if size % 2:
        down = [(j, i) for i, j in up]
        return lax.ppermute(last, axis, up), lax.ppermute(first, axis, down)
    odd = lax.rem(lax.axis_index(axis), 2) == 1
    got = []
    for parity in (0, 1):
        pairs = [pair for i, j in up if i % 2 == parity for pair in ((i, j), (j, i))]
        got.append(lax.ppermute(jnp.where(odd == bool(parity), last, first), axis, pairs))
    return jnp.where(odd, got[0], got[1]), jnp.where(odd, got[1], got[0])


def on_device(offsets, forces, counts):
    cells = offsets.shape[1:4]
    slots = offsets.shape[4]
    n_bins = cells[0] * cells[1] * cells[2]
    n_targets = n_bins * slots
    whole = pl.BlockSpec(memory_space=pltpu.VMEM)
    scalars = pl.BlockSpec(memory_space=pltpu.SMEM)

    def floats(*shape):
        return jax.ShapeDtypeStruct(shape, jnp.float32)

    def params(mib):
        return pltpu.CompilerParams(vmem_limit_bytes=mib << 20)

    loop_scratch = [pltpu.VMEM((UNITS, 2, CHUNK, LANES), jnp.float32)]
    loop_scratch += [pltpu.SMEM((2 * n_bins,), jnp.int32)] * 5
    cost = pl.CostEstimate(flops=1 << 28, bytes_accessed=1 << 16, transcendentals=1 << 20)

    def in_place(sums):
        return pltpu.with_memory_space_constraint(sums, pltpu.VMEM)

    def list_scratch(n_tiles):
        return [pltpu.VMEM((n_tiles, ROWS, LANES), jnp.float32)]

    own_list, all_targets = floats(n_bins + 1, ROWS, slots), floats(3, n_targets, slots)
    arguments = [pltpu.with_memory_space_constraint(x, pltpu.HBM) for x in (counts, offsets, forces)]
    sent, early = pl.pallas_call(
        functools.partial(pack_kernel, cells),
        out_shape=[floats(*cells, ROWS, slots), floats(EARLY, ROWS, slots)],
        in_specs=[pl.BlockSpec(memory_space=pltpu.HBM)] * 3,
        out_specs=[whole, whole],
        scratch_shapes=[
            pltpu.SMEM(counts.shape, jnp.int32),
            pltpu.VMEM(offsets.shape, jnp.float32),
            pltpu.VMEM(forces.shape, jnp.float32),
            pltpu.SemaphoreType.DMA((3,)),
            pltpu.VMEM(own_list.shape, jnp.float32),
            pltpu.VMEM((3, EARLY * slots, slots), jnp.float32),
            loop_scratch[0],
            pltpu.VMEM((4, EARLY * slots + CHUNK, slots), jnp.float32),
        ]
        + loop_scratch[1:],
        compiler_params=params(8),
        name="pack",
    )(*arguments)

    together = lax.optimization_barrier
    size = lax.axis_size("ha")
    other = lax.ppermute(sent, "ha", [(i, (i + 1) % size) for i in range(size)])
    own, listed, spread, first = pl.pallas_call(
        functools.partial(first_kernel, cells),
        out_shape=[sent, own_list, all_targets, floats(4, len(FIRST) * slots + CHUNK, slots)],
        in_specs=[whole],
        out_specs=[whole] * 4,
        scratch_shapes=loop_scratch,
        compiler_params=params(8),
        cost_estimate=cost,
        name="first",
    )(sent)
    other, own, listed, first = together((other, own, listed, first))
    column = jnp.concatenate([own, other], axis=2)
    x_lo, x_hi = shifted(column[:1], column[cells[0] - 1 :], "gx")
    second = pl.pallas_call(
        functools.partial(second_kernel, cells),
        out_shape=floats(4, n_targets + CHUNK, slots),
        in_specs=[scalars] + [whole] * 4,
        out_specs=whole,
        scratch_shapes=list_scratch(cells[2] * LIST_Z + n_bins + 1)
        + loop_scratch,
        compiler_params=params(8),
        cost_estimate=cost,
        name="second",
    )(counts, other, listed, spread, first)
    x_lo, x_hi, second = together((x_lo, x_hi, second))
    wide = jnp.concatenate([x_lo, column, x_hi], axis=0)
    y_lo, y_hi = shifted(wide[:, :1], wide[:, cells[1] - 1 :], "gy")
    middle = pl.pallas_call(
        functools.partial(middle_kernel, cells),
        out_shape=floats(4, n_targets + CHUNK, slots),
        in_specs=[scalars] + [whole] * 3,
        out_specs=whole,
        scratch_shapes=list_scratch(cells[0] * cells[2] * LIST_X) + loop_scratch,
        input_output_aliases={3: 0},
        compiler_params=params(8),
        cost_estimate=cost,
        name="middle",
    )(counts, wide, spread, in_place(second))
    y_lo, y_hi, middle = together((y_lo, y_hi, middle))
    return pl.pallas_call(
        functools.partial(last_kernel, cells),
        out_shape=[floats(3, *cells, slots), floats(4, n_targets + CHUNK, slots)],
        in_specs=[scalars] + [whole] * 6,
        out_specs=[whole, whole],
        scratch_shapes=list_scratch(n_bins * LIST_Y)
        + loop_scratch,
        input_output_aliases={5: 1},
        compiler_params=params(12),
        cost_estimate=cost,
        name="last",
    )(counts, own, y_lo, y_hi, spread, in_place(middle), early)[0]


def solution(mesh):
    in_specs = (
        P(None, "gx", "gy", "ha", None),
        P(None, "gx", "gy", "ha", None),
        P("gx", "gy", "ha"),
    )
    out_specs = P(None, "gx", "gy", "ha", None)
    return jax.shard_map(on_device, mesh=mesh, in_specs=in_specs, out_specs=out_specs, check_vma=False)
```

```python
import functools
import math

import jax
import jax.numpy as jnp
from jax import lax
from jax.experimental import pallas as pl
from jax.experimental.pallas import tpu as pltpu
from jax.sharding import PartitionSpec as P

SPLIT_XI = 2.0
SOFT_SQ = 0.01
GAUSS_COEF = 2.0 * SPLIT_XI / math.sqrt(math.pi)
STOKES_NORM = 1.0 / (8.0 * math.pi)

SOFT_U = SPLIT_XI * SPLIT_XI * SOFT_SQ
LOG2_E = math.log2(math.e)
LOG2_G = math.log2(GAUSS_COEF)
SELF_C = math.erfc(math.sqrt(SOFT_U)) / math.sqrt(SOFT_SQ) + GAUSS_COEF * (
    2.0 * SOFT_U - 3.0
) * math.exp(-SOFT_U)

LANES = 128
ROWS = 8
CHUNK = 32
UNITS = 4
COUNT_ROW = 3
MANY = 440
EARLY = 3
FIRST = (3, 4, 5)
SECOND = (6, 7, 5, 0, 1, 2, 3, 4)
FIRST_IF_MANY = (3, 4)
LIST_Z, LIST_X, LIST_Y = 5, 7, 10
FORCE_ROW = 4


def rows_and_lanes(shape=(ROWS, LANES)):
    return lax.broadcasted_iota(jnp.int32, shape, 0), lax.broadcasted_iota(jnp.int32, shape, 1)


def bins_of(cells):
    return [(i, j, k) for i in range(cells[0]) for j in range(cells[1]) for k in range(cells[2])]


def shift_tile(cells, at):
    row, _ = rows_and_lanes()
    moved = jnp.zeros((ROWS, LANES), jnp.float32)
    for i in range(3):
        moved = jnp.where(row == i, SPLIT_XI * (at[i] - 0.5 * (cells[i] - 1)), moved)
    return moved


def compact(listed, base, sources):
    _, lane = rows_and_lanes()
    filled = jnp.int32(0)
    moved = []
    for tile, count in sources:
        at = lax.bitwise_and(filled, LANES - 1)
        tile_id = base + lax.shift_right_logical(filled, 7)
        moved.append((pltpu.roll(tile, at, 1), lane >= at, tile_id, at + count >= LANES))
        filled = filled + count
    current = jnp.zeros((ROWS, LANES), jnp.float32)
    for tile, behind, tile_id, full in moved:
        current = jnp.where(behind, tile, current)
        spill = jnp.where(behind, 0.0, tile)
        listed[tile_id] = current
        listed[tile_id + 1] = spill
        current = jnp.where(full, spill, current)
    return filled


def up_to(count, size):
    return lax.shift_right_logical(count + (size - 1), size.bit_length() - 1)


def parts_of(value, n):
    parts = []
    for _ in range(n):
        part = value.astype(jnp.bfloat16)
        value = value - part.astype(jnp.float32)
        parts.append(part)
    return parts


def spread_targets(spread, first, tile):
    parts = [p.astype(jnp.float32) for p in parts_of(tile, 3)] + [jnp.zeros_like(tile)]
    row, lane = rows_and_lanes((4 * ROWS, 3 * LANES))
    pick = jnp.where(lax.bitwise_and(row, ROWS - 1) == lax.shift_right_logical(lane, 7), 1.0, 0.0)
    wide = lax.dot_general(
        jnp.concatenate(parts, axis=0).astype(jnp.bfloat16),
        pick.astype(jnp.bfloat16),
        (((0,), (0,)), ((), ())),
        preferred_element_type=jnp.float32,
    )
    for i in range(3):
        spread[i, first : first + LANES, :] = wide[:, i * LANES : (i + 1) * LANES]


def coefficients(target, source, force):
    delta = [t - s for t, s in zip(target, source)]
    u = (delta[0] * delta[0] + SOFT_U) + delta[1] * delta[1] + delta[2] * delta[2]
    inv = lax.rsqrt(u)
    tail = (1.0 - lax.erf(u * inv)) * inv
    gauss = jnp.exp2(LOG2_G - u * LOG2_E)
    rest = gauss * (u - 1.5)
    coef_d = ((tail - rest) - gauss) * pl.reciprocal(u, approx=True)
    along = coef_d * (delta[0] * force[0] + delta[1] * force[1] + delta[2] * force[2])
    return tail + rest, along


class Groups:
    def __init__(self, tables):
        self.tables = tables
        self.size = 0
        self.total = jnp.int32(0)

    def add(self, n_chunks, n_tiles, first_tile, spread_row, acc_row):
        for table, value in zip(self.tables, (n_chunks, n_tiles, first_tile, spread_row, acc_row)):
            table[self.size] = jnp.int32(value)
        self.size += 1
        self.total = self.total + n_chunks * n_tiles

    def run(self, listed, spread, coefs, acc):
        chunks_of, tiles_of, list_of, spread_of, acc_of = self.tables
        trash = acc.shape[1] - CHUNK

        def rows(tile_id):
            single = [listed[tile_id, i : i + 1, :] for i in (0, 1, 2, 4, 5, 6)]
            return single[:3], single[3:]

        def advance(group, chunk, tile):
            end_tile = tile + 1 == tiles_of[group]
            next_chunk = jnp.where(end_tile, chunk + CHUNK, chunk)
            end_chunk = next_chunk == chunks_of[group] * CHUNK
            next_group = jnp.where(end_chunk, jnp.minimum(group + 1, self.size - 1), group)
            return next_group, jnp.where(end_chunk, 0, next_chunk), jnp.where(end_tile, 0, tile + 1)

        def find(step, place):
            units, found = [], []
            for n in range(UNITS):
                group, chunk, tile = place
                valid = step * UNITS + n < self.total
                units += [jnp.where(valid, acc_of[group] + chunk, trash), list_of[group] + tile]
                at = pl.ds(pl.multiple_of(spread_of[group] + chunk, CHUNK), CHUNK)
                target = [spread[i, at, :] for i in range(3)]
                found.append(coefficients(target, *rows(units[-1])))
                place = advance(*place)
            return found, tuple(units), place

        def use(units):
            terms = []
            for n, tile in enumerate(units[1::2]):
                coef_c, along = coefs[n, 0], coefs[n, 1]
                source, force = rows(tile)
                terms.append([coef_c * force[i] - along * source[i] for i in range(3)] + [along])
            return terms

        def keep(found):
            for n, pair in enumerate(found):
                coefs[n, 0], coefs[n, 1] = pair

        def add(units, terms):
            for first, unit in zip(units[::2], terms):
                at = pl.ds(pl.multiple_of(first, CHUNK), CHUNK)
                for i in range(4):
                    acc[i, at, :] = acc[i, at, :] + unit[i]

        def body(step, state):
            place, olds = state[:3], state[3:]
            terms = use(olds)
            found, news, place = find(step, place)
            add(olds, terms)
            keep(found)
            return place + news

        zero = jnp.int32(0)
        found, units, place = find(0, (zero, zero, zero))
        keep(found)
        state = lax.fori_loop(1, lax.div(self.total + UNITS - 1, UNITS), body, place + units)
        add(state[3:], use(state[3:]))


def is_full(cells, count_ref):
    filled = jnp.int32(0)
    heavy = jnp.int32(0)
    for at in bins_of(cells):
        count = count_ref[at]
        filled = filled + count
        heavy = heavy + jnp.where(count > LANES // 2, 1, 0)
    return filled, heavy == len(bins_of(cells)), filled > MANY


def list_own(cells, count_ref, own_ref, listed):
    sources = [(own_ref[at] + shift_tile(cells, at), count_ref[at]) for at in bins_of(cells)]
    compact(listed, 0, sources)


def velocity_rows(cells, group, by_row, tile):
    position = tile + shift_tile(cells, bins_of(cells)[group])
    return (2.0 * STOKES_NORM) * (by_row + position * jnp.broadcast_to(by_row[3:4], (ROWS, LANES)))


def lane_sums(sums, n_bins):
    row, lane = rows_and_lanes((2 * LANES * len(sums), LANES))
    pick = lax.bitwise_and(lane, ROWS - 1) == lax.shift_right_logical(row, (2 * LANES).bit_length() - 1)
    pick = jnp.where(pick, 1.0, 0.0).astype(jnp.bfloat16)
    middle = n_bins // 2 * LANES
    merged = []
    for rows in (slice(0, middle), slice(middle, n_bins * LANES)):
        parts = [p for part in sums for p in parts_of(part[rows], 2)]
        product = jnp.dot(jnp.concatenate(parts, axis=1), pick, preferred_element_type=jnp.float32)
        merged += [product[n : n + LANES] for n in range(0, product.shape[0], LANES)]
    _, lane = rows_and_lanes((LANES, LANES))
    chosen = merged[0]
    for n in range(1, n_bins):
        chosen = jnp.where(lane >= n * ROWS, merged[n], chosen)
    turned = jnp.transpose(chosen)
    return [turned[n * ROWS : (n + 1) * ROWS] for n in range(n_bins)]


def pack_kernel(cells, count_hbm, offset_hbm, force_hbm, own_ref, early_ref, *refs):
    (count_ref, offset_v, force_v, sems, listed, spread, coefs, acc), tables = refs[:8], refs[8:]
    copies = [
        pltpu.make_async_copy(source, target, sems.at[n])
        for n, (source, target) in enumerate(
            ((count_hbm, count_ref), (offset_hbm, offset_v), (force_hbm, force_v))
        )
    ]
    for copy in copies:
        copy.start()
    for copy in copies:
        copy.wait()
    slot = lax.broadcasted_iota(jnp.int32, (1, LANES), 1)
    for at in bins_of(cells):
        ix, iy, iz = at
        count = count_ref[at]
        wide = jnp.full((1, LANES), count, jnp.int32).astype(jnp.float32)
        for i in range(3):
            position = offset_v[i, ix, iy, iz : iz + 1, :]
            own_ref[ix, iy, iz, i : i + 1, :] = position * SPLIT_XI - 0.5 * SPLIT_XI
            force = force_v[i, ix, iy, iz : iz + 1, :]
            own_ref[ix, iy, iz, 4 + i : 5 + i, :] = jnp.where(slot < count, force, 0.0)
        own_ref[ix, iy, iz, 3:4, :] = wide
        own_ref[ix, iy, iz, 7:8, :] = wide
    early_ref[...] = jnp.zeros_like(early_ref)
    filled, full, _ = is_full(cells, count_ref)

    @pl.when(full)
    def _():
        list_own(cells, count_ref, own_ref, listed)
        acc[...] = jnp.zeros_like(acc)
        groups = range(EARLY)
        tiles = [own_ref[bins_of(cells)[n]] for n in groups]
        work = Groups(tables)
        for n in groups:
            at = bins_of(cells)[n]
            spread_targets(spread, n * LANES, tiles[n] + shift_tile(cells, at))
            work.add(up_to(count_ref[at], CHUNK), up_to(filled, LANES), 0, n * LANES, n * LANES)
        work.run(listed, spread, coefs, acc)
        by_rows = lane_sums([acc[i, : EARLY * LANES, :] for i in range(4)], EARLY)
        for n, by_row in enumerate(by_rows):
            early_ref[n] = velocity_rows(cells, n, by_row, tiles[n])


def counts_of(tiles):
    return [tile[COUNT_ROW, 0].astype(jnp.int32) for tile in tiles]


def first_kernel(cells, sent_ref, own_ref, listed, spread, acc, coefs, *tables):
    bins = bins_of(cells)
    count_s = counts_of([sent_ref[at] for at in bins])
    own_ref[...] = sent_ref[...]
    for n, at in enumerate(bins):
        spread_targets(spread, n * LANES, own_ref[at] + shift_tile(cells, at))
    acc[...] = jnp.zeros_like(acc)
    count_ref = {at: count_s[n] for n, at in enumerate(bins)}
    list_own(cells, count_ref, own_ref, listed)
    filled, full, many = is_full(cells, count_ref)
    work = Groups(tables)
    for m, n in enumerate(FIRST):
        n_chunks = jnp.where(many if n in FIRST_IF_MANY else full, up_to(count_ref[bins[n]], CHUNK), 0)
        work.add(n_chunks, up_to(filled, LANES), 0, n * LANES, m * LANES)
    work.run(listed, spread, coefs, acc)


def second_kernel(cells, count_ref, other, own_list, spread, first, acc, listed, coefs, *tables):
    bins = bins_of(cells)
    size_x, size_y, size_z = cells
    count_s = counts_of([other[at] for at in bins])
    for n in range(len(bins)):
        here = slice(n * LANES, (n + 1) * LANES)
        if n in FIRST:
            m = FIRST.index(n)
            acc[:, here, :] = first[:, m * LANES : (m + 1) * LANES, :]
        else:
            acc[:, here, :] = jnp.zeros((4, LANES, LANES), jnp.float32)
    n_own = own_list.shape[0]
    for n in range(n_own):
        listed[n] = own_list[n]
    filled, full, many = is_full(cells, count_ref)
    work = Groups(tables)
    for bz in range(size_z):
        z = (-1, size_z)[bz]
        sources = []
        for x in range(size_x):
            for y in range(size_y):
                place = (x, y, z % size_z)
                tile = other[place] + shift_tile(cells, (x, y, z))
                sources.append((tile, count_s[bins.index(place)]))
        first_tile = n_own + bz * LIST_Z
        n_tiles = up_to(compact(listed, first_tile, sources), LANES)
        for n, at in enumerate(bins):
            if at[2] == bz:
                work.add(up_to(count_ref[at], CHUNK), n_tiles, first_tile, n * LANES, n * LANES)
    for n in SECOND:
        n_chunks = up_to(count_ref[bins[n]], CHUNK)
        if n < EARLY or n in FIRST:
            n_chunks = jnp.where(many if n in FIRST_IF_MANY else full, 0, n_chunks)
        work.add(n_chunks, up_to(filled, LANES), 0, n * LANES, n * LANES)
    work.run(listed, spread, coefs, acc)


def middle_kernel(cells, count_ref, wide, spread, _, acc, listed, coefs, *tables):
    size_x, size_y, size_z = cells
    n_z = 2 * size_z
    bins = bins_of(cells)
    places = [(i, j, k) for i in (0, size_x + 1) for j in range(size_y) for k in range(n_z)]
    count_s = counts_of([wide[at] for at in places])
    work = Groups(tables)
    for bx in range(size_x):
        for bz in range(size_z):
            x = (-1, size_x)[bx]
            sources = []
            for y in range(size_y):
                for z in (bz - 1, bz, bz + 1):
                    place = (x + 1, y, z % n_z)
                    tile = wide[place] + shift_tile(cells, (x, y, z))
                    sources.append((tile, count_s[places.index(place)]))
            first_tile = (bx * size_z + bz) * LIST_X
            n_tiles = up_to(compact(listed, first_tile, sources), LANES)
            for n, at in enumerate(bins):
                if (at[0], at[2]) == (bx, bz):
                    work.add(up_to(count_ref[at], CHUNK), n_tiles, first_tile, n * LANES, n * LANES)
    work.run(listed, spread, coefs, acc)


def last_kernel(cells, count_ref, own_ref, y_lo, y_hi, spread, *refs):
    (_, early, out_ref, acc, listed, coefs), tables = refs[:6], refs[6:]
    size_x, size_y, size_z = cells
    n_z = 2 * size_z
    bins = bins_of(cells)
    places = [(i, j, k) for i in range(size_x + 2) for j in range(2) for k in range(n_z)]
    tiles = [(y_lo, y_hi)[j][i, 0, k] for i, j, k in places]
    count_s = counts_of(tiles)
    work = Groups(tables)
    for n, (bx, by, bz) in enumerate(bins):
        sources = []
        for x in (bx - 1, bx, bx + 1):
            for z in (bz - 1, bz, bz + 1):
                cell = places.index((x + 1, by, z % n_z))
                tile = tiles[cell] + shift_tile(cells, (x, (-1, size_y)[by], z))
                sources.append((tile, count_s[cell]))
        n_tiles = up_to(compact(listed, n * LIST_Y, sources), LANES)
        first_tile = n * LIST_Y
        work.add(up_to(count_ref[bx, by, bz], CHUNK), n_tiles, first_tile, n * LANES, n * LANES)
    work.run(listed, spread, coefs, acc)

    slot = lax.broadcasted_iota(jnp.int32, (1, LANES), 1)
    by_rows = lane_sums([acc[i, : len(bins) * LANES, :] for i in range(4)], len(bins))
    for n, (at, by_row) in enumerate(zip(bins, by_rows)):
        tile = own_ref[at]
        total = velocity_rows(cells, n, by_row, tile)
        total = total - (STOKES_NORM * SELF_C) * pltpu.roll(tile, ROWS - FORCE_ROW, 0)
        if n < EARLY:
            total = total + early[n]
        total = jnp.where(slot < count_ref[at], total, 0.0)
        for i in range(3):
            out_ref[i, at[0], at[1], at[2] : at[2] + 1, :] = total[i : i + 1]


def shifted(first, last, axis):
    size = lax.axis_size(axis)
    up = [(i, (i + 1) % size) for i in range(size)]
    if size % 2:
        down = [(j, i) for i, j in up]
        return lax.ppermute(last, axis, up), lax.ppermute(first, axis, down)
    odd = lax.rem(lax.axis_index(axis), 2) == 1
    got = []
    for parity in (0, 1):
        pairs = [pair for i, j in up if i % 2 == parity for pair in ((i, j), (j, i))]
        got.append(lax.ppermute(jnp.where(odd == bool(parity), last, first), axis, pairs))
    return jnp.where(odd, got[0], got[1]), jnp.where(odd, got[1], got[0])


def on_device(offsets, forces, counts):
    cells = offsets.shape[1:4]
    slots = offsets.shape[4]
    n_bins = cells[0] * cells[1] * cells[2]
    n_targets = n_bins * slots
    whole = pl.BlockSpec(memory_space=pltpu.VMEM)
    scalars = pl.BlockSpec(memory_space=pltpu.SMEM)

    def floats(*shape):
        return jax.ShapeDtypeStruct(shape, jnp.float32)

    def params(mib):
        return pltpu.CompilerParams(vmem_limit_bytes=mib << 20)

    loop_scratch = [pltpu.VMEM((UNITS, 2, CHUNK, LANES), jnp.float32)]
    loop_scratch += [pltpu.SMEM((2 * n_bins,), jnp.int32)] * 5
    cost = pl.CostEstimate(flops=1 << 28, bytes_accessed=1 << 16, transcendentals=1 << 20)

    def in_place(sums):
        return pltpu.with_memory_space_constraint(sums, pltpu.VMEM)

    def list_scratch(n_tiles):
        return [pltpu.VMEM((n_tiles, ROWS, LANES), jnp.float32)]

    own_list, all_targets = floats(n_bins + 1, ROWS, slots), floats(3, n_targets, slots)
    arguments = [pltpu.with_memory_space_constraint(x, pltpu.HBM) for x in (counts, offsets, forces)]
    sent, early = pl.pallas_call(
        functools.partial(pack_kernel, cells),
        out_shape=[floats(*cells, ROWS, slots), floats(EARLY, ROWS, slots)],
        in_specs=[pl.BlockSpec(memory_space=pltpu.HBM)] * 3,
        out_specs=[whole, whole],
        scratch_shapes=[
            pltpu.SMEM(counts.shape, jnp.int32),
            pltpu.VMEM(offsets.shape, jnp.float32),
            pltpu.VMEM(forces.shape, jnp.float32),
            pltpu.SemaphoreType.DMA((3,)),
            pltpu.VMEM(own_list.shape, jnp.float32),
            pltpu.VMEM((3, EARLY * slots, slots), jnp.float32),
            loop_scratch[0],
            pltpu.VMEM((4, EARLY * slots + CHUNK, slots), jnp.float32),
        ]
        + loop_scratch[1:],
        compiler_params=params(8),
        name="pack",
    )(*arguments)

    together = lax.optimization_barrier
    size = lax.axis_size("ha")
    other = lax.ppermute(sent, "ha", [(i, (i + 1) % size) for i in range(size)])
    own, listed, spread, first = pl.pallas_call(
        functools.partial(first_kernel, cells),
        out_shape=[sent, own_list, all_targets, floats(4, len(FIRST) * slots + CHUNK, slots)],
        in_specs=[whole],
        out_specs=[whole] * 4,
        scratch_shapes=loop_scratch,
        compiler_params=params(8),
        cost_estimate=cost,
        name="first",
    )(sent)
    other, own, listed, first = together((other, own, listed, first))
    column = jnp.concatenate([own, other], axis=2)
    x_lo, x_hi = shifted(column[:1], column[cells[0] - 1 :], "gx")
    second = pl.pallas_call(
        functools.partial(second_kernel, cells),
        out_shape=floats(4, n_targets + CHUNK, slots),
        in_specs=[scalars] + [whole] * 4,
        out_specs=whole,
        scratch_shapes=list_scratch(cells[2] * LIST_Z + n_bins + 1)
        + loop_scratch,
        compiler_params=params(8),
        cost_estimate=cost,
        name="second",
    )(counts, other, listed, spread, first)
    x_lo, x_hi, second = together((x_lo, x_hi, second))
    wide = jnp.concatenate([x_lo, column, x_hi], axis=0)
    y_lo, y_hi = shifted(wide[:, :1], wide[:, cells[1] - 1 :], "gy")
    middle = pl.pallas_call(
        functools.partial(middle_kernel, cells),
        out_shape=floats(4, n_targets + CHUNK, slots),
        in_specs=[scalars] + [whole] * 3,
        out_specs=whole,
        scratch_shapes=list_scratch(cells[0] * cells[2] * LIST_X) + loop_scratch,
        input_output_aliases={3: 0},
        compiler_params=params(8),
        cost_estimate=cost,
        name="middle",
    )(counts, wide, spread, in_place(second))
    y_lo, y_hi, middle = together((y_lo, y_hi, middle))
    return pl.pallas_call(
        functools.partial(last_kernel, cells),
        out_shape=[floats(3, *cells, slots), floats(4, n_targets + CHUNK, slots)],
        in_specs=[scalars] + [whole] * 6,
        out_specs=[whole, whole],
        scratch_shapes=list_scratch(n_bins * LIST_Y)
        + loop_scratch,
        input_output_aliases={5: 1},
        compiler_params=params(12),
        cost_estimate=cost,
        name="last",
    )(counts, own, y_lo, y_hi, spread, in_place(middle), early)[0]


def solution(mesh):
    in_specs = (
        P(None, "gx", "gy", "ha", None),
        P(None, "gx", "gy", "ha", None),
        P("gx", "gy", "ha"),
    )
    out_specs = P(None, "gx", "gy", "ha", None)
    return jax.shard_map(on_device, mesh=mesh, in_specs=in_specs, out_specs=out_specs, check_vma=False)
```

```python
import functools
import math

import jax
import jax.numpy as jnp
from jax import lax
from jax.experimental import pallas as pl
from jax.experimental.pallas import tpu as pltpu
from jax.sharding import PartitionSpec as P

SPLIT_XI = 2.0
SOFT_SQ = 0.01
GAUSS_COEF = 2.0 * SPLIT_XI / math.sqrt(math.pi)
STOKES_NORM = 1.0 / (8.0 * math.pi)

SOFT_U = SPLIT_XI * SPLIT_XI * SOFT_SQ
LOG2_E = math.log2(math.e)
LOG2_G = math.log2(GAUSS_COEF)
SELF_C = math.erfc(math.sqrt(SOFT_U)) / math.sqrt(SOFT_SQ) + GAUSS_COEF * (
    2.0 * SOFT_U - 3.0
) * math.exp(-SOFT_U)

LANES = 128
ROWS = 8
CHUNK = 32
UNITS = 4
COUNT_ROW = 3
MANY = 440
EARLY = 3
FIRST = (3, 4, 5)
SECOND = (6, 7, 5, 0, 1, 2, 3, 4)
FIRST_IF_MANY = (3, 4)
LIST_Z, LIST_X, LIST_Y = 5, 7, 10
FORCE_ROW = 4


def rows_and_lanes(shape=(ROWS, LANES)):
    return lax.broadcasted_iota(jnp.int32, shape, 0), lax.broadcasted_iota(jnp.int32, shape, 1)


def bins_of(cells):
    return [(i, j, k) for i in range(cells[0]) for j in range(cells[1]) for k in range(cells[2])]


def shift_tile(cells, at):
    row, _ = rows_and_lanes()
    moved = jnp.zeros((ROWS, LANES), jnp.float32)
    for i in range(3):
        moved = jnp.where(row == i, SPLIT_XI * (at[i] - 0.5 * (cells[i] - 1)), moved)
    return moved


def compact(listed, base, sources):
    _, lane = rows_and_lanes()
    filled = jnp.int32(0)
    moved = []
    for tile, count in sources:
        at = lax.bitwise_and(filled, LANES - 1)
        tile_id = base + lax.shift_right_logical(filled, 7)
        moved.append((pltpu.roll(tile, at, 1), lane >= at, tile_id, at + count >= LANES))
        filled = filled + count
    current = jnp.zeros((ROWS, LANES), jnp.float32)
    for tile, behind, tile_id, full in moved:
        current = jnp.where(behind, tile, current)
        spill = jnp.where(behind, 0.0, tile)
        listed[tile_id] = current
        listed[tile_id + 1] = spill
        current = jnp.where(full, spill, current)
    return filled


def up_to(count, size):
    return lax.shift_right_logical(count + (size - 1), size.bit_length() - 1)


def parts_of(value, n):
    parts = []
    for _ in range(n):
        part = value.astype(jnp.bfloat16)
        value = value - part.astype(jnp.float32)
        parts.append(part)
    return parts


def spread_targets(spread, first, tile):
    parts = [p.astype(jnp.float32) for p in parts_of(tile, 3)] + [jnp.zeros_like(tile)]
    row, lane = rows_and_lanes((4 * ROWS, 3 * LANES))
    pick = jnp.where(lax.bitwise_and(row, ROWS - 1) == lax.shift_right_logical(lane, 7), 1.0, 0.0)
    wide = lax.dot_general(
        jnp.concatenate(parts, axis=0).astype(jnp.bfloat16),
        pick.astype(jnp.bfloat16),
        (((0,), (0,)), ((), ())),
        preferred_element_type=jnp.float32,
    )
    for i in range(3):
        spread[i, first : first + LANES, :] = wide[:, i * LANES : (i + 1) * LANES]


def coefficients(target, source, force):
    delta = [t - s for t, s in zip(target, source)]
    u = (delta[0] * delta[0] + SOFT_U) + delta[1] * delta[1] + delta[2] * delta[2]
    inv = lax.rsqrt(u)
    tail = (1.0 - lax.erf(u * inv)) * inv
    gauss = jnp.exp2(LOG2_G - u * LOG2_E)
    rest = gauss * (u - 1.5)
    coef_d = ((tail - rest) - gauss) * pl.reciprocal(u, approx=True)
    along = coef_d * (delta[0] * force[0] + delta[1] * force[1] + delta[2] * force[2])
    return tail + rest, along


class Groups:
    def __init__(self, tables):
        self.tables = tables
        self.size = 0
        self.total = jnp.int32(0)

    def add(self, n_chunks, n_tiles, first_tile, spread_row, acc_row):
        for table, value in zip(self.tables, (n_chunks, n_tiles, first_tile, spread_row, acc_row)):
            table[self.size] = jnp.int32(value)
        self.size += 1
        self.total = self.total + n_chunks * n_tiles

    def run(self, listed, spread, coefs, acc):
        chunks_of, tiles_of, list_of, spread_of, acc_of = self.tables
        trash = acc.shape[1] - CHUNK

        def rows(tile_id):
            single = [listed[tile_id, i : i + 1, :] for i in (0, 1, 2, 4, 5, 6)]
            return single[:3], single[3:]

        def advance(group, chunk, tile):
            end_tile = tile + 1 == tiles_of[group]
            next_chunk = jnp.where(end_tile, chunk + CHUNK, chunk)
            end_chunk = next_chunk == chunks_of[group] * CHUNK
            next_group = jnp.where(end_chunk, jnp.minimum(group + 1, self.size - 1), group)
            return next_group, jnp.where(end_chunk, 0, next_chunk), jnp.where(end_tile, 0, tile + 1)

        def find(step, place):
            units, found = [], []
            for n in range(UNITS):
                group, chunk, tile = place
                valid = step * UNITS + n < self.total
                units += [jnp.where(valid, acc_of[group] + chunk, trash), list_of[group] + tile]
                at = pl.ds(pl.multiple_of(spread_of[group] + chunk, CHUNK), CHUNK)
                target = [spread[i, at, :] for i in range(3)]
                found.append(coefficients(target, *rows(units[-1])))
                place = advance(*place)
            return found, tuple(units), place

        def use(units):
            terms = []
            for n, tile in enumerate(units[1::2]):
                coef_c, along = coefs[n, 0], coefs[n, 1]
                source, force = rows(tile)
                terms.append([coef_c * force[i] - along * source[i] for i in range(3)] + [along])
            return terms

        def keep(found):
            for n, pair in enumerate(found):
                coefs[n, 0], coefs[n, 1] = pair

        def add(units, terms):
            for first, unit in zip(units[::2], terms):
                at = pl.ds(pl.multiple_of(first, CHUNK), CHUNK)
                for i in range(4):
                    acc[i, at, :] = acc[i, at, :] + unit[i]

        def body(step, state):
            place, olds = state[:3], state[3:]
            terms = use(olds)
            found, news, place = find(step, place)
            add(olds, terms)
            keep(found)
            return place + news

        zero = jnp.int32(0)
        found, units, place = find(0, (zero, zero, zero))
        keep(found)
        state = lax.fori_loop(1, lax.div(self.total + UNITS - 1, UNITS), body, place + units)
        add(state[3:], use(state[3:]))


def is_full(cells, count_ref):
    filled = jnp.int32(0)
    heavy = jnp.int32(0)
    for at in bins_of(cells):
        count = count_ref[at]
        filled = filled + count
        heavy = heavy + jnp.where(count > LANES // 2, 1, 0)
    return filled, heavy == len(bins_of(cells)), filled > MANY


def list_own(cells, count_ref, own_ref, listed):
    sources = [(own_ref[at] + shift_tile(cells, at), count_ref[at]) for at in bins_of(cells)]
    compact(listed, 0, sources)


def velocity_rows(cells, group, by_row, tile):
    position = tile + shift_tile(cells, bins_of(cells)[group])
    return (2.0 * STOKES_NORM) * (by_row + position * jnp.broadcast_to(by_row[3:4], (ROWS, LANES)))


def lane_sums(sums, n_bins):
    row, lane = rows_and_lanes((2 * LANES * len(sums), LANES))
    pick = lax.bitwise_and(lane, ROWS - 1) == lax.shift_right_logical(row, (2 * LANES).bit_length() - 1)
    pick = jnp.where(pick, 1.0, 0.0).astype(jnp.bfloat16)
    merged = []
    for first in range(0, n_bins, 2):
        rows = slice(first * LANES, min(first + 2, n_bins) * LANES)
        parts = [p for part in sums for p in parts_of(part[rows], 2)]
        product = jnp.dot(jnp.concatenate(parts, axis=1), pick, preferred_element_type=jnp.float32)
        merged += [product[n : n + LANES] for n in range(0, product.shape[0], LANES)]
    _, lane = rows_and_lanes((LANES, LANES))
    chosen = merged[0]
    for n in range(1, n_bins):
        chosen = jnp.where(lane >= n * ROWS, merged[n], chosen)
    turned = jnp.transpose(chosen)
    return [turned[n * ROWS : (n + 1) * ROWS] for n in range(n_bins)]


def pack_kernel(cells, count_hbm, offset_hbm, force_hbm, own_ref, early_ref, *refs):
    (count_ref, offset_v, force_v, sems, listed, spread, coefs, acc), tables = refs[:8], refs[8:]
    copies = [
        pltpu.make_async_copy(source, target, sems.at[n])
        for n, (source, target) in enumerate(
            ((count_hbm, count_ref), (offset_hbm, offset_v), (force_hbm, force_v))
        )
    ]
    for copy in copies:
        copy.start()
    for copy in copies:
        copy.wait()
    slot = lax.broadcasted_iota(jnp.int32, (1, LANES), 1)
    for at in bins_of(cells):
        ix, iy, iz = at
        count = count_ref[at]
        wide = jnp.full((1, LANES), count, jnp.int32).astype(jnp.float32)
        for i in range(3):
            position = offset_v[i, ix, iy, iz : iz + 1, :]
            own_ref[ix, iy, iz, i : i + 1, :] = position * SPLIT_XI - 0.5 * SPLIT_XI
            force = force_v[i, ix, iy, iz : iz + 1, :]
            own_ref[ix, iy, iz, 4 + i : 5 + i, :] = jnp.where(slot < count, force, 0.0)
        own_ref[ix, iy, iz, 3:4, :] = wide
        own_ref[ix, iy, iz, 7:8, :] = wide
    early_ref[...] = jnp.zeros_like(early_ref)
    filled, full, _ = is_full(cells, count_ref)

    @pl.when(full)
    def _():
        list_own(cells, count_ref, own_ref, listed)
        acc[...] = jnp.zeros_like(acc)
        groups = range(EARLY)
        tiles = [own_ref[bins_of(cells)[n]] for n in groups]
        work = Groups(tables)
        for n in groups:
            at = bins_of(cells)[n]
            spread_targets(spread, n * LANES, tiles[n] + shift_tile(cells, at))
            work.add(up_to(count_ref[at], CHUNK), up_to(filled, LANES), 0, n * LANES, n * LANES)
        work.run(listed, spread, coefs, acc)
        by_rows = lane_sums([acc[i, : EARLY * LANES, :] for i in range(4)], EARLY)
        for n, by_row in enumerate(by_rows):
            early_ref[n] = velocity_rows(cells, n, by_row, tiles[n])


def counts_of(tiles):
    return [tile[COUNT_ROW, 0].astype(jnp.int32) for tile in tiles]


def first_kernel(cells, sent_ref, own_ref, listed, spread, acc, coefs, *tables):
    bins = bins_of(cells)
    count_s = counts_of([sent_ref[at] for at in bins])
    own_ref[...] = sent_ref[...]
    for n, at in enumerate(bins):
        spread_targets(spread, n * LANES, own_ref[at] + shift_tile(cells, at))
    acc[...] = jnp.zeros_like(acc)
    count_ref = {at: count_s[n] for n, at in enumerate(bins)}
    list_own(cells, count_ref, own_ref, listed)
    filled, full, many = is_full(cells, count_ref)
    work = Groups(tables)
    for m, n in enumerate(FIRST):
        n_chunks = jnp.where(many if n in FIRST_IF_MANY else full, up_to(count_ref[bins[n]], CHUNK), 0)
        work.add(n_chunks, up_to(filled, LANES), 0, n * LANES, m * LANES)
    work.run(listed, spread, coefs, acc)


def second_kernel(cells, count_ref, other, own_list, spread, first, acc, listed, coefs, *tables):
    bins = bins_of(cells)
    size_x, size_y, size_z = cells
    count_s = counts_of([other[at] for at in bins])
    for n in range(len(bins)):
        here = slice(n * LANES, (n + 1) * LANES)
        if n in FIRST:
            m = FIRST.index(n)
            acc[:, here, :] = first[:, m * LANES : (m + 1) * LANES, :]
        else:
            acc[:, here, :] = jnp.zeros((4, LANES, LANES), jnp.float32)
    n_own = own_list.shape[0]
    for n in range(n_own):
        listed[n] = own_list[n]
    filled, full, many = is_full(cells, count_ref)
    work = Groups(tables)
    for bz in range(size_z):
        z = (-1, size_z)[bz]
        sources = []
        for x in range(size_x):
            for y in range(size_y):
                place = (x, y, z % size_z)
                tile = other[place] + shift_tile(cells, (x, y, z))
                sources.append((tile, count_s[bins.index(place)]))
        first_tile = n_own + bz * LIST_Z
        n_tiles = up_to(compact(listed, first_tile, sources), LANES)
        for n, at in enumerate(bins):
            if at[2] == bz:
                work.add(up_to(count_ref[at], CHUNK), n_tiles, first_tile, n * LANES, n * LANES)
    for n in SECOND:
        n_chunks = up_to(count_ref[bins[n]], CHUNK)
        if n < EARLY or n in FIRST:
            n_chunks = jnp.where(many if n in FIRST_IF_MANY else full, 0, n_chunks)
        work.add(n_chunks, up_to(filled, LANES), 0, n * LANES, n * LANES)
    work.run(listed, spread, coefs, acc)


def middle_kernel(cells, count_ref, wide, spread, _, acc, listed, coefs, *tables):
    size_x, size_y, size_z = cells
    n_z = 2 * size_z
    bins = bins_of(cells)
    places = [(i, j, k) for i in (0, size_x + 1) for j in range(size_y) for k in range(n_z)]
    count_s = counts_of([wide[at] for at in places])
    work = Groups(tables)
    for bx in range(size_x):
        for bz in range(size_z):
            x = (-1, size_x)[bx]
            sources = []
            for y in range(size_y):
                for z in (bz - 1, bz, bz + 1):
                    place = (x + 1, y, z % n_z)
                    tile = wide[place] + shift_tile(cells, (x, y, z))
                    sources.append((tile, count_s[places.index(place)]))
            first_tile = (bx * size_z + bz) * LIST_X
            n_tiles = up_to(compact(listed, first_tile, sources), LANES)
            for n, at in enumerate(bins):
                if (at[0], at[2]) == (bx, bz):
                    work.add(up_to(count_ref[at], CHUNK), n_tiles, first_tile, n * LANES, n * LANES)
    work.run(listed, spread, coefs, acc)


def last_kernel(cells, count_ref, own_ref, y_lo, y_hi, spread, *refs):
    (_, early, out_ref, acc, listed, coefs), tables = refs[:6], refs[6:]
    size_x, size_y, size_z = cells
    n_z = 2 * size_z
    bins = bins_of(cells)
    places = [(i, j, k) for i in range(size_x + 2) for j in range(2) for k in range(n_z)]
    tiles = [(y_lo, y_hi)[j][i, 0, k] for i, j, k in places]
    count_s = counts_of(tiles)
    work = Groups(tables)
    for n, (bx, by, bz) in enumerate(bins):
        sources = []
        for x in (bx - 1, bx, bx + 1):
            for z in (bz - 1, bz, bz + 1):
                cell = places.index((x + 1, by, z % n_z))
                tile = tiles[cell] + shift_tile(cells, (x, (-1, size_y)[by], z))
                sources.append((tile, count_s[cell]))
        n_tiles = up_to(compact(listed, n * LIST_Y, sources), LANES)
        first_tile = n * LIST_Y
        work.add(up_to(count_ref[bx, by, bz], CHUNK), n_tiles, first_tile, n * LANES, n * LANES)
    work.run(listed, spread, coefs, acc)

    slot = lax.broadcasted_iota(jnp.int32, (1, LANES), 1)
    by_rows = lane_sums([acc[i, : len(bins) * LANES, :] for i in range(4)], len(bins))
    for n, (at, by_row) in enumerate(zip(bins, by_rows)):
        tile = own_ref[at]
        total = velocity_rows(cells, n, by_row, tile)
        total = total - (STOKES_NORM * SELF_C) * pltpu.roll(tile, ROWS - FORCE_ROW, 0)
        if n < EARLY:
            total = total + early[n]
        total = jnp.where(slot < count_ref[at], total, 0.0)
        for i in range(3):
            out_ref[i, at[0], at[1], at[2] : at[2] + 1, :] = total[i : i + 1]


def shifted(first, last, axis):
    size = lax.axis_size(axis)
    up = [(i, (i + 1) % size) for i in range(size)]
    if size % 2:
        down = [(j, i) for i, j in up]
        return lax.ppermute(last, axis, up), lax.ppermute(first, axis, down)
    odd = lax.rem(lax.axis_index(axis), 2) == 1
    got = []
    for parity in (0, 1):
        pairs = [pair for i, j in up if i % 2 == parity for pair in ((i, j), (j, i))]
        got.append(lax.ppermute(jnp.where(odd == bool(parity), last, first), axis, pairs))
    return jnp.where(odd, got[0], got[1]), jnp.where(odd, got[1], got[0])


def on_device(offsets, forces, counts):
    cells = offsets.shape[1:4]
    slots = offsets.shape[4]
    n_bins = cells[0] * cells[1] * cells[2]
    n_targets = n_bins * slots
    whole = pl.BlockSpec(memory_space=pltpu.VMEM)
    scalars = pl.BlockSpec(memory_space=pltpu.SMEM)

    def floats(*shape):
        return jax.ShapeDtypeStruct(shape, jnp.float32)

    def params(mib):
        return pltpu.CompilerParams(vmem_limit_bytes=mib << 20)

    loop_scratch = [pltpu.VMEM((UNITS, 2, CHUNK, LANES), jnp.float32)]
    loop_scratch += [pltpu.SMEM((2 * n_bins,), jnp.int32)] * 5
    cost = pl.CostEstimate(flops=1 << 28, bytes_accessed=1 << 16, transcendentals=1 << 20)

    def in_place(sums):
        return pltpu.with_memory_space_constraint(sums, pltpu.VMEM)

    def list_scratch(n_tiles):
        return [pltpu.VMEM((n_tiles, ROWS, LANES), jnp.float32)]

    own_list, all_targets = floats(n_bins + 1, ROWS, slots), floats(3, n_targets, slots)
    arguments = [pltpu.with_memory_space_constraint(x, pltpu.HBM) for x in (counts, offsets, forces)]
    sent, early = pl.pallas_call(
        functools.partial(pack_kernel, cells),
        out_shape=[floats(*cells, ROWS, slots), floats(EARLY, ROWS, slots)],
        in_specs=[pl.BlockSpec(memory_space=pltpu.HBM)] * 3,
        out_specs=[whole, whole],
        scratch_shapes=[
            pltpu.SMEM(counts.shape, jnp.int32),
            pltpu.VMEM(offsets.shape, jnp.float32),
            pltpu.VMEM(forces.shape, jnp.float32),
            pltpu.SemaphoreType.DMA((3,)),
            pltpu.VMEM(own_list.shape, jnp.float32),
            pltpu.VMEM((3, EARLY * slots, slots), jnp.float32),
            loop_scratch[0],
            pltpu.VMEM((4, EARLY * slots + CHUNK, slots), jnp.float32),
        ]
        + loop_scratch[1:],
        compiler_params=params(8),
        name="pack",
    )(*arguments)

    together = lax.optimization_barrier
    size = lax.axis_size("ha")
    other = lax.ppermute(sent, "ha", [(i, (i + 1) % size) for i in range(size)])
    own, listed, spread, first = pl.pallas_call(
        functools.partial(first_kernel, cells),
        out_shape=[sent, own_list, all_targets, floats(4, len(FIRST) * slots + CHUNK, slots)],
        in_specs=[whole],
        out_specs=[whole] * 4,
        scratch_shapes=loop_scratch,
        compiler_params=params(8),
        cost_estimate=cost,
        name="first",
    )(sent)
    other, own, listed, first = together((other, own, listed, first))
    column = jnp.concatenate([own, other], axis=2)
    x_lo, x_hi = shifted(column[:1], column[cells[0] - 1 :], "gx")
    second = pl.pallas_call(
        functools.partial(second_kernel, cells),
        out_shape=floats(4, n_targets + CHUNK, slots),
        in_specs=[scalars] + [whole] * 4,
        out_specs=whole,
        scratch_shapes=list_scratch(cells[2] * LIST_Z + n_bins + 1)
        + loop_scratch,
        compiler_params=params(8),
        cost_estimate=cost,
        name="second",
    )(counts, other, listed, spread, first)
    x_lo, x_hi, second = together((x_lo, x_hi, second))
    wide = jnp.concatenate([x_lo, column, x_hi], axis=0)
    y_lo, y_hi = shifted(wide[:, :1], wide[:, cells[1] - 1 :], "gy")
    middle = pl.pallas_call(
        functools.partial(middle_kernel, cells),
        out_shape=floats(4, n_targets + CHUNK, slots),
        in_specs=[scalars] + [whole] * 3,
        out_specs=whole,
        scratch_shapes=list_scratch(cells[0] * cells[2] * LIST_X) + loop_scratch,
        input_output_aliases={3: 0},
        compiler_params=params(8),
        cost_estimate=cost,
        name="middle",
    )(counts, wide, spread, in_place(second))
    y_lo, y_hi, middle = together((y_lo, y_hi, middle))
    return pl.pallas_call(
        functools.partial(last_kernel, cells),
        out_shape=[floats(3, *cells, slots), floats(4, n_targets + CHUNK, slots)],
        in_specs=[scalars] + [whole] * 6,
        out_specs=[whole, whole],
        scratch_shapes=list_scratch(n_bins * LIST_Y)
        + loop_scratch,
        input_output_aliases={5: 1},
        compiler_params=params(12),
        cost_estimate=cost,
        name="last",
    )(counts, own, y_lo, y_hi, spread, in_place(middle), early)[0]


def solution(mesh):
    in_specs = (
        P(None, "gx", "gy", "ha", None),
        P(None, "gx", "gy", "ha", None),
        P("gx", "gy", "ha"),
    )
    out_specs = P(None, "gx", "gy", "ha", None)
    return jax.shard_map(on_device, mesh=mesh, in_specs=in_specs, out_specs=out_specs, check_vma=False)
```

```python
import functools
import math

import jax
import jax.numpy as jnp
from jax import lax
from jax.experimental import pallas as pl
from jax.experimental.pallas import tpu as pltpu
from jax.sharding import PartitionSpec as P

SPLIT_XI = 2.0
SOFT_SQ = 0.01
GAUSS_COEF = 2.0 * SPLIT_XI / math.sqrt(math.pi)
STOKES_NORM = 1.0 / (8.0 * math.pi)

SOFT_U = SPLIT_XI * SPLIT_XI * SOFT_SQ
LOG2_E = math.log2(math.e)
LOG2_G = math.log2(GAUSS_COEF)
SELF_C = math.erfc(math.sqrt(SOFT_U)) / math.sqrt(SOFT_SQ) + GAUSS_COEF * (
    2.0 * SOFT_U - 3.0
) * math.exp(-SOFT_U)

LANES = 128
ROWS = 8
CHUNK = 16
UNITS = 8
COUNT_ROW = 3
MANY = 440
EARLY = 3
FIRST = (3, 4, 5)
SECOND = (6, 7, 5, 0, 1, 2, 3, 4)
FIRST_IF_MANY = (3, 4)
LIST_Z, LIST_X, LIST_Y = 5, 7, 10
FORCE_ROW = 4


def rows_and_lanes(shape=(ROWS, LANES)):
    return lax.broadcasted_iota(jnp.int32, shape, 0), lax.broadcasted_iota(jnp.int32, shape, 1)


def bins_of(cells):
    return [(i, j, k) for i in range(cells[0]) for j in range(cells[1]) for k in range(cells[2])]


def shift_tile(cells, at):
    row, _ = rows_and_lanes()
    moved = jnp.zeros((ROWS, LANES), jnp.float32)
    for i in range(3):
        moved = jnp.where(row == i, SPLIT_XI * (at[i] - 0.5 * (cells[i] - 1)), moved)
    return moved


def compact(listed, base, sources):
    _, lane = rows_and_lanes()
    filled = jnp.int32(0)
    moved = []
    for tile, count in sources:
        at = lax.bitwise_and(filled, LANES - 1)
        tile_id = base + lax.shift_right_logical(filled, 7)
        moved.append((pltpu.roll(tile, at, 1), lane >= at, tile_id, at + count >= LANES))
        filled = filled + count
    current = jnp.zeros((ROWS, LANES), jnp.float32)
    for tile, behind, tile_id, full in moved:
        current = jnp.where(behind, tile, current)
        spill = jnp.where(behind, 0.0, tile)
        listed[tile_id] = current
        listed[tile_id + 1] = spill
        current = jnp.where(full, spill, current)
    return filled


def up_to(count, size):
    return lax.shift_right_logical(count + (size - 1), size.bit_length() - 1)


def parts_of(value, n):
    parts = []
    for _ in range(n):
        part = value.astype(jnp.bfloat16)
        value = value - part.astype(jnp.float32)
        parts.append(part)
    return parts


def spread_targets(spread, first, tile):
    parts = [p.astype(jnp.float32) for p in parts_of(tile, 3)] + [jnp.zeros_like(tile)]
    row, lane = rows_and_lanes((4 * ROWS, 3 * LANES))
    pick = jnp.where(lax.bitwise_and(row, ROWS - 1) == lax.shift_right_logical(lane, 7), 1.0, 0.0)
    wide = lax.dot_general(
        jnp.concatenate(parts, axis=0).astype(jnp.bfloat16),
        pick.astype(jnp.bfloat16),
        (((0,), (0,)), ((), ())),
        preferred_element_type=jnp.float32,
    )
    for i in range(3):
        spread[i, first : first + LANES, :] = wide[:, i * LANES : (i + 1) * LANES]


def coefficients(target, source, force):
    delta = [t - s for t, s in zip(target, source)]
    u = (delta[0] * delta[0] + SOFT_U) + delta[1] * delta[1] + delta[2] * delta[2]
    inv = lax.rsqrt(u)
    tail = (1.0 - lax.erf(u * inv)) * inv
    gauss = jnp.exp2(LOG2_G - u * LOG2_E)
    rest = gauss * (u - 1.5)
    coef_d = ((tail - rest) - gauss) * pl.reciprocal(u, approx=True)
    along = coef_d * (delta[0] * force[0] + delta[1] * force[1] + delta[2] * force[2])
    return tail + rest, along


class Groups:
    def __init__(self, tables):
        self.tables = tables
        self.size = 0
        self.total = jnp.int32(0)

    def add(self, n_chunks, n_tiles, first_tile, spread_row, acc_row):
        for table, value in zip(self.tables, (n_chunks, n_tiles, first_tile, spread_row, acc_row)):
            table[self.size] = jnp.int32(value)
        self.size += 1
        self.total = self.total + n_chunks * n_tiles

    def run(self, listed, spread, coefs, acc):
        chunks_of, tiles_of, list_of, spread_of, acc_of = self.tables
        trash = acc.shape[1] - CHUNK

        def rows(tile_id):
            single = [listed[tile_id, i : i + 1, :] for i in (0, 1, 2, 4, 5, 6)]
            return single[:3], single[3:]

        def advance(group, chunk, tile):
            end_tile = tile + 1 == tiles_of[group]
            next_chunk = jnp.where(end_tile, chunk + CHUNK, chunk)
            end_chunk = next_chunk == chunks_of[group] * CHUNK
            next_group = jnp.where(end_chunk, jnp.minimum(group + 1, self.size - 1), group)
            return next_group, jnp.where(end_chunk, 0, next_chunk), jnp.where(end_tile, 0, tile + 1)

        def find(step, place):
            units, found = [], []
            for n in range(UNITS):
                group, chunk, tile = place
                valid = step * UNITS + n < self.total
                units += [jnp.where(valid, acc_of[group] + chunk, trash), list_of[group] + tile]
                at = pl.ds(pl.multiple_of(spread_of[group] + chunk, CHUNK), CHUNK)
                target = [spread[i, at, :] for i in range(3)]
                found.append(coefficients(target, *rows(units[-1])))
                place = advance(*place)
            return found, tuple(units), place

        def use(units):
            terms = []
            for n, tile in enumerate(units[1::2]):
                coef_c, along = coefs[n, 0], coefs[n, 1]
                source, force = rows(tile)
                terms.append([coef_c * force[i] - along * source[i] for i in range(3)] + [along])
            return terms

        def keep(found):
            for n, pair in enumerate(found):
                coefs[n, 0], coefs[n, 1] = pair

        def add(units, terms):
            for first, unit in zip(units[::2], terms):
                at = pl.ds(pl.multiple_of(first, CHUNK), CHUNK)
                for i in range(4):
                    acc[i, at, :] = acc[i, at, :] + unit[i]

        def body(step, state):
            place, olds = state[:3], state[3:]
            terms = use(olds)
            found, news, place = find(step, place)
            add(olds, terms)
            keep(found)
            return place + news

        zero = jnp.int32(0)
        found, units, place = find(0, (zero, zero, zero))
        keep(found)
        state = lax.fori_loop(1, lax.div(self.total + UNITS - 1, UNITS), body, place + units)
        add(state[3:], use(state[3:]))


def is_full(cells, count_ref):
    filled = jnp.int32(0)
    heavy = jnp.int32(0)
    for at in bins_of(cells):
        count = count_ref[at]
        filled = filled + count
        heavy = heavy + jnp.where(count > LANES // 2, 1, 0)
    return filled, heavy == len(bins_of(cells)), filled > MANY


def list_own(cells, count_ref, own_ref, listed):
    sources = [(own_ref[at] + shift_tile(cells, at), count_ref[at]) for at in bins_of(cells)]
    compact(listed, 0, sources)


def velocity_rows(cells, group, by_row, tile):
    position = tile + shift_tile(cells, bins_of(cells)[group])
    return (2.0 * STOKES_NORM) * (by_row + position * jnp.broadcast_to(by_row[3:4], (ROWS, LANES)))


def lane_sums(sums, n_bins):
    row, lane = rows_and_lanes((2 * LANES * len(sums), LANES))
    pick = lax.bitwise_and(lane, ROWS - 1) == lax.shift_right_logical(row, (2 * LANES).bit_length() - 1)
    pick = jnp.where(pick, 1.0, 0.0).astype(jnp.bfloat16)
    merged = []
    for first in range(0, n_bins, 2):
        rows = slice(first * LANES, min(first + 2, n_bins) * LANES)
        parts = [p for part in sums for p in parts_of(part[rows], 2)]
        product = jnp.dot(jnp.concatenate(parts, axis=1), pick, preferred_element_type=jnp.float32)
        merged += [product[n : n + LANES] for n in range(0, product.shape[0], LANES)]
    _, lane = rows_and_lanes((LANES, LANES))
    chosen = merged[0]
    for n in range(1, n_bins):
        chosen = jnp.where(lane >= n * ROWS, merged[n], chosen)
    turned = jnp.transpose(chosen)
    return [turned[n * ROWS : (n + 1) * ROWS] for n in range(n_bins)]


def pack_kernel(cells, count_hbm, offset_hbm, force_hbm, own_ref, early_ref, *refs):
    (count_ref, offset_v, force_v, sems, listed, spread, coefs, acc), tables = refs[:8], refs[8:]
    copies = [
        pltpu.make_async_copy(source, target, sems.at[n])
        for n, (source, target) in enumerate(
            ((count_hbm, count_ref), (offset_hbm, offset_v), (force_hbm, force_v))
        )
    ]
    for copy in copies:
        copy.start()
    for copy in copies:
        copy.wait()
    slot = lax.broadcasted_iota(jnp.int32, (1, LANES), 1)
    for at in bins_of(cells):
        ix, iy, iz = at
        count = count_ref[at]
        wide = jnp.full((1, LANES), count, jnp.int32).astype(jnp.float32)
        for i in range(3):
            position = offset_v[i, ix, iy, iz : iz + 1, :]
            own_ref[ix, iy, iz, i : i + 1, :] = position * SPLIT_XI - 0.5 * SPLIT_XI
            force = force_v[i, ix, iy, iz : iz + 1, :]
            own_ref[ix, iy, iz, 4 + i : 5 + i, :] = jnp.where(slot < count, force, 0.0)
        own_ref[ix, iy, iz, 3:4, :] = wide
        own_ref[ix, iy, iz, 7:8, :] = wide
    early_ref[...] = jnp.zeros_like(early_ref)
    filled, full, _ = is_full(cells, count_ref)

    @pl.when(full)
    def _():
        list_own(cells, count_ref, own_ref, listed)
        acc[...] = jnp.zeros_like(acc)
        groups = range(EARLY)
        tiles = [own_ref[bins_of(cells)[n]] for n in groups]
        work = Groups(tables)
        for n in groups:
            at = bins_of(cells)[n]
            spread_targets(spread, n * LANES, tiles[n] + shift_tile(cells, at))
            work.add(up_to(count_ref[at], CHUNK), up_to(filled, LANES), 0, n * LANES, n * LANES)
        work.run(listed, spread, coefs, acc)
        by_rows = lane_sums([acc[i, : EARLY * LANES, :] for i in range(4)], EARLY)
        for n, by_row in enumerate(by_rows):
            early_ref[n] = velocity_rows(cells, n, by_row, tiles[n])


def counts_of(tiles):
    return [tile[COUNT_ROW, 0].astype(jnp.int32) for tile in tiles]


def first_kernel(cells, sent_ref, own_ref, listed, spread, acc, coefs, *tables):
    bins = bins_of(cells)
    count_s = counts_of([sent_ref[at] for at in bins])
    own_ref[...] = sent_ref[...]
    for n, at in enumerate(bins):
        spread_targets(spread, n * LANES, own_ref[at] + shift_tile(cells, at))
    acc[...] = jnp.zeros_like(acc)
    count_ref = {at: count_s[n] for n, at in enumerate(bins)}
    list_own(cells, count_ref, own_ref, listed)
    filled, full, many = is_full(cells, count_ref)
    work = Groups(tables)
    for m, n in enumerate(FIRST):
        n_chunks = jnp.where(many if n in FIRST_IF_MANY else full, up_to(count_ref[bins[n]], CHUNK), 0)
        work.add(n_chunks, up_to(filled, LANES), 0, n * LANES, m * LANES)
    work.run(listed, spread, coefs, acc)


def second_kernel(cells, count_ref, other, own_list, spread, first, acc, listed, coefs, *tables):
    bins = bins_of(cells)
    size_x, size_y, size_z = cells
    count_s = counts_of([other[at] for at in bins])
    for n in range(len(bins)):
        here = slice(n * LANES, (n + 1) * LANES)
        if n in FIRST:
            m = FIRST.index(n)
            acc[:, here, :] = first[:, m * LANES : (m + 1) * LANES, :]
        else:
            acc[:, here, :] = jnp.zeros((4, LANES, LANES), jnp.float32)
    n_own = own_list.shape[0]
    for n in range(n_own):
        listed[n] = own_list[n]
    filled, full, many = is_full(cells, count_ref)
    work = Groups(tables)
    for bz in range(size_z):
        z = (-1, size_z)[bz]
        sources = []
        for x in range(size_x):
            for y in range(size_y):
                place = (x, y, z % size_z)
                tile = other[place] + shift_tile(cells, (x, y, z))
                sources.append((tile, count_s[bins.index(place)]))
        first_tile = n_own + bz * LIST_Z
        n_tiles = up_to(compact(listed, first_tile, sources), LANES)
        for n, at in enumerate(bins):
            if at[2] == bz:
                work.add(up_to(count_ref[at], CHUNK), n_tiles, first_tile, n * LANES, n * LANES)
    for n in SECOND:
        n_chunks = up_to(count_ref[bins[n]], CHUNK)
        if n < EARLY or n in FIRST:
            n_chunks = jnp.where(many if n in FIRST_IF_MANY else full, 0, n_chunks)
        work.add(n_chunks, up_to(filled, LANES), 0, n * LANES, n * LANES)
    work.run(listed, spread, coefs, acc)


def middle_kernel(cells, count_ref, wide, spread, _, acc, listed, coefs, *tables):
    size_x, size_y, size_z = cells
    n_z = 2 * size_z
    bins = bins_of(cells)
    places = [(i, j, k) for i in (0, size_x + 1) for j in range(size_y) for k in range(n_z)]
    count_s = counts_of([wide[at] for at in places])
    work = Groups(tables)
    for bx in range(size_x):
        for bz in range(size_z):
            x = (-1, size_x)[bx]
            sources = []
            for y in range(size_y):
                for z in (bz - 1, bz, bz + 1):
                    place = (x + 1, y, z % n_z)
                    tile = wide[place] + shift_tile(cells, (x, y, z))
                    sources.append((tile, count_s[places.index(place)]))
            first_tile = (bx * size_z + bz) * LIST_X
            n_tiles = up_to(compact(listed, first_tile, sources), LANES)
            for n, at in enumerate(bins):
                if (at[0], at[2]) == (bx, bz):
                    work.add(up_to(count_ref[at], CHUNK), n_tiles, first_tile, n * LANES, n * LANES)
    work.run(listed, spread, coefs, acc)


def last_kernel(cells, count_ref, own_ref, y_lo, y_hi, spread, *refs):
    (_, early, out_ref, acc, listed, coefs), tables = refs[:6], refs[6:]
    size_x, size_y, size_z = cells
    n_z = 2 * size_z
    bins = bins_of(cells)
    places = [(i, j, k) for i in range(size_x + 2) for j in range(2) for k in range(n_z)]
    tiles = [(y_lo, y_hi)[j][i, 0, k] for i, j, k in places]
    count_s = counts_of(tiles)
    work = Groups(tables)
    for n, (bx, by, bz) in enumerate(bins):
        sources = []
        for x in (bx - 1, bx, bx + 1):
            for z in (bz - 1, bz, bz + 1):
                cell = places.index((x + 1, by, z % n_z))
                tile = tiles[cell] + shift_tile(cells, (x, (-1, size_y)[by], z))
                sources.append((tile, count_s[cell]))
        n_tiles = up_to(compact(listed, n * LIST_Y, sources), LANES)
        first_tile = n * LIST_Y
        work.add(up_to(count_ref[bx, by, bz], CHUNK), n_tiles, first_tile, n * LANES, n * LANES)
    work.run(listed, spread, coefs, acc)

    slot = lax.broadcasted_iota(jnp.int32, (1, LANES), 1)
    by_rows = lane_sums([acc[i, : len(bins) * LANES, :] for i in range(4)], len(bins))
    for n, (at, by_row) in enumerate(zip(bins, by_rows)):
        tile = own_ref[at]
        total = velocity_rows(cells, n, by_row, tile)
        total = total - (STOKES_NORM * SELF_C) * pltpu.roll(tile, ROWS - FORCE_ROW, 0)
        if n < EARLY:
            total = total + early[n]
        total = jnp.where(slot < count_ref[at], total, 0.0)
        for i in range(3):
            out_ref[i, at[0], at[1], at[2] : at[2] + 1, :] = total[i : i + 1]


def shifted(first, last, axis):
    size = lax.axis_size(axis)
    up = [(i, (i + 1) % size) for i in range(size)]
    if size % 2:
        down = [(j, i) for i, j in up]
        return lax.ppermute(last, axis, up), lax.ppermute(first, axis, down)
    odd = lax.rem(lax.axis_index(axis), 2) == 1
    got = []
    for parity in (0, 1):
        pairs = [pair for i, j in up if i % 2 == parity for pair in ((i, j), (j, i))]
        got.append(lax.ppermute(jnp.where(odd == bool(parity), last, first), axis, pairs))
    return jnp.where(odd, got[0], got[1]), jnp.where(odd, got[1], got[0])


def on_device(offsets, forces, counts):
    cells = offsets.shape[1:4]
    slots = offsets.shape[4]
    n_bins = cells[0] * cells[1] * cells[2]
    n_targets = n_bins * slots
    whole = pl.BlockSpec(memory_space=pltpu.VMEM)
    scalars = pl.BlockSpec(memory_space=pltpu.SMEM)

    def floats(*shape):
        return jax.ShapeDtypeStruct(shape, jnp.float32)

    def params(mib):
        return pltpu.CompilerParams(vmem_limit_bytes=mib << 20)

    loop_scratch = [pltpu.VMEM((UNITS, 2, CHUNK, LANES), jnp.float32)]
    loop_scratch += [pltpu.SMEM((2 * n_bins,), jnp.int32)] * 5
    cost = pl.CostEstimate(flops=1 << 28, bytes_accessed=1 << 16, transcendentals=1 << 20)

    def in_place(sums):
        return pltpu.with_memory_space_constraint(sums, pltpu.VMEM)

    def list_scratch(n_tiles):
        return [pltpu.VMEM((n_tiles, ROWS, LANES), jnp.float32)]

    own_list, all_targets = floats(n_bins + 1, ROWS, slots), floats(3, n_targets, slots)
    arguments = [pltpu.with_memory_space_constraint(x, pltpu.HBM) for x in (counts, offsets, forces)]
    sent, early = pl.pallas_call(
        functools.partial(pack_kernel, cells),
        out_shape=[floats(*cells, ROWS, slots), floats(EARLY, ROWS, slots)],
        in_specs=[pl.BlockSpec(memory_space=pltpu.HBM)] * 3,
        out_specs=[whole, whole],
        scratch_shapes=[
            pltpu.SMEM(counts.shape, jnp.int32),
            pltpu.VMEM(offsets.shape, jnp.float32),
            pltpu.VMEM(forces.shape, jnp.float32),
            pltpu.SemaphoreType.DMA((3,)),
            pltpu.VMEM(own_list.shape, jnp.float32),
            pltpu.VMEM((3, EARLY * slots, slots), jnp.float32),
            loop_scratch[0],
            pltpu.VMEM((4, EARLY * slots + CHUNK, slots), jnp.float32),
        ]
        + loop_scratch[1:],
        compiler_params=params(8),
        name="pack",
    )(*arguments)

    together = lax.optimization_barrier
    size = lax.axis_size("ha")
    other = lax.ppermute(sent, "ha", [(i, (i + 1) % size) for i in range(size)])
    own, listed, spread, first = pl.pallas_call(
        functools.partial(first_kernel, cells),
        out_shape=[sent, own_list, all_targets, floats(4, len(FIRST) * slots + CHUNK, slots)],
        in_specs=[whole],
        out_specs=[whole] * 4,
        scratch_shapes=loop_scratch,
        compiler_params=params(8),
        cost_estimate=cost,
        name="first",
    )(sent)
    other, own, listed, first = together((other, own, listed, first))
    column = jnp.concatenate([own, other], axis=2)
    x_lo, x_hi = shifted(column[:1], column[cells[0] - 1 :], "gx")
    second = pl.pallas_call(
        functools.partial(second_kernel, cells),
        out_shape=floats(4, n_targets + CHUNK, slots),
        in_specs=[scalars] + [whole] * 4,
        out_specs=whole,
        scratch_shapes=list_scratch(cells[2] * LIST_Z + n_bins + 1)
        + loop_scratch,
        compiler_params=params(8),
        cost_estimate=cost,
        name="second",
    )(counts, other, listed, spread, first)
    x_lo, x_hi, second = together((x_lo, x_hi, second))
    wide = jnp.concatenate([x_lo, column, x_hi], axis=0)
    y_lo, y_hi = shifted(wide[:, :1], wide[:, cells[1] - 1 :], "gy")
    middle = pl.pallas_call(
        functools.partial(middle_kernel, cells),
        out_shape=floats(4, n_targets + CHUNK, slots),
        in_specs=[scalars] + [whole] * 3,
        out_specs=whole,
        scratch_shapes=list_scratch(cells[0] * cells[2] * LIST_X) + loop_scratch,
        input_output_aliases={3: 0},
        compiler_params=params(8),
        cost_estimate=cost,
        name="middle",
    )(counts, wide, spread, in_place(second))
    y_lo, y_hi, middle = together((y_lo, y_hi, middle))
    return pl.pallas_call(
        functools.partial(last_kernel, cells),
        out_shape=[floats(3, *cells, slots), floats(4, n_targets + CHUNK, slots)],
        in_specs=[scalars] + [whole] * 6,
        out_specs=[whole, whole],
        scratch_shapes=list_scratch(n_bins * LIST_Y)
        + loop_scratch,
        input_output_aliases={5: 1},
        compiler_params=params(12),
        cost_estimate=cost,
        name="last",
    )(counts, own, y_lo, y_hi, spread, in_place(middle), early)[0]


def solution(mesh):
    in_specs = (
        P(None, "gx", "gy", "ha", None),
        P(None, "gx", "gy", "ha", None),
        P("gx", "gy", "ha"),
    )
    out_specs = P(None, "gx", "gy", "ha", None)
    return jax.shard_map(on_device, mesh=mesh, in_specs=in_specs, out_specs=out_specs, check_vma=False)
```

```python
import functools
import math

import jax
import jax.numpy as jnp
from jax import lax
from jax.experimental import pallas as pl
from jax.experimental.pallas import tpu as pltpu
from jax.sharding import PartitionSpec as P

SPLIT_XI = 2.0
SOFT_SQ = 0.01
GAUSS_COEF = 2.0 * SPLIT_XI / math.sqrt(math.pi)
STOKES_NORM = 1.0 / (8.0 * math.pi)

SOFT_U = SPLIT_XI * SPLIT_XI * SOFT_SQ
LOG2_E = math.log2(math.e)
LOG2_G = math.log2(GAUSS_COEF)
SELF_C = math.erfc(math.sqrt(SOFT_U)) / math.sqrt(SOFT_SQ) + GAUSS_COEF * (
    2.0 * SOFT_U - 3.0
) * math.exp(-SOFT_U)

LANES = 128
ROWS = 8
CHUNK = 32
UNITS = 4
COUNT_ROW = 3
MANY = 440
EARLY = 3
FIRST = (3, 4, 5)
SECOND = (6, 7, 5, 0, 1, 2, 3, 4)
FIRST_IF_MANY = (3, 4)
LIST_Z, LIST_X, LIST_Y = 5, 7, 10
FORCE_ROW = 4


def rows_and_lanes(shape=(ROWS, LANES)):
    return lax.broadcasted_iota(jnp.int32, shape, 0), lax.broadcasted_iota(jnp.int32, shape, 1)


def bins_of(cells):
    return [(i, j, k) for i in range(cells[0]) for j in range(cells[1]) for k in range(cells[2])]


def shift_tile(cells, at):
    row, _ = rows_and_lanes()
    moved = jnp.zeros((ROWS, LANES), jnp.float32)
    for i in range(3):
        moved = jnp.where(row == i, SPLIT_XI * (at[i] - 0.5 * (cells[i] - 1)), moved)
    return moved


def compact(listed, base, sources):
    _, lane = rows_and_lanes()
    filled = jnp.int32(0)
    moved = []
    for tile, count in sources:
        at = lax.bitwise_and(filled, LANES - 1)
        tile_id = base + lax.shift_right_logical(filled, 7)
        moved.append((pltpu.roll(tile, at, 1), lane >= at, tile_id, at + count >= LANES))
        filled = filled + count
    current = jnp.zeros((ROWS, LANES), jnp.float32)
    for tile, behind, tile_id, full in moved:
        current = jnp.where(behind, tile, current)
        spill = jnp.where(behind, 0.0, tile)
        listed[tile_id] = current
        listed[tile_id + 1] = spill
        current = jnp.where(full, spill, current)
    return filled


def up_to(count, size):
    return lax.shift_right_logical(count + (size - 1), size.bit_length() - 1)


def parts_of(value, n):
    parts = []
    for _ in range(n):
        part = value.astype(jnp.bfloat16)
        value = value - part.astype(jnp.float32)
        parts.append(part)
    return parts


def spread_targets(spread, first, tile):
    parts = [p.astype(jnp.float32) for p in parts_of(tile, 3)] + [jnp.zeros_like(tile)]
    row, lane = rows_and_lanes((4 * ROWS, 3 * LANES))
    pick = jnp.where(lax.bitwise_and(row, ROWS - 1) == lax.shift_right_logical(lane, 7), 1.0, 0.0)
    wide = lax.dot_general(
        jnp.concatenate(parts, axis=0).astype(jnp.bfloat16),
        pick.astype(jnp.bfloat16),
        (((0,), (0,)), ((), ())),
        preferred_element_type=jnp.float32,
    )
    for i in range(3):
        spread[i, first : first + LANES, :] = wide[:, i * LANES : (i + 1) * LANES]


def coefficients(target, source, force):
    delta = [t - s for t, s in zip(target, source)]
    u = (delta[0] * delta[0] + SOFT_U) + delta[1] * delta[1] + delta[2] * delta[2]
    inv = lax.rsqrt(u)
    tail = (1.0 - lax.erf(u * inv)) * inv
    gauss = jnp.exp2(LOG2_G - u * LOG2_E)
    rest = gauss * (u - 1.5)
    coef_d = ((tail - rest) - gauss) * pl.reciprocal(u, approx=True)
    along = coef_d * (delta[0] * force[0] + delta[1] * force[1] + delta[2] * force[2])
    return tail + rest, along


class Groups:
    def __init__(self, tables):
        self.tables = tables
        self.size = 0
        self.total = jnp.int32(0)

    def add(self, n_chunks, n_tiles, first_tile, spread_row, acc_row):
        for table, value in zip(self.tables, (n_chunks, n_tiles, first_tile, spread_row, acc_row)):
            table[self.size] = jnp.int32(value)
        self.size += 1
        self.total = self.total + n_chunks * n_tiles

    def run(self, listed, spread, coefs, acc):
        chunks_of, tiles_of, list_of, spread_of, acc_of = self.tables
        trash = acc.shape[1] - CHUNK

        def rows(tile_id):
            single = [listed[tile_id, i : i + 1, :] for i in (0, 1, 2, 4, 5, 6)]
            return single[:3], single[3:]

        def advance(group, chunk, tile):
            end_tile = tile + 1 == tiles_of[group]
            next_chunk = jnp.where(end_tile, chunk + CHUNK, chunk)
            end_chunk = next_chunk == chunks_of[group] * CHUNK
            next_group = jnp.where(end_chunk, jnp.minimum(group + 1, self.size - 1), group)
            return next_group, jnp.where(end_chunk, 0, next_chunk), jnp.where(end_tile, 0, tile + 1)

        def find(step, place):
            units, found = [], []
            for n in range(UNITS):
                group, chunk, tile = place
                valid = step * UNITS + n < self.total
                units += [jnp.where(valid, acc_of[group] + chunk, trash), list_of[group] + tile]
                at = pl.ds(pl.multiple_of(spread_of[group] + chunk, CHUNK), CHUNK)
                target = [spread[i, at, :] for i in range(3)]
                found.append(coefficients(target, *rows(units[-1])))
                place = advance(*place)
            return found, tuple(units), place

        def use(units):
            terms = []
            for n, tile in enumerate(units[1::2]):
                coef_c, along = coefs[n, 0], coefs[n, 1]
                source, force = rows(tile)
                terms.append([coef_c * force[i] - along * source[i] for i in range(3)] + [along])
            return terms

        def keep(found):
            for n, pair in enumerate(found):
                coefs[n, 0], coefs[n, 1] = pair

        def add(units, terms):
            for first, unit in zip(units[::2], terms):
                at = pl.ds(pl.multiple_of(first, CHUNK), CHUNK)
                for i in range(4):
                    acc[i, at, :] = acc[i, at, :] + unit[i]

        def body(step, state):
            place, olds = state[:3], state[3:]
            terms = use(olds)
            found, news, place = find(step, place)
            add(olds, terms)
            keep(found)
            return place + news

        zero = jnp.int32(0)
        found, units, place = find(0, (zero, zero, zero))
        keep(found)
        state = lax.fori_loop(1, lax.div(self.total + UNITS - 1, UNITS), body, place + units)
        add(state[3:], use(state[3:]))


def is_full(cells, count_ref):
    filled = jnp.int32(0)
    heavy = jnp.int32(0)
    for at in bins_of(cells):
        count = count_ref[at]
        filled = filled + count
        heavy = heavy + jnp.where(count > LANES // 2, 1, 0)
    return filled, heavy == len(bins_of(cells)), filled > MANY


def list_own(cells, count_ref, own_ref, listed):
    sources = [(own_ref[at] + shift_tile(cells, at), count_ref[at]) for at in bins_of(cells)]
    compact(listed, 0, sources)


def velocity_rows(cells, group, by_row, tile):
    position = tile + shift_tile(cells, bins_of(cells)[group])
    return (2.0 * STOKES_NORM) * (by_row + position * jnp.broadcast_to(by_row[3:4], (ROWS, LANES)))


def lane_sums(sums, n_bins):
    row, lane = rows_and_lanes((2 * LANES * len(sums), LANES))
    pick = lax.bitwise_and(lane, ROWS - 1) == lax.shift_right_logical(row, (2 * LANES).bit_length() - 1)
    pick = jnp.where(pick, 1.0, 0.0).astype(jnp.bfloat16)
    merged = []
    for first in range(n_bins):
        rows = slice(first * LANES, (first + 1) * LANES)
        parts = [p for part in sums for p in parts_of(part[rows], 2)]
        product = jnp.dot(jnp.concatenate(parts, axis=1), pick, preferred_element_type=jnp.float32)
        merged += [product[n : n + LANES] for n in range(0, product.shape[0], LANES)]
    _, lane = rows_and_lanes((LANES, LANES))
    chosen = merged[0]
    for n in range(1, n_bins):
        chosen = jnp.where(lane >= n * ROWS, merged[n], chosen)
    turned = jnp.transpose(chosen)
    return [turned[n * ROWS : (n + 1) * ROWS] for n in range(n_bins)]


def pack_kernel(cells, count_hbm, offset_hbm, force_hbm, own_ref, early_ref, *refs):
    (count_ref, offset_v, force_v, sems, listed, spread, coefs, acc), tables = refs[:8], refs[8:]
    copies = [
        pltpu.make_async_copy(source, target, sems.at[n])
        for n, (source, target) in enumerate(
            ((count_hbm, count_ref), (offset_hbm, offset_v), (force_hbm, force_v))
        )
    ]
    for copy in copies:
        copy.start()
    for copy in copies:
        copy.wait()
    slot = lax.broadcasted_iota(jnp.int32, (1, LANES), 1)
    for at in bins_of(cells):
        ix, iy, iz = at
        count = count_ref[at]
        wide = jnp.full((1, LANES), count, jnp.int32).astype(jnp.float32)
        for i in range(3):
            position = offset_v[i, ix, iy, iz : iz + 1, :]
            own_ref[ix, iy, iz, i : i + 1, :] = position * SPLIT_XI - 0.5 * SPLIT_XI
            force = force_v[i, ix, iy, iz : iz + 1, :]
            own_ref[ix, iy, iz, 4 + i : 5 + i, :] = jnp.where(slot < count, force, 0.0)
        own_ref[ix, iy, iz, 3:4, :] = wide
        own_ref[ix, iy, iz, 7:8, :] = wide
    early_ref[...] = jnp.zeros_like(early_ref)
    filled, full, _ = is_full(cells, count_ref)

    @pl.when(full)
    def _():
        list_own(cells, count_ref, own_ref, listed)
        acc[...] = jnp.zeros_like(acc)
        groups = range(EARLY)
        tiles = [own_ref[bins_of(cells)[n]] for n in groups]
        work = Groups(tables)
        for n in groups:
            at = bins_of(cells)[n]
            spread_targets(spread, n * LANES, tiles[n] + shift_tile(cells, at))
            work.add(up_to(count_ref[at], CHUNK), up_to(filled, LANES), 0, n * LANES, n * LANES)
        work.run(listed, spread, coefs, acc)
        by_rows = lane_sums([acc[i, : EARLY * LANES, :] for i in range(4)], EARLY)
        for n, by_row in enumerate(by_rows):
            early_ref[n] = velocity_rows(cells, n, by_row, tiles[n])


def counts_of(tiles):
    return [tile[COUNT_ROW, 0].astype(jnp.int32) for tile in tiles]


def first_kernel(cells, sent_ref, own_ref, listed, spread, acc, coefs, *tables):
    bins = bins_of(cells)
    count_s = counts_of([sent_ref[at] for at in bins])
    own_ref[...] = sent_ref[...]
    for n, at in enumerate(bins):
        spread_targets(spread, n * LANES, own_ref[at] + shift_tile(cells, at))
    acc[...] = jnp.zeros_like(acc)
    count_ref = {at: count_s[n] for n, at in enumerate(bins)}
    list_own(cells, count_ref, own_ref, listed)
    filled, full, many = is_full(cells, count_ref)
    work = Groups(tables)
    for m, n in enumerate(FIRST):
        n_chunks = jnp.where(many if n in FIRST_IF_MANY else full, up_to(count_ref[bins[n]], CHUNK), 0)
        work.add(n_chunks, up_to(filled, LANES), 0, n * LANES, m * LANES)
    work.run(listed, spread, coefs, acc)


def second_kernel(cells, count_ref, other, own_list, spread, first, acc, listed, coefs, *tables):
    bins = bins_of(cells)
    size_x, size_y, size_z = cells
    count_s = counts_of([other[at] for at in bins])
    for n in range(len(bins)):
        here = slice(n * LANES, (n + 1) * LANES)
        if n in FIRST:
            m = FIRST.index(n)
            acc[:, here, :] = first[:, m * LANES : (m + 1) * LANES, :]
        else:
            acc[:, here, :] = jnp.zeros((4, LANES, LANES), jnp.float32)
    n_own = own_list.shape[0]
    for n in range(n_own):
        listed[n] = own_list[n]
    filled, full, many = is_full(cells, count_ref)
    work = Groups(tables)
    for bz in range(size_z):
        z = (-1, size_z)[bz]
        sources = []
        for x in range(size_x):
            for y in range(size_y):
                place = (x, y, z % size_z)
                tile = other[place] + shift_tile(cells, (x, y, z))
                sources.append((tile, count_s[bins.index(place)]))
        first_tile = n_own + bz * LIST_Z
        n_tiles = up_to(compact(listed, first_tile, sources), LANES)
        for n, at in enumerate(bins):
            if at[2] == bz:
                work.add(up_to(count_ref[at], CHUNK), n_tiles, first_tile, n * LANES, n * LANES)
    for n in SECOND:
        n_chunks = up_to(count_ref[bins[n]], CHUNK)
        if n < EARLY or n in FIRST:
            n_chunks = jnp.where(many if n in FIRST_IF_MANY else full, 0, n_chunks)
        work.add(n_chunks, up_to(filled, LANES), 0, n * LANES, n * LANES)
    work.run(listed, spread, coefs, acc)


def middle_kernel(cells, count_ref, wide, spread, _, acc, listed, coefs, *tables):
    size_x, size_y, size_z = cells
    n_z = 2 * size_z
    bins = bins_of(cells)
    places = [(i, j, k) for i in (0, size_x + 1) for j in range(size_y) for k in range(n_z)]
    count_s = counts_of([wide[at] for at in places])
    work = Groups(tables)
    for bx in range(size_x):
        for bz in range(size_z):
            x = (-1, size_x)[bx]
            sources = []
            for y in range(size_y):
                for z in (bz - 1, bz, bz + 1):
                    place = (x + 1, y, z % n_z)
                    tile = wide[place] + shift_tile(cells, (x, y, z))
                    sources.append((tile, count_s[places.index(place)]))
            first_tile = (bx * size_z + bz) * LIST_X
            n_tiles = up_to(compact(listed, first_tile, sources), LANES)
            for n, at in enumerate(bins):
                if (at[0], at[2]) == (bx, bz):
                    work.add(up_to(count_ref[at], CHUNK), n_tiles, first_tile, n * LANES, n * LANES)
    work.run(listed, spread, coefs, acc)


def last_kernel(cells, count_ref, own_ref, y_lo, y_hi, spread, *refs):
    (_, early, out_ref, acc, listed, coefs), tables = refs[:6], refs[6:]
    size_x, size_y, size_z = cells
    n_z = 2 * size_z
    bins = bins_of(cells)
    places = [(i, j, k) for i in range(size_x + 2) for j in range(2) for k in range(n_z)]
    tiles = [(y_lo, y_hi)[j][i, 0, k] for i, j, k in places]
    count_s = counts_of(tiles)
    work = Groups(tables)
    for n, (bx, by, bz) in enumerate(bins):
        sources = []
        for x in (bx - 1, bx, bx + 1):
            for z in (bz - 1, bz, bz + 1):
                cell = places.index((x + 1, by, z % n_z))
                tile = tiles[cell] + shift_tile(cells, (x, (-1, size_y)[by], z))
                sources.append((tile, count_s[cell]))
        n_tiles = up_to(compact(listed, n * LIST_Y, sources), LANES)
        first_tile = n * LIST_Y
        work.add(up_to(count_ref[bx, by, bz], CHUNK), n_tiles, first_tile, n * LANES, n * LANES)
    work.run(listed, spread, coefs, acc)

    slot = lax.broadcasted_iota(jnp.int32, (1, LANES), 1)
    by_rows = lane_sums([acc[i, : len(bins) * LANES, :] for i in range(4)], len(bins))
    for n, (at, by_row) in enumerate(zip(bins, by_rows)):
        tile = own_ref[at]
        total = velocity_rows(cells, n, by_row, tile)
        total = total - (STOKES_NORM * SELF_C) * pltpu.roll(tile, ROWS - FORCE_ROW, 0)
        if n < EARLY:
            total = total + early[n]
        total = jnp.where(slot < count_ref[at], total, 0.0)
        for i in range(3):
            out_ref[i, at[0], at[1], at[2] : at[2] + 1, :] = total[i : i + 1]


def shifted(first, last, axis):
    size = lax.axis_size(axis)
    up = [(i, (i + 1) % size) for i in range(size)]
    if size % 2:
        down = [(j, i) for i, j in up]
        return lax.ppermute(last, axis, up), lax.ppermute(first, axis, down)
    odd = lax.rem(lax.axis_index(axis), 2) == 1
    got = []
    for parity in (0, 1):
        pairs = [pair for i, j in up if i % 2 == parity for pair in ((i, j), (j, i))]
        got.append(lax.ppermute(jnp.where(odd == bool(parity), last, first), axis, pairs))
    return jnp.where(odd, got[0], got[1]), jnp.where(odd, got[1], got[0])


def on_device(offsets, forces, counts):
    cells = offsets.shape[1:4]
    slots = offsets.shape[4]
    n_bins = cells[0] * cells[1] * cells[2]
    n_targets = n_bins * slots
    whole = pl.BlockSpec(memory_space=pltpu.VMEM)
    scalars = pl.BlockSpec(memory_space=pltpu.SMEM)

    def floats(*shape):
        return jax.ShapeDtypeStruct(shape, jnp.float32)

    def params(mib):
        return pltpu.CompilerParams(vmem_limit_bytes=mib << 20)

    loop_scratch = [pltpu.VMEM((UNITS, 2, CHUNK, LANES), jnp.float32)]
    loop_scratch += [pltpu.SMEM((2 * n_bins,), jnp.int32)] * 5
    cost = pl.CostEstimate(flops=1 << 28, bytes_accessed=1 << 16, transcendentals=1 << 20)

    def in_place(sums):
        return pltpu.with_memory_space_constraint(sums, pltpu.VMEM)

    def list_scratch(n_tiles):
        return [pltpu.VMEM((n_tiles, ROWS, LANES), jnp.float32)]

    own_list, all_targets = floats(n_bins + 1, ROWS, slots), floats(3, n_targets, slots)
    arguments = [pltpu.with_memory_space_constraint(x, pltpu.HBM) for x in (counts, offsets, forces)]
    sent, early = pl.pallas_call(
        functools.partial(pack_kernel, cells),
        out_shape=[floats(*cells, ROWS, slots), floats(EARLY, ROWS, slots)],
        in_specs=[pl.BlockSpec(memory_space=pltpu.HBM)] * 3,
        out_specs=[whole, whole],
        scratch_shapes=[
            pltpu.SMEM(counts.shape, jnp.int32),
            pltpu.VMEM(offsets.shape, jnp.float32),
            pltpu.VMEM(forces.shape, jnp.float32),
            pltpu.SemaphoreType.DMA((3,)),
            pltpu.VMEM(own_list.shape, jnp.float32),
            pltpu.VMEM((3, EARLY * slots, slots), jnp.float32),
            loop_scratch[0],
            pltpu.VMEM((4, EARLY * slots + CHUNK, slots), jnp.float32),
        ]
        + loop_scratch[1:],
        compiler_params=params(8),
        name="pack",
    )(*arguments)

    together = lax.optimization_barrier
    size = lax.axis_size("ha")
    other = lax.ppermute(sent, "ha", [(i, (i + 1) % size) for i in range(size)])
    own, listed, spread, first = pl.pallas_call(
        functools.partial(first_kernel, cells),
        out_shape=[sent, own_list, all_targets, floats(4, len(FIRST) * slots + CHUNK, slots)],
        in_specs=[whole],
        out_specs=[whole] * 4,
        scratch_shapes=loop_scratch,
        compiler_params=params(8),
        cost_estimate=cost,
        name="first",
    )(sent)
    other, own, listed, first = together((other, own, listed, first))
    column = jnp.concatenate([own, other], axis=2)
    x_lo, x_hi = shifted(column[:1], column[cells[0] - 1 :], "gx")
    second = pl.pallas_call(
        functools.partial(second_kernel, cells),
        out_shape=floats(4, n_targets + CHUNK, slots),
        in_specs=[scalars] + [whole] * 4,
        out_specs=whole,
        scratch_shapes=list_scratch(cells[2] * LIST_Z + n_bins + 1)
        + loop_scratch,
        compiler_params=params(8),
        cost_estimate=cost,
        name="second",
    )(counts, other, listed, spread, first)
    x_lo, x_hi, second = together((x_lo, x_hi, second))
    wide = jnp.concatenate([x_lo, column, x_hi], axis=0)
    y_lo, y_hi = shifted(wide[:, :1], wide[:, cells[1] - 1 :], "gy")
    middle = pl.pallas_call(
        functools.partial(middle_kernel, cells),
        out_shape=floats(4, n_targets + CHUNK, slots),
        in_specs=[scalars] + [whole] * 3,
        out_specs=whole,
        scratch_shapes=list_scratch(cells[0] * cells[2] * LIST_X) + loop_scratch,
        input_output_aliases={3: 0},
        compiler_params=params(8),
        cost_estimate=cost,
        name="middle",
    )(counts, wide, spread, in_place(second))
    y_lo, y_hi, middle = together((y_lo, y_hi, middle))
    return pl.pallas_call(
        functools.partial(last_kernel, cells),
        out_shape=[floats(3, *cells, slots), floats(4, n_targets + CHUNK, slots)],
        in_specs=[scalars] + [whole] * 6,
        out_specs=[whole, whole],
        scratch_shapes=list_scratch(n_bins * LIST_Y)
        + loop_scratch,
        input_output_aliases={5: 1},
        compiler_params=params(12),
        cost_estimate=cost,
        name="last",
    )(counts, own, y_lo, y_hi, spread, in_place(middle), early)[0]


def solution(mesh):
    in_specs = (
        P(None, "gx", "gy", "ha", None),
        P(None, "gx", "gy", "ha", None),
        P("gx", "gy", "ha"),
    )
    out_specs = P(None, "gx", "gy", "ha", None)
    return jax.shard_map(on_device, mesh=mesh, in_specs=in_specs, out_specs=out_specs, check_vma=False)
```

```python
import functools
import math

import jax
import jax.numpy as jnp
from jax import lax
from jax.experimental import pallas as pl
from jax.experimental.pallas import tpu as pltpu
from jax.sharding import PartitionSpec as P

SPLIT_XI = 2.0
SOFT_SQ = 0.01
GAUSS_COEF = 2.0 * SPLIT_XI / math.sqrt(math.pi)
STOKES_NORM = 1.0 / (8.0 * math.pi)

SOFT_U = SPLIT_XI * SPLIT_XI * SOFT_SQ
LOG2_E = math.log2(math.e)
LOG2_G = math.log2(GAUSS_COEF)
SELF_C = math.erfc(math.sqrt(SOFT_U)) / math.sqrt(SOFT_SQ) + GAUSS_COEF * (
    2.0 * SOFT_U - 3.0
) * math.exp(-SOFT_U)

LANES = 128
ROWS = 8
CHUNK = 32
UNITS = 3
COUNT_ROW = 3
MANY = 440
EARLY = 3
FIRST = (3, 4, 5)
SECOND = (6, 7, 5, 0, 1, 2, 3, 4)
FIRST_IF_MANY = (3, 4)
LIST_Z, LIST_X, LIST_Y = 5, 7, 10
FORCE_ROW = 4


def rows_and_lanes(shape=(ROWS, LANES)):
    return lax.broadcasted_iota(jnp.int32, shape, 0), lax.broadcasted_iota(jnp.int32, shape, 1)


def bins_of(cells):
    return [(i, j, k) for i in range(cells[0]) for j in range(cells[1]) for k in range(cells[2])]


def shift_tile(cells, at):
    row, _ = rows_and_lanes()
    moved = jnp.zeros((ROWS, LANES), jnp.float32)
    for i in range(3):
        moved = jnp.where(row == i, SPLIT_XI * (at[i] - 0.5 * (cells[i] - 1)), moved)
    return moved


def compact(listed, base, sources):
    _, lane = rows_and_lanes()
    filled = jnp.int32(0)
    moved = []
    for tile, count in sources:
        at = lax.bitwise_and(filled, LANES - 1)
        tile_id = base + lax.shift_right_logical(filled, 7)
        moved.append((pltpu.roll(tile, at, 1), lane >= at, tile_id, at + count >= LANES))
        filled = filled + count
    current = jnp.zeros((ROWS, LANES), jnp.float32)
    for tile, behind, tile_id, full in moved:
        current = jnp.where(behind, tile, current)
        spill = jnp.where(behind, 0.0, tile)
        listed[tile_id] = current
        listed[tile_id + 1] = spill
        current = jnp.where(full, spill, current)
    return filled


def up_to(count, size):
    return lax.shift_right_logical(count + (size - 1), size.bit_length() - 1)


def parts_of(value, n):
    parts = []
    for _ in range(n):
        part = value.astype(jnp.bfloat16)
        value = value - part.astype(jnp.float32)
        parts.append(part)
    return parts


def spread_targets(spread, first, tile):
    parts = [p.astype(jnp.float32) for p in parts_of(tile, 3)] + [jnp.zeros_like(tile)]
    row, lane = rows_and_lanes((4 * ROWS, 3 * LANES))
    pick = jnp.where(lax.bitwise_and(row, ROWS - 1) == lax.shift_right_logical(lane, 7), 1.0, 0.0)
    wide = lax.dot_general(
        jnp.concatenate(parts, axis=0).astype(jnp.bfloat16),
        pick.astype(jnp.bfloat16),
        (((0,), (0,)), ((), ())),
        preferred_element_type=jnp.float32,
    )
    for i in range(3):
        spread[i, first : first + LANES, :] = wide[:, i * LANES : (i + 1) * LANES]


def coefficients(target, source, force):
    delta = [t - s for t, s in zip(target, source)]
    u = (delta[0] * delta[0] + SOFT_U) + delta[1] * delta[1] + delta[2] * delta[2]
    inv = lax.rsqrt(u)
    tail = (1.0 - lax.erf(u * inv)) * inv
    gauss = jnp.exp2(LOG2_G - u * LOG2_E)
    rest = gauss * (u - 1.5)
    coef_d = ((tail - rest) - gauss) * pl.reciprocal(u, approx=True)
    along = coef_d * (delta[0] * force[0] + delta[1] * force[1] + delta[2] * force[2])
    return tail + rest, along


class Groups:
    def __init__(self, tables):
        self.tables = tables
        self.size = 0
        self.total = jnp.int32(0)

    def add(self, n_chunks, n_tiles, first_tile, spread_row, acc_row):
        for table, value in zip(self.tables, (n_chunks, n_tiles, first_tile, spread_row, acc_row)):
            table[self.size] = jnp.int32(value)
        self.size += 1
        self.total = self.total + n_chunks * n_tiles

    def run(self, listed, spread, coefs, acc):
        chunks_of, tiles_of, list_of, spread_of, acc_of = self.tables
        trash = acc.shape[1] - CHUNK

        def rows(tile_id):
            single = [listed[tile_id, i : i + 1, :] for i in (0, 1, 2, 4, 5, 6)]
            return single[:3], single[3:]

        def advance(group, chunk, tile):
            end_tile = tile + 1 == tiles_of[group]
            next_chunk = jnp.where(end_tile, chunk + CHUNK, chunk)
            end_chunk = next_chunk == chunks_of[group] * CHUNK
            next_group = jnp.where(end_chunk, jnp.minimum(group + 1, self.size - 1), group)
            return next_group, jnp.where(end_chunk, 0, next_chunk), jnp.where(end_tile, 0, tile + 1)

        def find(step, place):
            units, found = [], []
            for n in range(UNITS):
                group, chunk, tile = place
                valid = step * UNITS + n < self.total
                units += [jnp.where(valid, acc_of[group] + chunk, trash), list_of[group] + tile]
                at = pl.ds(pl.multiple_of(spread_of[group] + chunk, CHUNK), CHUNK)
                target = [spread[i, at, :] for i in range(3)]
                found.append(coefficients(target, *rows(units[-1])))
                place = advance(*place)
            return found, tuple(units), place

        def use(units):
            terms = []
            for n, tile in enumerate(units[1::2]):
                coef_c, along = coefs[n, 0], coefs[n, 1]
                source, force = rows(tile)
                terms.append([coef_c * force[i] - along * source[i] for i in range(3)] + [along])
            return terms

        def keep(found):
            for n, pair in enumerate(found):
                coefs[n, 0], coefs[n, 1] = pair

        def add(units, terms):
            for first, unit in zip(units[::2], terms):
                at = pl.ds(pl.multiple_of(first, CHUNK), CHUNK)
                for i in range(4):
                    acc[i, at, :] = acc[i, at, :] + unit[i]

        def body(step, state):
            place, olds = state[:3], state[3:]
            terms = use(olds)
            found, news, place = find(step, place)
            add(olds, terms)
            keep(found)
            return place + news

        zero = jnp.int32(0)
        found, units, place = find(0, (zero, zero, zero))
        keep(found)
        state = lax.fori_loop(1, lax.div(self.total + UNITS - 1, UNITS), body, place + units)
        add(state[3:], use(state[3:]))


def is_full(cells, count_ref):
    filled = jnp.int32(0)
    heavy = jnp.int32(0)
    for at in bins_of(cells):
        count = count_ref[at]
        filled = filled + count
        heavy = heavy + jnp.where(count > LANES // 2, 1, 0)
    return filled, heavy == len(bins_of(cells)), filled > MANY


def list_own(cells, count_ref, own_ref, listed):
    sources = [(own_ref[at] + shift_tile(cells, at), count_ref[at]) for at in bins_of(cells)]
    compact(listed, 0, sources)


def velocity_rows(cells, group, by_row, tile):
    position = tile + shift_tile(cells, bins_of(cells)[group])
    return (2.0 * STOKES_NORM) * (by_row + position * jnp.broadcast_to(by_row[3:4], (ROWS, LANES)))


def lane_sums(sums, n_bins):
    row, lane = rows_and_lanes((2 * LANES * len(sums), LANES))
    pick = lax.bitwise_and(lane, ROWS - 1) == lax.shift_right_logical(row, (2 * LANES).bit_length() - 1)
    pick = jnp.where(pick, 1.0, 0.0).astype(jnp.bfloat16)
    merged = []
    for first in range(0, n_bins, 2):
        rows = slice(first * LANES, min(first + 2, n_bins) * LANES)
        parts = [p for part in sums for p in parts_of(part[rows], 2)]
        product = jnp.dot(jnp.concatenate(parts, axis=1), pick, preferred_element_type=jnp.float32)
        merged += [product[n : n + LANES] for n in range(0, product.shape[0], LANES)]
    _, lane = rows_and_lanes((LANES, LANES))
    chosen = merged[0]
    for n in range(1, n_bins):
        chosen = jnp.where(lane >= n * ROWS, merged[n], chosen)
    turned = jnp.transpose(chosen)
    return [turned[n * ROWS : (n + 1) * ROWS] for n in range(n_bins)]


def pack_kernel(cells, count_hbm, offset_hbm, force_hbm, own_ref, early_ref, *refs):
    (count_ref, offset_v, force_v, sems, listed, spread, coefs, acc), tables = refs[:8], refs[8:]
    copies = [
        pltpu.make_async_copy(source, target, sems.at[n])
        for n, (source, target) in enumerate(
            ((count_hbm, count_ref), (offset_hbm, offset_v), (force_hbm, force_v))
        )
    ]
    for copy in copies:
        copy.start()
    for copy in copies:
        copy.wait()
    slot = lax.broadcasted_iota(jnp.int32, (1, LANES), 1)
    for at in bins_of(cells):
        ix, iy, iz = at
        count = count_ref[at]
        wide = jnp.full((1, LANES), count, jnp.int32).astype(jnp.float32)
        for i in range(3):
            position = offset_v[i, ix, iy, iz : iz + 1, :]
            own_ref[ix, iy, iz, i : i + 1, :] = position * SPLIT_XI - 0.5 * SPLIT_XI
            force = force_v[i, ix, iy, iz : iz + 1, :]
            own_ref[ix, iy, iz, 4 + i : 5 + i, :] = jnp.where(slot < count, force, 0.0)
        own_ref[ix, iy, iz, 3:4, :] = wide
        own_ref[ix, iy, iz, 7:8, :] = wide
    early_ref[...] = jnp.zeros_like(early_ref)
    filled, full, _ = is_full(cells, count_ref)

    @pl.when(full)
    def _():
        list_own(cells, count_ref, own_ref, listed)
        acc[...] = jnp.zeros_like(acc)
        groups = range(EARLY)
        tiles = [own_ref[bins_of(cells)[n]] for n in groups]
        work = Groups(tables)
        for n in groups:
            at = bins_of(cells)[n]
            spread_targets(spread, n * LANES, tiles[n] + shift_tile(cells, at))
            work.add(up_to(count_ref[at], CHUNK), up_to(filled, LANES), 0, n * LANES, n * LANES)
        work.run(listed, spread, coefs, acc)
        by_rows = lane_sums([acc[i, : EARLY * LANES, :] for i in range(4)], EARLY)
        for n, by_row in enumerate(by_rows):
            early_ref[n] = velocity_rows(cells, n, by_row, tiles[n])


def counts_of(tiles):
    return [tile[COUNT_ROW, 0].astype(jnp.int32) for tile in tiles]


def first_kernel(cells, sent_ref, own_ref, listed, spread, acc, coefs, *tables):
    bins = bins_of(cells)
    count_s = counts_of([sent_ref[at] for at in bins])
    own_ref[...] = sent_ref[...]
    for n, at in enumerate(bins):
        spread_targets(spread, n * LANES, own_ref[at] + shift_tile(cells, at))
    acc[...] = jnp.zeros_like(acc)
    count_ref = {at: count_s[n] for n, at in enumerate(bins)}
    list_own(cells, count_ref, own_ref, listed)
    filled, full, many = is_full(cells, count_ref)
    work = Groups(tables)
    for m, n in enumerate(FIRST):
        n_chunks = jnp.where(many if n in FIRST_IF_MANY else full, up_to(count_ref[bins[n]], CHUNK), 0)
        work.add(n_chunks, up_to(filled, LANES), 0, n * LANES, m * LANES)
    work.run(listed, spread, coefs, acc)


def second_kernel(cells, count_ref, other, own_list, spread, first, acc, listed, coefs, *tables):
    bins = bins_of(cells)
    size_x, size_y, size_z = cells
    count_s = counts_of([other[at] for at in bins])
    for n in range(len(bins)):
        here = slice(n * LANES, (n + 1) * LANES)
        if n in FIRST:
            m = FIRST.index(n)
            acc[:, here, :] = first[:, m * LANES : (m + 1) * LANES, :]
        else:
            acc[:, here, :] = jnp.zeros((4, LANES, LANES), jnp.float32)
    n_own = own_list.shape[0]
    for n in range(n_own):
        listed[n] = own_list[n]
    filled, full, many = is_full(cells, count_ref)
    work = Groups(tables)
    for bz in range(size_z):
        z = (-1, size_z)[bz]
        sources = []
        for x in range(size_x):
            for y in range(size_y):
                place = (x, y, z % size_z)
                tile = other[place] + shift_tile(cells, (x, y, z))
                sources.append((tile, count_s[bins.index(place)]))
        first_tile = n_own + bz * LIST_Z
        n_tiles = up_to(compact(listed, first_tile, sources), LANES)
        for n, at in enumerate(bins):
            if at[2] == bz:
                work.add(up_to(count_ref[at], CHUNK), n_tiles, first_tile, n * LANES, n * LANES)
    for n in SECOND:
        n_chunks = up_to(count_ref[bins[n]], CHUNK)
        if n < EARLY or n in FIRST:
            n_chunks = jnp.where(many if n in FIRST_IF_MANY else full, 0, n_chunks)
        work.add(n_chunks, up_to(filled, LANES), 0, n * LANES, n * LANES)
    work.run(listed, spread, coefs, acc)


def middle_kernel(cells, count_ref, wide, spread, _, acc, listed, coefs, *tables):
    size_x, size_y, size_z = cells
    n_z = 2 * size_z
    bins = bins_of(cells)
    places = [(i, j, k) for i in (0, size_x + 1) for j in range(size_y) for k in range(n_z)]
    count_s = counts_of([wide[at] for at in places])
    work = Groups(tables)
    for bx in range(size_x):
        for bz in range(size_z):
            x = (-1, size_x)[bx]
            sources = []
            for y in range(size_y):
                for z in (bz - 1, bz, bz + 1):
                    place = (x + 1, y, z % n_z)
                    tile = wide[place] + shift_tile(cells, (x, y, z))
                    sources.append((tile, count_s[places.index(place)]))
            first_tile = (bx * size_z + bz) * LIST_X
            n_tiles = up_to(compact(listed, first_tile, sources), LANES)
            for n, at in enumerate(bins):
                if (at[0], at[2]) == (bx, bz):
                    work.add(up_to(count_ref[at], CHUNK), n_tiles, first_tile, n * LANES, n * LANES)
    work.run(listed, spread, coefs, acc)


def last_kernel(cells, count_ref, own_ref, y_lo, y_hi, spread, *refs):
    (_, early, out_ref, acc, listed, coefs), tables = refs[:6], refs[6:]
    size_x, size_y, size_z = cells
    n_z = 2 * size_z
    bins = bins_of(cells)
    places = [(i, j, k) for i in range(size_x + 2) for j in range(2) for k in range(n_z)]
    tiles = [(y_lo, y_hi)[j][i, 0, k] for i, j, k in places]
    count_s = counts_of(tiles)
    work = Groups(tables)
    for n, (bx, by, bz) in enumerate(bins):
        sources = []
        for x in (bx - 1, bx, bx + 1):
            for z in (bz - 1, bz, bz + 1):
                cell = places.index((x + 1, by, z % n_z))
                tile = tiles[cell] + shift_tile(cells, (x, (-1, size_y)[by], z))
                sources.append((tile, count_s[cell]))
        n_tiles = up_to(compact(listed, n * LIST_Y, sources), LANES)
        first_tile = n * LIST_Y
        work.add(up_to(count_ref[bx, by, bz], CHUNK), n_tiles, first_tile, n * LANES, n * LANES)
    work.run(listed, spread, coefs, acc)

    slot = lax.broadcasted_iota(jnp.int32, (1, LANES), 1)
    by_rows = lane_sums([acc[i, : len(bins) * LANES, :] for i in range(4)], len(bins))
    for n, (at, by_row) in enumerate(zip(bins, by_rows)):
        tile = own_ref[at]
        total = velocity_rows(cells, n, by_row, tile)
        total = total - (STOKES_NORM * SELF_C) * pltpu.roll(tile, ROWS - FORCE_ROW, 0)
        if n < EARLY:
            total = total + early[n]
        total = jnp.where(slot < count_ref[at], total, 0.0)
        for i in range(3):
            out_ref[i, at[0], at[1], at[2] : at[2] + 1, :] = total[i : i + 1]


def shifted(first, last, axis):
    size = lax.axis_size(axis)
    up = [(i, (i + 1) % size) for i in range(size)]
    if size % 2:
        down = [(j, i) for i, j in up]
        return lax.ppermute(last, axis, up), lax.ppermute(first, axis, down)
    odd = lax.rem(lax.axis_index(axis), 2) == 1
    got = []
    for parity in (0, 1):
        pairs = [pair for i, j in up if i % 2 == parity for pair in ((i, j), (j, i))]
        got.append(lax.ppermute(jnp.where(odd == bool(parity), last, first), axis, pairs))
    return jnp.where(odd, got[0], got[1]), jnp.where(odd, got[1], got[0])


def on_device(offsets, forces, counts):
    cells = offsets.shape[1:4]
    slots = offsets.shape[4]
    n_bins = cells[0] * cells[1] * cells[2]
    n_targets = n_bins * slots
    whole = pl.BlockSpec(memory_space=pltpu.VMEM)
    scalars = pl.BlockSpec(memory_space=pltpu.SMEM)

    def floats(*shape):
        return jax.ShapeDtypeStruct(shape, jnp.float32)

    def params(mib):
        return pltpu.CompilerParams(vmem_limit_bytes=mib << 20)

    loop_scratch = [pltpu.VMEM((UNITS, 2, CHUNK, LANES), jnp.float32)]
    loop_scratch += [pltpu.SMEM((2 * n_bins,), jnp.int32)] * 5
    cost = pl.CostEstimate(flops=1 << 28, bytes_accessed=1 << 16, transcendentals=1 << 20)

    def in_place(sums):
        return pltpu.with_memory_space_constraint(sums, pltpu.VMEM)

    def list_scratch(n_tiles):
        return [pltpu.VMEM((n_tiles, ROWS, LANES), jnp.float32)]

    own_list, all_targets = floats(n_bins + 1, ROWS, slots), floats(3, n_targets, slots)
    arguments = [pltpu.with_memory_space_constraint(x, pltpu.HBM) for x in (counts, offsets, forces)]
    sent, early = pl.pallas_call(
        functools.partial(pack_kernel, cells),
        out_shape=[floats(*cells, ROWS, slots), floats(EARLY, ROWS, slots)],
        in_specs=[pl.BlockSpec(memory_space=pltpu.HBM)] * 3,
        out_specs=[whole, whole],
        scratch_shapes=[
            pltpu.SMEM(counts.shape, jnp.int32),
            pltpu.VMEM(offsets.shape, jnp.float32),
            pltpu.VMEM(forces.shape, jnp.float32),
            pltpu.SemaphoreType.DMA((3,)),
            pltpu.VMEM(own_list.shape, jnp.float32),
            pltpu.VMEM((3, EARLY * slots, slots), jnp.float32),
            loop_scratch[0],
            pltpu.VMEM((4, EARLY * slots + CHUNK, slots), jnp.float32),
        ]
        + loop_scratch[1:],
        compiler_params=params(8),
        name="pack",
    )(*arguments)

    together = lax.optimization_barrier
    size = lax.axis_size("ha")
    other = lax.ppermute(sent, "ha", [(i, (i + 1) % size) for i in range(size)])
    own, listed, spread, first = pl.pallas_call(
        functools.partial(first_kernel, cells),
        out_shape=[sent, own_list, all_targets, floats(4, len(FIRST) * slots + CHUNK, slots)],
        in_specs=[whole],
        out_specs=[whole] * 4,
        scratch_shapes=loop_scratch,
        compiler_params=params(8),
        cost_estimate=cost,
        name="first",
    )(sent)
    other, own, listed, first = together((other, own, listed, first))
    column = jnp.concatenate([own, other], axis=2)
    x_lo, x_hi = shifted(column[:1], column[cells[0] - 1 :], "gx")
    second = pl.pallas_call(
        functools.partial(second_kernel, cells),
        out_shape=floats(4, n_targets + CHUNK, slots),
        in_specs=[scalars] + [whole] * 4,
        out_specs=whole,
        scratch_shapes=list_scratch(cells[2] * LIST_Z + n_bins + 1)
        + loop_scratch,
        compiler_params=params(8),
        cost_estimate=cost,
        name="second",
    )(counts, other, listed, spread, first)
    x_lo, x_hi, second = together((x_lo, x_hi, second))
    wide = jnp.concatenate([x_lo, column, x_hi], axis=0)
    y_lo, y_hi = shifted(wide[:, :1], wide[:, cells[1] - 1 :], "gy")
    middle = pl.pallas_call(
        functools.partial(middle_kernel, cells),
        out_shape=floats(4, n_targets + CHUNK, slots),
        in_specs=[scalars] + [whole] * 3,
        out_specs=whole,
        scratch_shapes=list_scratch(cells[0] * cells[2] * LIST_X) + loop_scratch,
        input_output_aliases={3: 0},
        compiler_params=params(8),
        cost_estimate=cost,
        name="middle",
    )(counts, wide, spread, in_place(second))
    y_lo, y_hi, middle = together((y_lo, y_hi, middle))
    return pl.pallas_call(
        functools.partial(last_kernel, cells),
        out_shape=[floats(3, *cells, slots), floats(4, n_targets + CHUNK, slots)],
        in_specs=[scalars] + [whole] * 6,
        out_specs=[whole, whole],
        scratch_shapes=list_scratch(n_bins * LIST_Y)
        + loop_scratch,
        input_output_aliases={5: 1},
        compiler_params=params(12),
        cost_estimate=cost,
        name="last",
    )(counts, own, y_lo, y_hi, spread, in_place(middle), early)[0]


def solution(mesh):
    in_specs = (
        P(None, "gx", "gy", "ha", None),
        P(None, "gx", "gy", "ha", None),
        P("gx", "gy", "ha"),
    )
    out_specs = P(None, "gx", "gy", "ha", None)
    return jax.shard_map(on_device, mesh=mesh, in_specs=in_specs, out_specs=out_specs, check_vma=False)
```

```python
import functools
import math

import jax
import jax.numpy as jnp
from jax import lax
from jax.experimental import pallas as pl
from jax.experimental.pallas import tpu as pltpu
from jax.sharding import PartitionSpec as P

SPLIT_XI = 2.0
SOFT_SQ = 0.01
GAUSS_COEF = 2.0 * SPLIT_XI / math.sqrt(math.pi)
STOKES_NORM = 1.0 / (8.0 * math.pi)

SOFT_U = SPLIT_XI * SPLIT_XI * SOFT_SQ
LOG2_E = math.log2(math.e)
LOG2_G = math.log2(GAUSS_COEF)
SELF_C = math.erfc(math.sqrt(SOFT_U)) / math.sqrt(SOFT_SQ) + GAUSS_COEF * (
    2.0 * SOFT_U - 3.0
) * math.exp(-SOFT_U)

LANES = 128
ROWS = 8
CHUNK = 32
UNITS = 4
COUNT_ROW = 3
MANY = 440
EARLY = 3
FIRST = (3, 4, 5)
SECOND = (6, 7, 5, 0, 1, 2, 3, 4)
FIRST_IF_MANY = (3, 4)
LIST_Z, LIST_X, LIST_Y = 5, 7, 10
FORCE_ROW = 4


def rows_and_lanes(shape=(ROWS, LANES)):
    return lax.broadcasted_iota(jnp.int32, shape, 0), lax.broadcasted_iota(jnp.int32, shape, 1)


def bins_of(cells):
    return [(i, j, k) for i in range(cells[0]) for j in range(cells[1]) for k in range(cells[2])]


def shift_tile(cells, at):
    row, _ = rows_and_lanes()
    moved = jnp.zeros((ROWS, LANES), jnp.float32)
    for i in range(3):
        moved = jnp.where(row == i, SPLIT_XI * (at[i] - 0.5 * (cells[i] - 1)), moved)
    return moved


def compact(listed, base, sources):
    _, lane = rows_and_lanes()
    filled = jnp.int32(0)
    moved = []
    for tile, count in sources:
        at = lax.bitwise_and(filled, LANES - 1)
        tile_id = base + lax.shift_right_logical(filled, 7)
        moved.append((pltpu.roll(tile, at, 1), lane >= at, tile_id, at + count >= LANES))
        filled = filled + count
    current = jnp.zeros((ROWS, LANES), jnp.float32)
    for tile, behind, tile_id, full in moved:
        current = jnp.where(behind, tile, current)
        spill = jnp.where(behind, 0.0, tile)
        listed[tile_id] = current
        listed[tile_id + 1] = spill
        current = jnp.where(full, spill, current)
    return filled


def up_to(count, size):
    return lax.shift_right_logical(count + (size - 1), size.bit_length() - 1)


def parts_of(value, n):
    parts = []
    for _ in range(n):
        part = value.astype(jnp.bfloat16)
        value = value - part.astype(jnp.float32)
        parts.append(part)
    return parts


def spread_targets(spread, first, tile):
    parts = [p.astype(jnp.float32) for p in parts_of(tile, 3)] + [jnp.zeros_like(tile)]
    row, lane = rows_and_lanes((4 * ROWS, 3 * LANES))
    pick = jnp.where(lax.bitwise_and(row, ROWS - 1) == lax.shift_right_logical(lane, 7), 1.0, 0.0)
    wide = lax.dot_general(
        jnp.concatenate(parts, axis=0).astype(jnp.bfloat16),
        pick.astype(jnp.bfloat16),
        (((0,), (0,)), ((), ())),
        preferred_element_type=jnp.float32,
    )
    for i in range(3):
        spread[i, first : first + LANES, :] = wide[:, i * LANES : (i + 1) * LANES]


def coefficients(target, source, force):
    delta = [t - s for t, s in zip(target, source)]
    u = (delta[0] * delta[0] + SOFT_U) + delta[1] * delta[1] + delta[2] * delta[2]
    inv = lax.rsqrt(u)
    tail = (1.0 - lax.erf(u * inv)) * inv
    gauss = jnp.exp2(LOG2_G - u * LOG2_E)
    rest = gauss * (u - 1.5)
    coef_d = ((tail - rest) - gauss) * pl.reciprocal(u, approx=True)
    along = coef_d * (delta[0] * force[0] + delta[1] * force[1] + delta[2] * force[2])
    return tail + rest, along


class Groups:
    def __init__(self, tables):
        self.tables = tables
        self.size = 0
        self.total = jnp.int32(0)

    def add(self, n_chunks, n_tiles, first_tile, spread_row, acc_row):
        for table, value in zip(self.tables, (n_chunks, n_tiles, first_tile, spread_row, acc_row)):
            table[self.size] = jnp.int32(value)
        self.size += 1
        self.total = self.total + n_chunks * n_tiles

    def run(self, listed, spread, coefs, acc):
        chunks_of, tiles_of, list_of, spread_of, acc_of = self.tables
        trash = acc.shape[1] - CHUNK

        def rows(tile_id):
            single = [listed[tile_id, i : i + 1, :] for i in (0, 1, 2, 4, 5, 6)]
            return single[:3], single[3:]

        def advance(group, chunk, tile):
            end_tile = tile + 1 == tiles_of[group]
            next_chunk = jnp.where(end_tile, chunk + CHUNK, chunk)
            end_chunk = next_chunk == chunks_of[group] * CHUNK
            next_group = jnp.where(end_chunk, jnp.minimum(group + 1, self.size - 1), group)
            return next_group, jnp.where(end_chunk, 0, next_chunk), jnp.where(end_tile, 0, tile + 1)

        def find(step, place):
            units, found = [], []
            for n in range(UNITS):
                group, chunk, tile = place
                valid = step * UNITS + n < self.total
                units += [jnp.where(valid, acc_of[group] + chunk, trash), list_of[group] + tile]
                at = pl.ds(pl.multiple_of(spread_of[group] + chunk, CHUNK), CHUNK)
                target = [spread[i, at, :] for i in range(3)]
                found.append(coefficients(target, *rows(units[-1])))
                place = advance(*place)
            return found, tuple(units), place

        def use(units):
            terms = []
            for n, tile in enumerate(units[1::2]):
                coef_c, along = coefs[n, 0], coefs[n, 1]
                source, force = rows(tile)
                terms.append([coef_c * force[i] - along * source[i] for i in range(3)] + [along])
            return terms

        def keep(found):
            for n, pair in enumerate(found):
                coefs[n, 0], coefs[n, 1] = pair

        def add(units, terms):
            for first, unit in zip(units[::2], terms):
                at = pl.ds(pl.multiple_of(first, CHUNK), CHUNK)
                for i in range(4):
                    acc[i, at, :] = acc[i, at, :] + unit[i]

        def body(step, state):
            place, olds = state[:3], state[3:]
            terms = use(olds)
            found, news, place = find(step, place)
            add(olds, terms)
            keep(found)
            return place + news

        zero = jnp.int32(0)
        found, units, place = find(0, (zero, zero, zero))
        keep(found)
        state = lax.fori_loop(1, lax.div(self.total + UNITS - 1, UNITS), body, place + units)
        add(state[3:], use(state[3:]))


def is_full(cells, count_ref):
    filled = jnp.int32(0)
    heavy = jnp.int32(0)
    for at in bins_of(cells):
        count = count_ref[at]
        filled = filled + count
        heavy = heavy + jnp.where(count > LANES // 2, 1, 0)
    return filled, heavy == len(bins_of(cells)), filled > MANY


def list_own(cells, count_ref, own_ref, listed):
    sources = [(own_ref[at] + shift_tile(cells, at), count_ref[at]) for at in bins_of(cells)]
    compact(listed, 0, sources)


def velocity_rows(cells, group, by_row, tile):
    position = tile + shift_tile(cells, bins_of(cells)[group])
    return (2.0 * STOKES_NORM) * (by_row + position * jnp.broadcast_to(by_row[3:4], (ROWS, LANES)))


def lane_sums(sums, n_bins):
    row, lane = rows_and_lanes((2 * LANES * len(sums), LANES))
    pick = lax.bitwise_and(lane, ROWS - 1) == lax.shift_right_logical(row, (2 * LANES).bit_length() - 1)
    pick = jnp.where(pick, 1.0, 0.0).astype(jnp.bfloat16)
    merged = []
    for first in range(0, n_bins, 2):
        rows = slice(first * LANES, min(first + 2, n_bins) * LANES)
        parts = [p for part in sums for p in parts_of(part[rows], 2)]
        product = jnp.dot(jnp.concatenate(parts, axis=1), pick, preferred_element_type=jnp.float32)
        merged += [product[n : n + LANES] for n in range(0, product.shape[0], LANES)]
    _, lane = rows_and_lanes((LANES, LANES))
    chosen = merged[0]
    for n in range(1, n_bins):
        chosen = jnp.where(lane >= n * ROWS, merged[n], chosen)
    turned = jnp.transpose(chosen)
    return [turned[n * ROWS : (n + 1) * ROWS] for n in range(n_bins)]


def pack_kernel(cells, count_hbm, offset_hbm, force_hbm, own_ref, early_ref, *refs):
    (count_ref, offset_v, force_v, sems, listed, spread, coefs, acc), tables = refs[:8], refs[8:]
    copies = [
        pltpu.make_async_copy(source, target, sems.at[n])
        for n, (source, target) in enumerate(
            ((count_hbm, count_ref), (offset_hbm, offset_v), (force_hbm, force_v))
        )
    ]
    for copy in copies:
        copy.start()
    for copy in copies:
        copy.wait()
    slot = lax.broadcasted_iota(jnp.int32, (1, LANES), 1)
    for at in bins_of(cells):
        ix, iy, iz = at
        count = count_ref[at]
        wide = jnp.full((1, LANES), count, jnp.int32).astype(jnp.float32)
        for i in range(3):
            position = offset_v[i, ix, iy, iz : iz + 1, :]
            own_ref[ix, iy, iz, i : i + 1, :] = position * SPLIT_XI - 0.5 * SPLIT_XI
            force = force_v[i, ix, iy, iz : iz + 1, :]
            own_ref[ix, iy, iz, 4 + i : 5 + i, :] = jnp.where(slot < count, force, 0.0)
        own_ref[ix, iy, iz, 3:4, :] = wide
        own_ref[ix, iy, iz, 7:8, :] = wide
    early_ref[...] = jnp.zeros_like(early_ref)
    filled, full, _ = is_full(cells, count_ref)

    @pl.when(full)
    def _():
        list_own(cells, count_ref, own_ref, listed)
        acc[...] = jnp.zeros_like(acc)
        groups = range(EARLY)
        tiles = [own_ref[bins_of(cells)[n]] for n in groups]
        work = Groups(tables)
        for n in groups:
            at = bins_of(cells)[n]
            spread_targets(spread, n * LANES, tiles[n] + shift_tile(cells, at))
            work.add(up_to(count_ref[at], CHUNK), up_to(filled, LANES), 0, n * LANES, n * LANES)
        work.run(listed, spread, coefs, acc)
        by_rows = lane_sums([acc[i, : EARLY * LANES, :] for i in range(4)], EARLY)
        for n, by_row in enumerate(by_rows):
            early_ref[n] = velocity_rows(cells, n, by_row, tiles[n])


def counts_of(tiles):
    return [tile[COUNT_ROW, 0].astype(jnp.int32) for tile in tiles]


def first_kernel(cells, sent_ref, own_ref, listed, spread, acc, coefs, *tables):
    bins = bins_of(cells)
    count_s = counts_of([sent_ref[at] for at in bins])
    own_ref[...] = sent_ref[...]
    for n, at in enumerate(bins):
        spread_targets(spread, n * LANES, own_ref[at] + shift_tile(cells, at))
    acc[...] = jnp.zeros_like(acc)
    count_ref = {at: count_s[n] for n, at in enumerate(bins)}
    list_own(cells, count_ref, own_ref, listed)
    filled, full, many = is_full(cells, count_ref)
    work = Groups(tables)
    for m, n in enumerate(FIRST):
        n_chunks = jnp.where(many if n in FIRST_IF_MANY else full, up_to(count_ref[bins[n]], CHUNK), 0)
        work.add(n_chunks, up_to(filled, LANES), 0, n * LANES, m * LANES)
    work.run(listed, spread, coefs, acc)


def second_kernel(cells, count_ref, other, own_list, spread, first, acc, listed, coefs, *tables):
    bins = bins_of(cells)
    size_x, size_y, size_z = cells
    count_s = counts_of([other[at] for at in bins])
    for n in range(len(bins)):
        here = slice(n * LANES, (n + 1) * LANES)
        if n in FIRST:
            m = FIRST.index(n)
            acc[:, here, :] = first[:, m * LANES : (m + 1) * LANES, :]
        else:
            acc[:, here, :] = jnp.zeros((4, LANES, LANES), jnp.float32)
    n_own = own_list.shape[0]
    for n in range(n_own):
        listed[n] = own_list[n]
    filled, full, many = is_full(cells, count_ref)
    work = Groups(tables)
    for bz in range(size_z):
        z = (-1, size_z)[bz]
        sources = []
        for x in range(size_x):
            for y in range(size_y):
                place = (x, y, z % size_z)
                tile = other[place] + shift_tile(cells, (x, y, z))
                sources.append((tile, count_s[bins.index(place)]))
        first_tile = n_own + bz * LIST_Z
        n_tiles = up_to(compact(listed, first_tile, sources), LANES)
        for n, at in enumerate(bins):
            if at[2] == bz:
                work.add(up_to(count_ref[at], CHUNK), n_tiles, first_tile, n * LANES, n * LANES)
    for n in SECOND:
        n_chunks = up_to(count_ref[bins[n]], CHUNK)
        if n < EARLY or n in FIRST:
            n_chunks = jnp.where(many if n in FIRST_IF_MANY else full, 0, n_chunks)
        work.add(n_chunks, up_to(filled, LANES), 0, n * LANES, n * LANES)
    work.run(listed, spread, coefs, acc)


def middle_kernel(cells, count_ref, wide, spread, _, acc, listed, coefs, *tables):
    size_x, size_y, size_z = cells
    n_z = 2 * size_z
    bins = bins_of(cells)
    places = [(i, j, k) for i in (0, size_x + 1) for j in range(size_y) for k in range(n_z)]
    count_s = counts_of([wide[at] for at in places])
    work = Groups(tables)
    for bx in range(size_x):
        for bz in range(size_z):
            x = (-1, size_x)[bx]
            sources = []
            for y in range(size_y):
                for z in (bz - 1, bz, bz + 1):
                    place = (x + 1, y, z % n_z)
                    tile = wide[place] + shift_tile(cells, (x, y, z))
                    sources.append((tile, count_s[places.index(place)]))
            first_tile = (bx * size_z + bz) * LIST_X
            n_tiles = up_to(compact(listed, first_tile, sources), LANES)
            for n, at in enumerate(bins):
                if (at[0], at[2]) == (bx, bz):
                    work.add(up_to(count_ref[at], CHUNK), n_tiles, first_tile, n * LANES, n * LANES)
    work.run(listed, spread, coefs, acc)


def last_kernel(cells, count_ref, own_ref, y_lo, y_hi, spread, *refs):
    (_, early, out_ref, acc, listed, coefs), tables = refs[:6], refs[6:]
    size_x, size_y, size_z = cells
    n_z = 2 * size_z
    bins = bins_of(cells)
    places = [(i, j, k) for i in range(size_x + 2) for j in range(2) for k in range(n_z)]
    tiles = [(y_lo, y_hi)[j][i, 0, k] for i, j, k in places]
    count_s = counts_of(tiles)
    work = Groups(tables)
    for n, (bx, by, bz) in enumerate(bins):
        sources = []
        for x in (bx - 1, bx, bx + 1):
            for z in (bz - 1, bz, bz + 1):
                cell = places.index((x + 1, by, z % n_z))
                tile = tiles[cell] + shift_tile(cells, (x, (-1, size_y)[by], z))
                sources.append((tile, count_s[cell]))
        n_tiles = up_to(compact(listed, n * LIST_Y, sources), LANES)
        first_tile = n * LIST_Y
        work.add(up_to(count_ref[bx, by, bz], CHUNK), n_tiles, first_tile, n * LANES, n * LANES)
    work.run(listed, spread, coefs, acc)

    slot = lax.broadcasted_iota(jnp.int32, (1, LANES), 1)
    by_rows = lane_sums([acc[i, : len(bins) * LANES, :] for i in range(4)], len(bins))
    for n, (at, by_row) in enumerate(zip(bins, by_rows)):
        tile = own_ref[at]
        total = velocity_rows(cells, n, by_row, tile)
        total = total - (STOKES_NORM * SELF_C) * pltpu.roll(tile, ROWS - FORCE_ROW, 0)
        if n < EARLY:
            total = total + early[n]
        total = jnp.where(slot < count_ref[at], total, 0.0)
        for i in range(3):
            out_ref[i, at[0], at[1], at[2] : at[2] + 1, :] = total[i : i + 1]


def shifted(first, last, axis):
    size = lax.axis_size(axis)
    up = [(i, (i + 1) % size) for i in range(size)]
    if size % 2:
        down = [(j, i) for i, j in up]
        return lax.ppermute(last, axis, up), lax.ppermute(first, axis, down)
    odd = lax.rem(lax.axis_index(axis), 2) == 1
    got = []
    for parity in (0, 1):
        pairs = [pair for i, j in up if i % 2 == parity for pair in ((i, j), (j, i))]
        got.append(lax.ppermute(jnp.where(odd == bool(parity), last, first), axis, pairs))
    return jnp.where(odd, got[0], got[1]), jnp.where(odd, got[1], got[0])


def on_device(offsets, forces, counts):
    cells = offsets.shape[1:4]
    slots = offsets.shape[4]
    n_bins = cells[0] * cells[1] * cells[2]
    n_targets = n_bins * slots
    whole = pl.BlockSpec(memory_space=pltpu.VMEM)
    scalars = pl.BlockSpec(memory_space=pltpu.SMEM)

    def floats(*shape):
        return jax.ShapeDtypeStruct(shape, jnp.float32)

    def params(mib):
        return pltpu.CompilerParams(vmem_limit_bytes=mib << 20)

    loop_scratch = [pltpu.VMEM((UNITS, 2, CHUNK, LANES), jnp.float32)]
    loop_scratch += [pltpu.SMEM((2 * n_bins,), jnp.int32)] * 5
    cost = pl.CostEstimate(flops=1 << 28, bytes_accessed=1 << 16, transcendentals=1 << 20)

    def in_place(sums):
        return pltpu.with_memory_space_constraint(sums, pltpu.VMEM)

    def list_scratch(n_tiles):
        return [pltpu.VMEM((n_tiles, ROWS, LANES), jnp.float32)]

    own_list, all_targets = floats(n_bins + 1, ROWS, slots), floats(3, n_targets, slots)
    arguments = [pltpu.with_memory_space_constraint(x, pltpu.HBM) for x in (counts, offsets, forces)]
    sent, early = pl.pallas_call(
        functools.partial(pack_kernel, cells),
        out_shape=[floats(*cells, ROWS, slots), floats(EARLY, ROWS, slots)],
        in_specs=[pl.BlockSpec(memory_space=pltpu.HBM)] * 3,
        out_specs=[whole, whole],
        scratch_shapes=[
            pltpu.SMEM(counts.shape, jnp.int32),
            pltpu.VMEM(offsets.shape, jnp.float32),
            pltpu.VMEM(forces.shape, jnp.float32),
            pltpu.SemaphoreType.DMA((3,)),
            pltpu.VMEM(own_list.shape, jnp.float32),
            pltpu.VMEM((3, EARLY * slots, slots), jnp.float32),
            loop_scratch[0],
            pltpu.VMEM((4, EARLY * slots + CHUNK, slots), jnp.float32),
        ]
        + loop_scratch[1:],
        compiler_params=params(8),
        name="pack",
    )(*arguments)

    together = lax.optimization_barrier
    size = lax.axis_size("ha")
    other = lax.ppermute(sent, "ha", [(i, (i + 1) % size) for i in range(size)])
    own, listed, spread, first = pl.pallas_call(
        functools.partial(first_kernel, cells),
        out_shape=[sent, own_list, all_targets, floats(4, len(FIRST) * slots + CHUNK, slots)],
        in_specs=[whole],
        out_specs=[whole] * 4,
        scratch_shapes=loop_scratch,
        compiler_params=params(8),
        cost_estimate=cost,
        name="first",
    )(sent)
    other, own, listed, first = together((other, own, listed, first))
    column = jnp.concatenate([own, other], axis=2)
    x_lo, x_hi = shifted(column[:1], column[cells[0] - 1 :], "gx")
    second = pl.pallas_call(
        functools.partial(second_kernel, cells),
        out_shape=floats(4, n_targets + CHUNK, slots),
        in_specs=[scalars] + [whole] * 4,
        out_specs=whole,
        scratch_shapes=list_scratch(cells[2] * LIST_Z + n_bins + 1)
        + loop_scratch,
        compiler_params=params(8),
        cost_estimate=cost,
        name="second",
    )(counts, other, listed, spread, first)
    x_lo, x_hi, second = together((x_lo, x_hi, second))
    wide = jnp.concatenate([x_lo, column, x_hi], axis=0)
    y_lo, y_hi = shifted(wide[:, :1], wide[:, cells[1] - 1 :], "gy")
    middle = pl.pallas_call(
        functools.partial(middle_kernel, cells),
        out_shape=floats(4, n_targets + CHUNK, slots),
        in_specs=[scalars] + [whole] * 3,
        out_specs=whole,
        scratch_shapes=list_scratch(cells[0] * cells[2] * LIST_X) + loop_scratch,
        input_output_aliases={3: 0},
        compiler_params=params(8),
        cost_estimate=cost,
        name="middle",
    )(counts, wide, spread, in_place(second))
    y_hi, y_lo, middle = together((y_hi, y_lo, middle))
    return pl.pallas_call(
        functools.partial(last_kernel, cells),
        out_shape=[floats(3, *cells, slots), floats(4, n_targets + CHUNK, slots)],
        in_specs=[scalars] + [whole] * 6,
        out_specs=[whole, whole],
        scratch_shapes=list_scratch(n_bins * LIST_Y)
        + loop_scratch,
        input_output_aliases={5: 1},
        compiler_params=params(12),
        cost_estimate=cost,
        name="last",
    )(counts, own, y_lo, y_hi, spread, in_place(middle), early)[0]


def solution(mesh):
    in_specs = (
        P(None, "gx", "gy", "ha", None),
        P(None, "gx", "gy", "ha", None),
        P("gx", "gy", "ha"),
    )
    out_specs = P(None, "gx", "gy", "ha", None)
    return jax.shard_map(on_device, mesh=mesh, in_specs=in_specs, out_specs=out_specs, check_vma=False)
```
